32 devices in a mesh: dp: 4 (over z), expert: 8 (over y, x, core).
Axes of the slice: x: 2, y: 2, z: 4, core: 2. Of those that a mesh axis runs over, the one named last changes fastest.
Arguments:
- tokens: bfloat16 [4096, 1536], P(('dp', 'expert')), may hold values from -6 to 6
- w_qkv: bfloat16 [2, 1536, 2048], P(None, ('dp', 'expert')), may hold values from -0.15625 to 0.15625
- w_out: bfloat16 [2, 1536, 1536], P(None, ('dp', 'expert')), may hold values from -1.25 to 1.25
- w_router: bfloat16 [2, 1536, 16], P(None, ('dp', 'expert')), may hold values from -0.078125 to 0.078125
- norm_gains: bfloat16 [2, 2, 1536], P(None, None, ('dp', 'expert')), may hold values from 0.099609375 to 1.8984375
- w_gate: bfloat16 [2, 16, 1536, 768], P(None, 'expert'), may hold values from -0.15625 to 0.15625
- w_up: bfloat16 [2, 16, 1536, 768], P(None, 'expert'), may hold values from -0.15625 to 0.15625
- w_down: bfloat16 [2, 16, 768, 1536], P(None, 'expert'), may hold values from -0.4375 to 0.4375
- out_grad: bfloat16 [4096, 1536], P(('dp', 'expert')), may hold values from -6 to 6
- segment_ids: int32 [4096], P(('dp', 'expert')), may hold values from 0 to 67, as said below
- routes: int32 [2, 4096, 4], P(None, ('dp', 'expert')), may hold values from 0 to 15, all different within a row; in each aligned block of 128 rows (0 to 127, 128 to 255, ..., all dimensions but the last counted through in order) at most 64 rows name the same one
- pair_order: int32 [2, 32, 512], P(None, ('dp', 'expert')), may hold values from 0 to 511, each once within a row
Outputs:
- layer_outs: bfloat16 [2, 4096, 1536], P(None, ('dp', 'expert'))
- tokens_grad: float32 [4096, 1536], P(('dp', 'expert'))
- grad_qkv: float32 [2, 1536, 2048], P(None, ('dp', 'expert'))
- grad_out: float32 [2, 1536, 1536], P(None, ('dp', 'expert'))
- grad_router: float32 [2, 1536, 16], P(None, ('dp', 'expert'))
- grad_gains: float32 [2, 2, 1536], P(None, None, ('dp', 'expert'))
- grad_gate: float32 [2, 16, 1536, 768], P(None, 'expert', 'dp')
- grad_up: float32 [2, 16, 1536, 768], P(None, 'expert', 'dp')
- grad_down: float32 [2, 16, 768, 1536], P(None, 'expert', None, 'dp')
The draws below stay inside these ranges and needn't reach their ends.
Inputs may be any that keep to these rules, and one draw needn't show every extreme that they name: `segment_ids`: never falling; a new document starts at every multiple of 1024; each document lies within the tokens of at most two devices that are next to each other along dp+expert. `routes`: each token names 4 different experts; among one device's tokens of one layer no expert is named more than 64 times, a bound that some block reaches. `pair_order`: for each layer and device a permutation of the device's pairs, pair t * 4 + k being the k-th route of its t-th token.
All inputs are finite; a program needn't handle non-finite values.
Results may differ from the reference program's by a relative error of at most 0.023.
Values may be sent and summed in bfloat16 or wider, within the bound.
A program may use at most 256 MiB of HBM per device.

```python
import math
import jax
import jax.numpy as jnp
import numpy as np
from jax import lax

D = 1536
QUERY_HEADS = 12
KEY_VALUE_HEADS = 2
HEAD_SIZE = 128
FF = 768
EXPERTS = 16
TOPK = 4
LAYERS = 2
DEVICE_TOKENS = 128
LENGTH = 1024
QD = 1536
QKV = 2048
TOKENS = 4096
MOST = 64
CAP = 288
N_DP = 4
N_EXPERT = 8


def draw_segment_ids(key, part):
    key = jax.random.fold_in(key, 7)
    block_count = TOKENS // DEVICE_TOKENS
    key_one, second = jax.random.split(key)
    lead_in = jax.random.randint(key_one, (block_count,), 1, DEVICE_TOKENS // 4 + 1)
    widths = jax.random.randint(second, (block_count,), DEVICE_TOKENS // 4, 3 * DEVICE_TOKENS // 4)
    places = jnp.arange(TOKENS, dtype=jnp.int32)
    block_of = places // DEVICE_TOKENS
    offset = places % DEVICE_TOKENS
    starts = (offset == lead_in[block_of]) | (offset == lead_in[block_of] + widths[block_of]) | (places % LENGTH == 0)
    return (jnp.cumsum(starts.astype(jnp.int32)) - 1).astype(jnp.int32)


def level_of(own_key, shape, cuts, smallest, largest):
    level = 1.0
    for dim, blocks in cuts:
        steps = jax.random.uniform(jax.random.fold_in(jax.random.fold_in(own_key, 6), dim), (blocks,), jnp.float32, smallest / len(cuts), largest / len(cuts))
        level = level * jnp.repeat(jnp.exp(steps), shape[dim] // blocks).reshape((-1,) + (1,) * (len(shape) - 1 - dim))
    return level


def shared_out(own_key, own, number, rows, number_of, top, most, skew):
    order = jax.random.permutation(own_key, number_of)
    packed, usual = portions_of(number_of, rows * top, most, skew, True), portions_of(number_of, rows * top, most, skew, False)
    places = jnp.arange(number_of)

    def named(sizes, turn):
        used = int((sizes > 0).sum())
        fixed = max(1, used // 4)
        passed = fixed + (places - fixed + turn * (used - fixed)) % max(1, number_of - fixed)
        return jnp.zeros((number_of,), jnp.int32).at[order[jnp.where(places < fixed, places, passed)]].set(jnp.asarray(sizes, jnp.int32))

    sizes = jnp.where(number % 4 == 0, named(packed, number // 4), named(usual, number - number // 4 - 1))
    mixed = jax.random.permutation(jax.random.fold_in(own, 3), number_of)
    donor, receiver = mixed[0:number_of // 2 * 2:2], mixed[1:number_of // 2 * 2:2]
    slack = jnp.minimum(sizes[donor] - 1, most - sizes[receiver]) // 2
    slack = jnp.where((donor == order[0]) | (receiver == order[0]) | (sizes[receiver] == 0), 0, jnp.maximum(slack, 0))
    passed = jax.random.randint(jax.random.fold_in(own, 4), (number_of // 2,), 0, 1 << 20) % (slack + 1)
    sizes = sizes.at[donor].add(-passed).at[receiver].add(passed)
    items = jnp.searchsorted(jnp.cumsum(sizes), jnp.arange(rows * top), side="right").astype(jnp.int32)
    grid = items.reshape(top, rows).T
    grid = grid[jax.random.permutation(jax.random.fold_in(own, 1), rows)]
    turn = jax.random.randint(jax.random.fold_in(own, 2), (rows, 1), 0, top)
    return jnp.take_along_axis(grid, (jnp.arange(top)[None, :] + turn) % top, axis=1)


def portions_of(number_of, total, reach, slope, full):
    loads = [(1 << 20) // math.isqrt(rank ** slope) + 1 for rank in range(1, number_of + 1)]
    largest = reach if full else min(reach, max(-(-total // number_of), total * loads[0] // sum(loads)))
    least = 1 if total - largest >= number_of - 1 else 0
    holding, surplus = [largest] + [least] * (number_of - 1), total - largest - least * (number_of - 1)
    while surplus > 0:
        candidates = [i for i in range(1, number_of) if holding[i] < largest] or [i for i in range(1, number_of) if holding[i] < reach]
        whole, remaining = sum([loads[i] for i in candidates]), surplus
        for i in candidates:
            extra = min(reach - holding[i], max(1, remaining * loads[i] // whole), surplus)
            holding[i] = holding[i] + extra
            surplus = surplus - extra
    return np.array(holding)


def noise(key, dims, spread, reach, pieces=(), held_as=jnp.bfloat16):
    array = jax.random.normal(key, dims, jnp.float32) * spread
    if len(pieces) > 0:
        array = level_of(key, dims, pieces, -0.22, 0.18) * array
    return jnp.clip(array, min=-reach, max=reach).astype(held_as)


def setup_inputs(seed: int = 0) -> dict:
    key_of = jax.random.split(jax.random.key(seed), 13)
    tokens = noise(key_of[0], (TOKENS, D), 1.0, 6.0, ((0, 32),))
    w_qkv = noise(key_of[1], (LAYERS, D, QKV), D ** -0.5, 0.15625, ((1, 32),))
    w_out = noise(key_of[2], (LAYERS, QD, D), (QD // 64) ** -0.5, 1.25, ((1, 32),))
    w_router = noise(key_of[3], (LAYERS, D, EXPERTS), (4 * D) ** -0.5, 0.078125, ((1, 32),))
    norm_gains = jnp.clip(1.0 + 0.18 * jax.random.normal(key_of[4], (LAYERS, 2, D), jnp.float32), 0.099609375, 1.8984375).astype(jnp.bfloat16)
    w_gate = noise(key_of[5], (LAYERS, EXPERTS, D, FF), D ** -0.5, 0.15625, ((1, 8),))
    w_up = noise(key_of[6], (LAYERS, EXPERTS, D, FF), D ** -0.5, 0.15625, ((1, 8),))
    w_down = noise(key_of[7], (LAYERS, EXPERTS, FF, D), (FF // 4) ** -0.5, 0.4375, ((1, 8),))
    out_grad = noise(key_of[8], (TOKENS, D), 1.0, 6.0, ((0, 32),))
    segment_ids = draw_segment_ids(jax.random.fold_in(key_of[12], 71), 0)
    routes_keys = jax.random.split(jax.random.fold_in(key_of[10], 1), LAYERS * TOKENS // DEVICE_TOKENS)
    routes_turns = jax.random.permutation(jax.random.fold_in(key_of[10], 3), LAYERS * TOKENS // DEVICE_TOKENS)
    routes = jax.vmap(lambda own, number: shared_out(jax.random.fold_in(key_of[10], 2), own, number, DEVICE_TOKENS, EXPERTS, TOPK, MOST, 2))(routes_keys, routes_turns).reshape((LAYERS, TOKENS, TOPK))
    pair_order = jax.vmap(lambda own: jax.random.permutation(own, DEVICE_TOKENS * TOPK))(jax.random.split(key_of[11], LAYERS * (N_DP * N_EXPERT))).reshape((LAYERS, N_DP * N_EXPERT, DEVICE_TOKENS * TOPK)).astype(jnp.int32)
    return {"tokens": tokens, "w_qkv": w_qkv, "w_out": w_out, "w_router": w_router, "norm_gains": norm_gains, "w_gate": w_gate, "w_up": w_up, "w_down": w_down, "out_grad": out_grad, "segment_ids": segment_ids, "routes": routes, "pair_order": pair_order}


epsilon = 1e-06
rope_base = 1000000.0
masked_score = -1e+30
highest = lax.Precision.HIGHEST

@jax.custom_vjp
def reduced_precision(v):
    return lax.optimization_barrier(v.astype(jnp.bfloat16)).astype(jnp.float32)

@jax.custom_vjp
def low_back(v):
    return v

def low_keep(v):
    return (reduced_precision(v), None)

def low_pass(kept, grad):
    return (grad,)

def back_keep(v):
    return (v, None)

def back_low(kept, grad):
    return (reduced_precision(grad),)
reduced_precision.defvjp(low_keep, low_pass)
low_back.defvjp(back_keep, back_low)

def rms_norm(stream, gain_row):
    return stream * lax.rsqrt(lax.optimization_barrier(jnp.mean(stream * stream, axis=-1, keepdims=True)) + epsilon) * gain_row

def apply_rotary(heads_in, token_positions):
    half_dim = heads_in.shape[-1] // 2
    steps_up = jnp.arange(half_dim).astype(jnp.float32)
    frequency = jnp.exp(steps_up * (-2.0 * math.log(rope_base) / heads_in.shape[-1]))
    angles = token_positions.astype(jnp.float32)[:, None] * frequency[None, :]
    cosine = jnp.cos(angles)[:, None, :]
    sine_part = jnp.sin(angles)[:, None, :]
    first_half = heads_in[..., :half_dim]
    second_half = heads_in[..., half_dim:]
    return jnp.concatenate([first_half * cosine - second_half * sine_part, second_half * cosine + first_half * sine_part], axis=-1)

def attend_block(inputs):
    query_rows, keys_prev, keys_own, values_prev, values_own, seg_prev, seg_own, has_prev = inputs
    rows_per_block = query_rows.shape[0]
    queries_per_group = QUERY_HEADS // KEY_VALUE_HEADS
    gathered_keys = jnp.concatenate([keys_prev, keys_own], axis=0)
    gathered_values = jnp.concatenate([values_prev, values_own], axis=0)
    grouped_queries = query_rows.reshape(rows_per_block, KEY_VALUE_HEADS, queries_per_group, HEAD_SIZE)
    score_scale = 1.0 / math.sqrt(HEAD_SIZE)
    scores = low_back(jnp.einsum('tkgd,skd->kgts', grouped_queries, gathered_keys, precision=highest) * score_scale)
    index_row = jnp.arange(rows_per_block)
    own_mask = (seg_own[None, :] == seg_own[:, None]) & (index_row[None, :] <= index_row[:, None])
    prev_mask = (seg_prev[None, :] == seg_own[:, None]) & has_prev
    allowed = jnp.concatenate([prev_mask, own_mask], axis=1)
    scores = jnp.where(allowed, scores, masked_score)
    weights = reduced_precision(jax.nn.softmax(scores, axis=-1))
    attended = jnp.einsum('kgts,skd->tkgd', weights, gathered_values, precision=highest)
    return attended.reshape(rows_per_block, QUERY_HEADS * HEAD_SIZE)

def local_rank(pair_args):
    chosen, priority = pair_args
    same_expert = chosen[:, None] == chosen[None, :]
    earlier = priority[None, :] < priority[:, None]
    return lax.optimization_barrier(jnp.sum((same_expert & earlier).astype(jnp.int32), axis=1)).astype(jnp.int32)

def place_pairs(routes_l, order_l):
    devices_n = order_l.shape[0]
    pair_count = DEVICE_TOKENS * TOPK
    chosen = routes_l.reshape(devices_n, pair_count).astype(jnp.int32)
    pair_rank = lax.map(local_rank, (chosen, order_l.astype(jnp.int32)))
    counts = lax.optimization_barrier(jnp.sum((chosen[:, :, None] == jnp.arange(EXPERTS).astype(jnp.int32)[None, None, :]).astype(jnp.int32), axis=1))
    counts = counts.reshape(N_DP, N_EXPERT, EXPERTS)
    before = (jnp.cumsum(counts, axis=1) - counts).reshape(devices_n, EXPERTS).astype(jnp.int32)
    seat_of = (jnp.take_along_axis(before, chosen, axis=1) + pair_rank).astype(jnp.int32)
    device_of = jnp.broadcast_to(jnp.arange(devices_n).astype(jnp.int32)[:, None], (devices_n, pair_count))
    group_of = (device_of // N_EXPERT).astype(jnp.int32)
    token_of = (device_of * DEVICE_TOKENS + jnp.arange(pair_count).astype(jnp.int32)[None, :] // TOPK).astype(jnp.int32)
    seat_token = jnp.zeros((N_DP, EXPERTS, CAP), jnp.int32).at[group_of, chosen, seat_of].set(token_of, mode='drop')
    filled = jnp.zeros((N_DP, EXPERTS, CAP), jnp.int32).at[group_of, chosen, seat_of].set(1, mode='drop')
    kept_pair = seat_of < CAP
    seat_clip = jnp.minimum(seat_of, CAP - 1).astype(jnp.int32)
    return (seat_token, filled, group_of, chosen, seat_clip, kept_pair)

def one_layer(stream, w_qkv_l, w_out_l, w_router_l, gain_l, w_gate_l, w_up_l, w_down_l, seg_ids, token_positions, placed, routes_l):
    seat_token, filled, group_of, chosen, seat_clip, kept_pair = placed
    row_count_total = stream.shape[0]
    query_width = QUERY_HEADS * HEAD_SIZE
    key_width = KEY_VALUE_HEADS * HEAD_SIZE
    normed_a = reduced_precision(rms_norm(stream, gain_l[0]))
    projected_output = low_back(jnp.dot(normed_a, w_qkv_l, precision=highest))
    query_rows = reduced_precision(apply_rotary(projected_output[:, :query_width].reshape(row_count_total, QUERY_HEADS, HEAD_SIZE), token_positions))
    gathered_keys = reduced_precision(apply_rotary(projected_output[:, query_width:query_width + key_width].reshape(row_count_total, KEY_VALUE_HEADS, HEAD_SIZE), token_positions))
    gathered_values = reduced_precision(projected_output[:, query_width + key_width:].reshape(row_count_total, KEY_VALUE_HEADS, HEAD_SIZE))
    block_count = row_count_total // DEVICE_TOKENS
    query_blocks = query_rows.reshape(block_count, DEVICE_TOKENS, QUERY_HEADS, HEAD_SIZE)
    blocked_keys = gathered_keys.reshape(block_count, DEVICE_TOKENS, KEY_VALUE_HEADS, HEAD_SIZE)
    blocked_values = gathered_values.reshape(block_count, DEVICE_TOKENS, KEY_VALUE_HEADS, HEAD_SIZE)
    key_prev = jnp.concatenate([jnp.zeros_like(blocked_keys[:1]), blocked_keys[:-1]], axis=0)
    value_prev = jnp.concatenate([jnp.zeros_like(blocked_values[:1]), blocked_values[:-1]], axis=0)
    seg_blocks = seg_ids.reshape(block_count, DEVICE_TOKENS)
    seg_prev = jnp.concatenate([jnp.zeros_like(seg_blocks[:1]), seg_blocks[:-1]], axis=0)
    has_prev = jnp.arange(block_count) > 0
    attended = lax.map(jax.checkpoint(attend_block), (query_blocks, key_prev, blocked_keys, value_prev, blocked_values, seg_prev, seg_blocks, has_prev))
    attended = low_back(reduced_precision(attended.reshape(row_count_total, query_width)))
    mixed_sum = stream + low_back(jnp.dot(attended, w_out_l, precision=highest))
    normed_b = reduced_precision(rms_norm(mixed_sum, gain_l[1]))
    logits = low_back(jnp.dot(normed_b, w_router_l, precision=highest))
    gate_soft = jax.nn.softmax(jnp.take_along_axis(logits, routes_l, axis=1), axis=-1)
    expert_in = low_back(jnp.where(filled[..., None] > 0, normed_b[seat_token], 0.0))
    gate_pre = low_back(jnp.einsum('recd,edf->recf', expert_in, w_gate_l, precision=highest))
    up_pre = low_back(jnp.einsum('recd,edf->recf', expert_in, w_up_l, precision=highest))
    hidden = reduced_precision(jax.nn.silu(gate_pre) * up_pre)
    expert_out = low_back(reduced_precision(jnp.einsum('recf,efd->recd', hidden, w_down_l, precision=highest)))
    pair_out = expert_out[group_of, chosen, seat_clip]
    pair_weight = gate_soft.reshape(chosen.shape) * kept_pair.astype(jnp.float32)
    branch = lax.optimization_barrier(jnp.sum((pair_weight[..., None] * pair_out).reshape(row_count_total, TOPK, D), axis=1))
    return mixed_sum + branch

def reference(tokens, w_qkv, w_out, w_router, norm_gains, w_gate, w_up, w_down, out_grad, segment_ids, routes, pair_order):
    row_count_total = tokens.shape[0]
    token_positions = (jnp.arange(row_count_total) % LENGTH).astype(jnp.int32)
    placed_all = [place_pairs(routes[layer_idx], pair_order[layer_idx]) for layer_idx in range(LAYERS)]

    def forward(stream, qkv_all, out_all, router_all, gains_all, gate_all, up_all, down_all):
        outputs = []
        for layer_idx in range(LAYERS):
            stream = one_layer(stream, qkv_all[layer_idx], out_all[layer_idx], router_all[layer_idx], gains_all[layer_idx], gate_all[layer_idx], up_all[layer_idx], down_all[layer_idx], segment_ids, token_positions, placed_all[layer_idx], routes[layer_idx])
            outputs.append(stream)
        return (stream, jnp.stack(outputs))
    final_stream, pull_back, layer_stack = jax.vjp(forward, tokens.astype(jnp.float32), w_qkv.astype(jnp.float32), w_out.astype(jnp.float32), w_router.astype(jnp.float32), norm_gains.astype(jnp.float32), w_gate.astype(jnp.float32), w_up.astype(jnp.float32), w_down.astype(jnp.float32), has_aux=True)
    gradients = pull_back(out_grad.astype(jnp.float32))
    return (layer_stack.astype(jnp.bfloat16), gradients[0], gradients[1], gradients[2], gradients[3], gradients[4], gradients[5], gradients[6], gradients[7])
```

```python
from functools import partial
import math

import jax
import jax.numpy as jnp
from jax import lax
from jax.experimental import pallas as pl
from jax.experimental.pallas import tpu as pltpu
from jax.sharding import PartitionSpec as P

D = 1536
QUERY_HEADS = 12
KEY_VALUE_HEADS = 2
HEAD_SIZE = 128
MESH = pl.DeviceIdType.MESH
DP, EX = "dp", "expert"
ANY = pl.ANY
bf16 = jnp.bfloat16
f32 = jnp.float32

epsilon = 1e-06
rope_base = 1000000.0
masked_score = -1e30
everywhere = (DP, EX)


def place():
    z = lax.axis_index(DP)
    e = lax.axis_index(EX)
    y, x, c = e // 4, (e // 2) % 2, e % 2
    near = {
        "own": e,
        "x": y * 4 + (1 - x) * 2 + c,
        "y": (1 - y) * 4 + x * 2 + c,
        "d": (1 - y) * 4 + (1 - x) * 2 + c,
        "c": y * 4 + x * 2 + (1 - c),
        "cx": y * 4 + (1 - x) * 2 + (1 - c),
        "cy": (1 - y) * 4 + x * 2 + (1 - c),
        "cd": (1 - y) * 4 + (1 - x) * 2 + (1 - c),
    }
    return z, near


def greet(z, near, plane, line):
    barrier = pltpu.get_barrier_semaphore()
    for name in plane:
        pl.semaphore_signal(
            barrier, inc=1, device_id={EX: near[name]}, device_id_type=MESH
        )
    count = len(plane)
    if line is None:
        pl.semaphore_wait(barrier, count)
        return

    @pl.when(z < line - 1)
    def up():
        pl.semaphore_signal(barrier, inc=1, device_id={DP: z + 1}, device_id_type=MESH)

    @pl.when(z > 0)
    def down():
        pl.semaphore_signal(barrier, inc=1, device_id={DP: z - 1}, device_id_type=MESH)

    inside = (z > 0) & (z < line - 1)

    @pl.when(inside)
    def wait_inside():
        pl.semaphore_wait(barrier, count + 2)

    @pl.when(jnp.logical_not(inside))
    def wait_end():
        pl.semaphore_wait(barrier, count + 1)


def halves(rows, columns):
    if rows % 32 == 0:
        return ((0, rows // 2), (0, columns)), ((rows // 2, rows // 2), (0, columns))
    if columns % 256 == 0:
        return ((0, rows), (0, columns // 2)), ((0, rows), (columns // 2, columns // 2))
    return ((0, 16), (0, columns)), ((16, rows - 16), (0, columns))


def cut(ref, part):
    (row, rows), (column, columns) = part
    return ref.at[pl.ds(row, rows), pl.ds(column, columns)]


KINDS = 10


class Gather:
    def __init__(self, ins, outs, send, recv, z, near, line):
        self.ins, self.outs, self.send, self.recv = ins, outs, send, recv
        self.z, self.near, self.line = z, near, line
        self.parts = [halves(*ref.shape) for ref in ins]
        self.all = range(len(ins))

    def hop(self, a, j, kind, whose, to, part=None, src=None):
        dst = self.outs[a].at[j, self.near[whose]]
        src = dst if src is None else src
        if part is not None:
            src, dst = cut(src, part), cut(dst, part)
        return pltpu.make_async_remote_copy(
            src_ref=src,
            dst_ref=dst,
            send_sem=self.send.at[a, j, kind],
            recv_sem=self.recv.at[a, j, kind],
            device_id={DP: to} if kind >= 8 else {EX: self.near[to]},
            device_id_type=MESH,
        )

    def landed(self, a, j, kind, whose, part=None):
        if kind < 8:
            self.hop(a, j, kind, whose, "c", part).wait_recv()
        else:
            self.hop(a, j, kind, whose, self.z).wait_recv()

    def line_first(self):
        z = self.z

        @pl.when(z < self.line - 1)
        def up_first():
            for a in self.all:
                self.hop(a, z, 8, "own", z + 1, src=self.ins[a]).start()

        @pl.when(z > 0)
        def down_first():
            for a in self.all:
                self.hop(a, z, 9, "own", z - 1, src=self.ins[a]).start()

    def first(self, j, src=None):
        for a in self.all:
            one = None if src is None else src[a]
            self.hop(a, j, 0, "own", "x", src=one).start()
            self.hop(a, j, 1, "own", "y", src=one).start()
            self.hop(a, j, 2, "own", "c", src=one).start()

    def second(self, j, kind=0):
        for a in self.all:
            self.landed(a, j, 0, "x")
            self.hop(a, j, 4, "x", "y", self.parts[a][1]).start()
            self.hop(a, j, 5, "x", "c").start()
            self.landed(a, j, 1, "y")
            self.hop(a, j, 3, "y", "x", self.parts[a][0]).start()
            self.hop(a, j, 6, "y", "c").start()

    def third(self, j, kind=0):
        for a in self.all:
            self.landed(a, j, 3, "d", self.parts[a][0])
            self.landed(a, j, 4, "d", self.parts[a][1])
            self.hop(a, j, 7, "d", "c").start()

    def finish(self, j, kind=0):
        for a in self.all:
            for kind, whose in ((2, "c"), (5, "cx"), (6, "cy"), (7, "cd")):
                self.landed(a, j, kind, whose)
            for kind in (0, 1, 2):
                self.hop(a, j, kind, "own", "c").wait_send()
            self.hop(a, j, 3, "y", "x", self.parts[a][0]).wait_send()
            self.hop(a, j, 4, "x", "y", self.parts[a][1]).wait_send()
            for kind in (5, 6, 7):
                self.hop(a, j, kind, "x", "c").wait_send()

    def arrivals(self, step, act):
        z = self.z

        @pl.when(z - step >= 0)
        def below():
            act(z - step, 8)

        @pl.when(z + step <= self.line - 1)
        def above():
            act(z + step, 9)

    def take(self, j, kind):
        for a in self.all:
            self.landed(a, j, kind, "own")
        z = self.z
        if kind == 8:

            @pl.when(z < self.line - 1)
            def on_up():
                for a in self.all:
                    self.hop(a, j, 8, "own", z + 1).start()

        else:

            @pl.when(z > 0)
            def on_down():
                for a in self.all:
                    self.hop(a, j, 9, "own", z - 1).start()

        self.first(j)

    def line_done(self):
        z = self.z
        for step in range(self.line):

            @pl.when((z - step >= 0) & (z < self.line - 1))
            def up_done():
                for a in self.all:
                    self.hop(a, z - step, 8, "own", z + 1).wait_send()

            @pl.when((z + step <= self.line - 1) & (z > 0))
            def down_done():
                for a in self.all:
                    self.hop(a, z + step, 9, "own", z - 1).wait_send()


def gather_kernel(n_arrays, line, *refs):
    ins, outs = refs[:n_arrays], refs[n_arrays : 2 * n_arrays]
    send, recv, keep = refs[2 * n_arrays :]
    z, near = place()
    g = Gather(ins, outs, send, recv, z, near, line)
    greet(z, near, ("x", "y", "c"), line)
    local = [
        pltpu.make_async_copy(ins[a], outs[a].at[z, near["own"]], keep.at[a])
        for a in range(n_arrays)
    ]
    g.line_first()
    g.first(z, ins)
    for copy_here in local:
        copy_here.start()
    g.arrivals(1, g.take)
    g.second(z)
    g.arrivals(2, g.take)
    g.third(z)
    g.arrivals(1, g.second)
    g.arrivals(3, g.take)
    g.arrivals(1, g.third)
    g.arrivals(2, g.second)
    g.arrivals(2, g.third)
    g.arrivals(3, g.second)
    g.arrivals(3, g.third)
    g.finish(z)
    for step in range(1, line):
        g.arrivals(step, g.finish)
    for copy_here in local:
        copy_here.wait()
    g.line_done()


def fast_mesh():
    return lax.axis_size(DP) == 4 and lax.axis_size(EX) == 8


def gather_all(shards, number):
    n_dp, n_expert = lax.axis_size(DP), lax.axis_size(EX)
    if not fast_mesh():
        return [
            lax.all_gather(shard, everywhere, axis=0).reshape((n_dp, n_expert) + shard.shape)
            for shard in shards
        ]
    n_arrays = len(shards)
    return pl.pallas_call(
        partial(gather_kernel, n_arrays, n_dp),
        out_shape=[
            jax.ShapeDtypeStruct((n_dp, n_expert) + shard.shape, shard.dtype) for shard in shards
        ],
        in_specs=[pl.BlockSpec(memory_space=ANY)] * n_arrays,
        out_specs=[pl.BlockSpec(memory_space=ANY)] * n_arrays,
        scratch_shapes=[
            pltpu.SemaphoreType.DMA((n_arrays, n_dp, KINDS)),
            pltpu.SemaphoreType.DMA((n_arrays, n_dp, KINDS)),
            pltpu.SemaphoreType.DMA((n_arrays,)),
        ],
        compiler_params=pltpu.CompilerParams(collective_id=number, has_side_effects=True),
        name="gather_all",
    )(*shards)


def plane_gather(src, dst, send, recv, near):
    parts = halves(*src.shape)

    def hop(kind, whose, to, part=None):
        one = dst.at[near[whose]] if part is None else cut(dst.at[near[whose]], part)
        return pltpu.make_async_remote_copy(
            src_ref=src if whose == "own" else one,
            dst_ref=one,
            send_sem=send.at[kind],
            recv_sem=recv.at[kind],
            device_id={EX: near[to]},
            device_id_type=MESH,
        )

    def first():
        hop(0, "own", "x").start()
        hop(1, "own", "y").start()
        hop(2, "own", "c").start()
        dst[near["own"]] = src[...]

    def second():
        hop(0, "x", "c").wait_recv()
        hop(4, "x", "y", parts[1]).start()
        hop(5, "x", "c").start()
        hop(1, "y", "c").wait_recv()
        hop(3, "y", "x", parts[0]).start()
        hop(6, "y", "c").start()

    def third():
        hop(3, "d", "c", parts[0]).wait_recv()
        hop(4, "d", "c", parts[1]).wait_recv()
        hop(7, "d", "c").start()

    def finish():
        for kind, whose in ((2, "c"), (5, "cx"), (6, "cy"), (7, "cd")):
            hop(kind, whose, "c").wait_recv()
        for kind in (0, 1, 2):
            hop(kind, "own", "c").wait_send()
        hop(3, "y", "x", parts[0]).wait_send()
        hop(4, "x", "y", parts[1]).wait_send()
        for kind in (5, 6, 7):
            hop(kind, "x", "c").wait_send()

    return first, second, third, finish


def sum_scratch(rows, columns):
    return [
        pltpu.VMEM((8, rows, columns), bf16),
        pltpu.VMEM((3, rows, columns), bf16),
        pltpu.VMEM((4, rows, columns), bf16),
        pltpu.VMEM((2, rows // 2, columns), bf16),
        pltpu.VMEM((2, rows // 2, columns), bf16),
        pltpu.VMEM((2, rows // 2, columns), bf16),
        pltpu.SemaphoreType.DMA((10,)),
        pltpu.SemaphoreType.DMA((10,)),
    ]


def plane_sum(make, out_ref, base, scratch, near):
    part_ref, paired, fromc, fromx, fromy, last, send, recv = scratch
    rows = out_ref.shape[0]
    half = rows // 2
    A, B = pl.ds(0, half), pl.ds(half, half)

    def copy(number, src, dst, to):
        return pltpu.make_async_remote_copy(
            src_ref=src,
            dst_ref=dst,
            send_sem=send.at[number],
            recv_sem=recv.at[number],
            device_id={EX: near[to]},
            device_id_type=MESH,
        )

    order = ("d", "x", "y", "own")
    across = ("cd", "cx", "cy", "c")
    core = [copy(s, part_ref.at[near[name]], fromc.at[s], "c") for s, name in enumerate(across)]
    to_x = [copy(4, paired.at[0, A], fromx.at[0], "x"), copy(5, paired.at[1, A], fromx.at[1], "x")]
    to_y = [copy(6, paired.at[0, B], fromy.at[0], "y"), copy(7, paired.at[2, B], fromy.at[1], "y")]
    late_y = copy(8, paired.at[2, A], last.at[0], "y")
    late_x = copy(9, paired.at[1, B], last.at[1], "x")

    def pair(s):
        core[s].wait_recv()
        paired[s] = (part_ref[near[order[s]]].astype(f32) + fromc[s].astype(f32)).astype(bf16)

    for s in range(3):
        make(across[s])
        core[s].start()
        make(order[s])
    pair(0)
    to_x[0].start()
    to_y[0].start()
    make(across[3])
    core[3].start()
    pair(1)
    to_x[1].start()
    pair(2)
    to_y[1].start()
    make(order[3])
    core[3].wait_recv()
    total = part_ref[near["own"]].astype(f32) + fromc[3].astype(f32)
    out_ref[...] = total if base is None else base[...] + total
    to_x[0].wait_recv()
    paired[2, A] = (paired[2, A].astype(f32) + fromx[0].astype(f32)).astype(bf16)
    late_y.start()
    to_y[0].wait_recv()
    paired[1, B] = (paired[1, B].astype(f32) + fromy[0].astype(f32)).astype(bf16)
    late_x.start()
    to_x[1].wait_recv()
    out_ref[A] += fromx[1].astype(f32)
    to_y[1].wait_recv()
    out_ref[B] += fromy[1].astype(f32)
    late_y.wait_recv()
    out_ref[A] += last[0].astype(f32)
    late_x.wait_recv()
    out_ref[B] += last[1].astype(f32)
    for one in core + to_x + to_y + [late_x, late_y]:
        one.wait_send()


def mul(a, b, over=((1,), (0,))):
    return lax.dot_general(a, b, (over, ((), ())), preferred_element_type=f32)


LAST = ((1,), (1,))


def seat_rows(seats, number):
    local_n, tokens_n = seats.shape
    rows = lax.broadcasted_iota(jnp.int32, (local_n * number, tokens_n), 0)
    hot = rows < 0
    for e in range(local_n):
        one = seats[e : e + 1, :]
        hot = hot | ((rows == one + (e * number - 1)) & (one > 0) & (one <= number))
    return jnp.where(hot, 1.0, 0.0).astype(bf16)


def seat_columns(seats, number):
    tokens_n, local_n = seats.shape
    columns = lax.broadcasted_iota(jnp.int32, (tokens_n, local_n * number), 1)
    hot = columns < 0
    for e in range(local_n):
        one = seats[:, e : e + 1]
        hot = hot | ((columns == one + (e * number - 1)) & (one > 0) & (one <= number))
    return jnp.where(hot, 1.0, 0.0).astype(bf16)


def masked_gates(logits, hit):
    top = jnp.max(jnp.where(hit, logits, masked_score), axis=0, keepdims=True)
    powers = jnp.where(hit, jnp.exp(jnp.where(hit, logits - top, 0.0)), 0.0)
    return powers / jnp.sum(powers, axis=0, keepdims=True)


def expert_kernel(
    layer,
    number,
    normed,
    mixed,
    router,
    hit,
    seats,
    seats_turned,
    w_gate,
    w_up,
    w_down,
    new_stream,
    rows_in,
    gate_pre,
    up_pre,
    gate_seat,
    tokens,
    gates,
    weighted,
    gate_w,
    up_w,
    down_w,
    weight_sem,
    send,
    recv,
    *scratch,
):
    z, near = place()
    local_n = seats.shape[0]
    rows = normed.shape[0]
    weights = [
        pltpu.make_async_copy(src.at[layer], dst, weight_sem.at[i])
        for i, (src, dst) in enumerate(((w_gate, gate_w), (w_up, up_w), (w_down, down_w)))
    ]
    greet(z, near, ("x", "y", "c"), None)
    first, second, third, finish = plane_gather(normed, tokens, send, recv, near)
    first()
    for one in weights:
        one.start()
    second()
    third()
    finish()
    everyone = tokens[...].reshape(-1, tokens.shape[2])
    gates[...] = masked_gates(mul(router[...], everyone, LAST), hit[...] > 0)
    pick = seat_rows(seats[...], number)
    for e in range(local_n):
        here = pl.ds(e * number, number)
        mine = gates[pl.ds(lax.axis_index(EX) * local_n + e, 1), :]
        gate_seat[here] = jnp.sum(
            pick[e * number : (e + 1) * number].astype(f32) * mine, axis=1, keepdims=True
        )
    rows_in[...] = mul(pick, everyone).astype(bf16)
    for one in weights:
        one.wait()

    def expert(e, carry):
        here = pl.ds(pl.multiple_of(e * number, 32), number)
        x = rows_in[here]
        gate = mul(x, gate_w[e])
        up = mul(x, up_w[e])
        gate_pre[here] = gate
        up_pre[here] = up
        hidden = (gate * (1.0 / (1.0 + jnp.exp(-gate))) * up).astype(bf16)
        weighted[here] = (mul(hidden, down_w[e]) * gate_seat[here]).astype(bf16)
        return carry

    lax.fori_loop(0, local_n, expert, 0)

    def make(name):
        d = near[name]
        back = seat_columns(seats_turned[pl.ds(pl.multiple_of(d * rows, rows), rows)], number)
        scratch[0][d] = mul(back, weighted[...]).astype(bf16)

    plane_sum(make, new_stream, mixed, scratch, near)


def expert_back_kernel(
    layer,
    number,
    experts_n,
    grads,
    seats,
    seats_turned,
    gate_pre,
    up_pre,
    gate_seat,
    w_gate,
    w_up,
    w_down,
    summed,
    rows_grad,
    hidden_low,
    dgate_low,
    dup_low,
    tokens,
    back_rows,
    gate_w,
    up_w,
    down_w,
    weight_sem,
    send,
    recv,
    *scratch,
):
    z, near = place()
    local_n = seats.shape[0]
    rows, width = grads.shape
    weights = [
        pltpu.make_async_copy(src.at[layer], dst, weight_sem.at[i])
        for i, (src, dst) in enumerate(((w_gate, gate_w), (w_up, up_w), (w_down, down_w)))
    ]
    greet(z, near, ("x", "y", "c"), None)
    first, second, third, finish = plane_gather(grads, tokens, send, recv, near)
    first()
    for one in weights:
        one.start()
    second()
    third()
    finish()
    everyone = tokens[...].reshape(-1, tokens.shape[2])
    picked = mul(seat_rows(seats[...], number), everyone)
    back_rows[:, pl.ds(0, width)] = picked.astype(bf16)
    rows_grad[...] = (picked * gate_seat[...]).astype(bf16)
    for one in weights:
        one.wait()

    def expert(e, carry):
        here = pl.ds(pl.multiple_of(e * number, 32), number)
        gate, up = gate_pre[here], up_pre[here]
        raw = mul(back_rows[here, pl.ds(0, width)], down_w[e], LAST)
        sigmoid = 1.0 / (1.0 + jnp.exp(-gate))
        silu = gate * sigmoid
        hidden = (silu * up).astype(bf16)
        hidden_low[here] = hidden
        dgate_seat = jnp.sum(hidden.astype(f32) * raw, axis=1, keepdims=True)
        raw = raw * gate_seat[here]
        dgate = (raw * up * sigmoid * (1.0 + gate * (1.0 - sigmoid))).astype(bf16)
        dup = (raw * silu).astype(bf16)
        dgate_low[here] = dgate
        dup_low[here] = dup
        back_rows[here, pl.ds(0, width)] = (
            mul(dgate, gate_w[e], LAST) + mul(dup, up_w[e], LAST)
        ).astype(bf16)
        high = dgate_seat.astype(bf16).astype(f32)
        lane = lax.broadcasted_iota(jnp.int32, (number, 128), 1)
        mine = lax.axis_index(EX) * local_n + e
        back_rows[here, pl.ds(width, 128)] = jnp.where(
            lane == mine, high, jnp.where(lane == experts_n + mine, dgate_seat - high, 0.0)
        ).astype(bf16)
        return carry

    lax.fori_loop(0, local_n, expert, 0)

    def make(name):
        d = near[name]
        back = seat_columns(seats_turned[pl.ds(pl.multiple_of(d * rows, rows), rows)], number)
        scratch[0][d] = mul(back, back_rows[...]).astype(bf16)

    plane_sum(make, summed, None, scratch, near)


def tail_kernel(layers_n, number, n_sums, *refs):
    refs = list(refs)

    def some(count):
        taken = refs[:count]
        del refs[:count]
        return taken

    tokens_all, grads_all = some(layers_n), some(layers_n - 1)
    (own_shard,) = some(1)
    routers, hit, seats = some(3)
    w_gate, w_up, w_down = some(3)
    owns = [some(5) for l in range(layers_n)]
    parts = some(n_sums)
    grad_gate, grad_up, grad_down, landing = some(4)
    sums = some(n_sums)
    (
        tokens,
        grads,
        gates,
        rows_in,
        rows_grad,
        cols_in,
        cols_grad,
        hidden_low,
        dgate_low,
        dup_low,
        gate_w,
        up_w,
        down_w,
        stage_wide,
        stage_tall,
        weight_sem,
        token_sem,
        own_sem,
        out_sem,
        gather_send,
        gather_recv,
    ) = some(21)
    held = [some(6) for a in range(n_sums)]
    z, near = place()
    n_dp, local_n = seats.shape[1], seats.shape[2]
    width = cols_in.shape[1]
    ours = pl.ds(pl.multiple_of(z * width, 128), width)
    gather = Gather([own_shard], [landing], gather_send, gather_recv, z, near, n_dp)
    total = Sums(parts, sums, held, *refs, z, near, n_dp)
    per_expert = n_dp - 1
    per_layer = local_n * per_expert
    steps = layers_n * per_layer

    def layer_of(i):
        return layers_n - 1 - i // per_layer

    def fetch(i, slot, act):
        j = lax.rem(z + 1 + lax.rem(i, per_expert), n_dp)
        for l in range(layers_n):

            @pl.when(layer_of(i) == l)
            def of_layer():
                tokens_from = tokens_all[l].at[pl.ds(j * 8, 8)]
                if l == 0:
                    grads_from = landing.at[j]
                else:
                    grads_from = grads_all[l - 1].at[pl.ds(j * 8, 8)]
                act(pltpu.make_async_copy(tokens_from, tokens.at[slot], token_sem.at[slot, 0]))
                act(pltpu.make_async_copy(grads_from, grads.at[slot], token_sem.at[slot, 1]))

    def weights(l, e):
        return [
            pltpu.make_async_copy(src.at[l, e], dst, weight_sem.at[i])
            for i, (src, dst) in enumerate(((w_gate, gate_w), (w_up, up_w), (w_down, down_w)))
        ]

    def own(l, e):
        here = pl.ds(pl.multiple_of(e * number, 32), number)
        inner = pl.ds(0, number)
        pairs = (
            (owns[l][0].at[here, ours], cols_in.at[inner]),
            (owns[l][1].at[here, ours], cols_grad.at[inner]),
            (owns[l][2].at[here], hidden_low.at[inner]),
            (owns[l][3].at[here], dgate_low.at[inner]),
            (owns[l][4].at[here], dup_low.at[inner]),
        )
        return [
            pltpu.make_async_copy(src, dst, own_sem.at[i]) for i, (src, dst) in enumerate(pairs)
        ]

    def of(i, make, act):
        e = lax.rem(i // per_expert, local_n)
        for l in range(layers_n):

            @pl.when(layer_of(i) == l)
            def of_layer():
                for one in make(l, e):
                    act(one)

    def start(one):
        one.start()

    def wait(one):
        one.wait()

    def results(l, e):
        return [
            pltpu.make_async_copy(stage_wide.at[0], grad_gate.at[l, e], out_sem.at[0]),
            pltpu.make_async_copy(stage_wide.at[1], grad_up.at[l, e], out_sem.at[1]),
            pltpu.make_async_copy(stage_tall, grad_down.at[l, e], out_sem.at[2]),
        ]

    greet(z, near, ("x", "y", "c"), n_dp)
    gather.line_first()
    total.at(3, total.first)
    total.at(2, total.first)
    of(0, weights, start)
    fetch(0, 0, start)

    services = {
        0: [lambda: gather.arrivals(1, gather.take)],
        1: [lambda: gather.arrivals(2, gather.take)],
        2: [
            lambda: gather.arrivals(1, gather.second),
            lambda: gather.arrivals(3, gather.take),
        ],
        3: [
            lambda: gather.arrivals(1, gather.third),
            lambda: gather.arrivals(2, gather.second),
            lambda: total.at(3, total.second),
            lambda: total.at(2, total.second),
        ],
        4: [
            lambda: gather.arrivals(2, gather.third),
            lambda: gather.arrivals(3, gather.second),
            lambda: total.at(1, total.first),
            lambda: total.at(0, total.first),
        ],
        5: [
            lambda: gather.arrivals(3, gather.third),
            lambda: gather.arrivals(1, gather.finish),
            lambda: gather.arrivals(2, gather.finish),
            lambda: gather.arrivals(3, gather.finish),
        ],
        7: [lambda: total.at(3, total.third)],
        8: [lambda: total.at(2, total.third)],
        9: [lambda: total.at(1, total.second)],
        10: [lambda: total.at(0, total.second)],
        11: [lambda: total.at(1, total.third)],
    }

    def step(i, carry):
        slot = lax.rem(i, 2)
        l = layer_of(i)
        k = lax.rem(i, per_expert)
        e = lax.rem(i // per_expert, local_n)
        j = lax.rem(z + 1 + k, n_dp)

        @pl.when(k == 0)
        def begin():
            of(i, own, start)

        @pl.when((i + 1 < steps) & (i != per_layer - 1))
        def ahead():
            fetch(i + 1, 1 - slot, start)

        fetch(i, slot, wait)
        everyone = tokens[slot].reshape(-1, tokens.shape[3])
        gates[...] = masked_gates(mul(routers[l], everyone, LAST), hit[l, j] > 0)
        pick = seat_rows(seats[l, j, pl.ds(e, 1)], number)
        rows_in[...] = mul(pick, everyone).astype(bf16)
        rows_grad[...] = mul(pick, grads[slot].reshape(-1, tokens.shape[3])).astype(bf16)
        place_of = pl.ds(pl.multiple_of((k + 1) * number, 32), number)
        mine = gates[pl.ds(lax.axis_index(EX) * local_n + e, 1), :]
        gate_seat = jnp.sum(pick.astype(f32) * mine, axis=1, keepdims=True)

        @pl.when(k == 0)
        def weights_here():
            of(i, weights, wait)

        gate = mul(rows_in[...], gate_w[...])
        up = mul(rows_in[...], up_w[...])
        raw = mul(rows_grad[...], down_w[...], LAST) * gate_seat
        sigmoid = 1.0 / (1.0 + jnp.exp(-gate))
        silu = gate * sigmoid
        hidden_low[place_of] = (silu * up).astype(bf16)
        dgate_low[place_of] = (raw * up * sigmoid * (1.0 + gate * (1.0 - sigmoid))).astype(bf16)
        dup_low[place_of] = (raw * silu).astype(bf16)
        cols_in[place_of] = rows_in[:, ours]
        cols_grad[place_of] = (rows_grad[:, ours].astype(f32) * gate_seat).astype(bf16)

        @pl.when(k == per_expert - 1)
        def close():
            @pl.when(i + 1 < steps)
            def next_weights():
                of(i + 1, weights, start)

            of(i, own, wait)

            @pl.when(i >= per_expert)
            def staged():
                of(i - per_expert, results, wait)

            over = ((0,), (0,))
            stage_wide[0] = mul(cols_in[...], dgate_low[...], over)
            stage_wide[1] = mul(cols_in[...], dup_low[...], over)
            stage_tall[...] = mul(hidden_low[...], cols_grad[...], over)
            of(i, results, start)

        for at, acts in services.items():

            @pl.when(i == at)
            def serve():
                for act in acts:
                    act()

        @pl.when(i == per_layer - 1)
        def late_ahead():
            fetch(i + 1, 1 - slot, start)

        return carry

    lax.fori_loop(0, steps, step, 0)
    total.at(0, total.third)
    for distance in (3, 2, 1, 0):
        total.at(distance, total.finish)
    gather.line_done()
    of(steps - 1, results, wait)


def tail(capacity, number, tokens_all, grads_all, own_shard, routers, hit, seats, weights, owns, parts):
    layers_n, n_dp, local_n, group_rows = seats.shape
    n_expert = lax.axis_size(EX)
    rows, width = own_shard.shape
    hidden = weights[0].shape[3]
    part = width // n_dp
    shape = jax.ShapeDtypeStruct
    n_sums = len(parts)
    flat = [one for own in owns for one in own]
    results = pl.pallas_call(
        partial(tail_kernel, layers_n, capacity, n_sums),
        out_shape=[
            shape((layers_n, local_n, part, hidden), f32),
            shape((layers_n, local_n, part, hidden), f32),
            shape((layers_n, local_n, hidden, part), f32),
            shape((n_dp, n_expert, rows, width), bf16),
        ]
        + [shape(one.shape[2:], f32) for one in parts],
        in_specs=[HBM] * (2 * layers_n) + [VMEM] * 3 + [HBM] * (3 + len(flat) + n_sums),
        out_specs=[HBM] * 4 + [VMEM] * n_sums,
        scratch_shapes=[
            pltpu.VMEM((2, n_expert, rows, width), bf16),
            pltpu.VMEM((2, n_expert, rows, width), bf16),
            pltpu.VMEM(hit.shape[2:], f32),
            pltpu.VMEM((capacity, width), bf16),
            pltpu.VMEM((capacity, width), bf16),
            pltpu.VMEM((n_dp * capacity, part), bf16),
            pltpu.VMEM((n_dp * capacity, part), bf16),
            pltpu.VMEM((n_dp * capacity, hidden), bf16),
            pltpu.VMEM((n_dp * capacity, hidden), bf16),
            pltpu.VMEM((n_dp * capacity, hidden), bf16),
            pltpu.VMEM((width, hidden), bf16),
            pltpu.VMEM((width, hidden), bf16),
            pltpu.VMEM((hidden, width), bf16),
            pltpu.VMEM((2, part, hidden), f32),
            pltpu.VMEM((hidden, part), f32),
            pltpu.SemaphoreType.DMA((3,)),
            pltpu.SemaphoreType.DMA((2, 2)),
            pltpu.SemaphoreType.DMA((5,)),
            pltpu.SemaphoreType.DMA((3,)),
            pltpu.SemaphoreType.DMA((1, n_dp, KINDS)),
            pltpu.SemaphoreType.DMA((1, n_dp, KINDS)),
        ]
        + sums_scratch([one.shape[2:] for one in parts], n_dp),
        compiler_params=settings(number),
        name="tail",
    )(*tokens_all, *grads_all, own_shard, routers, hit, seats, *weights, *flat, *parts)
    return results[:3], results[4:]


def expert_scratch(n_expert, rows, local_n, width, hidden):
    return [
        pltpu.VMEM((local_n, width, hidden), bf16),
        pltpu.VMEM((local_n, width, hidden), bf16),
        pltpu.VMEM((local_n, hidden, width), bf16),
        pltpu.SemaphoreType.DMA((3,)),
        pltpu.SemaphoreType.DMA((8,)),
        pltpu.SemaphoreType.DMA((8,)),
    ]


VMEM = pl.BlockSpec(memory_space=pltpu.VMEM)
HBM = pl.BlockSpec(memory_space=ANY)


def settings(number):
    return pltpu.CompilerParams(
        collective_id=number, has_side_effects=True, vmem_limit_bytes=60 << 20
    )


def experts_forward(l, capacity, number, normed, mixed, router, hit, seats, weights):
    rows, width = normed.shape
    local_n, hidden = weights[0].shape[1], weights[0].shape[3]
    n_expert = lax.axis_size(EX)
    seats_n = local_n * capacity
    shape = jax.ShapeDtypeStruct
    return pl.pallas_call(
        partial(expert_kernel, l, capacity),
        out_shape=[
            shape((rows, width), f32),
            shape((seats_n, width), bf16),
            shape((seats_n, hidden), f32),
            shape((seats_n, hidden), f32),
            shape((seats_n, 1), f32),
        ],
        in_specs=[VMEM] * 6 + [HBM] * 3,
        out_specs=[VMEM] * 5,
        scratch_shapes=[
            pltpu.VMEM((n_expert, rows, width), bf16),
            pltpu.VMEM((local_n * n_expert, n_expert * rows), f32),
            pltpu.VMEM((seats_n, width), bf16),
        ]
        + expert_scratch(n_expert, rows, local_n, width, hidden)
        + sum_scratch(rows, width),
        compiler_params=settings(number),
        name="experts_forward",
    )(normed, mixed, router, hit, seats, seats.T, *weights)


def experts_backward(l, capacity, number, grads, seats, gate_pre, up_pre, gate_seat, weights):
    rows, width = grads.shape
    local_n, hidden = weights[0].shape[1], weights[0].shape[3]
    n_expert = lax.axis_size(EX)
    seats_n = local_n * capacity
    shape = jax.ShapeDtypeStruct
    return pl.pallas_call(
        partial(expert_back_kernel, l, capacity, local_n * n_expert),
        out_shape=[
            shape((rows, width + 128), f32),
            shape((seats_n, width), bf16),
            shape((seats_n, hidden), bf16),
            shape((seats_n, hidden), bf16),
            shape((seats_n, hidden), bf16),
        ],
        in_specs=[VMEM] * 6 + [HBM] * 3,
        out_specs=[VMEM] * 5,
        scratch_shapes=[
            pltpu.VMEM((n_expert, rows, width), bf16),
            pltpu.VMEM((seats_n, width + 128), bf16),
        ]
        + expert_scratch(n_expert, rows, local_n, width, hidden)
        + sum_scratch(rows, width + 128),
        compiler_params=settings(number),
        name="experts_backward",
    )(grads, seats, seats.T, gate_pre, up_pre, gate_seat, *weights)


class Sums:
    def __init__(self, ins, outs, held, send, recv, keep, z, near, line):
        self.ins, self.outs, self.held = ins, outs, held
        self.send, self.recv, self.keep = send, recv, keep
        self.z, self.near, self.line = z, near, line
        self.all = range(len(ins))

    def split(self, a):
        half = self.outs[a].shape[1] // 2
        return pl.ds(0, half), pl.ds(half, half)

    def move(self, a, j, name):
        part = self.ins[a]
        fromx, fromy, late, later, total, got = self.held[a]
        A, B = self.split(a)
        near = self.near
        kind, src, dst, to = {
            "xd": lambda: (0, part.at[j, near["d"], :, A], fromx.at[j, 0], "x"),
            "xx": lambda: (1, part.at[j, near["x"], :, A], fromx.at[j, 1], "x"),
            "yd": lambda: (2, part.at[j, near["d"], :, B], fromy.at[j, 0], "y"),
            "yy": lambda: (3, part.at[j, near["y"], :, B], fromy.at[j, 1], "y"),
            "ly": lambda: (4, late.at[j, 0], later.at[j, 0], "y"),
            "lx": lambda: (5, late.at[j, 1], later.at[j, 1], "x"),
            "up": lambda: (6, total.at[j], got.at[j], self.z + 1),
            "down": lambda: (7, total.at[j], got.at[j], self.z - 1),
        }[name]()
        if name == "down":
            slot = jnp.where(j == self.z - 1, self.line, j)
            dst = got.at[slot]
        return pltpu.make_async_remote_copy(
            src_ref=src,
            dst_ref=dst,
            send_sem=self.send.at[a, j, kind],
            recv_sem=self.recv.at[a, j, kind],
            device_id={DP: to} if kind >= 6 else {EX: near[to]},
            device_id_type=MESH,
        )

    def own_down(self, a):
        got = self.held[a][5]
        return pltpu.make_async_remote_copy(
            src_ref=got.at[self.line],
            dst_ref=got.at[self.line],
            send_sem=self.send.at[a, self.z, 7],
            recv_sem=self.recv.at[a, self.z, 7],
            device_id={DP: self.z},
            device_id_type=MESH,
        )

    def prepare(self, a, j):
        late, total = self.held[a][2], self.held[a][4]
        A, B = self.split(a)
        near, part = self.near, self.ins[a]
        return [
            pltpu.make_async_copy(src, dst, self.keep.at[a, j, i])
            for i, (src, dst) in enumerate(
                (
                    (part.at[j, near["y"], :, A], late.at[j, 0]),
                    (part.at[j, near["x"], :, B], late.at[j, 1]),
                    (part.at[j, near["own"]], total.at[j]),
                )
            )
        ]

    def at(self, step, act):
        if step == 0:
            act(self.z, 0)
            return

        @pl.when(self.z + step <= self.line - 1)
        def above():
            act(self.z + step, 1)

        @pl.when(self.z - step >= 0)
        def below():
            act(self.z - step, -1)

    def first(self, j, way):
        for a in self.all:
            for name in ("xd", "yd", "xx", "yy"):
                self.move(a, j, name).start()
            for one in self.prepare(a, j):
                one.start()

    def second(self, j, way):
        for a in self.all:
            fromx, fromy, late = self.held[a][:3]
            ready = self.prepare(a, j)
            ready[0].wait()
            self.move(a, j, "xd").wait_recv()
            late[j, 0] = (late[j, 0].astype(f32) + fromx[j, 0].astype(f32)).astype(bf16)
            self.move(a, j, "ly").start()
            ready[1].wait()
            self.move(a, j, "yd").wait_recv()
            late[j, 1] = (late[j, 1].astype(f32) + fromy[j, 0].astype(f32)).astype(bf16)
            self.move(a, j, "lx").start()

    def third(self, j, way):
        for a in self.all:
            fromx, fromy, late, later, total, got = self.held[a]
            for name in ("xx", "yy", "ly", "lx"):
                self.move(a, j, name).wait_recv()
            self.prepare(a, j)[2].wait()
            for side, (columns, here) in enumerate(zip(self.split(a), (fromx, fromy))):
                value = (
                    total[j, :, columns].astype(f32)
                    + here[j, 1].astype(f32)
                    + later[j, side].astype(f32)
                )
                if way == 0:
                    self.outs[a][:, columns] = value
                else:
                    total[j, :, columns] = value.astype(bf16)
            if way == 1:

                @pl.when(self.z > 0)
                def more_up():
                    self.move(a, j, "up").wait_recv()
                    total[j] = (total[j].astype(f32) + got[j].astype(f32)).astype(bf16)

                self.move(a, j, "up").start()
            elif way == -1:

                @pl.when(self.z < self.line - 1)
                def more_down():
                    self.move(a, j, "down").wait_recv()
                    total[j] = (total[j].astype(f32) + got[j].astype(f32)).astype(bf16)

                self.move(a, j, "down").start()
            else:

                @pl.when(self.z > 0)
                def end_up():
                    self.move(a, j, "up").wait_recv()
                    self.outs[a][...] += got[j].astype(f32)

                @pl.when(self.z < self.line - 1)
                def end_down():
                    self.own_down(a).wait_recv()
                    self.outs[a][...] += got[self.line].astype(f32)

    def finish(self, j, way):
        for a in self.all:
            for name in ("xd", "yd", "xx", "yy", "lx", "ly"):
                self.move(a, j, name).wait_send()
            if way == 1:
                self.move(a, j, "up").wait_send()
            elif way == -1:
                self.move(a, j, "down").wait_send()


def sums_scratch(shapes, line):
    scratch = []
    for rows, columns in shapes:
        half = columns // 2
        scratch += [pltpu.VMEM((line, 2, rows, half), bf16) for i in range(4)]
        scratch += [
            pltpu.VMEM((line, rows, columns), bf16),
            pltpu.VMEM((line + 1, rows, columns), bf16),
        ]
    return scratch + [
        pltpu.SemaphoreType.DMA((len(shapes), line, 8)),
        pltpu.SemaphoreType.DMA((len(shapes), line, 8)),
        pltpu.SemaphoreType.DMA((len(shapes), line, 3)),
    ]


def from_behind(value, axis, steps):
    count = lax.axis_size(axis)
    leading, last = (max(0, -steps), min(count, count - steps))
    return lax.ppermute(value, axis, [(source, source + steps) for source in range(leading, last)])


def from_sibling(value):
    count = lax.axis_size(EX)
    return lax.ppermute(value, EX, [(s, s + 1 - 2 * (s % 2)) for s in range(count)])


def rms_norm(stream, gain_row):
    return (
        stream * lax.rsqrt(jnp.mean(stream * stream, axis=-1, keepdims=True) + epsilon) * gain_row
    )


def rotary_tables(token_positions):
    half_dim = HEAD_SIZE // 2
    steps_up = jnp.arange(half_dim).astype(f32)
    frequency = jnp.exp(steps_up * (-2.0 * math.log(rope_base) / HEAD_SIZE))
    angles = token_positions.astype(f32)[:, None] * frequency[None, :]
    return jnp.cos(angles)[:, None, :], jnp.sin(angles)[:, None, :]


def apply_rotary(heads_in, cosine, sine_part):
    half_dim = heads_in.shape[-1] // 2
    first_half = heads_in[..., :half_dim]
    second_half = heads_in[..., half_dim:]
    return jnp.concatenate(
        [
            first_half * cosine - second_half * sine_part,
            second_half * cosine + first_half * sine_part,
        ],
        axis=-1,
    )


def gated_unit(gate_pre, up_pre):
    return jax.nn.silu(gate_pre) * up_pre


def masked_scores(query_rows, gathered_keys, allowed):
    token_rows = query_rows.shape[0]
    grouped_queries = query_rows.reshape(
        token_rows, KEY_VALUE_HEADS, QUERY_HEADS // KEY_VALUE_HEADS, HEAD_SIZE
    )
    score_scale = 1.0 / math.sqrt(HEAD_SIZE)
    scores = (
        jnp.einsum(
            "tkgd,skd->kgts", grouped_queries, gathered_keys, preferred_element_type=f32
        )
        * score_scale
    )
    return (jnp.where(allowed, scores, masked_score), grouped_queries)


def rank_table(routes, pair_order, experts_n):
    layers_n, token_rows, topk_n = routes.shape
    chosen = jnp.swapaxes(routes, 1, 2)
    order = jnp.swapaxes(pair_order.reshape(layers_n, token_rows, topk_n), 1, 2)
    ids = jnp.arange(experts_n, dtype=jnp.int32)[None, :, None]
    none = token_rows * topk_n
    place_of = jnp.full((layers_n, experts_n, token_rows), none, jnp.int32)
    for k in range(topk_n):
        place_of = jnp.where(chosen[:, k][:, None, :] == ids, order[:, k][:, None, :], place_of)
    smaller = (place_of[:, :, :, None] < place_of[:, :, None, :]).astype(jnp.int32)
    return jnp.where(place_of < none, jnp.sum(smaller, axis=2) + 1, 0)


def dense_gates(logits, mask):
    top = jnp.max(jnp.where(mask, logits, masked_score), axis=0, keepdims=True)
    powers = jnp.where(mask, jnp.exp(jnp.where(mask, logits - top, 0.0)), 0.0)
    return powers / jnp.sum(powers, axis=0, keepdims=True)


def local(
    tokens,
    w_qkv,
    w_out,
    w_router,
    norm_gains,
    w_gate,
    w_up,
    w_down,
    out_grad,
    segment_ids,
    routes,
    pair_order,
):
    fast = fast_mesh()
    token_rows = tokens.shape[0]
    layers_n = w_qkv.shape[0]
    topk_n = routes.shape[2]
    n_expert = lax.axis_size(EX)
    n_dp = lax.axis_size(DP)
    expert_here = lax.axis_index(EX)
    dp_here = lax.axis_index(DP)
    device_here = dp_here * n_expert + expert_here
    local_n = w_gate.shape[1]
    experts_n = local_n * n_expert
    capacity = 9 * n_expert * token_rows * topk_n // (8 * experts_n)
    group_rows = n_expert * token_rows
    query_width = QUERY_HEADS * HEAD_SIZE
    key_width = KEY_VALUE_HEADS * HEAD_SIZE
    score_scale = 1.0 / math.sqrt(HEAD_SIZE)
    token_positions = expert_here * token_rows + jnp.arange(token_rows, dtype=jnp.int32)
    cosine, sine_part = rotary_tables(token_positions)
    seg_prev = from_behind(segment_ids, everywhere, 1)
    has_prev = device_here > 0
    row_index = jnp.arange(token_rows)
    own_mask = (segment_ids[None, :] == segment_ids[:, None]) & (
        row_index[None, :] <= row_index[:, None]
    )
    prev_mask = (seg_prev[None, :] == segment_ids[:, None]) & has_prev
    allowed = jnp.concatenate([prev_mask, own_mask], axis=1)

    ranks = rank_table(routes, pair_order, experts_n)
    small = jnp.concatenate(
        [w_router[l] for l in range(layers_n)]
        + [jnp.swapaxes(norm_gains.reshape(2 * layers_n, -1), 0, 1)],
        axis=1,
    )
    small = jnp.pad(small, ((0, 0), (0, 128 - small.shape[1])))
    small_full, ranks_full, qkv_0, out_0 = gather_all(
        [small, ranks.reshape(layers_n * experts_n, token_rows), w_qkv[0], w_out[0]], 1
    )
    qkv_fulls = [qkv_0.reshape(D, -1)]
    out_fulls = [out_0.reshape(query_width, D)]
    for layer_idx in range(1, layers_n):
        qkv_fulls.append(lax.all_gather(w_qkv[layer_idx], everywhere, axis=0, tiled=True))
        out_fulls.append(lax.all_gather(w_out[layer_idx], everywhere, axis=0, tiled=True))
    small_full = small_full.reshape(D, 128)
    gains = jnp.swapaxes(
        small_full[:, layers_n * experts_n : layers_n * (experts_n + 2)], 0, 1
    ).astype(f32)
    routers = [small_full[:, l * experts_n : (l + 1) * experts_n] for l in range(layers_n)]
    routers_turned = [jnp.swapaxes(router, 0, 1) for router in routers]
    ranks_full = ranks_full.reshape(n_dp, n_expert, layers_n, experts_n, token_rows)
    if not fast:
        ranks_full = lax.dynamic_slice_in_dim(ranks_full, dp_here, 1, 0)
    groups = ranks_full.shape[0]
    own_group = dp_here if fast else 0
    hit_all = jnp.transpose(ranks_full > 0, (2, 0, 3, 1, 4)).reshape(
        layers_n, groups, experts_n, group_rows
    )
    mine = lax.dynamic_slice_in_dim(ranks_full, expert_here * local_n, local_n, 3)
    counts = jnp.sum((mine > 0).astype(jnp.int32), axis=-1)
    before = jnp.cumsum(counts, axis=1) - counts
    seats = jnp.where(mine > 0, before[..., None] + mine, 0)
    seats = jnp.transpose(seats, (2, 0, 3, 1, 4)).reshape(layers_n, groups, local_n, group_rows)
    seat_ids = jnp.arange(1, capacity + 1, dtype=jnp.int32)

    def own_of(array):
        return lax.dynamic_index_in_dim(array, own_group, 0, keepdims=False)

    def seat_map(l):
        return (seats[l][:, :, None, :] == seat_ids[:, None]).astype(bf16)

    def gates_of(normed_rows, l, hit):
        logits = jnp.einsum("de,td->et", routers[l], normed_rows, preferred_element_type=f32)
        return dense_gates(logits, hit)

    own_hit = [(ranks[l] > 0) for l in range(layers_n)]

    stream = tokens.astype(f32)
    saved_layers = []
    outputs = []
    for l in range(layers_n):
        qkv_full, out_full = qkv_fulls[l], out_fulls[l]
        normed_a = rms_norm(stream, gains[2 * l]).astype(bf16)
        projected_output = jnp.dot(normed_a, qkv_full, preferred_element_type=f32)
        query_rows = apply_rotary(
            projected_output[:, :query_width].reshape(token_rows, QUERY_HEADS, HEAD_SIZE),
            cosine,
            sine_part,
        ).astype(bf16)
        key_own = apply_rotary(
            projected_output[:, query_width : query_width + key_width].reshape(
                token_rows, KEY_VALUE_HEADS, HEAD_SIZE
            ),
            cosine,
            sine_part,
        ).astype(bf16)
        value_own = (
            projected_output[:, query_width + key_width :]
            .reshape(token_rows, KEY_VALUE_HEADS, HEAD_SIZE)
            .astype(bf16)
        )
        key_prev, value_prev = from_behind((key_own, value_own), everywhere, 1)
        gathered_keys = jnp.concatenate([key_prev, key_own], axis=0)
        gathered_values = jnp.concatenate([value_prev, value_own], axis=0)
        scores, grouped_queries = masked_scores(query_rows, gathered_keys, allowed)
        top_score = jnp.max(scores, axis=-1, keepdims=True)
        exp_scores = jnp.exp(scores - top_score)
        row_total = jnp.sum(exp_scores, axis=-1, keepdims=True)
        prob_low = (exp_scores / row_total).astype(bf16)
        log_total = top_score + jnp.log(row_total)
        attended = (
            jnp.einsum("kgts,skd->tkgd", prob_low, gathered_values, preferred_element_type=f32)
            .reshape(token_rows, query_width)
            .astype(bf16)
        )
        mixed_sum = stream + jnp.dot(attended, out_full, preferred_element_type=f32)
        normed_b = rms_norm(mixed_sum, gains[2 * l + 1]).astype(bf16)

        kept = {}
        if fast:
            if fast:
                normed_all = lax.all_gather(normed_b, everywhere, axis=0, tiled=True)
                kept["normed_all"] = normed_all.reshape(-1, token_rows, D)
            new_stream, *kept["own"] = experts_forward(
                l,
                capacity,
                12 + l,
                normed_b,
                mixed_sum,
                routers_turned[l],
                own_of(hit_all[l]).astype(jnp.int32),
                own_of(seats[l]),
                (w_gate, w_up, w_down),
            )
        else:
            group_normed = lax.all_gather(normed_b, EX, axis=0, tiled=True)
            kept["normed_all"] = group_normed[None]
            seat_own = own_of(seat_map(l))
            gates_own = gates_of(group_normed, l, own_of(hit_all[l]))
            gates_own = lax.dynamic_slice_in_dim(gates_own, expert_here * local_n, local_n, 0)
            gate_seat = jnp.sum(seat_own.astype(f32) * gates_own[:, None, :], axis=-1)
            expert_in = jnp.einsum(
                "est,td->esd", seat_own, group_normed, preferred_element_type=f32
            ).astype(bf16)
            gate_pre = jnp.einsum("esd,edf->esf", expert_in, w_gate[l], preferred_element_type=f32)
            up_pre = jnp.einsum("esd,edf->esf", expert_in, w_up[l], preferred_element_type=f32)
            hidden = gated_unit(gate_pre, up_pre).astype(bf16)
            expert_out = jnp.einsum("esf,efd->esd", hidden, w_down[l], preferred_element_type=f32)
            weighted = (expert_out * gate_seat[..., None]).astype(bf16)
            branch_part = jnp.einsum("est,esd->td", seat_own, weighted, preferred_element_type=f32)
            new_stream = mixed_sum + lax.psum_scatter(
                branch_part, EX, scatter_dimension=0, tiled=True
            )
        saved_layers.append(
            {
                "stream_in": stream,
                "normed_a": normed_a,
                "queries": query_rows,
                "key_all": gathered_keys,
                "value_all": gathered_values,
                "log_total": log_total,
                "attended": attended,
                "mixed_sum": mixed_sum,
                "normed_b": normed_b,
            }
            | kept
        )
        outputs.append(new_stream)
        stream = new_stream

    grad_stream = out_grad.astype(f32)
    weight_parts = [None] * layers_n
    expert_parts = [None] * layers_n
    owns = [None] * layers_n
    for l in reversed(range(layers_n)):
        record = saved_layers[l]
        qkv_full, out_full = qkv_fulls[l], out_fulls[l]
        grad_low = grad_stream.astype(bf16)
        if fast:
            rows_in, gate_pre, up_pre, gate_seat = record["own"]
            summed, rows_grad, hidden_low, dgate_low, dup_low = experts_backward(
                l,
                capacity,
                16 + l,
                grad_low,
                own_of(seats[l]),
                gate_pre,
                up_pre,
                gate_seat,
                (w_gate, w_up, w_down),
            )
        if fast:
            if l == layers_n - 1:
                grads_all = [
                    lax.all_gather(out_grad, everywhere, axis=0, tiled=True).reshape(
                        -1, token_rows, D
                    )
                ]
            owns[l] = (rows_in, rows_grad, hidden_low, dgate_low, dup_low)
            own_shard = grad_low
        else:
            normed_all = record["normed_all"]
            grad_all = lax.all_gather(grad_low, EX, axis=0, tiled=True)[None]
            seat_all = seat_map(l)
            gates_all = jax.vmap(lambda rows, hit: gates_of(rows, l, hit))(normed_all, hit_all[l])
            gates_mine = lax.dynamic_slice_in_dim(gates_all, expert_here * local_n, local_n, 1)
            gate_seat = jnp.sum(seat_all.astype(f32) * gates_mine[:, :, None, :], axis=-1)
            rows_in = jnp.einsum(
                "gest,gtd->egsd", seat_all, normed_all, preferred_element_type=f32
            ).astype(bf16)
            rows_grad = jnp.einsum(
                "gest,gtd->egsd", seat_all, grad_all, preferred_element_type=f32
            ).astype(bf16)
            gate_seat = jnp.swapaxes(gate_seat, 0, 1)[..., None]
            gate_pre = jnp.einsum("egsd,edf->egsf", rows_in, w_gate[l], preferred_element_type=f32)
            up_pre = jnp.einsum("egsd,edf->egsf", rows_in, w_up[l], preferred_element_type=f32)
            dhidden_raw = jnp.einsum(
                "egsd,efd->egsf", rows_grad, w_down[l], preferred_element_type=f32
            )
            hidden, gate_pull = jax.vjp(gated_unit, gate_pre, up_pre)
            hidden_low = hidden.astype(bf16)
            dgate_pre, dup_pre = gate_pull(dhidden_raw * gate_seat)
            dgate_low = dgate_pre.astype(bf16)
            dup_low = dup_pre.astype(bf16)
            dgate_seat = jnp.sum(hidden_low.astype(f32) * dhidden_raw, axis=-1)
            rows_grad = (rows_grad.astype(f32) * gate_seat).astype(bf16)

        def by_expert(array):
            return array.reshape(local_n, -1, array.shape[-1])

        def outer(one, other):
            return jnp.einsum(
                "esa,esb->eab", by_expert(one), by_expert(other), preferred_element_type=f32
            )

        if not fast:
            grad_gate_l = outer(rows_in, dgate_low)
            grad_up_l = outer(rows_in, dup_low)
            grad_down_l = outer(hidden_low, rows_grad)
            grad_gate_l = lax.psum_scatter(
                grad_gate_l.astype(bf16), DP, scatter_dimension=1, tiled=True
            ).astype(f32)
            grad_up_l = lax.psum_scatter(
                grad_up_l.astype(bf16), DP, scatter_dimension=1, tiled=True
            ).astype(f32)
            grad_down_l = lax.psum_scatter(
                grad_down_l.astype(bf16), DP, scatter_dimension=2, tiled=True
            ).astype(f32)
            expert_parts[l] = (grad_gate_l, grad_up_l, grad_down_l)

        if fast:
            dnormed_b = summed[:, :D]
            dgates = summed[:, D : D + experts_n] + summed[:, D + experts_n : D + 2 * experts_n]
        else:
            dexpert_in = (
                jnp.einsum("egsf,edf->egsd", dgate_low, w_gate[l], preferred_element_type=f32)
                + jnp.einsum("egsf,edf->egsd", dup_low, w_up[l], preferred_element_type=f32)
            ).astype(bf16)
            back_part = jnp.einsum(
                "gest,egsd->td", seat_all, dexpert_in, preferred_element_type=f32
            )
            dgates_part = jnp.sum(
                seat_all[0].astype(f32) * dgate_seat[:, 0, :, None], axis=1
            )
            mine = expert_here * local_n + jnp.arange(local_n, dtype=jnp.int32)
            lane = jnp.arange(experts_n, dtype=jnp.int32)
            dgates_part = jnp.sum(
                jnp.where(mine[:, None, None] == lane, dgates_part[..., None], 0.0), axis=0
            )
            dnormed_b, dgates = [
                lax.psum_scatter(part, EX, scatter_dimension=0, tiled=True)
                for part in (back_part, dgates_part)
            ]
        gates_token = gates_of(record["normed_b"], l, own_hit[l]).T
        dlogits = (
            gates_token * (dgates - jnp.sum(gates_token * dgates, axis=1, keepdims=True))
        ).astype(bf16)
        dnormed_b = dnormed_b + jnp.einsum(
            "te,de->td", dlogits, routers[l], preferred_element_type=f32
        )
        unused_norm, norm_pull = jax.vjp(rms_norm, record["mixed_sum"], gains[2 * l + 1])
        dmixed_part, dgain_b = norm_pull(dnormed_b)
        dmixed = grad_stream + dmixed_part
        grad_attn = dmixed.astype(bf16)
        attended_gradient = jnp.einsum(
            "td,qd->tq", grad_attn, out_full, preferred_element_type=f32
        ).astype(bf16)
        gathered_keys = record["key_all"]
        gathered_values = record["value_all"]
        scores, grouped_queries = masked_scores(record["queries"], gathered_keys, allowed)
        prob_float = jnp.exp(scores - record["log_total"])
        prob_low = prob_float.astype(bf16)
        grouped_gradient = attended_gradient.reshape(
            token_rows, KEY_VALUE_HEADS, QUERY_HEADS // KEY_VALUE_HEADS, HEAD_SIZE
        )
        dvalue_all = jnp.einsum(
            "kgts,tkgd->skd", prob_low, grouped_gradient, preferred_element_type=f32
        )
        dprobs = jnp.einsum(
            "tkgd,skd->kgts", grouped_gradient, gathered_values, preferred_element_type=f32
        )
        delta_row = jnp.sum(prob_float * dprobs, axis=-1, keepdims=True)
        dscores = (prob_float * (dprobs - delta_row)).astype(bf16)
        dqueries = (
            jnp.einsum(
                "kgts,skd->tkgd", dscores, gathered_keys, preferred_element_type=f32
            ).reshape(token_rows, QUERY_HEADS, HEAD_SIZE)
            * score_scale
        )
        dkey_all = (
            jnp.einsum("kgts,tkgd->skd", dscores, grouped_queries, preferred_element_type=f32)
            * score_scale
        )
        dkey_next, dvalue_next = from_behind(
            (dkey_all[:token_rows].astype(bf16), dvalue_all[:token_rows].astype(bf16)),
            everywhere,
            -1,
        )
        dkey_own = dkey_all[token_rows:] + dkey_next.astype(f32)
        dvalue_own = dvalue_all[token_rows:] + dvalue_next.astype(f32)
        dq_raw = apply_rotary(dqueries, cosine, -sine_part)
        dk_raw = apply_rotary(dkey_own, cosine, -sine_part)
        dprojected = jnp.concatenate(
            [
                dq_raw.reshape(token_rows, query_width),
                dk_raw.reshape(token_rows, key_width),
                dvalue_own.reshape(token_rows, key_width),
            ],
            axis=1,
        ).astype(bf16)
        dnormed_a = jnp.einsum("tq,dq->td", dprojected, qkv_full, preferred_element_type=f32)
        unused_first, first_pull = jax.vjp(rms_norm, record["stream_in"], gains[2 * l])
        dstream_part, dgain_a = first_pull(dnormed_a)
        grad_stream = dmixed + dstream_part

        small_grad = jnp.concatenate(
            [
                jnp.einsum("td,te->de", record["normed_b"], dlogits, preferred_element_type=f32),
                dgain_a[:, None],
                dgain_b[:, None],
            ],
            axis=1,
        )
        normed_a, attended = record["normed_a"], record["attended"]
        if fast:
            other = from_sibling((normed_a, attended, dprojected, grad_attn))
            normed_a, attended, dprojected, grad_attn = [
                jnp.concatenate([own, sib], axis=0)
                for own, sib in zip((normed_a, attended, dprojected, grad_attn), other)
            ]
            small_grad = small_grad + from_sibling(small_grad)
        grad_qkv_l = jnp.einsum("td,tq->dq", normed_a, dprojected, preferred_element_type=f32)
        grad_out_l = jnp.einsum("tq,td->qd", attended, grad_attn, preferred_element_type=f32)
        weight_parts[l] = (grad_qkv_l, grad_out_l, small_grad)

    small_grads = jnp.concatenate([weight_parts[l][2] for l in range(layers_n)], axis=1)
    if fast:
        shape = (n_dp, n_expert, D // (n_dp * n_expert))
        small_grads = jnp.pad(small_grads, ((0, 0), (0, 128 - small_grads.shape[1])))
        high = small_grads.astype(bf16)
        low = (small_grads - high.astype(f32)).astype(bf16)
        pieces = [jnp.concatenate([high, low], axis=1).reshape(shape + (256,))]
        for l in reversed(range(layers_n)):
            pieces.append(weight_parts[l][0].astype(bf16).reshape(shape + (-1,)))
            pieces.append(weight_parts[l][1].astype(bf16).reshape(shape + (-1,)))
        experts, summed = tail(
            capacity,
            20,
            [record["normed_all"] for record in saved_layers],
            grads_all,
            own_shard,
            jnp.stack(routers_turned),
            hit_all.astype(jnp.int32),
            seats,
            (w_gate, w_up, w_down),
            owns,
            pieces,
        )
        small_sum = summed[0][:, :128] + summed[0][:, 128:]
        grad_qkv = jnp.stack([summed[1 + 2 * (layers_n - 1 - l)] for l in range(layers_n)])
        grad_out = jnp.stack([summed[2 + 2 * (layers_n - 1 - l)] for l in range(layers_n)])
    else:

        def scatter(array):
            return lax.psum_scatter(array, everywhere, scatter_dimension=0, tiled=True)

        small_sum = scatter(small_grads)
        grad_qkv = jnp.stack([scatter(weight_parts[l][0]) for l in range(layers_n)])
        grad_out = jnp.stack([scatter(weight_parts[l][1]) for l in range(layers_n)])
    wide = experts_n + 2
    grad_router = jnp.stack(
        [small_sum[:, l * wide : l * wide + experts_n] for l in range(layers_n)]
    )
    grad_gains = jnp.stack(
        [
            jnp.swapaxes(small_sum[:, l * wide + experts_n : (l + 1) * wide], 0, 1)
            for l in range(layers_n)
        ]
    )
    if fast:
        grad_gate, grad_up, grad_down = experts
    else:
        grad_gate, grad_up, grad_down = [
            jnp.stack([expert_parts[l][member] for l in range(layers_n)]) for member in range(3)
        ]
    layer_outs = jnp.stack(outputs).astype(bf16)
    return (
        layer_outs,
        grad_stream,
        grad_qkv,
        grad_out,
        grad_router,
        grad_gains,
        grad_gate,
        grad_up,
        grad_down,
    )


def solution(mesh):
    return jax.shard_map(
        local,
        mesh=mesh,
        in_specs=(
            P((DP, EX), None),
            P(None, (DP, EX), None),
            P(None, (DP, EX), None),
            P(None, (DP, EX), None),
            P(None, None, (DP, EX)),
            P(None, EX, None, None),
            P(None, EX, None, None),
            P(None, EX, None, None),
            P((DP, EX), None),
            P((DP, EX)),
            P(None, (DP, EX), None),
            P(None, (DP, EX), None),
        ),
        out_specs=(
            P(None, (DP, EX), None),
            P((DP, EX), None),
            P(None, (DP, EX), None),
            P(None, (DP, EX), None),
            P(None, (DP, EX), None),
            P(None, None, (DP, EX)),
            P(None, EX, DP, None),
            P(None, EX, DP, None),
            P(None, EX, None, DP),
        ),
        check_vma=False,
    )
```

```python
from functools import partial
import math

import jax
import jax.numpy as jnp
from jax import lax
from jax.experimental import pallas as pl
from jax.experimental.pallas import tpu as pltpu
from jax.sharding import PartitionSpec as P

D = 1536
QUERY_HEADS = 12
KEY_VALUE_HEADS = 2
HEAD_SIZE = 128
MESH = pl.DeviceIdType.MESH
DP, EX = "dp", "expert"
ANY = pl.ANY
bf16 = jnp.bfloat16
f32 = jnp.float32

epsilon = 1e-06
rope_base = 1000000.0
masked_score = -1e30
everywhere = (DP, EX)


def place():
    z = lax.axis_index(DP)
    e = lax.axis_index(EX)
    y, x, c = e // 4, (e // 2) % 2, e % 2
    near = {
        "own": e,
        "x": y * 4 + (1 - x) * 2 + c,
        "y": (1 - y) * 4 + x * 2 + c,
        "d": (1 - y) * 4 + (1 - x) * 2 + c,
        "c": y * 4 + x * 2 + (1 - c),
        "cx": y * 4 + (1 - x) * 2 + (1 - c),
        "cy": (1 - y) * 4 + x * 2 + (1 - c),
        "cd": (1 - y) * 4 + (1 - x) * 2 + (1 - c),
    }
    return z, near


def greet(z, near, plane, line, order=None):
    barrier = pltpu.get_barrier_semaphore()

    def tell(**target):
        pl.semaphore_signal(barrier, inc=1, device_id=target, device_id_type=MESH)

    for name in plane:
        tell(**{EX: near[name]})
    count = len(plane)
    links = []
    if line is not None:
        links += [(z < line - 1, {DP: z + 1}), (z > 0, {DP: z - 1})]
    if order is not None:
        behind, ahead, has_behind, has_ahead = order
        links += [
            (has_behind, {DP: behind[0], EX: behind[1]}),
            (has_ahead, {DP: ahead[0], EX: ahead[1]}),
        ]
    for there, target in links:

        @pl.when(there)
        def one():
            tell(**target)

        count = count + jnp.where(there, 1, 0)
    pl.semaphore_wait(barrier, count)


def halves(rows, columns):
    if rows % 32 == 0:
        return ((0, rows // 2), (0, columns)), ((rows // 2, rows // 2), (0, columns))
    if columns % 256 == 0:
        return ((0, rows), (0, columns // 2)), ((0, rows), (columns // 2, columns // 2))
    return ((0, 16), (0, columns)), ((16, rows - 16), (0, columns))


def cut(ref, part):
    (row, rows), (column, columns) = part
    return ref.at[pl.ds(row, rows), pl.ds(column, columns)]


KINDS = 10
QUAD = ("own", "x", "y", "d")
BESIDE = ("c", "cx", "cy", "cd")


class Gather:
    def __init__(self, ins, outs, send, recv, z, near, line):
        self.ins, self.outs, self.send, self.recv = ins, outs, send, recv
        self.z, self.near, self.line = z, near, line
        self.parts = [halves(*ref.shape) for ref in ins]
        self.all = range(len(ins))

    def hop(self, a, j, kind, whose, to, part=None, src=None):
        dst = self.outs[a].at[j, self.near[whose]]
        src = dst if src is None else src
        if part is not None:
            src, dst = cut(src, part), cut(dst, part)
        return pltpu.make_async_remote_copy(
            src_ref=src,
            dst_ref=dst,
            send_sem=self.send.at[a, j, kind],
            recv_sem=self.recv.at[a, j, kind],
            device_id={DP: to} if kind >= 8 else {EX: self.near[to]},
            device_id_type=MESH,
        )

    def landed(self, a, j, kind, whose, part=None):
        if kind < 8:
            self.hop(a, j, kind, whose, "c", part).wait_recv()
        else:
            self.hop(a, j, kind, whose, self.z).wait_recv()

    def line_first(self):
        z = self.z

        @pl.when(z < self.line - 1)
        def up_first():
            for a in self.all:
                self.hop(a, z, 8, "own", z + 1, src=self.ins[a]).start()

        @pl.when(z > 0)
        def down_first():
            for a in self.all:
                self.hop(a, z, 9, "own", z - 1, src=self.ins[a]).start()

    def first(self, j, src=None):
        for a in self.all:
            one = None if src is None else src[a]
            self.hop(a, j, 0, "own", "x", src=one).start()
            self.hop(a, j, 1, "own", "y", src=one).start()
            self.hop(a, j, 2, "own", "c", src=one).start()

    def second(self, j, kind=0):
        for a in self.all:
            self.landed(a, j, 0, "x")
            self.hop(a, j, 4, "x", "y", self.parts[a][1]).start()
            self.hop(a, j, 5, "x", "c").start()
            self.landed(a, j, 1, "y")
            self.hop(a, j, 3, "y", "x", self.parts[a][0]).start()
            self.hop(a, j, 6, "y", "c").start()

    def third(self, j, kind=0):
        for a in self.all:
            self.landed(a, j, 3, "d", self.parts[a][0])
            self.landed(a, j, 4, "d", self.parts[a][1])
            self.hop(a, j, 7, "d", "c").start()

    def finish(self, j, kind=0):
        for a in self.all:
            for kind, whose in ((2, "c"), (5, "cx"), (6, "cy"), (7, "cd")):
                self.landed(a, j, kind, whose)
            for kind in (0, 1, 2):
                self.hop(a, j, kind, "own", "c").wait_send()
            self.hop(a, j, 3, "y", "x", self.parts[a][0]).wait_send()
            self.hop(a, j, 4, "x", "y", self.parts[a][1]).wait_send()
            for kind in (5, 6, 7):
                self.hop(a, j, kind, "x", "c").wait_send()

    def arrivals(self, step, act):
        z = self.z

        @pl.when(z - step >= 0)
        def below():
            act(z - step, 8)

        @pl.when(z + step <= self.line - 1)
        def above():
            act(z + step, 9)

    def take(self, j, kind):
        for a in self.all:
            self.landed(a, j, kind, "own")
        z = self.z
        if kind == 8:

            @pl.when(z < self.line - 1)
            def on_up():
                for a in self.all:
                    self.hop(a, j, 8, "own", z + 1).start()

        else:

            @pl.when(z > 0)
            def on_down():
                for a in self.all:
                    self.hop(a, j, 9, "own", z - 1).start()

        self.first(j)

    def plane_of(self, k):
        return lax.rem(self.z + k, self.line)

    def spread(self, k, rows, sem):
        j = self.plane_of(k)
        self.first(j, [rows.at[j]])
        self.kept(k, rows, sem).start()

    def kept(self, k, rows, sem):
        j = self.plane_of(k)
        return pltpu.make_async_copy(rows.at[j], self.outs[0].at[j, self.near["own"]], sem.at[k])

    def spread_done(self, rows, sem):
        for k in range(1, self.line):
            self.finish(self.plane_of(k))
            self.kept(k, rows, sem).wait()

    def line_done(self):
        z = self.z
        for step in range(self.line):

            @pl.when((z - step >= 0) & (z < self.line - 1))
            def up_done():
                for a in self.all:
                    self.hop(a, z - step, 8, "own", z + 1).wait_send()

            @pl.when((z + step <= self.line - 1) & (z > 0))
            def down_done():
                for a in self.all:
                    self.hop(a, z + step, 9, "own", z - 1).wait_send()


def plane_gather(src, dst, send, recv, near):
    parts = halves(*src.shape)

    def hop(kind, whose, to, part=None):
        one = dst.at[near[whose]] if part is None else cut(dst.at[near[whose]], part)
        return pltpu.make_async_remote_copy(
            src_ref=src if whose == "own" else one,
            dst_ref=one,
            send_sem=send.at[kind],
            recv_sem=recv.at[kind],
            device_id={EX: near[to]},
            device_id_type=MESH,
        )

    def first():
        hop(0, "own", "x").start()
        hop(1, "own", "y").start()
        hop(2, "own", "c").start()
        dst[near["own"]] = src[...]

    def second():
        hop(0, "x", "c").wait_recv()
        hop(4, "x", "y", parts[1]).start()
        hop(5, "x", "c").start()
        hop(1, "y", "c").wait_recv()
        hop(3, "y", "x", parts[0]).start()
        hop(6, "y", "c").start()

    def third():
        hop(3, "d", "c", parts[0]).wait_recv()
        hop(4, "d", "c", parts[1]).wait_recv()
        hop(7, "d", "c").start()

    def finish():
        for kind, whose in ((2, "c"), (5, "cx"), (6, "cy"), (7, "cd")):
            hop(kind, whose, "c").wait_recv()
        for kind in (0, 1, 2):
            hop(kind, "own", "c").wait_send()
        hop(3, "y", "x", parts[0]).wait_send()
        hop(4, "x", "y", parts[1]).wait_send()
        for kind in (5, 6, 7):
            hop(kind, "x", "c").wait_send()

    return first, second, third, finish


def sum_scratch(rows, columns):
    return [
        pltpu.VMEM((8, rows, columns), bf16),
        pltpu.VMEM((3, rows, columns), bf16),
        pltpu.VMEM((4, rows, columns), bf16),
        pltpu.VMEM((2, rows // 2, columns), bf16),
        pltpu.VMEM((2, rows // 2, columns), bf16),
        pltpu.VMEM((2, rows // 2, columns), bf16),
        pltpu.SemaphoreType.DMA((10,)),
        pltpu.SemaphoreType.DMA((10,)),
    ]


def plane_sum(make, out_ref, base, scratch, near):
    part_ref, paired, fromc, fromx, fromy, last, send, recv = scratch
    rows = out_ref.shape[0]
    half = rows // 2
    A, B = pl.ds(0, half), pl.ds(half, half)

    def copy(number, src, dst, to):
        return pltpu.make_async_remote_copy(
            src_ref=src,
            dst_ref=dst,
            send_sem=send.at[number],
            recv_sem=recv.at[number],
            device_id={EX: near[to]},
            device_id_type=MESH,
        )

    order = ("d", "x", "y", "own")
    across = ("cd", "cx", "cy", "c")
    core = [copy(s, part_ref.at[near[name]], fromc.at[s], "c") for s, name in enumerate(across)]
    to_x = [copy(4, paired.at[0, A], fromx.at[0], "x"), copy(5, paired.at[1, A], fromx.at[1], "x")]
    to_y = [copy(6, paired.at[0, B], fromy.at[0], "y"), copy(7, paired.at[2, B], fromy.at[1], "y")]
    late_y = copy(8, paired.at[2, A], last.at[0], "y")
    late_x = copy(9, paired.at[1, B], last.at[1], "x")

    def pair(s):
        core[s].wait_recv()
        paired[s] = (part_ref[near[order[s]]].astype(f32) + fromc[s].astype(f32)).astype(bf16)

    for s in range(3):
        make(across[s])
        core[s].start()
        make(order[s])
    pair(0)
    to_x[0].start()
    to_y[0].start()
    make(across[3])
    core[3].start()
    pair(1)
    to_x[1].start()
    pair(2)
    to_y[1].start()
    make(order[3])
    core[3].wait_recv()
    total = part_ref[near["own"]].astype(f32) + fromc[3].astype(f32)
    out_ref[...] = total if base is None else base[...] + total
    to_x[0].wait_recv()
    paired[2, A] = (paired[2, A].astype(f32) + fromx[0].astype(f32)).astype(bf16)
    late_y.start()
    to_y[0].wait_recv()
    paired[1, B] = (paired[1, B].astype(f32) + fromy[0].astype(f32)).astype(bf16)
    late_x.start()
    to_x[1].wait_recv()
    out_ref[A] += fromx[1].astype(f32)
    to_y[1].wait_recv()
    out_ref[B] += fromy[1].astype(f32)
    late_y.wait_recv()
    out_ref[A] += last[0].astype(f32)
    late_x.wait_recv()
    out_ref[B] += last[1].astype(f32)
    for one in core + to_x + to_y + [late_x, late_y]:
        one.wait_send()


def mul(a, b, over=((1,), (0,))):
    return lax.dot_general(a, b, (over, ((), ())), preferred_element_type=f32)


LAST = ((1,), (1,))


def seat_rows(seats, number):
    local_n, tokens_n = seats.shape
    rows = lax.broadcasted_iota(jnp.int32, (local_n * number, tokens_n), 0).astype(f32)
    hot = rows < 0
    for e in range(local_n):
        one = seats[e : e + 1, :]
        hot = hot | ((rows == one + (e * number - 1)) & (one > 0) & (one <= number))
    return jnp.where(hot, 1.0, 0.0).astype(bf16)


def seat_columns(seats, number):
    tokens_n, local_n = seats.shape
    columns = lax.broadcasted_iota(jnp.int32, (tokens_n, local_n * number), 1).astype(f32)
    hot = columns < 0
    for e in range(local_n):
        one = seats[:, e : e + 1]
        hot = hot | ((columns == one + (e * number - 1)) & (one > 0) & (one <= number))
    return jnp.where(hot, 1.0, 0.0).astype(bf16)


def masked_gates(logits, hit):
    top = jnp.max(jnp.where(hit, logits, masked_score), axis=0, keepdims=True)
    powers = jnp.where(hit, jnp.exp(jnp.where(hit, logits - top, 0.0)), 0.0)
    return powers / jnp.sum(powers, axis=0, keepdims=True)


def tail_kernel(layers_n, number, n_sums, *refs):
    refs = list(refs)

    def some(count):
        taken = refs[:count]
        del refs[:count]
        return taken

    tokens_all, grads_all = some(layers_n), some(layers_n - 1)
    (own_shard,) = some(1)
    table, hit, seats = some(3)
    w_gate, w_up, w_down = some(3)
    owns = [some(5) for l in range(layers_n)]
    parts = some(n_sums)
    grad_gate, grad_up, grad_down, landing = some(4)
    beside = some(layers_n)
    sums = some(n_sums)
    (
        tokens,
        grads,
        gates,
        rows_in,
        rows_grad,
        cols_in,
        cols_grad,
        hidden_low,
        dgate_low,
        dup_low,
        gate_w,
        up_w,
        down_w,
        stage_wide,
        stage_tall,
        weight_sem,
        token_sem,
        own_sem,
        out_sem,
        gather_send,
        gather_recv,
        beside_send,
        beside_recv,
    ) = some(23)
    held = [some(6) for a in range(n_sums)]
    z, near = place()
    n_dp, local_n = seats.shape[1], seats.shape[2]
    width = cols_in.shape[1]
    ours = pl.ds(pl.multiple_of(z * width, 128), width)
    gather = Gather([own_shard], [landing], gather_send, gather_recv, z, near, n_dp)
    total = Sums(parts, sums, held, *refs, z, near, n_dp)
    per_expert = n_dp - 1
    per_layer = local_n * per_expert
    steps = layers_n * per_layer

    def layer_of(i):
        return layers_n - 1 - i // per_layer

    def across(l, j):
        return pltpu.make_async_remote_copy(
            src_ref=tokens_all[l].at[j],
            dst_ref=beside[l].at[j],
            send_sem=beside_send.at[l, j],
            recv_sem=beside_recv.at[l, j],
            device_id={EX: near["c"]},
            device_id_type=MESH,
        )

    def start(one):
        one.start()

    def wait(one):
        one.wait()

    def fetch(i, slot, act):
        j = lax.rem(z + 1 + lax.rem(i, per_expert), n_dp)
        for l in range(layers_n):

            @pl.when(layer_of(i) == l)
            def of_layer():
                if act is start:

                    @pl.when(lax.rem(i, per_layer) < per_expert)
                    def arrived():
                        across(l, j).wait_recv()

                for source, names, base in ((tokens_all[l], QUAD, 0), (beside[l], BESIDE, 4)):
                    for q, name in enumerate(names):
                        dst = tokens.at[slot, near[name]]
                        sem = token_sem.at[slot, base + q]
                        act(pltpu.make_async_copy(source.at[j, q], dst, sem))
                grads_from = (landing if l == 0 else grads_all[l - 1]).at[j]
                act(pltpu.make_async_copy(grads_from, grads.at[slot], token_sem.at[slot, 8]))

    def weights(l, e):
        return [
            pltpu.make_async_copy(src.at[l, e], dst, weight_sem.at[i])
            for i, (src, dst) in enumerate(((w_gate, gate_w), (w_up, up_w), (w_down, down_w)))
        ]

    def own(l, e):
        here = pl.ds(pl.multiple_of(e * number, 32), number)
        inner = pl.ds(0, number)
        pairs = (
            (owns[l][0].at[here, ours], cols_in.at[inner]),
            (owns[l][1].at[here, ours], cols_grad.at[inner]),
            (owns[l][2].at[here], hidden_low.at[inner]),
            (owns[l][3].at[here], dgate_low.at[inner]),
            (owns[l][4].at[here], dup_low.at[inner]),
        )
        return [
            pltpu.make_async_copy(src, dst, own_sem.at[i]) for i, (src, dst) in enumerate(pairs)
        ]

    def of(i, make, act):
        e = lax.rem(i // per_expert, local_n)
        for l in range(layers_n):

            @pl.when(layer_of(i) == l)
            def of_layer():
                for one in make(l, e):
                    act(one)

    def results(l, e):
        return [
            pltpu.make_async_copy(stage_wide.at[0], grad_gate.at[l, e], out_sem.at[0]),
            pltpu.make_async_copy(stage_wide.at[1], grad_up.at[l, e], out_sem.at[1]),
            pltpu.make_async_copy(stage_tall, grad_down.at[l, e], out_sem.at[2]),
        ]

    greet(z, near, ("x", "y", "c"), n_dp)
    gather.line_first()
    for l in reversed(range(layers_n)):
        for k in range(1, n_dp):
            across(l, lax.rem(z + k, n_dp)).start()
    total.at(3, total.first)
    total.at(2, total.first)
    of(0, weights, start)
    fetch(0, 0, start)

    services = {
        0: [lambda: gather.arrivals(1, gather.take)],
        1: [lambda: gather.arrivals(2, gather.take)],
        2: [
            lambda: gather.arrivals(1, gather.second),
            lambda: gather.arrivals(3, gather.take),
        ],
        3: [
            lambda: gather.arrivals(1, gather.third),
            lambda: gather.arrivals(2, gather.second),
            lambda: total.at(3, total.second),
            lambda: total.at(2, total.second),
        ],
        4: [
            lambda: gather.arrivals(2, gather.third),
            lambda: gather.arrivals(3, gather.second),
            lambda: total.at(1, total.first),
            lambda: total.at(0, total.first),
        ],
        5: [
            lambda: gather.arrivals(3, gather.third),
            lambda: gather.arrivals(1, gather.finish),
            lambda: gather.arrivals(2, gather.finish),
            lambda: gather.arrivals(3, gather.finish),
        ],
        7: [lambda: total.at(3, total.third)],
        8: [lambda: total.at(2, total.third)],
        9: [lambda: total.at(1, total.second)],
        10: [lambda: total.at(0, total.second)],
        11: [lambda: total.at(1, total.third)],
    }

    def step(i, carry):
        slot = lax.rem(i, 2)
        l = layer_of(i)
        k = lax.rem(i, per_expert)
        e = lax.rem(i // per_expert, local_n)
        j = lax.rem(z + 1 + k, n_dp)

        @pl.when(k == 0)
        def begin():
            of(i, own, start)

        @pl.when((i + 1 < steps) & (i != per_layer - 1))
        def ahead():
            fetch(i + 1, 1 - slot, start)

        fetch(i, slot, wait)
        everyone = tokens[slot].reshape(-1, tokens.shape[3])
        experts_n = hit.shape[2]
        router = table[pl.ds(pl.multiple_of(l * experts_n, experts_n), experts_n), :].astype(bf16)
        gates[...] = masked_gates(mul(router, everyone, LAST), hit[l, j] > 0)
        pick = seat_rows(seats[l, j, pl.ds(e, 1)], number)
        rows_in[...] = mul(pick, everyone).astype(bf16)
        rows_grad[...] = mul(pick, grads[slot].reshape(-1, tokens.shape[3])).astype(bf16)
        place_of = pl.ds(pl.multiple_of((k + 1) * number, 32), number)
        mine = gates[pl.ds(lax.axis_index(EX) * local_n + e, 1), :]
        gate_seat = jnp.sum(pick.astype(f32) * mine, axis=1, keepdims=True)

        @pl.when(k == 0)
        def weights_here():
            of(i, weights, wait)

        gate = mul(rows_in[...], gate_w[...])
        up = mul(rows_in[...], up_w[...])
        raw = mul(rows_grad[...], down_w[...], LAST) * gate_seat
        sigmoid = 1.0 / (1.0 + jnp.exp(-gate))
        silu = gate * sigmoid
        hidden_low[place_of] = (silu * up).astype(bf16)
        dgate_low[place_of] = (raw * up * sigmoid * (1.0 + gate * (1.0 - sigmoid))).astype(bf16)
        dup_low[place_of] = (raw * silu).astype(bf16)
        cols_in[place_of] = rows_in[:, ours]
        cols_grad[place_of] = (rows_grad[:, ours].astype(f32) * gate_seat).astype(bf16)

        @pl.when(k == per_expert - 1)
        def close():
            @pl.when(i + 1 < steps)
            def next_weights():
                of(i + 1, weights, start)

            of(i, own, wait)

            @pl.when(i >= per_expert)
            def staged():
                of(i - per_expert, results, wait)

            over = ((0,), (0,))
            stage_wide[0] = mul(cols_in[...], dgate_low[...], over)
            stage_wide[1] = mul(cols_in[...], dup_low[...], over)
            stage_tall[...] = mul(hidden_low[...], cols_grad[...], over)
            of(i, results, start)

        for at, acts in services.items():

            @pl.when(i == at)
            def serve():
                for act in acts:
                    act()

        @pl.when(i == per_layer - 1)
        def late_ahead():
            fetch(i + 1, 1 - slot, start)

        return carry

    lax.fori_loop(0, steps, step, 0)
    total.at(0, total.third)
    for distance in (3, 2, 1, 0):
        total.at(distance, total.finish)
    gather.line_done()
    for l in range(layers_n):
        for k in range(1, n_dp):
            across(l, lax.rem(z + k, n_dp)).wait_send()
    of(steps - 1, results, wait)


def tail(
    capacity, number, tokens_all, grads_all, own_shard, table, hit, seats, weights, owns, parts
):
    layers_n, n_dp, local_n, group_rows = seats.shape
    n_expert = lax.axis_size(EX)
    rows, width = own_shard.shape
    hidden = weights[0].shape[3]
    part = width // n_dp
    shape = jax.ShapeDtypeStruct
    n_sums = len(parts)
    flat = [one for own in owns for one in own]
    results = pl.pallas_call(
        partial(tail_kernel, layers_n, capacity, n_sums),
        out_shape=[
            shape((layers_n, local_n, part, hidden), f32),
            shape((layers_n, local_n, part, hidden), f32),
            shape((layers_n, local_n, hidden, part), f32),
            shape((n_dp, n_expert, rows, width), bf16),
        ]
        + [shape(tokens_all[0].shape, bf16)] * layers_n
        + [shape(one.shape[2:], f32) for one in parts],
        in_specs=[HBM] * (2 * layers_n) + [VMEM] * 3 + [HBM] * (3 + len(flat) + n_sums),
        out_specs=[HBM] * (4 + layers_n) + [VMEM] * n_sums,
        scratch_shapes=[
            pltpu.VMEM((2, n_expert, rows, width), bf16),
            pltpu.VMEM((2, n_expert, rows, width), bf16),
            pltpu.VMEM(hit.shape[2:], f32),
            pltpu.VMEM((capacity, width), bf16),
            pltpu.VMEM((capacity, width), bf16),
            pltpu.VMEM((n_dp * capacity, part), bf16),
            pltpu.VMEM((n_dp * capacity, part), bf16),
            pltpu.VMEM((n_dp * capacity, hidden), bf16),
            pltpu.VMEM((n_dp * capacity, hidden), bf16),
            pltpu.VMEM((n_dp * capacity, hidden), bf16),
            pltpu.VMEM((width, hidden), bf16),
            pltpu.VMEM((width, hidden), bf16),
            pltpu.VMEM((hidden, width), bf16),
            pltpu.VMEM((2, part, hidden), f32),
            pltpu.VMEM((hidden, part), f32),
            pltpu.SemaphoreType.DMA((3,)),
            pltpu.SemaphoreType.DMA((2, 9)),
            pltpu.SemaphoreType.DMA((5,)),
            pltpu.SemaphoreType.DMA((3,)),
            pltpu.SemaphoreType.DMA((1, n_dp, KINDS)),
            pltpu.SemaphoreType.DMA((1, n_dp, KINDS)),
            pltpu.SemaphoreType.DMA((layers_n, n_dp)),
            pltpu.SemaphoreType.DMA((layers_n, n_dp)),
        ]
        + sums_scratch([one.shape[2:] for one in parts], n_dp),
        compiler_params=settings(number),
        name="tail",
    )(*tokens_all, *grads_all, own_shard, table, hit, seats, *weights, *flat, *parts)
    return results[:3], results[4 + layers_n :]


VMEM = pl.BlockSpec(memory_space=pltpu.VMEM)
HBM = pl.BlockSpec(memory_space=ANY)


def settings(number):
    return pltpu.CompilerParams(
        collective_id=number, has_side_effects=True, vmem_limit_bytes=62 << 20
    )


def chain(z, e, line):
    n_expert = 8
    behind = (z - jnp.where(e == 0, 1, 0), lax.rem(e + n_expert - 1, n_expert))
    ahead = (z + jnp.where(e == n_expert - 1, 1, 0), lax.rem(e + 1, n_expert))
    has_behind = (z > 0) | (e > 0)
    has_ahead = (z < line - 1) | (e < n_expert - 1)
    return behind, ahead, has_behind, has_ahead


def normalized(value, gain):
    scale = lax.rsqrt(jnp.mean(value * value, axis=-1, keepdims=True) + epsilon)
    return value * scale * gain


def turn(head, cosine, signed_sine):
    return head * cosine + pltpu.roll(head, HEAD_SIZE // 2, 1) * signed_sine


def head_of(h):
    return pl.ds(h * HEAD_SIZE, HEAD_SIZE)


def allowed_keys(rk, row, z, e, behind, has_behind, seg_column):
    own = rk[z, e, pl.ds(row, 1), :]
    first = rk[jnp.where(has_behind, behind[0], z), behind[1], pl.ds(row, 1), :]
    rows = seg_column.shape[0]
    query = lax.broadcasted_iota(jnp.int32, (rows, rows), 0)
    key = lax.broadcasted_iota(jnp.int32, (rows, rows), 1)
    reach = jnp.where(has_behind, 0, -1)
    return jnp.concatenate(
        [(first == seg_column) & (key >= rows * -reach), (own == seg_column) & (key <= query)],
        axis=1,
    )


def head_probs(query, keys, allowed):
    scores = mul(query, keys, LAST) * (1.0 / math.sqrt(HEAD_SIZE))
    scores = jnp.where(allowed, scores, masked_score)
    powers = jnp.exp(scores - jnp.max(scores, axis=-1, keepdims=True))
    return powers / jnp.sum(powers, axis=-1, keepdims=True)


def forward_kernel(layer, layers_n, number, *refs):
    first = layer == 0
    refs = list(refs)

    def some(count):
        taken = refs[:count]
        del refs[:count]
        return taken

    stream, cosine, sine, seg_column = some(4)
    if first:
        small, ranks, w_qkv, w_out = some(4)
    else:
        table, rk, hit, seats, turned, cross_from, qkv_from, out_from = some(8)
    w_gate, w_up, w_down = some(3)
    new_stream, layer_out, normed_a, queries, kv_out, attended, mixed, normed_b = some(8)
    rows_in, gate_pre, up_pre, gate_seat, quad = some(5)
    if first:
        table, rk_out, hit, seats, turned, qkv_out, out_out, qkv_next, out_next = some(9)
        small_land, rk, seat_all = some(3)
    else:
        (cross_to,) = some(1)
    (
        qkv,
        w_o,
        kv,
        projected,
        tokens,
        gates,
        weighted,
        gate_w,
        up_w,
        down_w,
        weight_sem,
        load_sem,
        chain_sem,
        quad_sem,
        send,
        recv,
    ) = some(16)
    if first:
        send_0, recv_0, send_1, recv_1, send_2, recv_2, send_3, recv_3, keep = some(9)
    else:
        cross_send, cross_recv, cross_keep = some(3)
    scratch = refs
    z, near = place()
    e = near["own"]
    line = lax.axis_size(DP)
    local_n = seats.shape[2]
    rows = stream.shape[0]
    experts_n = hit.shape[2]
    behind, ahead, has_behind, has_ahead = chain(z, e, line)

    weights = [
        pltpu.make_async_copy(src.at[layer], dst, weight_sem.at[i])
        for i, (src, dst) in enumerate(((w_gate, gate_w), (w_up, up_w), (w_down, down_w)))
    ]
    greet(z, near, ("x", "y", "c"), line, (behind, ahead, has_behind, has_ahead))
    if not first:
        cross = Gather([cross_from.at[0]], [cross_to], cross_send, cross_recv, z, near, line)
        cross.spread(1, cross_from, cross_keep)
    if first:
        g0 = Gather([small, ranks], [small_land, rk], send_0, recv_0, z, near, line)
        g1 = Gather([w_qkv.at[0]], [qkv], send_1, recv_1, z, near, line)
        g2 = Gather([w_out.at[0]], [w_o], send_2, recv_2, z, near, line)
        g3 = Gather(
            [w_qkv.at[1], w_out.at[1]], [qkv_next, out_next], send_3, recv_3, z, near, line
        )
        local = [
            pltpu.make_async_copy(one, g.outs[i].at[z, e], keep.at[k])
            for k, (g, i, one) in enumerate(
                (g, i, one) for g in (g0, g1, g2, g3) for i, one in enumerate(g.ins)
            )
        ]
        g0.line_first()
        g0.first(z, g0.ins)
        g1.line_first()
        g1.first(z, g1.ins)
        for one in local:
            one.start()
        g0.arrivals(1, g0.take)
        g0.second(z)
        g0.arrivals(2, g0.take)
        g0.third(z)
        g0.arrivals(1, g0.second)
        g0.arrivals(3, g0.take)
        g1.arrivals(1, g1.take)
        g2.line_first()
        g2.first(z, g2.ins)
        g0.arrivals(1, g0.third)
        g0.arrivals(2, g0.second)
        g1.second(z)
        g0.arrivals(2, g0.third)
        g0.arrivals(3, g0.second)
        g1.arrivals(2, g1.take)
        g0.arrivals(3, g0.third)
        g0.finish(z)
        for step in range(1, line):
            g0.arrivals(step, g0.finish)
        local[0].wait()
        local[1].wait()
        table[...] = jnp.transpose(small_land[...].reshape(-1, 128).astype(f32))
        g1.third(z)
        g1.arrivals(1, g1.second)
        for g in range(line):
            before = jnp.zeros((layers_n * experts_n, 1), f32)
            for d in range(8):
                lanes = pl.ds(d * rows, rows)
                rank = rk[g, d, pl.ds(0, layers_n * experts_n), :].astype(f32)
                seat_all[g, :, lanes] = jnp.where(rank > 0, rank + before, 0.0)
                for l in range(layers_n):
                    hit[l, g, :, lanes] = rank[l * experts_n : (l + 1) * experts_n]
                here = jnp.where(rank > 0, 1.0, 0.0)
                before = before + jnp.sum(here, axis=1, keepdims=True)
            for l in range(layers_n):
                for k in range(local_n):
                    row = pl.ds(l * experts_n + e * local_n + k, 1)
                    seats[l, g, pl.ds(k, 1), :] = seat_all[g, row, :]
        g1.arrivals(3, g1.take)
        wide = jnp.zeros((rows - layers_n * local_n, rows), f32)
        for d in range(8):
            lanes = pl.ds(d * rows, rows)
            mine = [seats[l, z, :, lanes] for l in range(layers_n)]
            turned[lanes, :] = jnp.transpose(jnp.concatenate(mine + [wide], axis=0))
        rk_out[...] = rk[...]
        g1.arrivals(1, g1.third)
        g1.arrivals(2, g1.second)
        g2.arrivals(1, g2.take)
        g1.arrivals(2, g1.third)
        g1.arrivals(3, g1.second)
        g2.second(z)
        g2.arrivals(2, g2.take)
        g1.arrivals(3, g1.third)
        g2.third(z)
        g1.finish(z)
        for step in range(1, line):
            g1.arrivals(step, g1.finish)
        local[2].wait()
        g2.arrivals(1, g2.second)
        g2.arrivals(3, g2.take)
    else:
        loads = [
            pltpu.make_async_copy(qkv_from, qkv, load_sem.at[0]),
            pltpu.make_async_copy(out_from, w_o, load_sem.at[1]),
        ]
        for one in loads:
            one.start()
    for one in weights:
        one.start()
    gain = 2 * experts_n + 2 * layer
    x = stream[...].astype(f32)
    normed_a[...] = normalized(x, table[pl.ds(gain, 1), :]).astype(bf16)
    if not first:
        loads[0].wait()
    width = queries.shape[1]
    projected[...] = mul(normed_a[...], qkv[...].reshape(width, -1))
    keys_n = KEY_VALUE_HEADS * HEAD_SIZE
    cos, sin = cosine[...], sine[...]
    for h in range(KEY_VALUE_HEADS):
        key = turn(projected[:, head_of(QUERY_HEADS + h)], cos, sin)
        kv[1, :, head_of(h)] = key.astype(bf16)
    kv[1, :, pl.ds(keys_n, keys_n)] = projected[:, pl.ds(width + keys_n, keys_n)].astype(bf16)

    def pass_on(target):
        return pltpu.make_async_remote_copy(
            src_ref=kv.at[1],
            dst_ref=kv.at[0],
            send_sem=chain_sem.at[0],
            recv_sem=chain_sem.at[1],
            device_id={DP: target[0], EX: target[1]},
            device_id_type=MESH,
        )

    @pl.when(has_ahead)
    def pass_ahead():
        pass_on(ahead).start()

    if first:
        g2.arrivals(1, g2.third)
        g2.arrivals(2, g2.second)
        g3.line_first()
        g3.first(z, g3.ins)
    else:
        cross.spread(2, cross_from, cross_keep)
    for h in range(QUERY_HEADS):
        queries[:, head_of(h)] = turn(projected[:, head_of(h)], cos, sin).astype(bf16)
    allowed = allowed_keys(rk, layers_n * experts_n, z, e, behind, has_behind, seg_column[...])

    @pl.when(has_behind)
    def from_behind_here():
        pass_on(behind).wait_recv()

    @pl.when(jnp.logical_not(has_behind))
    def nobody_behind():
        kv[0] = jnp.zeros_like(kv[0])

    for h in range(QUERY_HEADS):
        group = h // (QUERY_HEADS // KEY_VALUE_HEADS)
        keys = kv[:, :, head_of(group)].reshape(2 * rows, HEAD_SIZE)
        values = kv[:, :, head_of(KEY_VALUE_HEADS + group)].reshape(2 * rows, HEAD_SIZE)
        probs = head_probs(queries[:, head_of(h)], keys, allowed).astype(bf16)
        attended[:, head_of(h)] = mul(probs, values).astype(bf16)
        if first and h == 3:
            g2.arrivals(2, g2.third)
            g2.arrivals(3, g2.second)
        if first and h == 7:
            g2.arrivals(3, g2.third)
            g3.arrivals(1, g3.take)
        if not first and h == 3:
            cross.second(cross.plane_of(1))
        if not first and h == 9:
            cross.second(cross.plane_of(2))
            cross.third(cross.plane_of(1))
    kv_out[...] = kv[...]
    if first:
        g2.finish(z)
        for step in range(1, line):
            g2.arrivals(step, g2.finish)
        local[3].wait()
    else:
        loads[1].wait()
    mixed[...] = x + mul(attended[...], w_o[...].reshape(width, -1))
    normed_b[...] = normalized(mixed[...], table[pl.ds(gain + 1, 1), :]).astype(bf16)

    one, two, three, four = plane_gather(normed_b, tokens, send, recv, near)
    one()
    if first:
        g3.second(z)
        g3.arrivals(2, g3.take)
    two()
    three()
    if first:
        g3.third(z)
        g3.arrivals(1, g3.second)
        g3.arrivals(3, g3.take)
    four()
    quads = [
        pltpu.make_async_copy(tokens.at[near[name]], quad.at[i], quad_sem.at[i])
        for i, name in enumerate(QUAD)
    ]
    for copied in quads:
        copied.start()
    everyone = tokens[...].reshape(-1, width)
    router = table[pl.ds(layer * experts_n, experts_n), :].astype(bf16)
    gates[...] = masked_gates(mul(router, everyone, LAST), hit[layer, z] > 0)
    pick = seat_rows(seats[layer, z], number)
    for k in range(local_n):
        here = pl.ds(k * number, number)
        mine = gates[pl.ds(e * local_n + k, 1), :]
        gate_seat[here] = jnp.sum(
            pick[k * number : (k + 1) * number].astype(f32) * mine, axis=1, keepdims=True
        )
    rows_in[...] = mul(pick, everyone).astype(bf16)
    for copied in weights:
        copied.wait()
    if first:
        g3.arrivals(1, g3.third)
        g3.arrivals(2, g3.second)
    else:
        cross.spread(3, cross_from, cross_keep)

    def expert(k, carry):
        here = pl.ds(pl.multiple_of(k * number, 32), number)
        x = rows_in[here]
        gate = mul(x, gate_w[k])
        up = mul(x, up_w[k])
        gate_pre[here] = gate
        up_pre[here] = up
        hidden = (gate * (1.0 / (1.0 + jnp.exp(-gate))) * up).astype(bf16)
        weighted[here] = (mul(hidden, down_w[k]) * gate_seat[here]).astype(bf16)
        return carry

    lax.fori_loop(0, local_n, expert, 0)
    if first:
        g3.arrivals(2, g3.third)
        g3.arrivals(3, g3.second)
        out_copies = [
            pltpu.make_async_copy(qkv, qkv_out, load_sem.at[0]),
            pltpu.make_async_copy(w_o, out_out, load_sem.at[1]),
        ]
        for copied in out_copies:
            copied.start()
    else:
        cross.second(cross.plane_of(3))
        cross.third(cross.plane_of(2))

    def make(name):
        d = near[name]
        lanes = pl.ds(pl.multiple_of(d * rows, rows), rows)
        mine = turned[lanes, pl.ds(layer * local_n, local_n)]
        scratch[0][d] = mul(seat_columns(mine, number), weighted[...]).astype(bf16)

    plane_sum(make, new_stream, mixed, scratch, near)
    layer_out[...] = new_stream[...].astype(bf16)

    for copied in quads:
        copied.wait()

    @pl.when(has_ahead)
    def passed_on():
        pass_on(ahead).wait_send()

    if first:
        g3.arrivals(3, g3.third)
        g3.finish(z)
        for step in range(1, line):
            g3.arrivals(step, g3.finish)
        for copied in local[4:] + out_copies:
            copied.wait()
        for g in (g0, g1, g2, g3):
            g.line_done()
    else:
        cross.third(cross.plane_of(3))
        cross.spread_done(cross_from, cross_keep)


def layer_forward(layer, number, shapes, stream, tables, given, weights):
    layers_n, n_dp, n_expert, local_n, capacity = shapes
    first = layer == 0
    rows, width = stream.shape
    hidden = weights[0].shape[3]
    experts_n = local_n * n_expert
    seats_n = local_n * capacity
    keys_n = KEY_VALUE_HEADS * HEAD_SIZE
    group = n_expert * rows
    cut_rows = width // (n_dp * n_expert)
    shape = jax.ShapeDtypeStruct
    outs = [
        shape((rows, width), f32),
        shape((rows, width), bf16),
        shape((rows, width), bf16),
        shape((rows, width), bf16),
        shape((2, rows, 2 * keys_n), bf16),
        shape((rows, width), bf16),
        shape((rows, width), f32),
        shape((rows, width), bf16),
        shape((seats_n, width), bf16),
        shape((seats_n, hidden), f32),
        shape((seats_n, hidden), f32),
        shape((seats_n, 1), f32),
        shape((len(QUAD), rows, width), bf16),
    ]
    specs = [VMEM] * 12 + [HBM]
    scratch = []
    full_qkv = (n_dp, n_expert, cut_rows, width + 2 * keys_n)
    full_out = (n_dp, n_expert, cut_rows, width)
    if first:
        rank_rows = given[1].shape[0]
        outs += [
            shape((128, width), f32),
            shape((n_dp, n_expert, rank_rows, rows), jnp.int32),
            shape((layers_n, n_dp, experts_n, group), f32),
            shape((layers_n, n_dp, local_n, group), f32),
            shape((group, 128), f32),
        ]
        outs += [shape(full_qkv, bf16), shape(full_out, bf16)] * 2
        specs += [VMEM] * 5 + [HBM] * 4
        scratch += [
            pltpu.VMEM((n_dp, n_expert, cut_rows, 128), bf16),
            pltpu.VMEM((n_dp, n_expert, rank_rows, rows), jnp.int32),
            pltpu.VMEM((n_dp, layers_n * experts_n, group), f32),
        ]
    else:
        outs.append(shape((n_dp, n_expert, rows, width), bf16))
        specs.append(HBM)
    scratch += [
        pltpu.VMEM(full_qkv, bf16),
        pltpu.VMEM(full_out, bf16),
        pltpu.VMEM((2, rows, 2 * keys_n), bf16),
        pltpu.VMEM((rows, width + 2 * keys_n), f32),
        pltpu.VMEM((n_expert, rows, width), bf16),
        pltpu.VMEM((experts_n, group), f32),
        pltpu.VMEM((seats_n, width), bf16),
        pltpu.VMEM((local_n, width, hidden), bf16),
        pltpu.VMEM((local_n, width, hidden), bf16),
        pltpu.VMEM((local_n, hidden, width), bf16),
        pltpu.SemaphoreType.DMA((3,)),
        pltpu.SemaphoreType.DMA((2,)),
        pltpu.SemaphoreType.DMA((2,)),
        pltpu.SemaphoreType.DMA((len(QUAD),)),
        pltpu.SemaphoreType.DMA((8,)),
        pltpu.SemaphoreType.DMA((8,)),
    ]
    if first:
        for count in (2, 1, 1, 2):
            scratch += [pltpu.SemaphoreType.DMA((count, n_dp, KINDS)) for i in range(2)]
        scratch.append(pltpu.SemaphoreType.DMA((6,)))
    else:
        scratch += [pltpu.SemaphoreType.DMA((1, n_dp, KINDS)) for i in range(2)]
        scratch.append(pltpu.SemaphoreType.DMA((n_dp,)))
    given_specs = [HBM] * 4 if first else [VMEM] * 5 + [HBM] * 3
    return pl.pallas_call(
        partial(forward_kernel, layer, layers_n, capacity),
        out_shape=outs,
        in_specs=[VMEM] * 4 + given_specs + [HBM] * 3,
        out_specs=specs,
        scratch_shapes=scratch + sum_scratch(rows, width),
        compiler_params=settings(number),
        name="layer_forward",
    )(stream, *tables, *given, *weights)


def norm_back(value, gain, grad):
    scale = lax.rsqrt(jnp.mean(value * value, axis=-1, keepdims=True) + epsilon)
    unit = value * scale
    inner = grad * gain
    back = scale * (inner - unit * jnp.mean(inner * unit, axis=-1, keepdims=True))
    return back, jnp.sum(grad * unit, axis=0, keepdims=True)


def backward_kernel(layer, layers_n, number, *refs):
    refs = list(refs)

    def some(count):
        taken = refs[:count]
        del refs[:count]
        return taken

    grad_stream, stream, cosine, sine, seg_column = some(5)
    mixed, normed_b, queries, kv, gate_pre, up_pre, gate_seat = some(7)
    table, rk, hit, seats, turned = some(5)
    qkv_from, out_from, w_gate, w_up, w_down = some(5)
    grad_out, grad_low, rows_grad, hidden_low, dgate_low, dup_low = some(6)
    dprojected, grad_attn, small = some(3)
    (
        summed,
        qkv,
        w_o,
        datt,
        dkv,
        dkv_send,
        dkv_got,
        tokens,
        back_rows,
        gate_w,
        up_w,
        down_w,
        weight_sem,
        load_sem,
        chain_sem,
        send,
        recv,
    ) = some(17)
    scratch = refs
    z, near = place()
    e = near["own"]
    line = lax.axis_size(DP)
    local_n = seats.shape[2]
    rows, width = stream.shape
    experts_n = hit.shape[2]
    behind, ahead, has_behind, has_ahead = chain(z, e, line)
    weights = [
        pltpu.make_async_copy(src.at[layer], dst, weight_sem.at[i])
        for i, (src, dst) in enumerate(((w_gate, gate_w), (w_up, up_w), (w_down, down_w)))
    ]
    loads = [
        pltpu.make_async_copy(qkv_from, qkv, load_sem.at[0]),
        pltpu.make_async_copy(out_from, w_o, load_sem.at[1]),
    ]
    grad_low[...] = grad_stream[...].astype(bf16)
    greet(z, near, ("x", "y", "c"), None, (behind, ahead, has_behind, has_ahead))

    first, second, third, finish = plane_gather(grad_low, tokens, send, recv, near)
    first()
    for one in weights + loads:
        one.start()
    second()
    third()
    finish()
    everyone = tokens[...].reshape(-1, width)
    picked = mul(seat_rows(seats[layer, z], number), everyone)
    back_rows[:, pl.ds(0, width)] = picked.astype(bf16)
    rows_grad[...] = (picked * gate_seat[...]).astype(bf16)
    for one in weights:
        one.wait()

    def expert(k, carry):
        here = pl.ds(pl.multiple_of(k * number, 32), number)
        gate, up = gate_pre[here], up_pre[here]
        raw = mul(back_rows[here, pl.ds(0, width)], down_w[k], LAST)
        sigmoid = 1.0 / (1.0 + jnp.exp(-gate))
        silu = gate * sigmoid
        hidden = (silu * up).astype(bf16)
        hidden_low[here] = hidden
        dgate_seat = jnp.sum(hidden.astype(f32) * raw, axis=1, keepdims=True)
        raw = raw * gate_seat[here]
        dgate = (raw * up * sigmoid * (1.0 + gate * (1.0 - sigmoid))).astype(bf16)
        dup = (raw * silu).astype(bf16)
        dgate_low[here] = dgate
        dup_low[here] = dup
        back_rows[here, pl.ds(0, width)] = (
            mul(dgate, gate_w[k], LAST) + mul(dup, up_w[k], LAST)
        ).astype(bf16)
        high = dgate_seat.astype(bf16).astype(f32)
        lane = lax.broadcasted_iota(jnp.int32, (number, 128), 1)
        mine = e * local_n + k
        back_rows[here, pl.ds(width, 128)] = jnp.where(
            lane == mine, high, jnp.where(lane == experts_n + mine, dgate_seat - high, 0.0)
        ).astype(bf16)
        return carry

    lax.fori_loop(0, local_n, expert, 0)

    def make(name):
        d = near[name]
        lanes = pl.ds(pl.multiple_of(d * rows, rows), rows)
        mine = turned[lanes, pl.ds(layer * local_n, local_n)]
        scratch[0][d] = mul(seat_columns(mine, number), back_rows[...]).astype(bf16)

    plane_sum(make, summed, None, scratch, near)

    over = ((0,), (0,))
    gain = 2 * experts_n + 2 * layer
    router = table[pl.ds(layer * experts_n, experts_n), :].astype(bf16)
    own_lanes = pl.ds(pl.multiple_of(e * rows, rows), rows)
    gates = masked_gates(mul(router, normed_b[...], LAST), hit[layer, z, :, own_lanes] > 0)
    turned_sum = jnp.transpose(summed[:, pl.ds(width, 128)])
    dgates = turned_sum[:experts_n] + turned_sum[experts_n : 2 * experts_n]
    inner = jnp.sum(gates * dgates, axis=0, keepdims=True)
    dlogits = (gates * (dgates - inner)).astype(bf16)
    small[pl.ds(0, experts_n)] = mul(dlogits, normed_b[...])
    dnormed = summed[:, pl.ds(0, width)] + mul(dlogits, router, over)
    back, dgain = norm_back(mixed[...], table[pl.ds(gain + 1, 1), :], dnormed)
    small[pl.ds(experts_n + 1, 1)] = dgain
    dmixed = grad_stream[...].astype(f32) + back
    grad_out[...] = dmixed
    grad_attn[...] = dmixed.astype(bf16)

    loads[1].wait()
    datt[...] = mul(grad_attn[...], w_o[...].reshape(width, -1), LAST).astype(bf16)
    allowed = allowed_keys(rk, layers_n * experts_n, z, e, behind, has_behind, seg_column[...])
    cos, sin = cosine[...], sine[...]
    per_group = QUERY_HEADS // KEY_VALUE_HEADS
    scale = 1.0 / math.sqrt(HEAD_SIZE)
    for group in range(KEY_VALUE_HEADS):
        keys = kv[:, :, head_of(group)].reshape(2 * rows, HEAD_SIZE)
        values = kv[:, :, head_of(KEY_VALUE_HEADS + group)].reshape(2 * rows, HEAD_SIZE)
        dkeys = jnp.zeros((2 * rows, HEAD_SIZE), f32)
        dvalues = jnp.zeros((2 * rows, HEAD_SIZE), f32)
        for h in range(group * per_group, (group + 1) * per_group):
            query = queries[:, head_of(h)]
            probs = head_probs(query, keys, allowed)
            given = datt[:, head_of(h)]
            dprobs = mul(given, values, LAST)
            delta = jnp.sum(probs * dprobs, axis=-1, keepdims=True)
            dscores = (probs * (dprobs - delta)).astype(bf16)
            dquery = mul(dscores, keys) * scale
            dprojected[:, head_of(h)] = turn(dquery, cos, -sin).astype(bf16)
            dkeys = dkeys + mul(dscores, query, over)
            dvalues = dvalues + mul(probs.astype(bf16), given, over)
        dkv[:, head_of(group)] = dkeys * scale
        dkv[:, head_of(KEY_VALUE_HEADS + group)] = dvalues
    dkv_send[...] = dkv[pl.ds(0, rows)].astype(bf16)

    def pass_on(target):
        return pltpu.make_async_remote_copy(
            src_ref=dkv_send,
            dst_ref=dkv_got,
            send_sem=chain_sem.at[0],
            recv_sem=chain_sem.at[1],
            device_id={DP: target[0], EX: target[1]},
            device_id_type=MESH,
        )

    @pl.when(has_behind)
    def pass_back():
        pass_on(behind).start()

    loads[0].wait()
    query_part = pl.ds(0, width)
    key_part = pl.ds(width, dkv.shape[1])
    weights_q = qkv[:, :, :, query_part].reshape(-1, width)
    dnormed = mul(dprojected[:, query_part], weights_q, LAST)

    @pl.when(has_ahead)
    def from_ahead_here():
        pass_on(ahead).wait_recv()
        dkv[pl.ds(rows, rows)] += dkv_got[...].astype(f32)

    for h in range(KEY_VALUE_HEADS):
        dkey = turn(dkv[pl.ds(rows, rows), head_of(h)], cos, -sin)
        dprojected[:, head_of(QUERY_HEADS + h)] = dkey.astype(bf16)
        dvalue = dkv[pl.ds(rows, rows), head_of(KEY_VALUE_HEADS + h)]
        dprojected[:, head_of(QUERY_HEADS + KEY_VALUE_HEADS + h)] = dvalue.astype(bf16)
    weights_kv = qkv[:, :, :, key_part].reshape(-1, dkv.shape[1])
    dnormed = dnormed + mul(dprojected[:, key_part], weights_kv, LAST)
    back, dgain = norm_back(stream[...].astype(f32), table[pl.ds(gain, 1), :], dnormed)
    small[pl.ds(experts_n, 1)] = dgain
    grad_out[...] += back

    @pl.when(has_behind)
    def passed_back():
        pass_on(behind).wait_send()


def layer_backward(layer, number, shapes, grads, stream, tables, saved, plan, weights):
    layers_n, n_dp, n_expert, local_n, capacity = shapes
    rows, width = stream.shape
    hidden = weights[-1].shape[2]
    experts_n = local_n * n_expert
    seats_n = local_n * capacity
    keys_n = KEY_VALUE_HEADS * HEAD_SIZE
    cut_rows = width // (n_dp * n_expert)
    shape = jax.ShapeDtypeStruct
    outs = [
        shape((rows, width), f32),
        shape((rows, width), bf16),
        shape((seats_n, width), bf16),
        shape((seats_n, hidden), bf16),
        shape((seats_n, hidden), bf16),
        shape((seats_n, hidden), bf16),
        shape((rows, width + 2 * keys_n), bf16),
        shape((rows, width), bf16),
        shape((experts_n + 2, width), f32),
    ]
    scratch = [
        pltpu.VMEM((rows, width + 128), f32),
        pltpu.VMEM((n_dp, n_expert, cut_rows, width + 2 * keys_n), bf16),
        pltpu.VMEM((n_dp, n_expert, cut_rows, width), bf16),
        pltpu.VMEM((rows, width), bf16),
        pltpu.VMEM((2 * rows, 2 * keys_n), f32),
        pltpu.VMEM((rows, 2 * keys_n), bf16),
        pltpu.VMEM((rows, 2 * keys_n), bf16),
        pltpu.VMEM((n_expert, rows, width), bf16),
        pltpu.VMEM((seats_n, width + 128), bf16),
        pltpu.VMEM((local_n, width, hidden), bf16),
        pltpu.VMEM((local_n, width, hidden), bf16),
        pltpu.VMEM((local_n, hidden, width), bf16),
        pltpu.SemaphoreType.DMA((3,)),
        pltpu.SemaphoreType.DMA((2,)),
        pltpu.SemaphoreType.DMA((2,)),
        pltpu.SemaphoreType.DMA((8,)),
        pltpu.SemaphoreType.DMA((8,)),
    ]
    return pl.pallas_call(
        partial(backward_kernel, layer, layers_n, capacity),
        out_shape=outs,
        in_specs=[VMEM] * 17 + [HBM] * 5,
        out_specs=[VMEM] * 9,
        scratch_shapes=scratch + sum_scratch(rows, width + 128),
        compiler_params=settings(number),
        name="layer_backward",
    )(grads, stream, *tables, *saved, *plan, *weights)


class Sums:
    def __init__(self, ins, outs, held, send, recv, keep, z, near, line):
        self.ins, self.outs, self.held = ins, outs, held
        self.send, self.recv, self.keep = send, recv, keep
        self.z, self.near, self.line = z, near, line
        self.all = range(len(ins))

    def split(self, a):
        half = self.outs[a].shape[1] // 2
        return pl.ds(0, half), pl.ds(half, half)

    def move(self, a, j, name):
        part = self.ins[a]
        fromx, fromy, late, later, total, got = self.held[a]
        A, B = self.split(a)
        near = self.near
        kind, src, dst, to = {
            "xd": lambda: (0, part.at[j, near["d"], :, A], fromx.at[j, 0], "x"),
            "xx": lambda: (1, part.at[j, near["x"], :, A], fromx.at[j, 1], "x"),
            "yd": lambda: (2, part.at[j, near["d"], :, B], fromy.at[j, 0], "y"),
            "yy": lambda: (3, part.at[j, near["y"], :, B], fromy.at[j, 1], "y"),
            "ly": lambda: (4, late.at[j, 0], later.at[j, 0], "y"),
            "lx": lambda: (5, late.at[j, 1], later.at[j, 1], "x"),
            "up": lambda: (6, total.at[j], got.at[j], self.z + 1),
            "down": lambda: (7, total.at[j], got.at[j], self.z - 1),
        }[name]()
        if name == "down":
            slot = jnp.where(j == self.z - 1, self.line, j)
            dst = got.at[slot]
        return pltpu.make_async_remote_copy(
            src_ref=src,
            dst_ref=dst,
            send_sem=self.send.at[a, j, kind],
            recv_sem=self.recv.at[a, j, kind],
            device_id={DP: to} if kind >= 6 else {EX: near[to]},
            device_id_type=MESH,
        )

    def own_down(self, a):
        got = self.held[a][5]
        return pltpu.make_async_remote_copy(
            src_ref=got.at[self.line],
            dst_ref=got.at[self.line],
            send_sem=self.send.at[a, self.z, 7],
            recv_sem=self.recv.at[a, self.z, 7],
            device_id={DP: self.z},
            device_id_type=MESH,
        )

    def prepare(self, a, j):
        late, total = self.held[a][2], self.held[a][4]
        A, B = self.split(a)
        near, part = self.near, self.ins[a]
        return [
            pltpu.make_async_copy(src, dst, self.keep.at[a, j, i])
            for i, (src, dst) in enumerate(
                (
                    (part.at[j, near["y"], :, A], late.at[j, 0]),
                    (part.at[j, near["x"], :, B], late.at[j, 1]),
                    (part.at[j, near["own"]], total.at[j]),
                )
            )
        ]

    def at(self, step, act):
        if step == 0:
            act(self.z, 0)
            return

        @pl.when(self.z + step <= self.line - 1)
        def above():
            act(self.z + step, 1)

        @pl.when(self.z - step >= 0)
        def below():
            act(self.z - step, -1)

    def first(self, j, way):
        for a in self.all:
            for name in ("xd", "yd", "xx", "yy"):
                self.move(a, j, name).start()
            for one in self.prepare(a, j):
                one.start()

    def second(self, j, way):
        for a in self.all:
            fromx, fromy, late = self.held[a][:3]
            ready = self.prepare(a, j)
            ready[0].wait()
            self.move(a, j, "xd").wait_recv()
            late[j, 0] = (late[j, 0].astype(f32) + fromx[j, 0].astype(f32)).astype(bf16)
            self.move(a, j, "ly").start()
            ready[1].wait()
            self.move(a, j, "yd").wait_recv()
            late[j, 1] = (late[j, 1].astype(f32) + fromy[j, 0].astype(f32)).astype(bf16)
            self.move(a, j, "lx").start()

    def third(self, j, way):
        for a in self.all:
            fromx, fromy, late, later, total, got = self.held[a]
            for name in ("xx", "yy", "ly", "lx"):
                self.move(a, j, name).wait_recv()
            self.prepare(a, j)[2].wait()
            for side, (columns, here) in enumerate(zip(self.split(a), (fromx, fromy))):
                value = (
                    total[j, :, columns].astype(f32)
                    + here[j, 1].astype(f32)
                    + later[j, side].astype(f32)
                )
                if way == 0:
                    self.outs[a][:, columns] = value
                else:
                    total[j, :, columns] = value.astype(bf16)
            if way == 1:

                @pl.when(self.z > 0)
                def more_up():
                    self.move(a, j, "up").wait_recv()
                    total[j] = (total[j].astype(f32) + got[j].astype(f32)).astype(bf16)

                self.move(a, j, "up").start()
            elif way == -1:

                @pl.when(self.z < self.line - 1)
                def more_down():
                    self.move(a, j, "down").wait_recv()
                    total[j] = (total[j].astype(f32) + got[j].astype(f32)).astype(bf16)

                self.move(a, j, "down").start()
            else:

                @pl.when(self.z > 0)
                def end_up():
                    self.move(a, j, "up").wait_recv()
                    self.outs[a][...] += got[j].astype(f32)

                @pl.when(self.z < self.line - 1)
                def end_down():
                    self.own_down(a).wait_recv()
                    self.outs[a][...] += got[self.line].astype(f32)

    def finish(self, j, way):
        for a in self.all:
            for name in ("xd", "yd", "xx", "yy", "lx", "ly"):
                self.move(a, j, name).wait_send()
            if way == 1:
                self.move(a, j, "up").wait_send()
            elif way == -1:
                self.move(a, j, "down").wait_send()


def sums_scratch(shapes, line):
    scratch = []
    for rows, columns in shapes:
        half = columns // 2
        scratch += [pltpu.VMEM((line, 2, rows, half), bf16) for i in range(4)]
        scratch += [
            pltpu.VMEM((line, rows, columns), bf16),
            pltpu.VMEM((line + 1, rows, columns), bf16),
        ]
    return scratch + [
        pltpu.SemaphoreType.DMA((len(shapes), line, 8)),
        pltpu.SemaphoreType.DMA((len(shapes), line, 8)),
        pltpu.SemaphoreType.DMA((len(shapes), line, 3)),
    ]


def from_behind(value, axis, steps):
    count = lax.axis_size(axis)
    leading, last = (max(0, -steps), min(count, count - steps))
    return lax.ppermute(value, axis, [(source, source + steps) for source in range(leading, last)])


def from_sibling(value):
    count = lax.axis_size(EX)
    return lax.ppermute(value, EX, [(s, s + 1 - 2 * (s % 2)) for s in range(count)])


def rms_norm(stream, gain_row):
    return (
        stream * lax.rsqrt(jnp.mean(stream * stream, axis=-1, keepdims=True) + epsilon) * gain_row
    )


def rotary_tables(token_positions):
    half_dim = HEAD_SIZE // 2
    steps_up = jnp.arange(half_dim).astype(f32)
    frequency = jnp.exp(steps_up * (-2.0 * math.log(rope_base) / HEAD_SIZE))
    angles = token_positions.astype(f32)[:, None] * frequency[None, :]
    return jnp.cos(angles)[:, None, :], jnp.sin(angles)[:, None, :]


def apply_rotary(heads_in, cosine, sine_part):
    half_dim = heads_in.shape[-1] // 2
    first_half = heads_in[..., :half_dim]
    second_half = heads_in[..., half_dim:]
    return jnp.concatenate(
        [
            first_half * cosine - second_half * sine_part,
            second_half * cosine + first_half * sine_part,
        ],
        axis=-1,
    )


def gated_unit(gate_pre, up_pre):
    return jax.nn.silu(gate_pre) * up_pre


def masked_scores(query_rows, gathered_keys, allowed):
    token_rows = query_rows.shape[0]
    grouped_queries = query_rows.reshape(
        token_rows, KEY_VALUE_HEADS, QUERY_HEADS // KEY_VALUE_HEADS, HEAD_SIZE
    )
    score_scale = 1.0 / math.sqrt(HEAD_SIZE)
    scores = (
        jnp.einsum(
            "tkgd,skd->kgts", grouped_queries, gathered_keys, preferred_element_type=f32
        )
        * score_scale
    )
    return (jnp.where(allowed, scores, masked_score), grouped_queries)


def rank_table(routes, pair_order, experts_n):
    layers_n, token_rows, topk_n = routes.shape
    chosen = jnp.swapaxes(routes, 1, 2)
    order = jnp.swapaxes(pair_order.reshape(layers_n, token_rows, topk_n), 1, 2)
    ids = jnp.arange(experts_n, dtype=jnp.int32)[None, :, None]
    none = token_rows * topk_n
    place_of = jnp.full((layers_n, experts_n, token_rows), none, jnp.int32)
    for k in range(topk_n):
        place_of = jnp.where(chosen[:, k][:, None, :] == ids, order[:, k][:, None, :], place_of)
    smaller = (place_of[:, :, :, None] < place_of[:, :, None, :]).astype(jnp.int32)
    return jnp.where(place_of < none, jnp.sum(smaller, axis=2) + 1, 0)


def dense_gates(logits, mask):
    top = jnp.max(jnp.where(mask, logits, masked_score), axis=0, keepdims=True)
    powers = jnp.where(mask, jnp.exp(jnp.where(mask, logits - top, 0.0)), 0.0)
    return powers / jnp.sum(powers, axis=0, keepdims=True)


def local_chips(
    tokens,
    w_qkv,
    w_out,
    w_router,
    norm_gains,
    w_gate,
    w_up,
    w_down,
    out_grad,
    segment_ids,
    routes,
    pair_order,
):
    token_rows = tokens.shape[0]
    layers_n = w_qkv.shape[0]
    topk_n = routes.shape[2]
    n_expert = lax.axis_size(EX)
    n_dp = lax.axis_size(DP)
    local_n = w_gate.shape[1]
    experts_n = local_n * n_expert
    capacity = 9 * n_expert * token_rows * topk_n // (8 * experts_n)
    shapes = (layers_n, n_dp, n_expert, local_n, capacity)
    positions = lax.axis_index(EX) * token_rows + jnp.arange(token_rows, dtype=jnp.int32)
    cosine, sine = rotary_tables(positions)
    tables = (
        jnp.concatenate([cosine, cosine], axis=-1)[:, 0],
        jnp.concatenate([-sine, sine], axis=-1)[:, 0],
        segment_ids[:, None],
    )
    ranks = rank_table(routes, pair_order, experts_n).reshape(layers_n * experts_n, token_rows)
    ranks = jnp.concatenate([ranks, segment_ids[None], jnp.zeros((7, token_rows), jnp.int32)])
    small = jnp.concatenate(
        [w_router[l] for l in range(layers_n)]
        + [jnp.swapaxes(norm_gains.reshape(2 * layers_n, -1), 0, 1)],
        axis=1,
    )
    small = jnp.pad(small, ((0, 0), (0, 128 - small.shape[1])))
    experts = (w_gate, w_up, w_down)

    def along_line(rows):
        return lax.all_gather(rows, DP, axis=0)

    saved, outputs, normed_all, streams = [], [], [], [tokens]
    for l in range(layers_n):
        given = (small, ranks, w_qkv, w_out) if l == 0 else (*plan, along_line(out_grad), *full[l])
        results = layer_forward(l, 1 + l, shapes, streams[l], tables, given, experts)
        if l == 0:
            plan = results[13:18]
            full = [results[18:20], results[20:22]]
        else:
            grads_all = [results[13]]
        streams.append(results[0])
        outputs.append(results[1])
        saved.append(results[2:12])
        normed_all.append(along_line(results[12]))

    grads = out_grad
    owns, parts, smalls = [None] * layers_n, [None] * layers_n, [None] * layers_n
    for l in reversed(range(layers_n)):
        normed_a, queries, kv, attended, mixed, normed_b, rows_in = saved[l][:7]
        kept = (mixed, normed_b, queries, kv, *saved[l][7:])
        sources = (*full[l], *experts)
        results = layer_backward(
            l, 4 + l, shapes, grads, streams[l], tables, kept, plan, sources
        )
        grads, own_shard = results[:2]
        owns[l] = (rows_in, *results[2:6])
        dprojected, grad_attn, small_grad = results[6:9]
        other = from_sibling((normed_a, attended, dprojected, grad_attn))
        pairs = [
            jnp.concatenate([own, sib], axis=0)
            for own, sib in zip((normed_a, attended, dprojected, grad_attn), other)
        ]
        parts[l] = [
            lax.dot_general(
                one, another, (((0,), (0,)), ((), ())), preferred_element_type=f32
            ).astype(bf16)
            for one, another in ((pairs[0], pairs[2]), (pairs[1], pairs[3]))
        ]
        smalls[l] = small_grad + from_sibling(small_grad)
    cut_shape = (n_dp, n_expert, D // (n_dp * n_expert))
    wide = experts_n + 2
    small_grads = jnp.pad(jnp.concatenate(smalls), ((0, 128 - layers_n * wide), (0, 0))).T
    high = small_grads.astype(bf16)
    low = (small_grads - high.astype(f32)).astype(bf16)
    pieces = [jnp.concatenate([high, low], axis=1).reshape(cut_shape + (256,))]
    for l in reversed(range(layers_n)):
        pieces += [part.reshape(cut_shape + (-1,)) for part in parts[l]]
    table, rk, hit, seats, turned = plan
    grad_experts, summed = tail(
        capacity,
        8,
        normed_all,
        grads_all,
        own_shard,
        table,
        hit,
        seats,
        experts,
        owns,
        pieces,
    )
    small_sum = summed[0][:, :128] + summed[0][:, 128:]
    grad_qkv = jnp.stack([summed[1 + 2 * (layers_n - 1 - l)] for l in range(layers_n)])
    grad_out = jnp.stack([summed[2 + 2 * (layers_n - 1 - l)] for l in range(layers_n)])
    small_sum = small_sum[:, : layers_n * wide].reshape(-1, layers_n, wide)
    small_sum = jnp.swapaxes(small_sum, 0, 1)
    grad_router = small_sum[:, :, :experts_n]
    grad_gains = jnp.swapaxes(small_sum[:, :, experts_n:], 1, 2)
    return (
        jnp.stack(outputs),
        grads,
        grad_qkv,
        grad_out,
        grad_router,
        grad_gains,
        *grad_experts,
    )


def local(
    tokens,
    w_qkv,
    w_out,
    w_router,
    norm_gains,
    w_gate,
    w_up,
    w_down,
    out_grad,
    segment_ids,
    routes,
    pair_order,
):
    token_rows = tokens.shape[0]
    layers_n = w_qkv.shape[0]
    topk_n = routes.shape[2]
    n_expert = lax.axis_size(EX)
    n_dp = lax.axis_size(DP)
    expert_here = lax.axis_index(EX)
    dp_here = lax.axis_index(DP)
    device_here = dp_here * n_expert + expert_here
    local_n = w_gate.shape[1]
    experts_n = local_n * n_expert
    capacity = 9 * n_expert * token_rows * topk_n // (8 * experts_n)
    group_rows = n_expert * token_rows
    query_width = QUERY_HEADS * HEAD_SIZE
    key_width = KEY_VALUE_HEADS * HEAD_SIZE
    score_scale = 1.0 / math.sqrt(HEAD_SIZE)
    token_positions = expert_here * token_rows + jnp.arange(token_rows, dtype=jnp.int32)
    cosine, sine_part = rotary_tables(token_positions)
    seg_prev = from_behind(segment_ids, everywhere, 1)
    has_prev = device_here > 0
    row_index = jnp.arange(token_rows)
    own_mask = (segment_ids[None, :] == segment_ids[:, None]) & (
        row_index[None, :] <= row_index[:, None]
    )
    prev_mask = (seg_prev[None, :] == segment_ids[:, None]) & has_prev
    allowed = jnp.concatenate([prev_mask, own_mask], axis=1)

    ranks = rank_table(routes, pair_order, experts_n)
    small = jnp.concatenate(
        [w_router[l] for l in range(layers_n)]
        + [jnp.swapaxes(norm_gains.reshape(2 * layers_n, -1), 0, 1)],
        axis=1,
    )
    small = jnp.pad(small, ((0, 0), (0, 128 - small.shape[1])))
    small_full, ranks_full, qkv_0, out_0 = [
        lax.all_gather(one, everywhere, axis=0)
        for one in (small, ranks.reshape(layers_n * experts_n, token_rows), w_qkv[0], w_out[0])
    ]
    qkv_fulls = [qkv_0.reshape(D, -1)]
    out_fulls = [out_0.reshape(query_width, D)]
    for layer_idx in range(1, layers_n):
        qkv_fulls.append(lax.all_gather(w_qkv[layer_idx], everywhere, axis=0, tiled=True))
        out_fulls.append(lax.all_gather(w_out[layer_idx], everywhere, axis=0, tiled=True))
    small_full = small_full.reshape(D, 128)
    gains = jnp.swapaxes(
        small_full[:, layers_n * experts_n : layers_n * (experts_n + 2)], 0, 1
    ).astype(f32)
    routers = [small_full[:, l * experts_n : (l + 1) * experts_n] for l in range(layers_n)]
    routers_turned = [jnp.swapaxes(router, 0, 1) for router in routers]
    ranks_full = ranks_full.reshape(n_dp, n_expert, layers_n, experts_n, token_rows)
    ranks_full = lax.dynamic_slice_in_dim(ranks_full, dp_here, 1, 0)
    groups = ranks_full.shape[0]
    hit_all = jnp.transpose(ranks_full > 0, (2, 0, 3, 1, 4)).reshape(
        layers_n, groups, experts_n, group_rows
    )
    mine = lax.dynamic_slice_in_dim(ranks_full, expert_here * local_n, local_n, 3)
    counts = jnp.sum((mine > 0).astype(jnp.int32), axis=-1)
    before = jnp.cumsum(counts, axis=1) - counts
    seats = jnp.where(mine > 0, before[..., None] + mine, 0)
    seats = jnp.transpose(seats, (2, 0, 3, 1, 4)).reshape(layers_n, groups, local_n, group_rows)
    seat_ids = jnp.arange(1, capacity + 1, dtype=jnp.int32)

    def own_of(array):
        return lax.dynamic_index_in_dim(array, 0, 0, keepdims=False)

    def seat_map(l):
        return (seats[l][:, :, None, :] == seat_ids[:, None]).astype(bf16)

    def gates_of(normed_rows, l, hit):
        logits = jnp.einsum("de,td->et", routers[l], normed_rows, preferred_element_type=f32)
        return dense_gates(logits, hit)

    own_hit = [(ranks[l] > 0) for l in range(layers_n)]

    stream = tokens.astype(f32)
    saved_layers = []
    outputs = []
    for l in range(layers_n):
        qkv_full, out_full = qkv_fulls[l], out_fulls[l]
        normed_a = rms_norm(stream, gains[2 * l]).astype(bf16)
        projected_output = jnp.dot(normed_a, qkv_full, preferred_element_type=f32)
        query_rows = apply_rotary(
            projected_output[:, :query_width].reshape(token_rows, QUERY_HEADS, HEAD_SIZE),
            cosine,
            sine_part,
        ).astype(bf16)
        key_own = apply_rotary(
            projected_output[:, query_width : query_width + key_width].reshape(
                token_rows, KEY_VALUE_HEADS, HEAD_SIZE
            ),
            cosine,
            sine_part,
        ).astype(bf16)
        value_own = (
            projected_output[:, query_width + key_width :]
            .reshape(token_rows, KEY_VALUE_HEADS, HEAD_SIZE)
            .astype(bf16)
        )
        key_prev, value_prev = from_behind((key_own, value_own), everywhere, 1)
        gathered_keys = jnp.concatenate([key_prev, key_own], axis=0)
        gathered_values = jnp.concatenate([value_prev, value_own], axis=0)
        scores, grouped_queries = masked_scores(query_rows, gathered_keys, allowed)
        top_score = jnp.max(scores, axis=-1, keepdims=True)
        exp_scores = jnp.exp(scores - top_score)
        row_total = jnp.sum(exp_scores, axis=-1, keepdims=True)
        prob_low = (exp_scores / row_total).astype(bf16)
        log_total = top_score + jnp.log(row_total)
        attended = (
            jnp.einsum("kgts,skd->tkgd", prob_low, gathered_values, preferred_element_type=f32)
            .reshape(token_rows, query_width)
            .astype(bf16)
        )
        mixed_sum = stream + jnp.dot(attended, out_full, preferred_element_type=f32)
        normed_b = rms_norm(mixed_sum, gains[2 * l + 1]).astype(bf16)

        if True:
            kept = {}
            group_normed = lax.all_gather(normed_b, EX, axis=0, tiled=True)
            kept["normed_all"] = group_normed[None]
            seat_own = own_of(seat_map(l))
            gates_own = gates_of(group_normed, l, own_of(hit_all[l]))
            gates_own = lax.dynamic_slice_in_dim(gates_own, expert_here * local_n, local_n, 0)
            gate_seat = jnp.sum(seat_own.astype(f32) * gates_own[:, None, :], axis=-1)
            expert_in = jnp.einsum(
                "est,td->esd", seat_own, group_normed, preferred_element_type=f32
            ).astype(bf16)
            gate_pre = jnp.einsum("esd,edf->esf", expert_in, w_gate[l], preferred_element_type=f32)
            up_pre = jnp.einsum("esd,edf->esf", expert_in, w_up[l], preferred_element_type=f32)
            hidden = gated_unit(gate_pre, up_pre).astype(bf16)
            expert_out = jnp.einsum("esf,efd->esd", hidden, w_down[l], preferred_element_type=f32)
            weighted = (expert_out * gate_seat[..., None]).astype(bf16)
            branch_part = jnp.einsum("est,esd->td", seat_own, weighted, preferred_element_type=f32)
            new_stream = mixed_sum + lax.psum_scatter(
                branch_part, EX, scatter_dimension=0, tiled=True
            )
        saved_layers.append(
            {
                "stream_in": stream,
                "normed_a": normed_a,
                "queries": query_rows,
                "key_all": gathered_keys,
                "value_all": gathered_values,
                "log_total": log_total,
                "attended": attended,
                "mixed_sum": mixed_sum,
                "normed_b": normed_b,
            }
            | kept
        )
        outputs.append(new_stream)
        stream = new_stream

    grad_stream = out_grad.astype(f32)
    weight_parts = [None] * layers_n
    expert_parts = [None] * layers_n
    owns = [None] * layers_n
    for l in reversed(range(layers_n)):
        record = saved_layers[l]
        qkv_full, out_full = qkv_fulls[l], out_fulls[l]
        grad_low = grad_stream.astype(bf16)
        if True:
            normed_all = record["normed_all"]
            grad_all = lax.all_gather(grad_low, EX, axis=0, tiled=True)[None]
            seat_all = seat_map(l)
            gates_all = jax.vmap(lambda rows, hit: gates_of(rows, l, hit))(normed_all, hit_all[l])
            gates_mine = lax.dynamic_slice_in_dim(gates_all, expert_here * local_n, local_n, 1)
            gate_seat = jnp.sum(seat_all.astype(f32) * gates_mine[:, :, None, :], axis=-1)
            rows_in = jnp.einsum(
                "gest,gtd->egsd", seat_all, normed_all, preferred_element_type=f32
            ).astype(bf16)
            rows_grad = jnp.einsum(
                "gest,gtd->egsd", seat_all, grad_all, preferred_element_type=f32
            ).astype(bf16)
            gate_seat = jnp.swapaxes(gate_seat, 0, 1)[..., None]
            gate_pre = jnp.einsum("egsd,edf->egsf", rows_in, w_gate[l], preferred_element_type=f32)
            up_pre = jnp.einsum("egsd,edf->egsf", rows_in, w_up[l], preferred_element_type=f32)
            dhidden_raw = jnp.einsum(
                "egsd,efd->egsf", rows_grad, w_down[l], preferred_element_type=f32
            )
            hidden, gate_pull = jax.vjp(gated_unit, gate_pre, up_pre)
            hidden_low = hidden.astype(bf16)
            dgate_pre, dup_pre = gate_pull(dhidden_raw * gate_seat)
            dgate_low = dgate_pre.astype(bf16)
            dup_low = dup_pre.astype(bf16)
            dgate_seat = jnp.sum(hidden_low.astype(f32) * dhidden_raw, axis=-1)
            rows_grad = (rows_grad.astype(f32) * gate_seat).astype(bf16)

        def by_expert(array):
            return array.reshape(local_n, -1, array.shape[-1])

        def outer(one, other):
            return jnp.einsum(
                "esa,esb->eab", by_expert(one), by_expert(other), preferred_element_type=f32
            )

        if True:
            grad_gate_l = outer(rows_in, dgate_low)
            grad_up_l = outer(rows_in, dup_low)
            grad_down_l = outer(hidden_low, rows_grad)
            grad_gate_l = lax.psum_scatter(
                grad_gate_l.astype(bf16), DP, scatter_dimension=1, tiled=True
            ).astype(f32)
            grad_up_l = lax.psum_scatter(
                grad_up_l.astype(bf16), DP, scatter_dimension=1, tiled=True
            ).astype(f32)
            grad_down_l = lax.psum_scatter(
                grad_down_l.astype(bf16), DP, scatter_dimension=2, tiled=True
            ).astype(f32)
            expert_parts[l] = (grad_gate_l, grad_up_l, grad_down_l)

        if True:
            dexpert_in = (
                jnp.einsum("egsf,edf->egsd", dgate_low, w_gate[l], preferred_element_type=f32)
                + jnp.einsum("egsf,edf->egsd", dup_low, w_up[l], preferred_element_type=f32)
            ).astype(bf16)
            back_part = jnp.einsum(
                "gest,egsd->td", seat_all, dexpert_in, preferred_element_type=f32
            )
            dgates_part = jnp.sum(
                seat_all[0].astype(f32) * dgate_seat[:, 0, :, None], axis=1
            )
            mine = expert_here * local_n + jnp.arange(local_n, dtype=jnp.int32)
            lane = jnp.arange(experts_n, dtype=jnp.int32)
            dgates_part = jnp.sum(
                jnp.where(mine[:, None, None] == lane, dgates_part[..., None], 0.0), axis=0
            )
            dnormed_b, dgates = [
                lax.psum_scatter(part, EX, scatter_dimension=0, tiled=True)
                for part in (back_part, dgates_part)
            ]
        gates_token = gates_of(record["normed_b"], l, own_hit[l]).T
        dlogits = (
            gates_token * (dgates - jnp.sum(gates_token * dgates, axis=1, keepdims=True))
        ).astype(bf16)
        dnormed_b = dnormed_b + jnp.einsum(
            "te,de->td", dlogits, routers[l], preferred_element_type=f32
        )
        unused_norm, norm_pull = jax.vjp(rms_norm, record["mixed_sum"], gains[2 * l + 1])
        dmixed_part, dgain_b = norm_pull(dnormed_b)
        dmixed = grad_stream + dmixed_part
        grad_attn = dmixed.astype(bf16)
        attended_gradient = jnp.einsum(
            "td,qd->tq", grad_attn, out_full, preferred_element_type=f32
        ).astype(bf16)
        gathered_keys = record["key_all"]
        gathered_values = record["value_all"]
        scores, grouped_queries = masked_scores(record["queries"], gathered_keys, allowed)
        prob_float = jnp.exp(scores - record["log_total"])
        prob_low = prob_float.astype(bf16)
        grouped_gradient = attended_gradient.reshape(
            token_rows, KEY_VALUE_HEADS, QUERY_HEADS // KEY_VALUE_HEADS, HEAD_SIZE
        )
        dvalue_all = jnp.einsum(
            "kgts,tkgd->skd", prob_low, grouped_gradient, preferred_element_type=f32
        )
        dprobs = jnp.einsum(
            "tkgd,skd->kgts", grouped_gradient, gathered_values, preferred_element_type=f32
        )
        delta_row = jnp.sum(prob_float * dprobs, axis=-1, keepdims=True)
        dscores = (prob_float * (dprobs - delta_row)).astype(bf16)
        dqueries = (
            jnp.einsum(
                "kgts,skd->tkgd", dscores, gathered_keys, preferred_element_type=f32
            ).reshape(token_rows, QUERY_HEADS, HEAD_SIZE)
            * score_scale
        )
        dkey_all = (
            jnp.einsum("kgts,tkgd->skd", dscores, grouped_queries, preferred_element_type=f32)
            * score_scale
        )
        dkey_next, dvalue_next = from_behind(
            (dkey_all[:token_rows].astype(bf16), dvalue_all[:token_rows].astype(bf16)),
            everywhere,
            -1,
        )
        dkey_own = dkey_all[token_rows:] + dkey_next.astype(f32)
        dvalue_own = dvalue_all[token_rows:] + dvalue_next.astype(f32)
        dq_raw = apply_rotary(dqueries, cosine, -sine_part)
        dk_raw = apply_rotary(dkey_own, cosine, -sine_part)
        dprojected = jnp.concatenate(
            [
                dq_raw.reshape(token_rows, query_width),
                dk_raw.reshape(token_rows, key_width),
                dvalue_own.reshape(token_rows, key_width),
            ],
            axis=1,
        ).astype(bf16)
        dnormed_a = jnp.einsum("tq,dq->td", dprojected, qkv_full, preferred_element_type=f32)
        unused_first, first_pull = jax.vjp(rms_norm, record["stream_in"], gains[2 * l])
        dstream_part, dgain_a = first_pull(dnormed_a)
        grad_stream = dmixed + dstream_part

        small_grad = jnp.concatenate(
            [
                jnp.einsum("td,te->de", record["normed_b"], dlogits, preferred_element_type=f32),
                dgain_a[:, None],
                dgain_b[:, None],
            ],
            axis=1,
        )
        normed_a, attended = record["normed_a"], record["attended"]
        grad_qkv_l = jnp.einsum("td,tq->dq", normed_a, dprojected, preferred_element_type=f32)
        grad_out_l = jnp.einsum("tq,td->qd", attended, grad_attn, preferred_element_type=f32)
        weight_parts[l] = (grad_qkv_l, grad_out_l, small_grad)

    small_grads = jnp.concatenate([weight_parts[l][2] for l in range(layers_n)], axis=1)
    if True:

        def scatter(array):
            return lax.psum_scatter(array, everywhere, scatter_dimension=0, tiled=True)

        small_sum = scatter(small_grads)
        grad_qkv = jnp.stack([scatter(weight_parts[l][0]) for l in range(layers_n)])
        grad_out = jnp.stack([scatter(weight_parts[l][1]) for l in range(layers_n)])
    wide = experts_n + 2
    grad_router = jnp.stack(
        [small_sum[:, l * wide : l * wide + experts_n] for l in range(layers_n)]
    )
    grad_gains = jnp.stack(
        [
            jnp.swapaxes(small_sum[:, l * wide + experts_n : (l + 1) * wide], 0, 1)
            for l in range(layers_n)
        ]
    )
    if True:
        grad_gate, grad_up, grad_down = [
            jnp.stack([expert_parts[l][member] for l in range(layers_n)]) for member in range(3)
        ]
    layer_outs = jnp.stack(outputs).astype(bf16)
    return (
        layer_outs,
        grad_stream,
        grad_qkv,
        grad_out,
        grad_router,
        grad_gains,
        grad_gate,
        grad_up,
        grad_down,
    )


def solution(mesh):
    sizes = (mesh.shape[DP], mesh.shape[EX])
    return jax.shard_map(
        local_chips if sizes == (4, 8) else local,
        mesh=mesh,
        in_specs=(
            P((DP, EX), None),
            P(None, (DP, EX), None),
            P(None, (DP, EX), None),
            P(None, (DP, EX), None),
            P(None, None, (DP, EX)),
            P(None, EX, None, None),
            P(None, EX, None, None),
            P(None, EX, None, None),
            P((DP, EX), None),
            P((DP, EX)),
            P(None, (DP, EX), None),
            P(None, (DP, EX), None),
        ),
        out_specs=(
            P(None, (DP, EX), None),
            P((DP, EX), None),
            P(None, (DP, EX), None),
            P(None, (DP, EX), None),
            P(None, (DP, EX), None),
            P(None, None, (DP, EX)),
            P(None, EX, DP, None),
            P(None, EX, DP, None),
            P(None, EX, None, DP),
        ),
        check_vma=False,
    )
```

```python
from functools import partial
import math

import jax
import jax.numpy as jnp
from jax import lax
from jax.experimental import pallas as pl
from jax.experimental.pallas import tpu as pltpu
from jax.sharding import PartitionSpec as P

D = 1536
QUERY_HEADS = 12
KEY_VALUE_HEADS = 2
HEAD_SIZE = 128
MESH = pl.DeviceIdType.MESH
DP, EX = "dp", "expert"
ANY = pl.ANY
bf16 = jnp.bfloat16
f32 = jnp.float32

epsilon = 1e-06
rope_base = 1000000.0
masked_score = -1e30
everywhere = (DP, EX)


def place():
    z = lax.axis_index(DP)
    e = lax.axis_index(EX)
    y, x, c = e // 4, (e // 2) % 2, e % 2
    near = {
        "own": e,
        "x": y * 4 + (1 - x) * 2 + c,
        "y": (1 - y) * 4 + x * 2 + c,
        "d": (1 - y) * 4 + (1 - x) * 2 + c,
        "c": y * 4 + x * 2 + (1 - c),
        "cx": y * 4 + (1 - x) * 2 + (1 - c),
        "cy": (1 - y) * 4 + x * 2 + (1 - c),
        "cd": (1 - y) * 4 + (1 - x) * 2 + (1 - c),
    }
    return z, near


def greet(z, near, plane, line, order=None):
    barrier = pltpu.get_barrier_semaphore()

    def tell(**target):
        pl.semaphore_signal(barrier, inc=1, device_id=target, device_id_type=MESH)

    for name in plane:
        tell(**{EX: near[name]})
    count = len(plane)
    links = []
    if line is not None:
        links += [(z < line - 1, {DP: z + 1}), (z > 0, {DP: z - 1})]
    if order is not None:
        behind, ahead, has_behind, has_ahead = order
        links += [
            (has_behind, {DP: behind[0], EX: behind[1]}),
            (has_ahead, {DP: ahead[0], EX: ahead[1]}),
        ]
    for there, target in links:

        @pl.when(there)
        def one():
            tell(**target)

        count = count + jnp.where(there, 1, 0)
    pl.semaphore_wait(barrier, count)


def halves(rows, columns):
    if rows % 32 == 0:
        return ((0, rows // 2), (0, columns)), ((rows // 2, rows // 2), (0, columns))
    if columns % 256 == 0:
        return ((0, rows), (0, columns // 2)), ((0, rows), (columns // 2, columns // 2))
    return ((0, 16), (0, columns)), ((16, rows - 16), (0, columns))


def cut(ref, part):
    (row, rows), (column, columns) = part
    return ref.at[pl.ds(row, rows), pl.ds(column, columns)]


KINDS = 10
SMALL = 24
BLOCK = 512
QUAD = ("own", "x", "y", "d")
BESIDE = ("c", "cx", "cy", "cd")


class Gather:
    def __init__(self, ins, outs, send, recv, z, near, line, flat=False):
        self.ins, self.outs, self.send, self.recv = ins, outs, send, recv
        self.z, self.near, self.line, self.flat = z, near, line, flat
        self.parts = [halves(*ref.shape) for ref in ins]
        self.all = range(len(ins))

    def hop(self, a, j, kind, whose, to, part=None, src=None):
        dst = self.outs[a].at[j] if self.flat else self.outs[a].at[j, self.near[whose]]
        src = dst if src is None else src
        if part is not None:
            src, dst = cut(src, part), cut(dst, part)
        return pltpu.make_async_remote_copy(
            src_ref=src,
            dst_ref=dst,
            send_sem=self.send.at[a, j, kind],
            recv_sem=self.recv.at[a, j, kind],
            device_id={DP: to} if kind >= 8 else {EX: self.near[to]},
            device_id_type=MESH,
        )

    def landed(self, a, j, kind, whose, part=None):
        if kind < 8:
            self.hop(a, j, kind, whose, "c", part).wait_recv()
        else:
            self.hop(a, j, kind, whose, self.z).wait_recv()

    def line_first(self):
        z = self.z

        @pl.when(z < self.line - 1)
        def up_first():
            for a in self.all:
                self.hop(a, z, 8, "own", z + 1, src=self.ins[a]).start()

        @pl.when(z > 0)
        def down_first():
            for a in self.all:
                self.hop(a, z, 9, "own", z - 1, src=self.ins[a]).start()

    def first(self, j, src=None):
        for a in self.all:
            one = None if src is None else src[a]
            self.hop(a, j, 0, "own", "x", src=one).start()
            self.hop(a, j, 1, "own", "y", src=one).start()
            self.hop(a, j, 2, "own", "c", src=one).start()

    def second(self, j, kind=0):
        for a in self.all:
            self.landed(a, j, 0, "x")
            self.hop(a, j, 4, "x", "y", self.parts[a][1]).start()
            self.hop(a, j, 5, "x", "c").start()
            self.landed(a, j, 1, "y")
            self.hop(a, j, 3, "y", "x", self.parts[a][0]).start()
            self.hop(a, j, 6, "y", "c").start()

    def third(self, j, kind=0):
        for a in self.all:
            self.landed(a, j, 3, "d", self.parts[a][0])
            self.landed(a, j, 4, "d", self.parts[a][1])
            self.hop(a, j, 7, "d", "c").start()

    def finish(self, j, kind=0):
        for a in self.all:
            for kind, whose in ((2, "c"), (5, "cx"), (6, "cy"), (7, "cd")):
                self.landed(a, j, kind, whose)
            for kind in (0, 1, 2):
                self.hop(a, j, kind, "own", "c").wait_send()
            self.hop(a, j, 3, "y", "x", self.parts[a][0]).wait_send()
            self.hop(a, j, 4, "x", "y", self.parts[a][1]).wait_send()
            for kind in (5, 6, 7):
                self.hop(a, j, kind, "x", "c").wait_send()

    def arrivals(self, step, act):
        z = self.z

        @pl.when(z - step >= 0)
        def below():
            act(z - step, 8)

        @pl.when(z + step <= self.line - 1)
        def above():
            act(z + step, 9)

    def take(self, j, kind):
        for a in self.all:
            self.landed(a, j, kind, "own")
        z = self.z
        if kind == 8:

            @pl.when(z < self.line - 1)
            def on_up():
                for a in self.all:
                    self.hop(a, j, 8, "own", z + 1).start()

        else:

            @pl.when(z > 0)
            def on_down():
                for a in self.all:
                    self.hop(a, j, 9, "own", z - 1).start()

        self.first(j)

    def carry(self, j, kind):
        z = self.z
        for a in self.all:
            self.landed(a, j, kind, "own")
        more, target = (z < self.line - 1, z + 1) if kind == 8 else (z > 0, z - 1)

        @pl.when(more)
        def on():
            for a in self.all:
                self.hop(a, j, kind, "own", target).start()

    def plane_of(self, k):
        return lax.rem(self.z + k, self.line)

    def spread(self, k, rows, sem):
        j = self.plane_of(k)
        self.first(j, [rows.at[j]])
        self.kept(k, rows, sem).start()

    def kept(self, k, rows, sem):
        j = self.plane_of(k)
        return pltpu.make_async_copy(rows.at[j], self.outs[0].at[j, self.near["own"]], sem.at[k])

    def spread_done(self, rows, sem):
        for k in range(1, self.line):
            self.finish(self.plane_of(k))
            self.kept(k, rows, sem).wait()

    def line_done(self):
        z = self.z
        for step in range(self.line):

            @pl.when((z - step >= 0) & (z < self.line - 1))
            def up_done():
                for a in self.all:
                    self.hop(a, z - step, 8, "own", z + 1).wait_send()

            @pl.when((z + step <= self.line - 1) & (z > 0))
            def down_done():
                for a in self.all:
                    self.hop(a, z + step, 9, "own", z - 1).wait_send()


def plane_gather(src, dst, send, recv, near):
    parts = halves(*src.shape)

    def hop(kind, whose, to, part=None):
        one = dst.at[near[whose]] if part is None else cut(dst.at[near[whose]], part)
        return pltpu.make_async_remote_copy(
            src_ref=src if whose == "own" else one,
            dst_ref=one,
            send_sem=send.at[kind],
            recv_sem=recv.at[kind],
            device_id={EX: near[to]},
            device_id_type=MESH,
        )

    def first():
        hop(0, "own", "x").start()
        hop(1, "own", "y").start()
        hop(2, "own", "c").start()
        dst[near["own"]] = src[...]

    def second():
        hop(0, "x", "c").wait_recv()
        hop(4, "x", "y", parts[1]).start()
        hop(5, "x", "c").start()
        hop(1, "y", "c").wait_recv()
        hop(3, "y", "x", parts[0]).start()
        hop(6, "y", "c").start()

    def third():
        hop(3, "d", "c", parts[0]).wait_recv()
        hop(4, "d", "c", parts[1]).wait_recv()
        hop(7, "d", "c").start()

    def finish():
        for kind, whose in ((2, "c"), (5, "cx"), (6, "cy"), (7, "cd")):
            hop(kind, whose, "c").wait_recv()
        for kind in (0, 1, 2):
            hop(kind, "own", "c").wait_send()
        hop(3, "y", "x", parts[0]).wait_send()
        hop(4, "x", "y", parts[1]).wait_send()
        for kind in (5, 6, 7):
            hop(kind, "x", "c").wait_send()

    return first, second, third, finish


def sum_scratch(rows, columns):
    return [
        pltpu.VMEM((8, rows, columns), bf16),
        pltpu.VMEM((3, rows, columns), bf16),
        pltpu.VMEM((4, rows, columns), bf16),
        pltpu.VMEM((2, rows // 2, columns), bf16),
        pltpu.VMEM((2, rows // 2, columns), bf16),
        pltpu.VMEM((2, rows // 2, columns), bf16),
        pltpu.SemaphoreType.DMA((10,)),
        pltpu.SemaphoreType.DMA((10,)),
    ]


def plane_sum(make, out_ref, base, scratch, near):
    part_ref, paired, fromc, fromx, fromy, last, send, recv = scratch
    rows = out_ref.shape[0]
    half = rows // 2
    A, B = pl.ds(0, half), pl.ds(half, half)

    def copy(number, src, dst, to):
        return pltpu.make_async_remote_copy(
            src_ref=src,
            dst_ref=dst,
            send_sem=send.at[number],
            recv_sem=recv.at[number],
            device_id={EX: near[to]},
            device_id_type=MESH,
        )

    order = ("d", "x", "y", "own")
    across = ("cd", "cx", "cy", "c")
    core = [copy(s, part_ref.at[near[name]], fromc.at[s], "c") for s, name in enumerate(across)]
    to_x = [copy(4, paired.at[0, A], fromx.at[0], "x"), copy(5, paired.at[1, A], fromx.at[1], "x")]
    to_y = [copy(6, paired.at[0, B], fromy.at[0], "y"), copy(7, paired.at[2, B], fromy.at[1], "y")]
    late_y = copy(8, paired.at[2, A], last.at[0], "y")
    late_x = copy(9, paired.at[1, B], last.at[1], "x")

    def pair(s):
        core[s].wait_recv()
        paired[s] = (part_ref[near[order[s]]].astype(f32) + fromc[s].astype(f32)).astype(bf16)

    for s in range(3):
        make(across[s])
        core[s].start()
        make(order[s])
    pair(0)
    to_x[0].start()
    to_y[0].start()
    make(across[3])
    core[3].start()
    pair(1)
    to_x[1].start()
    pair(2)
    to_y[1].start()
    make(order[3])
    core[3].wait_recv()
    total = part_ref[near["own"]].astype(f32) + fromc[3].astype(f32)
    out_ref[...] = total if base is None else base[...] + total
    to_x[0].wait_recv()
    paired[2, A] = (paired[2, A].astype(f32) + fromx[0].astype(f32)).astype(bf16)
    late_y.start()
    to_y[0].wait_recv()
    paired[1, B] = (paired[1, B].astype(f32) + fromy[0].astype(f32)).astype(bf16)
    late_x.start()
    to_x[1].wait_recv()
    out_ref[A] += fromx[1].astype(f32)
    to_y[1].wait_recv()
    out_ref[B] += fromy[1].astype(f32)
    late_y.wait_recv()
    out_ref[A] += last[0].astype(f32)
    late_x.wait_recv()
    out_ref[B] += last[1].astype(f32)
    for one in core + to_x + to_y + [late_x, late_y]:
        one.wait_send()


def mul(a, b, over=((1,), (0,))):
    return lax.dot_general(a, b, (over, ((), ())), preferred_element_type=f32)


LAST = ((1,), (1,))


def seat_rows(seats, number):
    local_n, tokens_n = seats.shape
    rows = lax.broadcasted_iota(jnp.int32, (local_n * number, tokens_n), 0).astype(f32)
    hot = rows < 0
    for e in range(local_n):
        one = seats[e : e + 1, :]
        hot = hot | ((rows == one + (e * number - 1)) & (one > 0) & (one <= number))
    return jnp.where(hot, 1.0, 0.0).astype(bf16)


def seat_columns(seats, number):
    tokens_n, local_n = seats.shape
    columns = lax.broadcasted_iota(jnp.int32, (tokens_n, local_n * number), 1).astype(f32)
    hot = columns < 0
    for e in range(local_n):
        one = seats[:, e : e + 1]
        hot = hot | ((columns == one + (e * number - 1)) & (one > 0) & (one <= number))
    return jnp.where(hot, 1.0, 0.0).astype(bf16)


def masked_gates(logits, hit):
    top = jnp.max(jnp.where(hit, logits, masked_score), axis=0, keepdims=True)
    powers = jnp.where(hit, jnp.exp(jnp.where(hit, logits - top, 0.0)), 0.0)
    return powers / jnp.sum(powers, axis=0, keepdims=True)


def tail_kernel(layers_n, number, *refs):
    refs = list(refs)

    def some(count):
        taken = refs[:count]
        del refs[:count]
        return taken

    tokens_all, grads_all = some(layers_n), some(layers_n - 1)
    (own_shard,) = some(1)
    table, hit, seats = some(3)
    w_gate, w_up, w_down = some(3)
    owns = [some(5) for l in range(layers_n)]
    row_sources = [some(2) for l in range(layers_n)]
    column_sources = [some(2) for l in range(layers_n)]
    smalls = some(layers_n)
    grad_gate, grad_up, grad_down, landing = some(4)
    beside = some(layers_n)
    small_sum, grad_qkv, grad_out = some(3)
    (
        tokens,
        grads,
        gates,
        rows_in,
        rows_grad,
        cols_in,
        cols_grad,
        hidden_low,
        dgate_low,
        dup_low,
        gate_w,
        up_w,
        down_w,
        stage_wide,
        stage_tall,
        weight_sem,
        token_sem,
        own_sem,
        out_sem,
        gather_send,
        gather_recv,
        beside_send,
        beside_recv,
        small_own,
        small_got,
        small_part,
        small_sem,
        columns,
        row_block,
        block_sum,
        block_got,
        final,
        final_got,
        column_send,
        column_recv,
        column_keep,
        row_sem,
        block_send,
        block_recv,
        final_send,
        final_recv,
    ) = some(41)
    held = [some(6)]
    z, near = place()
    n_dp, local_n = seats.shape[1], seats.shape[2]
    width = cols_in.shape[1]
    ours = pl.ds(pl.multiple_of(z * width, 128), width)
    gather = Gather([own_shard], [landing], gather_send, gather_recv, z, near, n_dp)
    total = Sums([small_part], [small_sum], held, *refs, z, near, n_dp)
    own_e = near["own"]
    plane_n = columns.shape[1]
    over = ((0,), (0,))
    per_expert = n_dp - 1
    per_layer = local_n * per_expert
    steps = layers_n * per_layer

    def layer_of(i):
        return layers_n - 1 - i // per_layer

    def across(l, j):
        return pltpu.make_async_remote_copy(
            src_ref=tokens_all[l].at[j],
            dst_ref=beside[l].at[j],
            send_sem=beside_send.at[l, j],
            recv_sem=beside_recv.at[l, j],
            device_id={EX: near["c"]},
            device_id_type=MESH,
        )

    def start(one):
        one.start()

    def wait(one):
        one.wait()

    def fetch(i, slot, act):
        j = lax.rem(z + 1 + lax.rem(i, per_expert), n_dp)
        for l in range(layers_n):

            @pl.when(layer_of(i) == l)
            def of_layer():
                if act is start:

                    @pl.when(lax.rem(i, per_layer) < per_expert)
                    def arrived():
                        across(l, j).wait_recv()

                for source, names, base in ((tokens_all[l], QUAD, 0), (beside[l], BESIDE, 4)):
                    for q, name in enumerate(names):
                        dst = tokens.at[slot, near[name]]
                        sem = token_sem.at[slot, base + q]
                        act(pltpu.make_async_copy(source.at[j, q], dst, sem))
                grads_from = (landing if l == 0 else grads_all[l - 1]).at[j]
                act(pltpu.make_async_copy(grads_from, grads.at[slot], token_sem.at[slot, 8]))

    def weights(l, e):
        return [
            pltpu.make_async_copy(src.at[l, e], dst, weight_sem.at[i])
            for i, (src, dst) in enumerate(((w_gate, gate_w), (w_up, up_w), (w_down, down_w)))
        ]

    def own(l, e):
        here = pl.ds(pl.multiple_of(e * number, 32), number)
        inner = pl.ds(0, number)
        pairs = (
            (owns[l][0].at[here, ours], cols_in.at[inner]),
            (owns[l][1].at[here, ours], cols_grad.at[inner]),
            (owns[l][2].at[here], hidden_low.at[inner]),
            (owns[l][3].at[here], dgate_low.at[inner]),
            (owns[l][4].at[here], dup_low.at[inner]),
        )
        return [
            pltpu.make_async_copy(src, dst, own_sem.at[i]) for i, (src, dst) in enumerate(pairs)
        ]

    def of(i, make, act):
        e = lax.rem(i // per_expert, local_n)
        for l in range(layers_n):

            @pl.when(layer_of(i) == l)
            def of_layer():
                for one in make(l, e):
                    act(one)

    def results(l, e):
        return [
            pltpu.make_async_copy(stage_wide.at[0], grad_gate.at[l, e], out_sem.at[0]),
            pltpu.make_async_copy(stage_wide.at[1], grad_up.at[l, e], out_sem.at[1]),
            pltpu.make_async_copy(stage_tall, grad_down.at[l, e], out_sem.at[2]),
        ]

    def column_pieces(l, owner):
        first, second = column_sources[l]
        extra = second.shape[1] // 128 - plane_n
        return [
            (first.at[:, pl.ds(pl.multiple_of(owner * 256, 256), 256)], 0, 256),
            (second.at[:, pl.ds(pl.multiple_of(owner * 128, 128), 128)], 256, 128),
            (
                second.at[
                    :, pl.ds(pl.multiple_of((plane_n + owner // 2 % extra) * 128, 128), 128)
                ],
                384,
                128,
            ),
        ]

    def column_copy(l, owner, source, piece):
        src, at, size = column_pieces(l, owner)[piece]
        return pltpu.make_async_remote_copy(
            src_ref=src,
            dst_ref=columns.at[l, source, :, pl.ds(at, size)],
            send_sem=column_send.at[l, owner, piece],
            recv_sem=column_recv.at[l, source, piece],
            device_id={EX: owner},
            device_id_type=MESH,
        )

    def column_own(l, piece):
        src, at, size = column_pieces(l, own_e)[piece]
        dst = columns.at[l, own_e, :, pl.ds(at, size)]
        return pltpu.make_async_copy(src, dst, column_keep.at[l, piece])

    def column_each(l, act_send, act_recv, act_own):
        for d in range(1, plane_n):
            owner = lax.rem(own_e + d, plane_n)
            source = lax.rem(own_e + plane_n - d, plane_n)
            for piece in range(3):
                if piece < 2:
                    if act_send is not None:
                        act_send(column_copy(l, owner, own_e, piece))
                    if act_recv is not None:
                        act_recv(column_copy(l, owner, source, piece))
                    continue
                if act_send is not None:

                    @pl.when(lax.rem(owner, 2) == 0)
                    def extra_out():
                        act_send(column_copy(l, owner, own_e, piece))

                if act_recv is not None:

                    @pl.when(lax.rem(own_e, 2) == 0)
                    def extra_in():
                        act_recv(column_copy(l, owner, source, piece))

        if act_own is not None:
            act_own(column_own(l, 0))
            act_own(column_own(l, 1))

            @pl.when(lax.rem(own_e, 2) == 0)
            def extra_own():
                act_own(column_own(l, 2))

    def row_loads(l):
        return [
            pltpu.make_async_copy(src.at[0], row_block.at[i], row_sem.at[i])
            for i, src in enumerate(row_sources[l])
        ]

    def blocks(l):
        column_each(l, None, lambda one: one.wait_recv(), wait)
        for one in row_loads(l):
            one.wait()
        height = block_sum.shape[2]
        for i in range(2):
            here = pl.ds(i * 256, 256)
            given = columns[l, :, :, here].reshape(-1, 256)
            for j in range(n_dp):
                rows = row_block[i, :, :, pl.ds(j * height, height)].reshape(-1, height)
                block_sum[l, j, :, here] = mul(rows, given, over).astype(bf16)
        if l > 0:
            for one in row_loads(l - 1):
                one.start()

    def block_move(l, j, way):
        slot = jnp.where(j == z + way, n_dp, j) if way < 0 else j
        return pltpu.make_async_remote_copy(
            src_ref=block_sum.at[l, j],
            dst_ref=block_got.at[l, slot],
            send_sem=block_send.at[l, j],
            recv_sem=block_recv.at[l, slot],
            device_id={DP: z + way},
            device_id_type=MESH,
        )

    def block_landed(l, slot):
        pltpu.make_async_remote_copy(
            src_ref=block_got.at[l, slot],
            dst_ref=block_got.at[l, slot],
            send_sem=block_send.at[l, 0],
            recv_sem=block_recv.at[l, slot],
            device_id={DP: z},
            device_id_type=MESH,
        ).wait_recv()

    def block_step(l):
        def act(j, way):
            if way == 0:
                return
            more = (z > 0) if way > 0 else (z < n_dp - 1)

            @pl.when(more)
            def add():
                block_landed(l, j)
                block_sum[l, j] = (
                    block_sum[l, j].astype(f32) + block_got[l, j].astype(f32)
                ).astype(bf16)

            block_move(l, j, way).start()

        return act

    def final_copy(l, owner, source):
        return pltpu.make_async_remote_copy(
            src_ref=final.at[l, owner],
            dst_ref=final_got.at[l, source],
            send_sem=final_send.at[l, owner],
            recv_sem=final_recv.at[l, source],
            device_id={EX: owner},
            device_id_type=MESH,
        )

    def block_end(l):
        final[l] = block_sum[l, z].reshape(final.shape[1:])

        @pl.when(z > 0)
        def below():
            block_landed(l, z)
            got = block_got[l, z].reshape(final.shape[1:])
            final[l] = (final[l].astype(f32) + got.astype(f32)).astype(bf16)

        @pl.when(z < n_dp - 1)
        def above():
            block_landed(l, n_dp)
            got = block_got[l, n_dp].reshape(final.shape[1:])
            final[l] = (final[l].astype(f32) + got.astype(f32)).astype(bf16)

        for d in range(1, plane_n):
            final_copy(l, lax.rem(own_e + d, plane_n), own_e).start()
        final_got[l, own_e] = final[l, own_e]

    def block_out(l):
        for d in range(1, plane_n):
            final_copy(l, own_e, lax.rem(own_e + d, plane_n)).wait_recv()
        for source in range(plane_n):
            got = final_got[l, source].astype(f32)
            grad_qkv[l, :, pl.ds(source * 256, 256)] = got[:, :256]
            grad_out[l, :, pl.ds(source * 128, 128)] = got[:, 256:384]
            if source % 2 == 0:
                grad_out[l, :, pl.ds((plane_n + source // 2) * 128, 128)] = got[:, 384:]

    def small_exchange():
        return pltpu.make_async_remote_copy(
            src_ref=small_own,
            dst_ref=small_got,
            send_sem=small_sem.at[0],
            recv_sem=small_sem.at[1],
            device_id={EX: near["c"]},
            device_id_type=MESH,
        )

    def small_parts():
        small_exchange().wait_recv()
        both = small_own[...] + small_got[...]
        rest = jnp.zeros((128 - both.shape[0], both.shape[1]), f32)
        turned = jnp.transpose(jnp.concatenate([both, rest], axis=0))
        high = turned.astype(bf16)
        low = (turned - high.astype(f32)).astype(bf16)
        shape = small_part.shape[:3] + (128,)
        small_part[:, :, :, pl.ds(0, 128)] = high.reshape(shape)
        small_part[:, :, :, pl.ds(128, 128)] = low.reshape(shape)
        for distance in (3, 2, 1, 0):
            total.at(distance, total.first)

    for l in range(layers_n):
        small_own[pl.ds(l * SMALL, SMALL)] = smalls[l][...]

    @pl.when(lax.rem(own_e, 2) == 1)
    def no_extra():
        columns[:, :, :, pl.ds(384, 128)] = jnp.zeros(columns.shape[:3] + (128,), bf16)

    greet(z, near, ("x", "y", "d", "c", "cx", "cy", "cd"), n_dp)
    gather.line_first()
    small_exchange().start()
    for l in reversed(range(layers_n)):
        for k in range(1, n_dp):
            across(l, lax.rem(z + k, n_dp)).start()
    for l in reversed(range(layers_n)):
        column_each(l, start, None, start)
    for one in row_loads(layers_n - 1):
        one.start()
    of(0, weights, start)
    fetch(0, 0, start)

    def block_at(l, distance):
        return lambda: total.at(distance, block_step(l))

    services = {
        0: [lambda: gather.arrivals(1, gather.take), small_parts],
        1: [lambda: gather.arrivals(2, gather.take), lambda: blocks(1)],
        2: [
            lambda: gather.arrivals(1, gather.second),
            lambda: gather.arrivals(3, gather.take),
            block_at(1, 3),
        ],
        3: [
            lambda: gather.arrivals(1, gather.third),
            lambda: gather.arrivals(2, gather.second),
            block_at(1, 2),
            lambda: blocks(0),
        ],
        4: [
            lambda: gather.arrivals(2, gather.third),
            lambda: gather.arrivals(3, gather.second),
            block_at(0, 3),
            block_at(1, 1),
        ],
        5: [
            lambda: gather.arrivals(3, gather.third),
            lambda: gather.arrivals(1, gather.finish),
            lambda: gather.arrivals(2, gather.finish),
            lambda: gather.arrivals(3, gather.finish),
            block_at(0, 2),
        ],
        6: [
            lambda: total.at(3, total.second),
            lambda: total.at(2, total.second),
            lambda: total.at(1, total.second),
            lambda: total.at(0, total.second),
            block_at(0, 1),
        ],
        7: [lambda: block_end(1)],
        8: [lambda: total.at(3, total.third), lambda: total.at(2, total.third)],
        9: [lambda: total.at(1, total.third)],
        10: [lambda: block_end(0)],
        11: [lambda: total.at(0, total.third), lambda: block_out(1)],
    }

    def step(i, carry):
        slot = lax.rem(i, 2)
        l = layer_of(i)
        k = lax.rem(i, per_expert)
        e = lax.rem(i // per_expert, local_n)
        j = lax.rem(z + 1 + k, n_dp)

        @pl.when(k == 0)
        def begin():
            of(i, own, start)

        @pl.when((i + 1 < steps) & (i != per_layer - 1))
        def ahead():
            fetch(i + 1, 1 - slot, start)

        fetch(i, slot, wait)
        everyone = tokens[slot].reshape(-1, tokens.shape[3])
        experts_n = hit.shape[2]

        @pl.when(e == 0)
        def gates_here():
            here = pl.ds(pl.multiple_of(l * experts_n, experts_n), experts_n)
            router = table[here, :].astype(bf16)
            gates[k] = masked_gates(mul(router, everyone, LAST), hit[l, j] > 0)

        pick = seat_rows(seats[l, j, pl.ds(e, 1)], number)
        rows_in[...] = mul(pick, everyone).astype(bf16)
        rows_grad[...] = mul(pick, grads[slot].reshape(-1, tokens.shape[3])).astype(bf16)
        place_of = pl.ds(pl.multiple_of((k + 1) * number, 32), number)
        mine = gates[k, pl.ds(own_e * local_n + e, 1), :]
        gate_seat = jnp.sum(pick.astype(f32) * mine, axis=1, keepdims=True)

        @pl.when(k == 0)
        def weights_here():
            of(i, weights, wait)

        gate = mul(rows_in[...], gate_w[...])
        up = mul(rows_in[...], up_w[...])
        raw = mul(rows_grad[...], down_w[...], LAST) * gate_seat
        sigmoid = 1.0 / (1.0 + jnp.exp(-gate))
        silu = gate * sigmoid
        hidden_low[place_of] = (silu * up).astype(bf16)
        dgate_low[place_of] = (raw * up * sigmoid * (1.0 + gate * (1.0 - sigmoid))).astype(bf16)
        dup_low[place_of] = (raw * silu).astype(bf16)
        cols_in[place_of] = rows_in[:, ours]
        cols_grad[place_of] = (rows_grad[:, ours].astype(f32) * gate_seat).astype(bf16)

        @pl.when(k == per_expert - 1)
        def close():
            @pl.when(i + 1 < steps)
            def next_weights():
                of(i + 1, weights, start)

            of(i, own, wait)

            @pl.when(i >= per_expert)
            def staged():
                of(i - per_expert, results, wait)

            stage_wide[0] = mul(cols_in[...], dgate_low[...], over)
            stage_wide[1] = mul(cols_in[...], dup_low[...], over)
            stage_tall[...] = mul(hidden_low[...], cols_grad[...], over)
            of(i, results, start)

        for at, acts in services.items():

            @pl.when(i == at)
            def serve():
                for act in acts:
                    act()

        @pl.when(i == per_layer - 1)
        def late_ahead():
            fetch(i + 1, 1 - slot, start)

        return carry

    lax.fori_loop(0, steps, step, 0)
    block_out(0)
    for distance in (3, 2, 1, 0):
        total.at(distance, total.finish)
    small_exchange().wait_send()
    for l in range(layers_n):
        column_each(l, lambda one: one.wait_send(), None, None)
        for d in range(1, plane_n):
            final_copy(l, lax.rem(own_e + d, plane_n), own_e).wait_send()
        for distance in (3, 2, 1):
            total.at(distance, lambda j, way: block_move(l, j, way).wait_send())
    gather.line_done()
    for l in range(layers_n):
        for k in range(1, n_dp):
            across(l, lax.rem(z + k, n_dp)).wait_send()
    of(steps - 1, results, wait)


def tail(
    capacity,
    number,
    tokens_all,
    grads_all,
    own_shard,
    plan,
    weights,
    owns,
    row_sources,
    column_sources,
    smalls,
):
    table, hit, seats = plan
    layers_n, n_dp, local_n, group_rows = seats.shape
    n_expert = lax.axis_size(EX)
    rows, width = own_shard.shape
    hidden = weights[0].shape[3]
    part = width // n_dp
    cut_rows = part // n_expert
    wide = column_sources[0][0].shape[1]
    shape = jax.ShapeDtypeStruct
    several = [one for group in (owns, row_sources, column_sources) for l in group for one in l]
    results = pl.pallas_call(
        partial(tail_kernel, layers_n, capacity),
        out_shape=[
            shape((layers_n, local_n, part, hidden), f32),
            shape((layers_n, local_n, part, hidden), f32),
            shape((layers_n, local_n, hidden, part), f32),
            shape((n_dp, n_expert, rows, width), bf16),
        ]
        + [shape(tokens_all[0].shape, bf16)] * layers_n
        + [
            shape((cut_rows, 256), f32),
            shape((layers_n, cut_rows, wide), f32),
            shape((layers_n, cut_rows, width), f32),
        ],
        in_specs=[HBM] * (2 * layers_n) + [VMEM] * 3 + [HBM] * (3 + len(several)) + [VMEM] * layers_n,
        out_specs=[HBM] * (4 + layers_n) + [VMEM] * 3,
        scratch_shapes=[
            pltpu.VMEM((2, n_expert, rows, width), bf16),
            pltpu.VMEM((2, n_expert, rows, width), bf16),
            pltpu.VMEM((n_dp - 1,) + hit.shape[2:], f32),
            pltpu.VMEM((capacity, width), bf16),
            pltpu.VMEM((capacity, width), bf16),
            pltpu.VMEM((n_dp * capacity, part), bf16),
            pltpu.VMEM((n_dp * capacity, part), bf16),
            pltpu.VMEM((n_dp * capacity, hidden), bf16),
            pltpu.VMEM((n_dp * capacity, hidden), bf16),
            pltpu.VMEM((n_dp * capacity, hidden), bf16),
            pltpu.VMEM((width, hidden), bf16),
            pltpu.VMEM((width, hidden), bf16),
            pltpu.VMEM((hidden, width), bf16),
            pltpu.VMEM((2, part, hidden), f32),
            pltpu.VMEM((hidden, part), f32),
            pltpu.SemaphoreType.DMA((3,)),
            pltpu.SemaphoreType.DMA((2, 9)),
            pltpu.SemaphoreType.DMA((5,)),
            pltpu.SemaphoreType.DMA((3,)),
            pltpu.SemaphoreType.DMA((1, n_dp, KINDS)),
            pltpu.SemaphoreType.DMA((1, n_dp, KINDS)),
            pltpu.SemaphoreType.DMA((layers_n, n_dp)),
            pltpu.SemaphoreType.DMA((layers_n, n_dp)),
            pltpu.VMEM((layers_n * SMALL, width), f32),
            pltpu.VMEM((layers_n * SMALL, width), f32),
            pltpu.VMEM((n_dp, n_expert, cut_rows, 256), bf16),
            pltpu.SemaphoreType.DMA((2,)),
            pltpu.VMEM((layers_n, n_expert, rows, BLOCK), bf16),
            pltpu.VMEM((2, n_expert, rows, width), bf16),
            pltpu.VMEM((layers_n, n_dp, part, BLOCK), bf16),
            pltpu.VMEM((layers_n, n_dp + 1, part, BLOCK), bf16),
            pltpu.VMEM((layers_n, n_expert, cut_rows, BLOCK), bf16),
            pltpu.VMEM((layers_n, n_expert, cut_rows, BLOCK), bf16),
            pltpu.SemaphoreType.DMA((layers_n, n_expert, 3)),
            pltpu.SemaphoreType.DMA((layers_n, n_expert, 3)),
            pltpu.SemaphoreType.DMA((layers_n, 3)),
            pltpu.SemaphoreType.DMA((2,)),
            pltpu.SemaphoreType.DMA((layers_n, n_dp)),
            pltpu.SemaphoreType.DMA((layers_n, n_dp + 1)),
            pltpu.SemaphoreType.DMA((layers_n, n_expert)),
            pltpu.SemaphoreType.DMA((layers_n, n_expert)),
        ]
        + sums_scratch([(cut_rows, 256)], n_dp),
        compiler_params=settings(number),
        name="tail",
    )(
        *tokens_all,
        *grads_all,
        own_shard,
        *plan,
        *weights,
        *several,
        *smalls,
    )
    return results[:3], results[4 + layers_n :]


VMEM = pl.BlockSpec(memory_space=pltpu.VMEM)
HBM = pl.BlockSpec(memory_space=ANY)


def settings(number):
    return pltpu.CompilerParams(
        collective_id=number, has_side_effects=True, vmem_limit_bytes=63 << 20
    )


def chain(z, e):
    n_expert = 8
    behind = (z, lax.rem(e + n_expert - 1, n_expert))
    ahead = (z, lax.rem(e + 1, n_expert))
    return behind, ahead, e > 0, e < n_expert - 1


def normalized(value, gain):
    scale = lax.rsqrt(jnp.mean(value * value, axis=-1, keepdims=True) + epsilon)
    return value * scale * gain


def turn(head, cosine, signed_sine):
    return head * cosine + pltpu.roll(head, HEAD_SIZE // 2, 1) * signed_sine


def head_of(h):
    return pl.ds(h * HEAD_SIZE, HEAD_SIZE)


def allowed_keys(rk, row, z, e, behind, has_behind, seg_column):
    own = rk[z, e, pl.ds(row, 1), :]
    first = rk[z, behind[1], pl.ds(row, 1), :]
    rows = seg_column.shape[0]
    query = lax.broadcasted_iota(jnp.int32, (rows, rows), 0)
    key = lax.broadcasted_iota(jnp.int32, (rows, rows), 1)
    reach = jnp.where(has_behind, 0, -1)
    return jnp.concatenate(
        [(first == seg_column) & (key >= rows * -reach), (own == seg_column) & (key <= query)],
        axis=1,
    )


def head_probs(query, keys, allowed):
    scores = mul(query, keys, LAST) * (1.0 / math.sqrt(HEAD_SIZE))
    scores = jnp.where(allowed, scores, masked_score)
    powers = jnp.exp(scores - jnp.max(scores, axis=-1, keepdims=True))
    return powers / jnp.sum(powers, axis=-1, keepdims=True)


def forward_kernel(layer, layers_n, number, *refs):
    first = layer == 0
    refs = list(refs)

    def some(count):
        taken = refs[:count]
        del refs[:count]
        return taken

    stream, cosine, sine, seg_column = some(4)
    if first:
        small, ranks, w_qkv, w_out, out_grad = some(5)
    else:
        table, rk, hit, seats, turned, cross_from, qkv_from, out_from = some(8)
    w_gate, w_up, w_down = some(3)
    new_stream, layer_out, normed_a, queries, kv_out, attended, mixed, normed_b = some(8)
    rows_in, gate_pre, up_pre, gate_seat, quad = some(5)
    if first:
        table, rk_out, hit, seats, turned, qkv_out, out_out, qkv_next, out_next = some(9)
        (line_grads,) = some(1)
        small_land, rk, seat_all = some(3)
    else:
        (cross_to,) = some(1)
    (
        qkv,
        w_o,
        kv,
        projected,
        tokens,
        gates,
        weighted,
        gate_w,
        up_w,
        down_w,
        weight_sem,
        load_sem,
        chain_sem,
        quad_sem,
        send,
        recv,
    ) = some(16)
    if first:
        send_0, recv_0, send_1, recv_1, send_2, recv_2, send_3, recv_3 = some(8)
        send_4, recv_4, keep = some(3)
    else:
        cross_send, cross_recv, cross_keep = some(3)
    scratch = refs
    z, near = place()
    e = near["own"]
    line = lax.axis_size(DP)
    local_n = seats.shape[2]
    rows = stream.shape[0]
    experts_n = hit.shape[2]
    behind, ahead, has_behind, has_ahead = chain(z, e)

    weights = [
        pltpu.make_async_copy(src.at[layer], dst, weight_sem.at[i])
        for i, (src, dst) in enumerate(((w_gate, gate_w), (w_up, up_w), (w_down, down_w)))
    ]
    greet(z, near, ("x", "y", "c"), line, (behind, ahead, has_behind, has_ahead))
    if not first:
        cross = Gather([cross_from.at[0]], [cross_to], cross_send, cross_recv, z, near, line)
        cross.spread(1, cross_from, cross_keep)
    if first:
        g0 = Gather([small, ranks], [small_land, rk], send_0, recv_0, z, near, line)
        g1 = Gather([w_qkv.at[0]], [qkv], send_1, recv_1, z, near, line)
        g2 = Gather([w_out.at[0]], [w_o], send_2, recv_2, z, near, line)
        g3 = Gather(
            [w_qkv.at[1], w_out.at[1]], [qkv_next, out_next], send_3, recv_3, z, near, line
        )
        g4 = Gather([out_grad], [line_grads], send_4, recv_4, z, near, line, flat=True)
        local = [
            pltpu.make_async_copy(one, g.outs[i].at[z, e], keep.at[k])
            for k, (g, i, one) in enumerate(
                (g, i, one) for g in (g0, g1, g2, g3) for i, one in enumerate(g.ins)
            )
        ]
        g0.line_first()
        g0.first(z, g0.ins)
        g1.line_first()
        g1.first(z, g1.ins)
        for one in local:
            one.start()
        g0.arrivals(1, g0.take)
        g0.second(z)
        g0.arrivals(2, g0.take)
        g0.third(z)
        g0.arrivals(1, g0.second)
        g0.arrivals(3, g0.take)
        g1.arrivals(1, g1.take)
        g2.line_first()
        g2.first(z, g2.ins)
        g0.arrivals(1, g0.third)
        g0.arrivals(2, g0.second)
        g1.second(z)
        g0.arrivals(2, g0.third)
        g0.arrivals(3, g0.second)
        g1.arrivals(2, g1.take)
        g0.arrivals(3, g0.third)
        g0.finish(z)
        for step in range(1, line):
            g0.arrivals(step, g0.finish)
        local[0].wait()
        local[1].wait()
        table[...] = jnp.transpose(small_land[...].reshape(-1, 128).astype(f32))
        g1.third(z)
        g1.arrivals(1, g1.second)
        for g in range(line):
            before = jnp.zeros((layers_n * experts_n, 1), f32)
            for d in range(8):
                lanes = pl.ds(d * rows, rows)
                rank = rk[g, d, pl.ds(0, layers_n * experts_n), :].astype(f32)
                seat_all[g, :, lanes] = jnp.where(rank > 0, rank + before, 0.0)
                for l in range(layers_n):
                    hit[l, g, :, lanes] = rank[l * experts_n : (l + 1) * experts_n]
                here = jnp.where(rank > 0, 1.0, 0.0)
                before = before + jnp.sum(here, axis=1, keepdims=True)
            for l in range(layers_n):
                for k in range(local_n):
                    row = pl.ds(l * experts_n + e * local_n + k, 1)
                    seats[l, g, pl.ds(k, 1), :] = seat_all[g, row, :]
        g1.arrivals(3, g1.take)
        wide = jnp.zeros((rows - layers_n * local_n, rows), f32)
        for d in range(8):
            lanes = pl.ds(d * rows, rows)
            mine = [seats[l, z, :, lanes] for l in range(layers_n)]
            turned[lanes, :] = jnp.transpose(jnp.concatenate(mine + [wide], axis=0))
        rk_out[...] = rk[...]
        g1.arrivals(1, g1.third)
        g1.arrivals(2, g1.second)
        g2.arrivals(1, g2.take)
        g1.arrivals(2, g1.third)
        g1.arrivals(3, g1.second)
        g2.second(z)
        g2.arrivals(2, g2.take)
        g1.arrivals(3, g1.third)
        g2.third(z)
        g1.finish(z)
        for step in range(1, line):
            g1.arrivals(step, g1.finish)
        local[2].wait()
        g2.arrivals(1, g2.second)
        g2.arrivals(3, g2.take)
    else:
        loads = [
            pltpu.make_async_copy(qkv_from, qkv, load_sem.at[0]),
            pltpu.make_async_copy(out_from, w_o, load_sem.at[1]),
        ]
        for one in loads:
            one.start()
    for one in weights:
        one.start()
    gain = 2 * experts_n + 2 * layer
    x = stream[...].astype(f32)
    normed_a[...] = normalized(x, table[pl.ds(gain, 1), :]).astype(bf16)
    if not first:
        loads[0].wait()
    width = queries.shape[1]
    projected[...] = mul(normed_a[...], qkv[...].reshape(width, -1))
    keys_n = KEY_VALUE_HEADS * HEAD_SIZE
    cos, sin = cosine[...], sine[...]
    for h in range(KEY_VALUE_HEADS):
        key = turn(projected[:, head_of(QUERY_HEADS + h)], cos, sin)
        kv[1, :, head_of(h)] = key.astype(bf16)
    kv[1, :, pl.ds(keys_n, keys_n)] = projected[:, pl.ds(width + keys_n, keys_n)].astype(bf16)

    def pass_on(target):
        return pltpu.make_async_remote_copy(
            src_ref=kv.at[1],
            dst_ref=kv.at[0],
            send_sem=chain_sem.at[0],
            recv_sem=chain_sem.at[1],
            device_id={DP: target[0], EX: target[1]},
            device_id_type=MESH,
        )

    @pl.when(has_ahead)
    def pass_ahead():
        pass_on(ahead).start()

    if first:
        g2.arrivals(1, g2.third)
        g2.arrivals(2, g2.second)
        g3.line_first()
        g3.first(z, g3.ins)
    else:
        cross.spread(2, cross_from, cross_keep)
    for h in range(QUERY_HEADS):
        queries[:, head_of(h)] = turn(projected[:, head_of(h)], cos, sin).astype(bf16)
    allowed = allowed_keys(rk, layers_n * experts_n, z, e, behind, has_behind, seg_column[...])

    @pl.when(has_behind)
    def from_behind_here():
        pass_on(behind).wait_recv()

    @pl.when(jnp.logical_not(has_behind))
    def nobody_behind():
        kv[0] = jnp.zeros_like(kv[0])

    for h in range(QUERY_HEADS):
        group = h // (QUERY_HEADS // KEY_VALUE_HEADS)
        keys = kv[:, :, head_of(group)].reshape(2 * rows, HEAD_SIZE)
        values = kv[:, :, head_of(KEY_VALUE_HEADS + group)].reshape(2 * rows, HEAD_SIZE)
        probs = head_probs(queries[:, head_of(h)], keys, allowed).astype(bf16)
        attended[:, head_of(h)] = mul(probs, values).astype(bf16)
        if first and h == 3:
            g2.arrivals(2, g2.third)
            g2.arrivals(3, g2.second)
        if first and h == 7:
            g2.arrivals(3, g2.third)
            g3.arrivals(1, g3.take)
            g4.line_first()
        if not first and h == 8:
            cross.second(cross.plane_of(1))
    kv_out[...] = kv[...]
    if first:
        g2.finish(z)
        for step in range(1, line):
            g2.arrivals(step, g2.finish)
        local[3].wait()
    else:
        loads[1].wait()
    mixed[...] = x + mul(attended[...], w_o[...].reshape(width, -1))
    normed_b[...] = normalized(mixed[...], table[pl.ds(gain + 1, 1), :]).astype(bf16)

    one, two, three, four = plane_gather(normed_b, tokens, send, recv, near)
    one()
    if first:
        g3.second(z)
        g3.arrivals(2, g3.take)
    two()
    three()
    if first:
        g3.third(z)
        g3.arrivals(1, g3.second)
        g3.arrivals(3, g3.take)
    four()
    quads = [
        pltpu.make_async_copy(tokens.at[near[name]], quad.at[i], quad_sem.at[i])
        for i, name in enumerate(QUAD)
    ]
    for copied in quads:
        copied.start()
    everyone = tokens[...].reshape(-1, width)
    router = table[pl.ds(layer * experts_n, experts_n), :].astype(bf16)
    gates[...] = masked_gates(mul(router, everyone, LAST), hit[layer, z] > 0)
    pick = seat_rows(seats[layer, z], number)
    for k in range(local_n):
        here = pl.ds(k * number, number)
        mine = gates[pl.ds(e * local_n + k, 1), :]
        gate_seat[here] = jnp.sum(
            pick[k * number : (k + 1) * number].astype(f32) * mine, axis=1, keepdims=True
        )
    rows_in[...] = mul(pick, everyone).astype(bf16)
    for copied in weights:
        copied.wait()
    if first:
        g3.arrivals(1, g3.third)
        g3.arrivals(2, g3.second)
        g4.arrivals(1, g4.carry)
    else:
        cross.second(cross.plane_of(2))
        cross.spread(3, cross_from, cross_keep)

    def expert(k, carry):
        here = pl.ds(pl.multiple_of(k * number, 32), number)
        x = rows_in[here]
        gate = mul(x, gate_w[k])
        up = mul(x, up_w[k])
        gate_pre[here] = gate
        up_pre[here] = up
        hidden = (gate * (1.0 / (1.0 + jnp.exp(-gate))) * up).astype(bf16)
        weighted[here] = (mul(hidden, down_w[k]) * gate_seat[here]).astype(bf16)
        return carry

    lax.fori_loop(0, local_n, expert, 0)
    if first:
        g3.arrivals(2, g3.third)
        g3.arrivals(3, g3.second)
        g4.arrivals(2, g4.carry)
        out_copies = [
            pltpu.make_async_copy(qkv, qkv_out, load_sem.at[0]),
            pltpu.make_async_copy(w_o, out_out, load_sem.at[1]),
        ]
        for copied in out_copies:
            copied.start()
    else:
        cross.third(cross.plane_of(1))
        cross.second(cross.plane_of(3))

    def make(name):
        d = near[name]
        lanes = pl.ds(pl.multiple_of(d * rows, rows), rows)
        mine = turned[lanes, pl.ds(layer * local_n, local_n)]
        scratch[0][d] = mul(seat_columns(mine, number), weighted[...]).astype(bf16)

    plane_sum(make, new_stream, mixed, scratch, near)
    layer_out[...] = new_stream[...].astype(bf16)

    for copied in quads:
        copied.wait()

    @pl.when(has_ahead)
    def passed_on():
        pass_on(ahead).wait_send()

    if first:
        g3.arrivals(3, g3.third)
        g4.arrivals(3, g4.carry)
        g3.finish(z)
        for step in range(1, line):
            g3.arrivals(step, g3.finish)
        for copied in local[4:] + out_copies:
            copied.wait()
        for g in (g0, g1, g2, g3, g4):
            g.line_done()
    else:
        cross.third(cross.plane_of(2))
        cross.third(cross.plane_of(3))
        cross.spread_done(cross_from, cross_keep)


def layer_forward(layer, number, shapes, stream, tables, given, weights):
    layers_n, n_dp, n_expert, local_n, capacity = shapes
    first = layer == 0
    rows, width = stream.shape
    hidden = weights[0].shape[3]
    experts_n = local_n * n_expert
    seats_n = local_n * capacity
    keys_n = KEY_VALUE_HEADS * HEAD_SIZE
    group = n_expert * rows
    cut_rows = width // (n_dp * n_expert)
    shape = jax.ShapeDtypeStruct
    outs = [
        shape((rows, width), f32),
        shape((rows, width), bf16),
        shape((rows, width), bf16),
        shape((rows, width), bf16),
        shape((2, rows, 2 * keys_n), bf16),
        shape((rows, width), bf16),
        shape((rows, width), f32),
        shape((rows, width), bf16),
        shape((seats_n, width), bf16),
        shape((seats_n, hidden), f32),
        shape((seats_n, hidden), f32),
        shape((seats_n, 1), f32),
        shape((len(QUAD), rows, width), bf16),
    ]
    specs = [VMEM] * 12 + [HBM]
    scratch = []
    full_qkv = (n_dp, n_expert, cut_rows, width + 2 * keys_n)
    full_out = (n_dp, n_expert, cut_rows, width)
    if first:
        rank_rows = given[1].shape[0]
        outs += [
            shape((128, width), f32),
            shape((n_dp, n_expert, rank_rows, rows), jnp.int32),
            shape((layers_n, n_dp, experts_n, group), f32),
            shape((layers_n, n_dp, local_n, group), f32),
            shape((group, 128), f32),
        ]
        outs += [shape(full_qkv, bf16), shape(full_out, bf16)] * 2
        outs.append(shape((n_dp, rows, width), bf16))
        specs += [VMEM] * 5 + [HBM] * 5
        scratch += [
            pltpu.VMEM((n_dp, n_expert, cut_rows, 128), bf16),
            pltpu.VMEM((n_dp, n_expert, rank_rows, rows), jnp.int32),
            pltpu.VMEM((n_dp, layers_n * experts_n, group), f32),
        ]
    else:
        outs.append(shape((n_dp, n_expert, rows, width), bf16))
        specs.append(HBM)
    scratch += [
        pltpu.VMEM(full_qkv, bf16),
        pltpu.VMEM(full_out, bf16),
        pltpu.VMEM((2, rows, 2 * keys_n), bf16),
        pltpu.VMEM((rows, width + 2 * keys_n), f32),
        pltpu.VMEM((n_expert, rows, width), bf16),
        pltpu.VMEM((experts_n, group), f32),
        pltpu.VMEM((seats_n, width), bf16),
        pltpu.VMEM((local_n, width, hidden), bf16),
        pltpu.VMEM((local_n, width, hidden), bf16),
        pltpu.VMEM((local_n, hidden, width), bf16),
        pltpu.SemaphoreType.DMA((3,)),
        pltpu.SemaphoreType.DMA((2,)),
        pltpu.SemaphoreType.DMA((2,)),
        pltpu.SemaphoreType.DMA((len(QUAD),)),
        pltpu.SemaphoreType.DMA((8,)),
        pltpu.SemaphoreType.DMA((8,)),
    ]
    if first:
        for count in (2, 1, 1, 2, 1):
            scratch += [pltpu.SemaphoreType.DMA((count, n_dp, KINDS)) for i in range(2)]
        scratch.append(pltpu.SemaphoreType.DMA((6,)))
    else:
        scratch += [pltpu.SemaphoreType.DMA((1, n_dp, KINDS)) for i in range(2)]
        scratch.append(pltpu.SemaphoreType.DMA((n_dp,)))
    given_specs = [HBM] * 5 if first else [VMEM] * 5 + [HBM] * 3
    return pl.pallas_call(
        partial(forward_kernel, layer, layers_n, capacity),
        out_shape=outs,
        in_specs=[VMEM] * 4 + given_specs + [HBM] * 3,
        out_specs=specs,
        scratch_shapes=scratch + sum_scratch(rows, width),
        compiler_params=settings(number),
        name="layer_forward",
    )(stream, *tables, *given, *weights)


def norm_back(value, gain, grad):
    scale = lax.rsqrt(jnp.mean(value * value, axis=-1, keepdims=True) + epsilon)
    unit = value * scale
    inner = grad * gain
    back = scale * (inner - unit * jnp.mean(inner * unit, axis=-1, keepdims=True))
    return back, jnp.sum(grad * unit, axis=0, keepdims=True)


def backward_kernel(layer, layers_n, number, *refs):
    refs = list(refs)

    def some(count):
        taken = refs[:count]
        del refs[:count]
        return taken

    grad_stream, stream, cosine, sine, seg_column = some(5)
    mixed, normed_b, queries, kv, gate_pre, up_pre, gate_seat = some(7)
    table, rk, hit, seats, turned = some(5)
    row_sources = some(2)
    qkv_from, out_from, w_gate, w_up, w_down = some(5)
    grad_out, grad_low, rows_grad, hidden_low, dgate_low, dup_low = some(6)
    dprojected, grad_attn, small = some(3)
    row_lands = some(2)
    (
        summed,
        qkv,
        w_o,
        datt,
        dkv,
        dkv_send,
        dkv_got,
        all_probs,
        tokens,
        back_rows,
        gate_w,
        up_w,
        down_w,
        weight_sem,
        load_sem,
        chain_sem,
        send,
        recv,
        row_send,
        row_recv,
        row_keep,
    ) = some(21)
    scratch = refs
    z, near = place()
    e = near["own"]
    line = lax.axis_size(DP)
    local_n = seats.shape[2]
    rows, width = stream.shape
    experts_n = hit.shape[2]
    behind, ahead, has_behind, has_ahead = chain(z, e)
    weights = [
        pltpu.make_async_copy(src.at[layer], dst, weight_sem.at[i])
        for i, (src, dst) in enumerate(((w_gate, gate_w), (w_up, up_w), (w_down, down_w)))
    ]
    loads = [
        pltpu.make_async_copy(qkv_from, qkv, load_sem.at[0]),
        pltpu.make_async_copy(out_from, w_o, load_sem.at[1]),
    ]
    grad_low[...] = grad_stream[...].astype(bf16)
    greet(z, near, ("x", "y", "c"), None, (behind, ahead, has_behind, has_ahead))

    spreads = [
        Gather([src], [dst], row_send.at[i], row_recv.at[i], 0, near, None)
        for i, (src, dst) in enumerate(zip(row_sources, row_lands))
    ]
    kept = [
        pltpu.make_async_copy(src, dst.at[0, e], row_keep.at[i])
        for i, (src, dst) in enumerate(zip(row_sources, row_lands))
    ]

    first, second, third, finish = plane_gather(grad_low, tokens, send, recv, near)
    first()
    for one in weights + loads:
        one.start()
    allowed = allowed_keys(rk, layers_n * experts_n, z, e, behind, has_behind, seg_column[...])
    per_group = QUERY_HEADS // KEY_VALUE_HEADS

    def keys_of(group):
        return kv[:, :, head_of(group)].reshape(2 * rows, HEAD_SIZE)

    def prepare(heads):
        for h in heads:
            all_probs[h] = head_probs(queries[:, head_of(h)], keys_of(h // per_group), allowed)

    prepare(range(0, 5))
    second()
    prepare(range(5, 9))
    third()
    prepare(range(9, QUERY_HEADS))
    finish()
    spreads[0].first(0, spreads[0].ins)
    for one in kept:
        one.start()
    everyone = tokens[...].reshape(-1, width)
    picked = mul(seat_rows(seats[layer, z], number), everyone)
    back_rows[:, pl.ds(0, width)] = picked.astype(bf16)
    rows_grad[...] = (picked * gate_seat[...]).astype(bf16)
    for one in weights:
        one.wait()

    def expert(k, carry):
        here = pl.ds(pl.multiple_of(k * number, 32), number)
        gate, up = gate_pre[here], up_pre[here]
        raw = mul(back_rows[here, pl.ds(0, width)], down_w[k], LAST)
        sigmoid = 1.0 / (1.0 + jnp.exp(-gate))
        silu = gate * sigmoid
        hidden = (silu * up).astype(bf16)
        hidden_low[here] = hidden
        dgate_seat = jnp.sum(hidden.astype(f32) * raw, axis=1, keepdims=True)
        raw = raw * gate_seat[here]
        dgate = (raw * up * sigmoid * (1.0 + gate * (1.0 - sigmoid))).astype(bf16)
        dup = (raw * silu).astype(bf16)
        dgate_low[here] = dgate
        dup_low[here] = dup
        back_rows[here, pl.ds(0, width)] = (
            mul(dgate, gate_w[k], LAST) + mul(dup, up_w[k], LAST)
        ).astype(bf16)
        high = dgate_seat.astype(bf16).astype(f32)
        lane = lax.broadcasted_iota(jnp.int32, (number, 128), 1)
        mine = e * local_n + k
        back_rows[here, pl.ds(width, 128)] = jnp.where(
            lane == mine, high, jnp.where(lane == experts_n + mine, dgate_seat - high, 0.0)
        ).astype(bf16)
        return carry

    lax.fori_loop(0, local_n, expert, 0)

    def make(name):
        d = near[name]
        lanes = pl.ds(pl.multiple_of(d * rows, rows), rows)
        mine = turned[lanes, pl.ds(layer * local_n, local_n)]
        scratch[0][d] = mul(seat_columns(mine, number), back_rows[...]).astype(bf16)

    spreads[0].second(0)
    plane_sum(make, summed, None, scratch, near)
    spreads[0].third(0)
    spreads[1].first(0, spreads[1].ins)

    over = ((0,), (0,))
    gain = 2 * experts_n + 2 * layer
    router = table[pl.ds(layer * experts_n, experts_n), :].astype(bf16)
    own_lanes = pl.ds(pl.multiple_of(e * rows, rows), rows)
    gates = masked_gates(mul(router, normed_b[...], LAST), hit[layer, z, :, own_lanes] > 0)
    turned_sum = jnp.transpose(summed[:, pl.ds(width, 128)])
    dgates = turned_sum[:experts_n] + turned_sum[experts_n : 2 * experts_n]
    inner = jnp.sum(gates * dgates, axis=0, keepdims=True)
    dlogits = (gates * (dgates - inner)).astype(bf16)
    small[...] = jnp.zeros_like(small)
    small[pl.ds(0, experts_n)] = mul(dlogits, normed_b[...])
    dnormed = summed[:, pl.ds(0, width)] + mul(dlogits, router, over)
    back, dgain = norm_back(mixed[...], table[pl.ds(gain + 1, 1), :], dnormed)
    small[pl.ds(experts_n + 1, 1)] = dgain
    dmixed = grad_stream[...].astype(f32) + back
    grad_out[...] = dmixed
    grad_attn[...] = dmixed.astype(bf16)

    loads[1].wait()
    datt[...] = mul(grad_attn[...], w_o[...].reshape(width, -1), LAST).astype(bf16)
    cos, sin = cosine[...], sine[...]
    scale = 1.0 / math.sqrt(HEAD_SIZE)
    for group in range(KEY_VALUE_HEADS):
        keys = keys_of(group)
        values = keys_of(KEY_VALUE_HEADS + group)
        dkeys = jnp.zeros((2 * rows, HEAD_SIZE), f32)
        dvalues = jnp.zeros((2 * rows, HEAD_SIZE), f32)
        for h in range(group * per_group, (group + 1) * per_group):
            query = queries[:, head_of(h)]
            probs = all_probs[h]
            given = datt[:, head_of(h)]
            dprobs = mul(given, values, LAST)
            delta = jnp.sum(probs * dprobs, axis=-1, keepdims=True)
            dscores = (probs * (dprobs - delta)).astype(bf16)
            dquery = mul(dscores, keys) * scale
            dprojected[:, head_of(h)] = turn(dquery, cos, -sin).astype(bf16)
            dkeys = dkeys + mul(dscores, query, over)
            dvalues = dvalues + mul(probs.astype(bf16), given, over)
        if group == 0:
            spreads[1].second(0)
        dkv[:, head_of(group)] = dkeys * scale
        dkv[:, head_of(KEY_VALUE_HEADS + group)] = dvalues
    dkv_send[...] = dkv[pl.ds(0, rows)].astype(bf16)

    def pass_on(target):
        return pltpu.make_async_remote_copy(
            src_ref=dkv_send,
            dst_ref=dkv_got,
            send_sem=chain_sem.at[0],
            recv_sem=chain_sem.at[1],
            device_id={DP: target[0], EX: target[1]},
            device_id_type=MESH,
        )

    @pl.when(has_behind)
    def pass_back():
        pass_on(behind).start()

    loads[0].wait()
    query_part = pl.ds(0, width)
    key_part = pl.ds(width, dkv.shape[1])
    weights_q = qkv[:, :, :, query_part].reshape(-1, width)
    dnormed = mul(dprojected[:, query_part], weights_q, LAST)

    @pl.when(has_ahead)
    def from_ahead_here():
        pass_on(ahead).wait_recv()
        dkv[pl.ds(rows, rows)] += dkv_got[...].astype(f32)

    for h in range(KEY_VALUE_HEADS):
        dkey = turn(dkv[pl.ds(rows, rows), head_of(h)], cos, -sin)
        dprojected[:, head_of(QUERY_HEADS + h)] = dkey.astype(bf16)
        dvalue = dkv[pl.ds(rows, rows), head_of(KEY_VALUE_HEADS + h)]
        dprojected[:, head_of(QUERY_HEADS + KEY_VALUE_HEADS + h)] = dvalue.astype(bf16)
    weights_kv = qkv[:, :, :, key_part].reshape(-1, dkv.shape[1])
    dnormed = dnormed + mul(dprojected[:, key_part], weights_kv, LAST)
    back, dgain = norm_back(stream[...].astype(f32), table[pl.ds(gain, 1), :], dnormed)
    small[pl.ds(experts_n, 1)] = dgain
    grad_out[...] += back

    @pl.when(has_behind)
    def passed_back():
        pass_on(behind).wait_send()

    spreads[1].third(0)
    for i in range(2):
        spreads[i].finish(0)
        kept[i].wait()


def layer_backward(layer, number, shapes, grads, stream, tables, saved, plan, weights):
    layers_n, n_dp, n_expert, local_n, capacity = shapes
    rows, width = stream.shape
    hidden = weights[-1].shape[2]
    experts_n = local_n * n_expert
    seats_n = local_n * capacity
    keys_n = KEY_VALUE_HEADS * HEAD_SIZE
    cut_rows = width // (n_dp * n_expert)
    shape = jax.ShapeDtypeStruct
    outs = [
        shape((rows, width), f32),
        shape((rows, width), bf16),
        shape((seats_n, width), bf16),
        shape((seats_n, hidden), bf16),
        shape((seats_n, hidden), bf16),
        shape((seats_n, hidden), bf16),
        shape((rows, width + 2 * keys_n), bf16),
        shape((rows, width), bf16),
        shape((SMALL, width), f32),
        shape((1, n_expert, rows, width), bf16),
        shape((1, n_expert, rows, width), bf16),
    ]
    scratch = [
        pltpu.VMEM((rows, width + 128), f32),
        pltpu.VMEM((n_dp, n_expert, cut_rows, width + 2 * keys_n), bf16),
        pltpu.VMEM((n_dp, n_expert, cut_rows, width), bf16),
        pltpu.VMEM((rows, width), bf16),
        pltpu.VMEM((2 * rows, 2 * keys_n), f32),
        pltpu.VMEM((rows, 2 * keys_n), bf16),
        pltpu.VMEM((rows, 2 * keys_n), bf16),
        pltpu.VMEM((QUERY_HEADS, rows, 2 * rows), f32),
        pltpu.VMEM((n_expert, rows, width), bf16),
        pltpu.VMEM((seats_n, width + 128), bf16),
        pltpu.VMEM((local_n, width, hidden), bf16),
        pltpu.VMEM((local_n, width, hidden), bf16),
        pltpu.VMEM((local_n, hidden, width), bf16),
        pltpu.SemaphoreType.DMA((3,)),
        pltpu.SemaphoreType.DMA((2,)),
        pltpu.SemaphoreType.DMA((2,)),
        pltpu.SemaphoreType.DMA((8,)),
        pltpu.SemaphoreType.DMA((8,)),
        pltpu.SemaphoreType.DMA((2, 1, 1, KINDS)),
        pltpu.SemaphoreType.DMA((2, 1, 1, KINDS)),
        pltpu.SemaphoreType.DMA((2,)),
    ]
    return pl.pallas_call(
        partial(backward_kernel, layer, layers_n, capacity),
        out_shape=outs,
        in_specs=[VMEM] * 17 + [HBM] * 7,
        out_specs=[VMEM] * 9 + [HBM] * 2,
        scratch_shapes=scratch + sum_scratch(rows, width + 128),
        compiler_params=settings(number),
        name="layer_backward",
    )(grads, stream, *tables, *saved, *plan, *weights)


class Sums:
    def __init__(self, ins, outs, held, send, recv, keep, z, near, line):
        self.ins, self.outs, self.held = ins, outs, held
        self.send, self.recv, self.keep = send, recv, keep
        self.z, self.near, self.line = z, near, line
        self.all = range(len(ins))

    def split(self, a):
        half = self.outs[a].shape[1] // 2
        return pl.ds(0, half), pl.ds(half, half)

    def move(self, a, j, name):
        part = self.ins[a]
        fromx, fromy, late, later, total, got = self.held[a]
        A, B = self.split(a)
        near = self.near
        kind, src, dst, to = {
            "xd": lambda: (0, part.at[j, near["d"], :, A], fromx.at[j, 0], "x"),
            "xx": lambda: (1, part.at[j, near["x"], :, A], fromx.at[j, 1], "x"),
            "yd": lambda: (2, part.at[j, near["d"], :, B], fromy.at[j, 0], "y"),
            "yy": lambda: (3, part.at[j, near["y"], :, B], fromy.at[j, 1], "y"),
            "ly": lambda: (4, late.at[j, 0], later.at[j, 0], "y"),
            "lx": lambda: (5, late.at[j, 1], later.at[j, 1], "x"),
            "up": lambda: (6, total.at[j], got.at[j], self.z + 1),
            "down": lambda: (7, total.at[j], got.at[j], self.z - 1),
        }[name]()
        if name == "down":
            slot = jnp.where(j == self.z - 1, self.line, j)
            dst = got.at[slot]
        return pltpu.make_async_remote_copy(
            src_ref=src,
            dst_ref=dst,
            send_sem=self.send.at[a, j, kind],
            recv_sem=self.recv.at[a, j, kind],
            device_id={DP: to} if kind >= 6 else {EX: near[to]},
            device_id_type=MESH,
        )

    def own_down(self, a):
        got = self.held[a][5]
        return pltpu.make_async_remote_copy(
            src_ref=got.at[self.line],
            dst_ref=got.at[self.line],
            send_sem=self.send.at[a, self.z, 7],
            recv_sem=self.recv.at[a, self.z, 7],
            device_id={DP: self.z},
            device_id_type=MESH,
        )

    def prepare(self, a, j):
        late, total = self.held[a][2], self.held[a][4]
        A, B = self.split(a)
        near, part = self.near, self.ins[a]
        return [
            pltpu.make_async_copy(src, dst, self.keep.at[a, j, i])
            for i, (src, dst) in enumerate(
                (
                    (part.at[j, near["y"], :, A], late.at[j, 0]),
                    (part.at[j, near["x"], :, B], late.at[j, 1]),
                    (part.at[j, near["own"]], total.at[j]),
                )
            )
        ]

    def at(self, step, act):
        if step == 0:
            act(self.z, 0)
            return

        @pl.when(self.z + step <= self.line - 1)
        def above():
            act(self.z + step, 1)

        @pl.when(self.z - step >= 0)
        def below():
            act(self.z - step, -1)

    def first(self, j, way):
        for a in self.all:
            for name in ("xd", "yd", "xx", "yy"):
                self.move(a, j, name).start()
            for one in self.prepare(a, j):
                one.start()

    def second(self, j, way):
        for a in self.all:
            fromx, fromy, late = self.held[a][:3]
            ready = self.prepare(a, j)
            ready[0].wait()
            self.move(a, j, "xd").wait_recv()
            late[j, 0] = (late[j, 0].astype(f32) + fromx[j, 0].astype(f32)).astype(bf16)
            self.move(a, j, "ly").start()
            ready[1].wait()
            self.move(a, j, "yd").wait_recv()
            late[j, 1] = (late[j, 1].astype(f32) + fromy[j, 0].astype(f32)).astype(bf16)
            self.move(a, j, "lx").start()

    def third(self, j, way):
        for a in self.all:
            fromx, fromy, late, later, total, got = self.held[a]
            for name in ("xx", "yy", "ly", "lx"):
                self.move(a, j, name).wait_recv()
            self.prepare(a, j)[2].wait()
            for side, (columns, here) in enumerate(zip(self.split(a), (fromx, fromy))):
                value = (
                    total[j, :, columns].astype(f32)
                    + here[j, 1].astype(f32)
                    + later[j, side].astype(f32)
                )
                if way == 0:
                    self.outs[a][:, columns] = value
                else:
                    total[j, :, columns] = value.astype(bf16)
            if way == 1:

                @pl.when(self.z > 0)
                def more_up():
                    self.move(a, j, "up").wait_recv()
                    total[j] = (total[j].astype(f32) + got[j].astype(f32)).astype(bf16)

                self.move(a, j, "up").start()
            elif way == -1:

                @pl.when(self.z < self.line - 1)
                def more_down():
                    self.move(a, j, "down").wait_recv()
                    total[j] = (total[j].astype(f32) + got[j].astype(f32)).astype(bf16)

                self.move(a, j, "down").start()
            else:

                @pl.when(self.z > 0)
                def end_up():
                    self.move(a, j, "up").wait_recv()
                    self.outs[a][...] += got[j].astype(f32)

                @pl.when(self.z < self.line - 1)
                def end_down():
                    self.own_down(a).wait_recv()
                    self.outs[a][...] += got[self.line].astype(f32)

    def finish(self, j, way):
        for a in self.all:
            for name in ("xd", "yd", "xx", "yy", "lx", "ly"):
                self.move(a, j, name).wait_send()
            if way == 1:
                self.move(a, j, "up").wait_send()
            elif way == -1:
                self.move(a, j, "down").wait_send()


def sums_scratch(shapes, line):
    scratch = []
    for rows, columns in shapes:
        half = columns // 2
        scratch += [pltpu.VMEM((line, 2, rows, half), bf16) for i in range(4)]
        scratch += [
            pltpu.VMEM((line, rows, columns), bf16),
            pltpu.VMEM((line + 1, rows, columns), bf16),
        ]
    return scratch + [
        pltpu.SemaphoreType.DMA((len(shapes), line, 8)),
        pltpu.SemaphoreType.DMA((len(shapes), line, 8)),
        pltpu.SemaphoreType.DMA((len(shapes), line, 3)),
    ]


def from_behind(value, axis, steps):
    count = lax.axis_size(axis)
    leading, last = (max(0, -steps), min(count, count - steps))
    return lax.ppermute(value, axis, [(source, source + steps) for source in range(leading, last)])


def from_sibling(value):
    count = lax.axis_size(EX)
    return lax.ppermute(value, EX, [(s, s + 1 - 2 * (s % 2)) for s in range(count)])


def rms_norm(stream, gain_row):
    return (
        stream * lax.rsqrt(jnp.mean(stream * stream, axis=-1, keepdims=True) + epsilon) * gain_row
    )


def rotary_tables(token_positions):
    half_dim = HEAD_SIZE // 2
    steps_up = jnp.arange(half_dim).astype(f32)
    frequency = jnp.exp(steps_up * (-2.0 * math.log(rope_base) / HEAD_SIZE))
    angles = token_positions.astype(f32)[:, None] * frequency[None, :]
    return jnp.cos(angles)[:, None, :], jnp.sin(angles)[:, None, :]


def apply_rotary(heads_in, cosine, sine_part):
    half_dim = heads_in.shape[-1] // 2
    first_half = heads_in[..., :half_dim]
    second_half = heads_in[..., half_dim:]
    return jnp.concatenate(
        [
            first_half * cosine - second_half * sine_part,
            second_half * cosine + first_half * sine_part,
        ],
        axis=-1,
    )


def gated_unit(gate_pre, up_pre):
    return jax.nn.silu(gate_pre) * up_pre


def masked_scores(query_rows, gathered_keys, allowed):
    token_rows = query_rows.shape[0]
    grouped_queries = query_rows.reshape(
        token_rows, KEY_VALUE_HEADS, QUERY_HEADS // KEY_VALUE_HEADS, HEAD_SIZE
    )
    score_scale = 1.0 / math.sqrt(HEAD_SIZE)
    scores = (
        jnp.einsum(
            "tkgd,skd->kgts", grouped_queries, gathered_keys, preferred_element_type=f32
        )
        * score_scale
    )
    return (jnp.where(allowed, scores, masked_score), grouped_queries)


def rank_table(routes, pair_order, experts_n):
    layers_n, token_rows, topk_n = routes.shape
    chosen = jnp.swapaxes(routes, 1, 2)
    order = jnp.swapaxes(pair_order.reshape(layers_n, token_rows, topk_n), 1, 2)
    ids = jnp.arange(experts_n, dtype=jnp.int32)[None, :, None]
    none = token_rows * topk_n
    place_of = jnp.full((layers_n, experts_n, token_rows), none, jnp.int32)
    for k in range(topk_n):
        place_of = jnp.where(chosen[:, k][:, None, :] == ids, order[:, k][:, None, :], place_of)
    smaller = (place_of[:, :, :, None] < place_of[:, :, None, :]).astype(jnp.int32)
    return jnp.where(place_of < none, jnp.sum(smaller, axis=2) + 1, 0)


def dense_gates(logits, mask):
    top = jnp.max(jnp.where(mask, logits, masked_score), axis=0, keepdims=True)
    powers = jnp.where(mask, jnp.exp(jnp.where(mask, logits - top, 0.0)), 0.0)
    return powers / jnp.sum(powers, axis=0, keepdims=True)


def local_chips(
    tokens,
    w_qkv,
    w_out,
    w_router,
    norm_gains,
    w_gate,
    w_up,
    w_down,
    out_grad,
    segment_ids,
    routes,
    pair_order,
):
    token_rows = tokens.shape[0]
    layers_n = w_qkv.shape[0]
    topk_n = routes.shape[2]
    n_expert = lax.axis_size(EX)
    n_dp = lax.axis_size(DP)
    local_n = w_gate.shape[1]
    experts_n = local_n * n_expert
    capacity = 9 * n_expert * token_rows * topk_n // (8 * experts_n)
    shapes = (layers_n, n_dp, n_expert, local_n, capacity)
    positions = lax.axis_index(EX) * token_rows + jnp.arange(token_rows, dtype=jnp.int32)
    cosine, sine = rotary_tables(positions)
    tables = (
        jnp.concatenate([cosine, cosine], axis=-1)[:, 0],
        jnp.concatenate([-sine, sine], axis=-1)[:, 0],
        segment_ids[:, None],
    )
    ranks = rank_table(routes, pair_order, experts_n).reshape(layers_n * experts_n, token_rows)
    ranks = jnp.concatenate([ranks, segment_ids[None], jnp.zeros((7, token_rows), jnp.int32)])
    small = jnp.concatenate(
        [w_router[l] for l in range(layers_n)]
        + [jnp.swapaxes(norm_gains.reshape(2 * layers_n, -1), 0, 1)],
        axis=1,
    )
    small = jnp.pad(small, ((0, 0), (0, 128 - small.shape[1])))
    experts = (w_gate, w_up, w_down)

    def along_line(rows):
        return lax.all_gather(rows, DP, axis=0)

    saved, outputs, normed_all, streams = [], [], [], [tokens]
    for l in range(layers_n):
        given = (small, ranks, w_qkv, w_out, out_grad)
        if l > 0:
            given = (*plan, line_grads, *full[l])
        results = layer_forward(l, 1 + l, shapes, streams[l], tables, given, experts)
        if l == 0:
            plan = results[13:18]
            full = [results[18:20], results[20:22]]
            line_grads = results[22]
        else:
            grads_all = [results[13]]
        streams.append(results[0])
        outputs.append(results[1])
        saved.append(results[2:12])
        normed_all.append(along_line(results[12]))

    grads = out_grad
    owns, smalls = [None] * layers_n, [None] * layers_n
    row_sources, column_sources = [None] * layers_n, [None] * layers_n
    for l in reversed(range(layers_n)):
        normed_a, queries, kv, attended, mixed, normed_b, rows_in = saved[l][:7]
        kept = (mixed, normed_b, queries, kv, *saved[l][7:])
        sources = (normed_a, attended, *full[l], *experts)
        results = layer_backward(l, 4 + l, shapes, grads, streams[l], tables, kept, plan, sources)
        grads, own_shard = results[:2]
        owns[l] = (rows_in, *results[2:6])
        column_sources[l] = results[6:8]
        smalls[l] = results[8]
        row_sources[l] = results[9:11]
    grad_experts, (small_sum, grad_qkv, grad_out) = tail(
        capacity,
        8,
        normed_all,
        grads_all,
        own_shard,
        (plan[0], plan[2], plan[3]),
        experts,
        owns,
        row_sources,
        column_sources,
        smalls,
    )
    small_sum = small_sum[:, :128] + small_sum[:, 128:]
    small_sum = small_sum[:, : layers_n * SMALL].reshape(-1, layers_n, SMALL)
    small_sum = jnp.swapaxes(small_sum, 0, 1)
    grad_router = small_sum[:, :, :experts_n]
    grad_gains = jnp.swapaxes(small_sum[:, :, experts_n : experts_n + 2], 1, 2)
    return (
        jnp.stack(outputs),
        grads,
        grad_qkv,
        grad_out,
        grad_router,
        grad_gains,
        *grad_experts,
    )


def local(
    tokens,
    w_qkv,
    w_out,
    w_router,
    norm_gains,
    w_gate,
    w_up,
    w_down,
    out_grad,
    segment_ids,
    routes,
    pair_order,
):
    token_rows = tokens.shape[0]
    layers_n = w_qkv.shape[0]
    topk_n = routes.shape[2]
    n_expert = lax.axis_size(EX)
    n_dp = lax.axis_size(DP)
    expert_here = lax.axis_index(EX)
    dp_here = lax.axis_index(DP)
    device_here = dp_here * n_expert + expert_here
    local_n = w_gate.shape[1]
    experts_n = local_n * n_expert
    capacity = 9 * n_expert * token_rows * topk_n // (8 * experts_n)
    group_rows = n_expert * token_rows
    query_width = QUERY_HEADS * HEAD_SIZE
    key_width = KEY_VALUE_HEADS * HEAD_SIZE
    score_scale = 1.0 / math.sqrt(HEAD_SIZE)
    token_positions = expert_here * token_rows + jnp.arange(token_rows, dtype=jnp.int32)
    cosine, sine_part = rotary_tables(token_positions)
    seg_prev = from_behind(segment_ids, everywhere, 1)
    has_prev = device_here > 0
    row_index = jnp.arange(token_rows)
    own_mask = (segment_ids[None, :] == segment_ids[:, None]) & (
        row_index[None, :] <= row_index[:, None]
    )
    prev_mask = (seg_prev[None, :] == segment_ids[:, None]) & has_prev
    allowed = jnp.concatenate([prev_mask, own_mask], axis=1)

    ranks = rank_table(routes, pair_order, experts_n)
    small = jnp.concatenate(
        [w_router[l] for l in range(layers_n)]
        + [jnp.swapaxes(norm_gains.reshape(2 * layers_n, -1), 0, 1)],
        axis=1,
    )
    small = jnp.pad(small, ((0, 0), (0, 128 - small.shape[1])))
    small_full, ranks_full, qkv_0, out_0 = [
        lax.all_gather(one, everywhere, axis=0)
        for one in (small, ranks.reshape(layers_n * experts_n, token_rows), w_qkv[0], w_out[0])
    ]
    qkv_fulls = [qkv_0.reshape(D, -1)]
    out_fulls = [out_0.reshape(query_width, D)]
    for layer_idx in range(1, layers_n):
        qkv_fulls.append(lax.all_gather(w_qkv[layer_idx], everywhere, axis=0, tiled=True))
        out_fulls.append(lax.all_gather(w_out[layer_idx], everywhere, axis=0, tiled=True))
    small_full = small_full.reshape(D, 128)
    gains = jnp.swapaxes(
        small_full[:, layers_n * experts_n : layers_n * (experts_n + 2)], 0, 1
    ).astype(f32)
    routers = [small_full[:, l * experts_n : (l + 1) * experts_n] for l in range(layers_n)]
    routers_turned = [jnp.swapaxes(router, 0, 1) for router in routers]
    ranks_full = ranks_full.reshape(n_dp, n_expert, layers_n, experts_n, token_rows)
    ranks_full = lax.dynamic_slice_in_dim(ranks_full, dp_here, 1, 0)
    groups = ranks_full.shape[0]
    hit_all = jnp.transpose(ranks_full > 0, (2, 0, 3, 1, 4)).reshape(
        layers_n, groups, experts_n, group_rows
    )
    mine = lax.dynamic_slice_in_dim(ranks_full, expert_here * local_n, local_n, 3)
    counts = jnp.sum((mine > 0).astype(jnp.int32), axis=-1)
    before = jnp.cumsum(counts, axis=1) - counts
    seats = jnp.where(mine > 0, before[..., None] + mine, 0)
    seats = jnp.transpose(seats, (2, 0, 3, 1, 4)).reshape(layers_n, groups, local_n, group_rows)
    seat_ids = jnp.arange(1, capacity + 1, dtype=jnp.int32)

    def own_of(array):
        return lax.dynamic_index_in_dim(array, 0, 0, keepdims=False)

    def seat_map(l):
        return (seats[l][:, :, None, :] == seat_ids[:, None]).astype(bf16)

    def gates_of(normed_rows, l, hit):
        logits = jnp.einsum("de,td->et", routers[l], normed_rows, preferred_element_type=f32)
        return dense_gates(logits, hit)

    own_hit = [(ranks[l] > 0) for l in range(layers_n)]

    stream = tokens.astype(f32)
    saved_layers = []
    outputs = []
    for l in range(layers_n):
        qkv_full, out_full = qkv_fulls[l], out_fulls[l]
        normed_a = rms_norm(stream, gains[2 * l]).astype(bf16)
        projected_output = jnp.dot(normed_a, qkv_full, preferred_element_type=f32)
        query_rows = apply_rotary(
            projected_output[:, :query_width].reshape(token_rows, QUERY_HEADS, HEAD_SIZE),
            cosine,
            sine_part,
        ).astype(bf16)
        key_own = apply_rotary(
            projected_output[:, query_width : query_width + key_width].reshape(
                token_rows, KEY_VALUE_HEADS, HEAD_SIZE
            ),
            cosine,
            sine_part,
        ).astype(bf16)
        value_own = (
            projected_output[:, query_width + key_width :]
            .reshape(token_rows, KEY_VALUE_HEADS, HEAD_SIZE)
            .astype(bf16)
        )
        key_prev, value_prev = from_behind((key_own, value_own), everywhere, 1)
        gathered_keys = jnp.concatenate([key_prev, key_own], axis=0)
        gathered_values = jnp.concatenate([value_prev, value_own], axis=0)
        scores, grouped_queries = masked_scores(query_rows, gathered_keys, allowed)
        top_score = jnp.max(scores, axis=-1, keepdims=True)
        exp_scores = jnp.exp(scores - top_score)
        row_total = jnp.sum(exp_scores, axis=-1, keepdims=True)
        prob_low = (exp_scores / row_total).astype(bf16)
        log_total = top_score + jnp.log(row_total)
        attended = (
            jnp.einsum("kgts,skd->tkgd", prob_low, gathered_values, preferred_element_type=f32)
            .reshape(token_rows, query_width)
            .astype(bf16)
        )
        mixed_sum = stream + jnp.dot(attended, out_full, preferred_element_type=f32)
        normed_b = rms_norm(mixed_sum, gains[2 * l + 1]).astype(bf16)

        if True:
            kept = {}
            group_normed = lax.all_gather(normed_b, EX, axis=0, tiled=True)
            kept["normed_all"] = group_normed[None]
            seat_own = own_of(seat_map(l))
            gates_own = gates_of(group_normed, l, own_of(hit_all[l]))
            gates_own = lax.dynamic_slice_in_dim(gates_own, expert_here * local_n, local_n, 0)
            gate_seat = jnp.sum(seat_own.astype(f32) * gates_own[:, None, :], axis=-1)
            expert_in = jnp.einsum(
                "est,td->esd", seat_own, group_normed, preferred_element_type=f32
            ).astype(bf16)
            gate_pre = jnp.einsum("esd,edf->esf", expert_in, w_gate[l], preferred_element_type=f32)
            up_pre = jnp.einsum("esd,edf->esf", expert_in, w_up[l], preferred_element_type=f32)
            hidden = gated_unit(gate_pre, up_pre).astype(bf16)
            expert_out = jnp.einsum("esf,efd->esd", hidden, w_down[l], preferred_element_type=f32)
            weighted = (expert_out * gate_seat[..., None]).astype(bf16)
            branch_part = jnp.einsum("est,esd->td", seat_own, weighted, preferred_element_type=f32)
            new_stream = mixed_sum + lax.psum_scatter(
                branch_part, EX, scatter_dimension=0, tiled=True
            )
        saved_layers.append(
            {
                "stream_in": stream,
                "normed_a": normed_a,
                "queries": query_rows,
                "key_all": gathered_keys,
                "value_all": gathered_values,
                "log_total": log_total,
                "attended": attended,
                "mixed_sum": mixed_sum,
                "normed_b": normed_b,
            }
            | kept
        )
        outputs.append(new_stream)
        stream = new_stream

    grad_stream = out_grad.astype(f32)
    weight_parts = [None] * layers_n
    expert_parts = [None] * layers_n
    owns = [None] * layers_n
    for l in reversed(range(layers_n)):
        record = saved_layers[l]
        qkv_full, out_full = qkv_fulls[l], out_fulls[l]
        grad_low = grad_stream.astype(bf16)
        if True:
            normed_all = record["normed_all"]
            grad_all = lax.all_gather(grad_low, EX, axis=0, tiled=True)[None]
            seat_all = seat_map(l)
            gates_all = jax.vmap(lambda rows, hit: gates_of(rows, l, hit))(normed_all, hit_all[l])
            gates_mine = lax.dynamic_slice_in_dim(gates_all, expert_here * local_n, local_n, 1)
            gate_seat = jnp.sum(seat_all.astype(f32) * gates_mine[:, :, None, :], axis=-1)
            rows_in = jnp.einsum(
                "gest,gtd->egsd", seat_all, normed_all, preferred_element_type=f32
            ).astype(bf16)
            rows_grad = jnp.einsum(
                "gest,gtd->egsd", seat_all, grad_all, preferred_element_type=f32
            ).astype(bf16)
            gate_seat = jnp.swapaxes(gate_seat, 0, 1)[..., None]
            gate_pre = jnp.einsum("egsd,edf->egsf", rows_in, w_gate[l], preferred_element_type=f32)
            up_pre = jnp.einsum("egsd,edf->egsf", rows_in, w_up[l], preferred_element_type=f32)
            dhidden_raw = jnp.einsum(
                "egsd,efd->egsf", rows_grad, w_down[l], preferred_element_type=f32
            )
            hidden, gate_pull = jax.vjp(gated_unit, gate_pre, up_pre)
            hidden_low = hidden.astype(bf16)
            dgate_pre, dup_pre = gate_pull(dhidden_raw * gate_seat)
            dgate_low = dgate_pre.astype(bf16)
            dup_low = dup_pre.astype(bf16)
            dgate_seat = jnp.sum(hidden_low.astype(f32) * dhidden_raw, axis=-1)
            rows_grad = (rows_grad.astype(f32) * gate_seat).astype(bf16)

        def by_expert(array):
            return array.reshape(local_n, -1, array.shape[-1])

        def outer(one, other):
            return jnp.einsum(
                "esa,esb->eab", by_expert(one), by_expert(other), preferred_element_type=f32
            )

        if True:
            grad_gate_l = outer(rows_in, dgate_low)
            grad_up_l = outer(rows_in, dup_low)
            grad_down_l = outer(hidden_low, rows_grad)
            grad_gate_l = lax.psum_scatter(
                grad_gate_l.astype(bf16), DP, scatter_dimension=1, tiled=True
            ).astype(f32)
            grad_up_l = lax.psum_scatter(
                grad_up_l.astype(bf16), DP, scatter_dimension=1, tiled=True
            ).astype(f32)
            grad_down_l = lax.psum_scatter(
                grad_down_l.astype(bf16), DP, scatter_dimension=2, tiled=True
            ).astype(f32)
            expert_parts[l] = (grad_gate_l, grad_up_l, grad_down_l)

        if True:
            dexpert_in = (
                jnp.einsum("egsf,edf->egsd", dgate_low, w_gate[l], preferred_element_type=f32)
                + jnp.einsum("egsf,edf->egsd", dup_low, w_up[l], preferred_element_type=f32)
            ).astype(bf16)
            back_part = jnp.einsum(
                "gest,egsd->td", seat_all, dexpert_in, preferred_element_type=f32
            )
            dgates_part = jnp.sum(
                seat_all[0].astype(f32) * dgate_seat[:, 0, :, None], axis=1
            )
            mine = expert_here * local_n + jnp.arange(local_n, dtype=jnp.int32)
            lane = jnp.arange(experts_n, dtype=jnp.int32)
            dgates_part = jnp.sum(
                jnp.where(mine[:, None, None] == lane, dgates_part[..., None], 0.0), axis=0
            )
            dnormed_b, dgates = [
                lax.psum_scatter(part, EX, scatter_dimension=0, tiled=True)
                for part in (back_part, dgates_part)
            ]
        gates_token = gates_of(record["normed_b"], l, own_hit[l]).T
        dlogits = (
            gates_token * (dgates - jnp.sum(gates_token * dgates, axis=1, keepdims=True))
        ).astype(bf16)
        dnormed_b = dnormed_b + jnp.einsum(
            "te,de->td", dlogits, routers[l], preferred_element_type=f32
        )
        unused_norm, norm_pull = jax.vjp(rms_norm, record["mixed_sum"], gains[2 * l + 1])
        dmixed_part, dgain_b = norm_pull(dnormed_b)
        dmixed = grad_stream + dmixed_part
        grad_attn = dmixed.astype(bf16)
        attended_gradient = jnp.einsum(
            "td,qd->tq", grad_attn, out_full, preferred_element_type=f32
        ).astype(bf16)
        gathered_keys = record["key_all"]
        gathered_values = record["value_all"]
        scores, grouped_queries = masked_scores(record["queries"], gathered_keys, allowed)
        prob_float = jnp.exp(scores - record["log_total"])
        prob_low = prob_float.astype(bf16)
        grouped_gradient = attended_gradient.reshape(
            token_rows, KEY_VALUE_HEADS, QUERY_HEADS // KEY_VALUE_HEADS, HEAD_SIZE
        )
        dvalue_all = jnp.einsum(
            "kgts,tkgd->skd", prob_low, grouped_gradient, preferred_element_type=f32
        )
        dprobs = jnp.einsum(
            "tkgd,skd->kgts", grouped_gradient, gathered_values, preferred_element_type=f32
        )
        delta_row = jnp.sum(prob_float * dprobs, axis=-1, keepdims=True)
        dscores = (prob_float * (dprobs - delta_row)).astype(bf16)
        dqueries = (
            jnp.einsum(
                "kgts,skd->tkgd", dscores, gathered_keys, preferred_element_type=f32
            ).reshape(token_rows, QUERY_HEADS, HEAD_SIZE)
            * score_scale
        )
        dkey_all = (
            jnp.einsum("kgts,tkgd->skd", dscores, grouped_queries, preferred_element_type=f32)
            * score_scale
        )
        dkey_next, dvalue_next = from_behind(
            (dkey_all[:token_rows].astype(bf16), dvalue_all[:token_rows].astype(bf16)),
            everywhere,
            -1,
        )
        dkey_own = dkey_all[token_rows:] + dkey_next.astype(f32)
        dvalue_own = dvalue_all[token_rows:] + dvalue_next.astype(f32)
        dq_raw = apply_rotary(dqueries, cosine, -sine_part)
        dk_raw = apply_rotary(dkey_own, cosine, -sine_part)
        dprojected = jnp.concatenate(
            [
                dq_raw.reshape(token_rows, query_width),
                dk_raw.reshape(token_rows, key_width),
                dvalue_own.reshape(token_rows, key_width),
            ],
            axis=1,
        ).astype(bf16)
        dnormed_a = jnp.einsum("tq,dq->td", dprojected, qkv_full, preferred_element_type=f32)
        unused_first, first_pull = jax.vjp(rms_norm, record["stream_in"], gains[2 * l])
        dstream_part, dgain_a = first_pull(dnormed_a)
        grad_stream = dmixed + dstream_part

        small_grad = jnp.concatenate(
            [
                jnp.einsum("td,te->de", record["normed_b"], dlogits, preferred_element_type=f32),
                dgain_a[:, None],
                dgain_b[:, None],
            ],
            axis=1,
        )
        normed_a, attended = record["normed_a"], record["attended"]
        grad_qkv_l = jnp.einsum("td,tq->dq", normed_a, dprojected, preferred_element_type=f32)
        grad_out_l = jnp.einsum("tq,td->qd", attended, grad_attn, preferred_element_type=f32)
        weight_parts[l] = (grad_qkv_l, grad_out_l, small_grad)

    small_grads = jnp.concatenate([weight_parts[l][2] for l in range(layers_n)], axis=1)
    if True:

        def scatter(array):
            return lax.psum_scatter(array, everywhere, scatter_dimension=0, tiled=True)

        small_sum = scatter(small_grads)
        grad_qkv = jnp.stack([scatter(weight_parts[l][0]) for l in range(layers_n)])
        grad_out = jnp.stack([scatter(weight_parts[l][1]) for l in range(layers_n)])
    wide = experts_n + 2
    grad_router = jnp.stack(
        [small_sum[:, l * wide : l * wide + experts_n] for l in range(layers_n)]
    )
    grad_gains = jnp.stack(
        [
            jnp.swapaxes(small_sum[:, l * wide + experts_n : (l + 1) * wide], 0, 1)
            for l in range(layers_n)
        ]
    )
    if True:
        grad_gate, grad_up, grad_down = [
            jnp.stack([expert_parts[l][member] for l in range(layers_n)]) for member in range(3)
        ]
    layer_outs = jnp.stack(outputs).astype(bf16)
    return (
        layer_outs,
        grad_stream,
        grad_qkv,
        grad_out,
        grad_router,
        grad_gains,
        grad_gate,
        grad_up,
        grad_down,
    )


def solution(mesh):
    sizes = (mesh.shape[DP], mesh.shape[EX])
    return jax.shard_map(
        local_chips if sizes == (4, 8) else local,
        mesh=mesh,
        in_specs=(
            P((DP, EX), None),
            P(None, (DP, EX), None),
            P(None, (DP, EX), None),
            P(None, (DP, EX), None),
            P(None, None, (DP, EX)),
            P(None, EX, None, None),
            P(None, EX, None, None),
            P(None, EX, None, None),
            P((DP, EX), None),
            P((DP, EX)),
            P(None, (DP, EX), None),
            P(None, (DP, EX), None),
        ),
        out_specs=(
            P(None, (DP, EX), None),
            P((DP, EX), None),
            P(None, (DP, EX), None),
            P(None, (DP, EX), None),
            P(None, (DP, EX), None),
            P(None, None, (DP, EX)),
            P(None, EX, DP, None),
            P(None, EX, DP, None),
            P(None, EX, None, DP),
        ),
        check_vma=False,
    )
```

```python
from functools import partial
import math

import jax
import jax.numpy as jnp
from jax import lax
from jax.experimental import pallas as pl
from jax.experimental.pallas import tpu as pltpu
from jax.sharding import PartitionSpec as P

D = 1536
QUERY_HEADS = 12
KEY_VALUE_HEADS = 2
HEAD_SIZE = 128
MESH = pl.DeviceIdType.MESH
DP, EX = "dp", "expert"
ANY = pl.ANY
bf16 = jnp.bfloat16
f32 = jnp.float32

epsilon = 1e-06
rope_base = 1000000.0
masked_score = -1e30
everywhere = (DP, EX)


def place():
    z = lax.axis_index(DP)
    e = lax.axis_index(EX)
    y, x, c = e // 4, (e // 2) % 2, e % 2
    near = {
        "own": e,
        "x": y * 4 + (1 - x) * 2 + c,
        "y": (1 - y) * 4 + x * 2 + c,
        "d": (1 - y) * 4 + (1 - x) * 2 + c,
        "c": y * 4 + x * 2 + (1 - c),
        "cx": y * 4 + (1 - x) * 2 + (1 - c),
        "cy": (1 - y) * 4 + x * 2 + (1 - c),
        "cd": (1 - y) * 4 + (1 - x) * 2 + (1 - c),
    }
    return z, near


def greet(z, near, plane, line, order=None):
    barrier = pltpu.get_barrier_semaphore()

    def tell(**target):
        pl.semaphore_signal(barrier, inc=1, device_id=target, device_id_type=MESH)

    for name in plane:
        tell(**{EX: near[name]})
    count = len(plane)
    links = []
    if line is not None:
        links += [(z < line - 1, {DP: z + 1}), (z > 0, {DP: z - 1})]
    if order is not None:
        behind, ahead, has_behind, has_ahead = order
        links += [
            (has_behind, {DP: behind[0], EX: behind[1]}),
            (has_ahead, {DP: ahead[0], EX: ahead[1]}),
        ]
    for there, target in links:

        @pl.when(there)
        def one():
            tell(**target)

        count = count + jnp.where(there, 1, 0)
    pl.semaphore_wait(barrier, count)


def halves(rows, columns):
    if rows % 32 == 0:
        return ((0, rows // 2), (0, columns)), ((rows // 2, rows // 2), (0, columns))
    if columns % 256 == 0:
        return ((0, rows), (0, columns // 2)), ((0, rows), (columns // 2, columns // 2))
    return ((0, 16), (0, columns)), ((16, rows - 16), (0, columns))


def cut(ref, part):
    (row, rows), (column, columns) = part
    return ref.at[pl.ds(row, rows), pl.ds(column, columns)]


KINDS = 10
SMALL = 24
BLOCK = 512
QUAD = ("own", "x", "y", "d")
BESIDE = ("c", "cx", "cy", "cd")


class Gather:
    def __init__(self, ins, outs, send, recv, z, near, line, flat=False):
        self.ins, self.outs, self.send, self.recv = ins, outs, send, recv
        self.z, self.near, self.line, self.flat = z, near, line, flat
        self.parts = [halves(*ref.shape) for ref in ins]
        self.all = range(len(ins))

    def hop(self, a, j, kind, whose, to, part=None, src=None):
        dst = self.outs[a].at[j] if self.flat else self.outs[a].at[j, self.near[whose]]
        src = dst if src is None else src
        if part is not None:
            src, dst = cut(src, part), cut(dst, part)
        return pltpu.make_async_remote_copy(
            src_ref=src,
            dst_ref=dst,
            send_sem=self.send.at[a, j, kind],
            recv_sem=self.recv.at[a, j, kind],
            device_id={DP: to} if kind >= 8 else {EX: self.near[to]},
            device_id_type=MESH,
        )

    def landed(self, a, j, kind, whose, part=None):
        if kind < 8:
            self.hop(a, j, kind, whose, "c", part).wait_recv()
        else:
            self.hop(a, j, kind, whose, self.z).wait_recv()

    def line_first(self):
        z = self.z

        @pl.when(z < self.line - 1)
        def up_first():
            for a in self.all:
                self.hop(a, z, 8, "own", z + 1, src=self.ins[a]).start()

        @pl.when(z > 0)
        def down_first():
            for a in self.all:
                self.hop(a, z, 9, "own", z - 1, src=self.ins[a]).start()

    def first(self, j, src=None):
        for a in self.all:
            one = None if src is None else src[a]
            self.hop(a, j, 0, "own", "x", src=one).start()
            self.hop(a, j, 1, "own", "y", src=one).start()
            self.hop(a, j, 2, "own", "c", src=one).start()

    def second(self, j, kind=0):
        for a in self.all:
            self.landed(a, j, 0, "x")
            self.hop(a, j, 4, "x", "y", self.parts[a][1]).start()
            self.hop(a, j, 5, "x", "c").start()
            self.landed(a, j, 1, "y")
            self.hop(a, j, 3, "y", "x", self.parts[a][0]).start()
            self.hop(a, j, 6, "y", "c").start()

    def third(self, j, kind=0):
        for a in self.all:
            self.landed(a, j, 3, "d", self.parts[a][0])
            self.landed(a, j, 4, "d", self.parts[a][1])
            self.hop(a, j, 7, "d", "c").start()

    def finish(self, j, kind=0):
        for a in self.all:
            for kind, whose in ((2, "c"), (5, "cx"), (6, "cy"), (7, "cd")):
                self.landed(a, j, kind, whose)
            for kind in (0, 1, 2):
                self.hop(a, j, kind, "own", "c").wait_send()
            self.hop(a, j, 3, "y", "x", self.parts[a][0]).wait_send()
            self.hop(a, j, 4, "x", "y", self.parts[a][1]).wait_send()
            for kind in (5, 6, 7):
                self.hop(a, j, kind, "x", "c").wait_send()

    def arrivals(self, step, act):
        z = self.z

        @pl.when(z - step >= 0)
        def below():
            act(z - step, 8)

        @pl.when(z + step <= self.line - 1)
        def above():
            act(z + step, 9)

    def take(self, j, kind):
        for a in self.all:
            self.landed(a, j, kind, "own")
        z = self.z
        if kind == 8:

            @pl.when(z < self.line - 1)
            def on_up():
                for a in self.all:
                    self.hop(a, j, 8, "own", z + 1).start()

        else:

            @pl.when(z > 0)
            def on_down():
                for a in self.all:
                    self.hop(a, j, 9, "own", z - 1).start()

        self.first(j)

    def carry(self, j, kind):
        z = self.z
        for a in self.all:
            self.landed(a, j, kind, "own")
        more, target = (z < self.line - 1, z + 1) if kind == 8 else (z > 0, z - 1)

        @pl.when(more)
        def on():
            for a in self.all:
                self.hop(a, j, kind, "own", target).start()

    def plane_of(self, k):
        return lax.rem(self.z + k, self.line)

    def spread(self, k, rows, sem):
        j = self.plane_of(k)
        self.first(j, [rows.at[j]])
        self.kept(k, rows, sem).start()

    def kept(self, k, rows, sem):
        j = self.plane_of(k)
        return pltpu.make_async_copy(rows.at[j], self.outs[0].at[j, self.near["own"]], sem.at[k])

    def spread_done(self, rows, sem):
        for k in range(1, self.line):
            self.finish(self.plane_of(k))
            self.kept(k, rows, sem).wait()

    def line_done(self):
        z = self.z
        for step in range(self.line):

            @pl.when((z - step >= 0) & (z < self.line - 1))
            def up_done():
                for a in self.all:
                    self.hop(a, z - step, 8, "own", z + 1).wait_send()

            @pl.when((z + step <= self.line - 1) & (z > 0))
            def down_done():
                for a in self.all:
                    self.hop(a, z + step, 9, "own", z - 1).wait_send()


def plane_gather(src, dst, send, recv, near):
    parts = halves(*src.shape)

    def hop(kind, whose, to, part=None):
        one = dst.at[near[whose]] if part is None else cut(dst.at[near[whose]], part)
        return pltpu.make_async_remote_copy(
            src_ref=src if whose == "own" else one,
            dst_ref=one,
            send_sem=send.at[kind],
            recv_sem=recv.at[kind],
            device_id={EX: near[to]},
            device_id_type=MESH,
        )

    def first():
        hop(0, "own", "x").start()
        hop(1, "own", "y").start()
        hop(2, "own", "c").start()
        dst[near["own"]] = src[...]

    def second():
        hop(0, "x", "c").wait_recv()
        hop(4, "x", "y", parts[1]).start()
        hop(5, "x", "c").start()
        hop(1, "y", "c").wait_recv()
        hop(3, "y", "x", parts[0]).start()
        hop(6, "y", "c").start()

    def third():
        hop(3, "d", "c", parts[0]).wait_recv()
        hop(4, "d", "c", parts[1]).wait_recv()
        hop(7, "d", "c").start()

    def finish():
        for kind, whose in ((2, "c"), (5, "cx"), (6, "cy"), (7, "cd")):
            hop(kind, whose, "c").wait_recv()
        for kind in (0, 1, 2):
            hop(kind, "own", "c").wait_send()
        hop(3, "y", "x", parts[0]).wait_send()
        hop(4, "x", "y", parts[1]).wait_send()
        for kind in (5, 6, 7):
            hop(kind, "x", "c").wait_send()

    return first, second, third, finish


def sum_scratch(rows, columns):
    return [
        pltpu.VMEM((8, rows, columns), bf16),
        pltpu.VMEM((3, rows, columns), bf16),
        pltpu.VMEM((4, rows, columns), bf16),
        pltpu.VMEM((2, rows // 2, columns), bf16),
        pltpu.VMEM((2, rows // 2, columns), bf16),
        pltpu.VMEM((2, rows // 2, columns), bf16),
        pltpu.SemaphoreType.DMA((10,)),
        pltpu.SemaphoreType.DMA((10,)),
    ]


def plane_sum(make, out_ref, base, scratch, near):
    part_ref, paired, fromc, fromx, fromy, last, send, recv = scratch
    rows = out_ref.shape[0]
    half = rows // 2
    A, B = pl.ds(0, half), pl.ds(half, half)

    def copy(number, src, dst, to):
        return pltpu.make_async_remote_copy(
            src_ref=src,
            dst_ref=dst,
            send_sem=send.at[number],
            recv_sem=recv.at[number],
            device_id={EX: near[to]},
            device_id_type=MESH,
        )

    order = ("d", "x", "y", "own")
    across = ("cd", "cx", "cy", "c")
    core = [copy(s, part_ref.at[near[name]], fromc.at[s], "c") for s, name in enumerate(across)]
    to_x = [copy(4, paired.at[0, A], fromx.at[0], "x"), copy(5, paired.at[1, A], fromx.at[1], "x")]
    to_y = [copy(6, paired.at[0, B], fromy.at[0], "y"), copy(7, paired.at[2, B], fromy.at[1], "y")]
    late_y = copy(8, paired.at[2, A], last.at[0], "y")
    late_x = copy(9, paired.at[1, B], last.at[1], "x")

    def pair(s):
        core[s].wait_recv()
        paired[s] = (part_ref[near[order[s]]].astype(f32) + fromc[s].astype(f32)).astype(bf16)

    for s in range(3):
        make(across[s])
        core[s].start()
        make(order[s])
    pair(0)
    to_x[0].start()
    to_y[0].start()
    make(across[3])
    core[3].start()
    pair(1)
    to_x[1].start()
    pair(2)
    to_y[1].start()
    make(order[3])
    core[3].wait_recv()
    total = part_ref[near["own"]].astype(f32) + fromc[3].astype(f32)
    out_ref[...] = total if base is None else base[...] + total
    to_x[0].wait_recv()
    paired[2, A] = (paired[2, A].astype(f32) + fromx[0].astype(f32)).astype(bf16)
    late_y.start()
    to_y[0].wait_recv()
    paired[1, B] = (paired[1, B].astype(f32) + fromy[0].astype(f32)).astype(bf16)
    late_x.start()
    to_x[1].wait_recv()
    out_ref[A] += fromx[1].astype(f32)
    to_y[1].wait_recv()
    out_ref[B] += fromy[1].astype(f32)
    late_y.wait_recv()
    out_ref[A] += last[0].astype(f32)
    late_x.wait_recv()
    out_ref[B] += last[1].astype(f32)
    for one in core + to_x + to_y + [late_x, late_y]:
        one.wait_send()


def mul(a, b, over=((1,), (0,))):
    return lax.dot_general(a, b, (over, ((), ())), preferred_element_type=f32)


LAST = ((1,), (1,))


def seat_rows(seats, number):
    local_n, tokens_n = seats.shape
    rows = lax.broadcasted_iota(jnp.int32, (local_n * number, tokens_n), 0).astype(f32)
    hot = rows < 0
    for e in range(local_n):
        one = seats[e : e + 1, :]
        hot = hot | ((rows == one + (e * number - 1)) & (one > 0) & (one <= number))
    return jnp.where(hot, 1.0, 0.0).astype(bf16)


def seat_columns(seats, number):
    tokens_n, local_n = seats.shape
    columns = lax.broadcasted_iota(jnp.int32, (tokens_n, local_n * number), 1).astype(f32)
    hot = columns < 0
    for e in range(local_n):
        one = seats[:, e : e + 1]
        hot = hot | ((columns == one + (e * number - 1)) & (one > 0) & (one <= number))
    return jnp.where(hot, 1.0, 0.0).astype(bf16)


def masked_gates(logits, hit):
    top = jnp.max(jnp.where(hit, logits, masked_score), axis=0, keepdims=True)
    powers = jnp.where(hit, jnp.exp(jnp.where(hit, logits - top, 0.0)), 0.0)
    return powers / jnp.sum(powers, axis=0, keepdims=True)


def tail_kernel(layers_n, number, *refs):
    refs = list(refs)

    def some(count):
        taken = refs[:count]
        del refs[:count]
        return taken

    tokens_all, grads_all = some(layers_n), some(layers_n - 1)
    (own_shard,) = some(1)
    table, hit, seats = some(3)
    w_gate, w_up, w_down = some(3)
    owns = [some(5) for l in range(layers_n)]
    row_sources = [some(2) for l in range(layers_n)]
    column_sources = [some(2) for l in range(layers_n)]
    smalls = some(layers_n)
    grad_gate, grad_up, grad_down, landing = some(4)
    beside = some(layers_n)
    small_sum, grad_qkv, grad_out = some(3)
    (
        tokens,
        grads,
        gates,
        rows_in,
        rows_grad,
        cols_in,
        cols_grad,
        hidden_low,
        dgate_low,
        dup_low,
        gate_w,
        up_w,
        down_w,
        stage_wide,
        stage_tall,
        weight_sem,
        token_sem,
        own_sem,
        out_sem,
        gather_send,
        gather_recv,
        beside_send,
        beside_recv,
        small_own,
        small_got,
        small_part,
        small_sem,
        columns,
        row_block,
        block_sum,
        block_got,
        final,
        final_got,
        column_send,
        column_recv,
        column_keep,
        row_sem,
        block_send,
        block_recv,
        final_send,
        final_recv,
    ) = some(41)
    held = [some(6)]
    z, near = place()
    n_dp, local_n = seats.shape[1], seats.shape[2]
    width = cols_in.shape[1]
    ours = pl.ds(pl.multiple_of(z * width, 128), width)
    gather = Gather([own_shard], [landing], gather_send, gather_recv, z, near, n_dp)
    total = Sums([small_part], [small_sum], held, *refs, z, near, n_dp)
    own_e = near["own"]
    plane_n = columns.shape[1]
    over = ((0,), (0,))
    per_expert = n_dp - 1
    per_layer = local_n * per_expert
    steps = layers_n * per_layer

    def layer_of(i):
        return layers_n - 1 - i // per_layer

    def across(l, j):
        return pltpu.make_async_remote_copy(
            src_ref=tokens_all[l].at[j],
            dst_ref=beside[l].at[j],
            send_sem=beside_send.at[l, j],
            recv_sem=beside_recv.at[l, j],
            device_id={EX: near["c"]},
            device_id_type=MESH,
        )

    def start(one):
        one.start()

    def wait(one):
        one.wait()

    def fetch(i, slot, act):
        j = lax.rem(z + 1 + lax.rem(i, per_expert), n_dp)
        for l in range(layers_n):

            @pl.when(layer_of(i) == l)
            def of_layer():
                if act is start:

                    @pl.when(lax.rem(i, per_layer) < per_expert)
                    def arrived():
                        across(l, j).wait_recv()

                for source, names, base in ((tokens_all[l], QUAD, 0), (beside[l], BESIDE, 4)):
                    for q, name in enumerate(names):
                        dst = tokens.at[slot, near[name]]
                        sem = token_sem.at[slot, base + q]
                        act(pltpu.make_async_copy(source.at[j, q], dst, sem))
                grads_from = (landing if l == 0 else grads_all[l - 1]).at[j]
                act(pltpu.make_async_copy(grads_from, grads.at[slot], token_sem.at[slot, 8]))

    def weights(l, e):
        return [
            pltpu.make_async_copy(src.at[l, e], dst, weight_sem.at[i])
            for i, (src, dst) in enumerate(((w_gate, gate_w), (w_up, up_w), (w_down, down_w)))
        ]

    def own(l, e):
        here = pl.ds(pl.multiple_of(e * number, 32), number)
        inner = pl.ds(0, number)
        pairs = (
            (owns[l][0].at[here, ours], cols_in.at[inner]),
            (owns[l][1].at[here, ours], cols_grad.at[inner]),
            (owns[l][2].at[here], hidden_low.at[inner]),
            (owns[l][3].at[here], dgate_low.at[inner]),
            (owns[l][4].at[here], dup_low.at[inner]),
        )
        return [
            pltpu.make_async_copy(src, dst, own_sem.at[i]) for i, (src, dst) in enumerate(pairs)
        ]

    def of(i, make, act):
        e = lax.rem(i // per_expert, local_n)
        for l in range(layers_n):

            @pl.when(layer_of(i) == l)
            def of_layer():
                for one in make(l, e):
                    act(one)

    def results(l, e):
        return [
            pltpu.make_async_copy(stage_wide.at[0], grad_gate.at[l, e], out_sem.at[0]),
            pltpu.make_async_copy(stage_wide.at[1], grad_up.at[l, e], out_sem.at[1]),
            pltpu.make_async_copy(stage_tall, grad_down.at[l, e], out_sem.at[2]),
        ]

    def column_pieces(l, owner):
        first, second = column_sources[l]
        extra = second.shape[1] // 128 - plane_n
        return [
            (first.at[:, pl.ds(pl.multiple_of(owner * 256, 256), 256)], 0, 256),
            (second.at[:, pl.ds(pl.multiple_of(owner * 128, 128), 128)], 256, 128),
            (
                second.at[
                    :, pl.ds(pl.multiple_of((plane_n + owner // 2 % extra) * 128, 128), 128)
                ],
                384,
                128,
            ),
        ]

    def column_copy(l, owner, source, piece):
        src, at, size = column_pieces(l, owner)[piece]
        return pltpu.make_async_remote_copy(
            src_ref=src,
            dst_ref=columns.at[l, source, :, pl.ds(at, size)],
            send_sem=column_send.at[l, owner, piece],
            recv_sem=column_recv.at[l, source, piece],
            device_id={EX: owner},
            device_id_type=MESH,
        )

    def column_own(l, piece):
        src, at, size = column_pieces(l, own_e)[piece]
        dst = columns.at[l, own_e, :, pl.ds(at, size)]
        return pltpu.make_async_copy(src, dst, column_keep.at[l, piece])

    def column_each(l, act_send, act_recv, act_own):
        for d in range(1, plane_n):
            owner = lax.rem(own_e + d, plane_n)
            source = lax.rem(own_e + plane_n - d, plane_n)
            for piece in range(3):
                if piece < 2:
                    if act_send is not None:
                        act_send(column_copy(l, owner, own_e, piece))
                    if act_recv is not None:
                        act_recv(column_copy(l, owner, source, piece))
                    continue
                if act_send is not None:

                    @pl.when(lax.rem(owner, 2) == 0)
                    def extra_out():
                        act_send(column_copy(l, owner, own_e, piece))

                if act_recv is not None:

                    @pl.when(lax.rem(own_e, 2) == 0)
                    def extra_in():
                        act_recv(column_copy(l, owner, source, piece))

        if act_own is not None:
            act_own(column_own(l, 0))
            act_own(column_own(l, 1))

            @pl.when(lax.rem(own_e, 2) == 0)
            def extra_own():
                act_own(column_own(l, 2))

    def row_loads(l):
        return [
            pltpu.make_async_copy(src.at[0], row_block.at[i], row_sem.at[i])
            for i, src in enumerate(row_sources[l])
        ]

    def blocks(l):
        column_each(l, None, lambda one: one.wait_recv(), wait)
        for one in row_loads(l):
            one.wait()
        height = block_sum.shape[2]
        for i in range(2):
            here = pl.ds(i * 256, 256)
            given = columns[l, :, :, here].reshape(-1, 256)
            for j in range(n_dp):
                rows = row_block[i, :, :, pl.ds(j * height, height)].reshape(-1, height)
                block_sum[l, j, :, here] = mul(rows, given, over).astype(bf16)
        if l > 0:
            for one in row_loads(l - 1):
                one.start()

    def block_move(l, j, way):
        slot = jnp.where(j == z + way, n_dp, j) if way < 0 else j
        return pltpu.make_async_remote_copy(
            src_ref=block_sum.at[l, j],
            dst_ref=block_got.at[l, slot],
            send_sem=block_send.at[l, j],
            recv_sem=block_recv.at[l, slot],
            device_id={DP: z + way},
            device_id_type=MESH,
        )

    def block_landed(l, slot):
        pltpu.make_async_remote_copy(
            src_ref=block_got.at[l, slot],
            dst_ref=block_got.at[l, slot],
            send_sem=block_send.at[l, 0],
            recv_sem=block_recv.at[l, slot],
            device_id={DP: z},
            device_id_type=MESH,
        ).wait_recv()

    def block_step(l):
        def act(j, way):
            if way == 0:
                return
            more = (z > 0) if way > 0 else (z < n_dp - 1)

            @pl.when(more)
            def add():
                block_landed(l, j)
                block_sum[l, j] = (
                    block_sum[l, j].astype(f32) + block_got[l, j].astype(f32)
                ).astype(bf16)

            block_move(l, j, way).start()

        return act

    def final_copy(l, owner, source):
        return pltpu.make_async_remote_copy(
            src_ref=final.at[l, owner],
            dst_ref=final_got.at[l, source],
            send_sem=final_send.at[l, owner],
            recv_sem=final_recv.at[l, source],
            device_id={EX: owner},
            device_id_type=MESH,
        )

    def block_end(l):
        final[l] = block_sum[l, z].reshape(final.shape[1:])

        @pl.when(z > 0)
        def below():
            block_landed(l, z)
            got = block_got[l, z].reshape(final.shape[1:])
            final[l] = (final[l].astype(f32) + got.astype(f32)).astype(bf16)

        @pl.when(z < n_dp - 1)
        def above():
            block_landed(l, n_dp)
            got = block_got[l, n_dp].reshape(final.shape[1:])
            final[l] = (final[l].astype(f32) + got.astype(f32)).astype(bf16)

        for d in range(1, plane_n):
            final_copy(l, lax.rem(own_e + d, plane_n), own_e).start()
        final_got[l, own_e] = final[l, own_e]

    def block_out(l):
        for d in range(1, plane_n):
            final_copy(l, own_e, lax.rem(own_e + d, plane_n)).wait_recv()
        for source in range(plane_n):
            got = final_got[l, source].astype(f32)
            grad_qkv[l, :, pl.ds(source * 256, 256)] = got[:, :256]
            grad_out[l, :, pl.ds(source * 128, 128)] = got[:, 256:384]
            if source % 2 == 0:
                grad_out[l, :, pl.ds((plane_n + source // 2) * 128, 128)] = got[:, 384:]

    def small_exchange():
        return pltpu.make_async_remote_copy(
            src_ref=small_own,
            dst_ref=small_got,
            send_sem=small_sem.at[0],
            recv_sem=small_sem.at[1],
            device_id={EX: near["c"]},
            device_id_type=MESH,
        )

    def small_parts():
        small_exchange().wait_recv()
        both = small_own[...] + small_got[...]
        rest = jnp.zeros((128 - both.shape[0], both.shape[1]), f32)
        turned = jnp.transpose(jnp.concatenate([both, rest], axis=0))
        high = turned.astype(bf16)
        low = (turned - high.astype(f32)).astype(bf16)
        shape = small_part.shape[:3] + (128,)
        small_part[:, :, :, pl.ds(0, 128)] = high.reshape(shape)
        small_part[:, :, :, pl.ds(128, 128)] = low.reshape(shape)
        for distance in (3, 2, 1, 0):
            total.at(distance, total.first)

    for l in range(layers_n):
        small_own[pl.ds(l * SMALL, SMALL)] = smalls[l][...]

    @pl.when(lax.rem(own_e, 2) == 1)
    def no_extra():
        columns[:, :, :, pl.ds(384, 128)] = jnp.zeros(columns.shape[:3] + (128,), bf16)

    greet(z, near, ("x", "y", "d", "c", "cx", "cy", "cd"), n_dp)
    gather.line_first()
    small_exchange().start()
    for l in reversed(range(layers_n)):
        for k in range(1, n_dp):
            across(l, lax.rem(z + k, n_dp)).start()
    for l in reversed(range(layers_n)):
        column_each(l, start, None, start)
    for one in row_loads(layers_n - 1):
        one.start()
    of(0, weights, start)
    fetch(0, 0, start)

    def block_at(l, distance):
        return lambda: total.at(distance, block_step(l))

    services = {
        0: [lambda: gather.arrivals(1, gather.take), small_parts],
        1: [lambda: gather.arrivals(2, gather.take), lambda: blocks(1)],
        2: [
            lambda: gather.arrivals(1, gather.second),
            lambda: gather.arrivals(3, gather.take),
            block_at(1, 3),
        ],
        3: [
            lambda: gather.arrivals(1, gather.third),
            lambda: gather.arrivals(2, gather.second),
            block_at(1, 2),
            lambda: blocks(0),
        ],
        4: [
            lambda: gather.arrivals(2, gather.third),
            lambda: gather.arrivals(3, gather.second),
            block_at(0, 3),
            block_at(1, 1),
        ],
        5: [
            lambda: gather.arrivals(3, gather.third),
            lambda: gather.arrivals(1, gather.finish),
            lambda: gather.arrivals(2, gather.finish),
            lambda: gather.arrivals(3, gather.finish),
            block_at(0, 2),
        ],
        6: [
            lambda: total.at(3, total.second),
            lambda: total.at(2, total.second),
            lambda: total.at(1, total.second),
            lambda: total.at(0, total.second),
            block_at(0, 1),
        ],
        7: [lambda: block_end(1)],
        8: [lambda: total.at(3, total.third), lambda: total.at(2, total.third)],
        9: [lambda: total.at(1, total.third)],
        10: [lambda: block_end(0)],
        11: [lambda: total.at(0, total.third), lambda: block_out(1)],
    }

    def step(i, carry):
        slot = lax.rem(i, 2)
        l = layer_of(i)
        k = lax.rem(i, per_expert)
        e = lax.rem(i // per_expert, local_n)
        j = lax.rem(z + 1 + k, n_dp)

        @pl.when(k == 0)
        def begin():
            of(i, own, start)

        @pl.when((i + 1 < steps) & (i != per_layer - 1))
        def ahead():
            fetch(i + 1, 1 - slot, start)

        fetch(i, slot, wait)
        everyone = tokens[slot].reshape(-1, tokens.shape[3])
        experts_n = hit.shape[2]

        @pl.when(e == 0)
        def gates_here():
            here = pl.ds(pl.multiple_of(l * experts_n, experts_n), experts_n)
            router = table[here, :].astype(bf16)
            gates[k] = masked_gates(mul(router, everyone, LAST), hit[l, j] > 0)

        pick = seat_rows(seats[l, j, pl.ds(e, 1)], number)
        rows_in[...] = mul(pick, everyone).astype(bf16)
        rows_grad[...] = mul(pick, grads[slot].reshape(-1, tokens.shape[3])).astype(bf16)
        place_of = pl.ds(pl.multiple_of((k + 1) * number, 32), number)
        mine = gates[k, pl.ds(own_e * local_n + e, 1), :]
        gate_seat = jnp.sum(pick.astype(f32) * mine, axis=1, keepdims=True)

        @pl.when(k == 0)
        def weights_here():
            of(i, weights, wait)

        gate = mul(rows_in[...], gate_w[...])
        up = mul(rows_in[...], up_w[...])
        raw = mul(rows_grad[...], down_w[...], LAST) * gate_seat
        sigmoid = 1.0 / (1.0 + jnp.exp(-gate))
        silu = gate * sigmoid
        hidden_low[place_of] = (silu * up).astype(bf16)
        dgate_low[place_of] = (raw * up * sigmoid * (1.0 + gate * (1.0 - sigmoid))).astype(bf16)
        dup_low[place_of] = (raw * silu).astype(bf16)
        cols_in[place_of] = rows_in[:, ours]
        cols_grad[place_of] = (rows_grad[:, ours].astype(f32) * gate_seat).astype(bf16)

        @pl.when(k == per_expert - 1)
        def close():
            @pl.when(i + 1 < steps)
            def next_weights():
                of(i + 1, weights, start)

            of(i, own, wait)

            @pl.when(i >= per_expert)
            def staged():
                of(i - per_expert, results, wait)

            stage_wide[0] = mul(cols_in[...], dgate_low[...], over)
            stage_wide[1] = mul(cols_in[...], dup_low[...], over)
            stage_tall[...] = mul(hidden_low[...], cols_grad[...], over)
            of(i, results, start)

        for at, acts in services.items():

            @pl.when(i == at)
            def serve():
                for act in acts:
                    act()

        @pl.when(i == per_layer - 1)
        def late_ahead():
            fetch(i + 1, 1 - slot, start)

        return carry

    lax.fori_loop(0, steps, step, 0)
    block_out(0)
    for distance in (3, 2, 1, 0):
        total.at(distance, total.finish)
    small_exchange().wait_send()
    for l in range(layers_n):
        column_each(l, lambda one: one.wait_send(), None, None)
        for d in range(1, plane_n):
            final_copy(l, lax.rem(own_e + d, plane_n), own_e).wait_send()
        for distance in (3, 2, 1):
            total.at(distance, lambda j, way: block_move(l, j, way).wait_send())
    gather.line_done()
    for l in range(layers_n):
        for k in range(1, n_dp):
            across(l, lax.rem(z + k, n_dp)).wait_send()
    of(steps - 1, results, wait)


def tail(
    capacity,
    number,
    tokens_all,
    grads_all,
    own_shard,
    plan,
    weights,
    owns,
    row_sources,
    column_sources,
    smalls,
):
    table, hit, seats = plan
    layers_n, n_dp, local_n, group_rows = seats.shape
    n_expert = lax.axis_size(EX)
    rows, width = own_shard.shape
    hidden = weights[0].shape[3]
    part = width // n_dp
    cut_rows = part // n_expert
    wide = column_sources[0][0].shape[1]
    shape = jax.ShapeDtypeStruct
    several = [one for group in (owns, row_sources, column_sources) for l in group for one in l]
    results = pl.pallas_call(
        partial(tail_kernel, layers_n, capacity),
        out_shape=[
            shape((layers_n, local_n, part, hidden), f32),
            shape((layers_n, local_n, part, hidden), f32),
            shape((layers_n, local_n, hidden, part), f32),
            shape((n_dp, n_expert, rows, width), bf16),
        ]
        + [shape(tokens_all[0].shape, bf16)] * layers_n
        + [
            shape((cut_rows, 256), f32),
            shape((layers_n, cut_rows, wide), f32),
            shape((layers_n, cut_rows, width), f32),
        ],
        in_specs=[HBM] * (2 * layers_n) + [VMEM] * 3 + [HBM] * (3 + len(several)) + [VMEM] * layers_n,
        out_specs=[HBM] * (4 + layers_n) + [VMEM] * 3,
        scratch_shapes=[
            pltpu.VMEM((2, n_expert, rows, width), bf16),
            pltpu.VMEM((2, n_expert, rows, width), bf16),
            pltpu.VMEM((n_dp - 1,) + hit.shape[2:], f32),
            pltpu.VMEM((capacity, width), bf16),
            pltpu.VMEM((capacity, width), bf16),
            pltpu.VMEM((n_dp * capacity, part), bf16),
            pltpu.VMEM((n_dp * capacity, part), bf16),
            pltpu.VMEM((n_dp * capacity, hidden), bf16),
            pltpu.VMEM((n_dp * capacity, hidden), bf16),
            pltpu.VMEM((n_dp * capacity, hidden), bf16),
            pltpu.VMEM((width, hidden), bf16),
            pltpu.VMEM((width, hidden), bf16),
            pltpu.VMEM((hidden, width), bf16),
            pltpu.VMEM((2, part, hidden), f32),
            pltpu.VMEM((hidden, part), f32),
            pltpu.SemaphoreType.DMA((3,)),
            pltpu.SemaphoreType.DMA((2, 9)),
            pltpu.SemaphoreType.DMA((5,)),
            pltpu.SemaphoreType.DMA((3,)),
            pltpu.SemaphoreType.DMA((1, n_dp, KINDS)),
            pltpu.SemaphoreType.DMA((1, n_dp, KINDS)),
            pltpu.SemaphoreType.DMA((layers_n, n_dp)),
            pltpu.SemaphoreType.DMA((layers_n, n_dp)),
            pltpu.VMEM((layers_n * SMALL, width), f32),
            pltpu.VMEM((layers_n * SMALL, width), f32),
            pltpu.VMEM((n_dp, n_expert, cut_rows, 256), bf16),
            pltpu.SemaphoreType.DMA((2,)),
            pltpu.VMEM((layers_n, n_expert, rows, BLOCK), bf16),
            pltpu.VMEM((2, n_expert, rows, width), bf16),
            pltpu.VMEM((layers_n, n_dp, part, BLOCK), bf16),
            pltpu.VMEM((layers_n, n_dp + 1, part, BLOCK), bf16),
            pltpu.VMEM((layers_n, n_expert, cut_rows, BLOCK), bf16),
            pltpu.VMEM((layers_n, n_expert, cut_rows, BLOCK), bf16),
            pltpu.SemaphoreType.DMA((layers_n, n_expert, 3)),
            pltpu.SemaphoreType.DMA((layers_n, n_expert, 3)),
            pltpu.SemaphoreType.DMA((layers_n, 3)),
            pltpu.SemaphoreType.DMA((2,)),
            pltpu.SemaphoreType.DMA((layers_n, n_dp)),
            pltpu.SemaphoreType.DMA((layers_n, n_dp + 1)),
            pltpu.SemaphoreType.DMA((layers_n, n_expert)),
            pltpu.SemaphoreType.DMA((layers_n, n_expert)),
        ]
        + sums_scratch([(cut_rows, 256)], n_dp),
        compiler_params=settings(number),
        name="tail",
    )(
        *tokens_all,
        *grads_all,
        own_shard,
        *plan,
        *weights,
        *several,
        *smalls,
    )
    return results[:3], results[4 + layers_n :]


VMEM = pl.BlockSpec(memory_space=pltpu.VMEM)
HBM = pl.BlockSpec(memory_space=ANY)


def settings(number):
    return pltpu.CompilerParams(
        collective_id=number, has_side_effects=True, vmem_limit_bytes=63 << 20
    )


def chain(z, e):
    n_expert = 8
    behind = (z, lax.rem(e + n_expert - 1, n_expert))
    ahead = (z, lax.rem(e + 1, n_expert))
    return behind, ahead, e > 0, e < n_expert - 1


def normalized(value, gain):
    scale = lax.rsqrt(jnp.mean(value * value, axis=-1, keepdims=True) + epsilon)
    return value * scale * gain


def turn(head, cosine, signed_sine):
    return head * cosine + pltpu.roll(head, HEAD_SIZE // 2, 1) * signed_sine


def head_of(h):
    return pl.ds(h * HEAD_SIZE, HEAD_SIZE)


def allowed_keys(rk, row, z, e, behind, has_behind, seg_column):
    own = rk[z, e, pl.ds(row, 1), :]
    first = rk[z, behind[1], pl.ds(row, 1), :]
    rows = seg_column.shape[0]
    query = lax.broadcasted_iota(jnp.int32, (rows, rows), 0)
    key = lax.broadcasted_iota(jnp.int32, (rows, rows), 1)
    reach = jnp.where(has_behind, 0, -1)
    return jnp.concatenate(
        [(first == seg_column) & (key >= rows * -reach), (own == seg_column) & (key <= query)],
        axis=1,
    )


def head_probs(query, keys, allowed):
    scores = mul(query, keys, LAST) * (1.0 / math.sqrt(HEAD_SIZE))
    scores = jnp.where(allowed, scores, masked_score)
    powers = jnp.exp(scores - jnp.max(scores, axis=-1, keepdims=True))
    return powers / jnp.sum(powers, axis=-1, keepdims=True)


def forward_kernel(layer, layers_n, number, *refs):
    first = layer == 0
    refs = list(refs)

    def some(count):
        taken = refs[:count]
        del refs[:count]
        return taken

    stream, cosine, sine, seg_column = some(4)
    if first:
        small, ranks, w_qkv, w_out, out_grad = some(5)
    else:
        table, rk, hit, seats, turned, cross_from, qkv_from, out_from = some(8)
    w_gate, w_up, w_down = some(3)
    new_stream, layer_out, normed_a, queries, kv_out, attended, mixed, normed_b = some(8)
    rows_out, gate_out, up_out, gate_seat, quad = some(5)
    if first:
        table, rk_out, hit, seats, turned, qkv_out, out_out, qkv_next, out_next = some(9)
        (line_grads,) = some(1)
        small_land, rk, seat_all = some(3)
    else:
        (cross_to,) = some(1)
    (
        qkv,
        w_o,
        kv,
        projected,
        tokens,
        gates,
        weighted,
        gate_w,
        up_w,
        down_w,
        weight_sem,
        load_sem,
        chain_sem,
        quad_sem,
        send,
        recv,
        rows_in,
        gate_pre,
        up_pre,
        leave_sem,
    ) = some(20)
    if first:
        send_0, recv_0, send_1, recv_1, send_2, recv_2, send_3, recv_3 = some(8)
        send_4, recv_4, keep = some(3)
    else:
        cross_send, cross_recv, cross_keep = some(3)
    scratch = refs
    z, near = place()
    e = near["own"]
    line = lax.axis_size(DP)
    local_n = seats.shape[2]
    rows = stream.shape[0]
    experts_n = hit.shape[2]
    behind, ahead, has_behind, has_ahead = chain(z, e)

    weights = [
        pltpu.make_async_copy(src.at[layer], dst, weight_sem.at[i])
        for i, (src, dst) in enumerate(((w_gate, gate_w), (w_up, up_w), (w_down, down_w)))
    ]
    order = (behind, ahead, has_behind, has_ahead)
    greet(z, near, ("x", "y", "c"), line if first else None, order)
    if not first:
        cross = Gather([cross_from.at[0]], [cross_to], cross_send, cross_recv, z, near, line)
        cross.spread(1, cross_from, cross_keep)
    if first:
        g0 = Gather([small, ranks], [small_land, rk], send_0, recv_0, z, near, line)
        g1 = Gather([w_qkv.at[0]], [qkv], send_1, recv_1, z, near, line)
        g2 = Gather([w_out.at[0]], [w_o], send_2, recv_2, z, near, line)
        g3 = Gather(
            [w_qkv.at[1], w_out.at[1]], [qkv_next, out_next], send_3, recv_3, z, near, line
        )
        g4 = Gather([out_grad], [line_grads], send_4, recv_4, z, near, line, flat=True)
        local = [
            pltpu.make_async_copy(one, g.outs[i].at[z, e], keep.at[k])
            for k, (g, i, one) in enumerate(
                (g, i, one) for g in (g0, g1, g2, g3) for i, one in enumerate(g.ins)
            )
        ]
        g0.line_first()
        g0.first(z, g0.ins)
        g1.line_first()
        g1.first(z, g1.ins)
        for one in local:
            one.start()
        g0.arrivals(1, g0.take)
        g0.second(z)
        g0.arrivals(2, g0.take)
        g0.third(z)
        g0.arrivals(1, g0.second)
        g0.arrivals(3, g0.take)
        g1.arrivals(1, g1.take)
        g2.line_first()
        g2.first(z, g2.ins)
        g0.arrivals(1, g0.third)
        g0.arrivals(2, g0.second)
        g1.second(z)
        g0.arrivals(2, g0.third)
        g0.arrivals(3, g0.second)
        g1.arrivals(2, g1.take)
        g0.arrivals(3, g0.third)
        g0.finish(z)
        for step in range(1, line):
            g0.arrivals(step, g0.finish)
        local[0].wait()
        local[1].wait()
        table[...] = jnp.transpose(small_land[...].reshape(-1, 128).astype(f32))
        g1.third(z)
        g1.arrivals(1, g1.second)
        for g in range(line):
            before = jnp.zeros((layers_n * experts_n, 1), f32)
            for d in range(8):
                lanes = pl.ds(d * rows, rows)
                rank = rk[g, d, pl.ds(0, layers_n * experts_n), :].astype(f32)
                seat_all[g, :, lanes] = jnp.where(rank > 0, rank + before, 0.0)
                for l in range(layers_n):
                    hit[l, g, :, lanes] = rank[l * experts_n : (l + 1) * experts_n]
                here = jnp.where(rank > 0, 1.0, 0.0)
                before = before + jnp.sum(here, axis=1, keepdims=True)
            for l in range(layers_n):
                for k in range(local_n):
                    row = pl.ds(l * experts_n + e * local_n + k, 1)
                    seats[l, g, pl.ds(k, 1), :] = seat_all[g, row, :]
        g1.arrivals(3, g1.take)
        wide = jnp.zeros((rows - layers_n * local_n, rows), f32)
        for d in range(8):
            lanes = pl.ds(d * rows, rows)
            mine = [seats[l, z, :, lanes] for l in range(layers_n)]
            turned[lanes, :] = jnp.transpose(jnp.concatenate(mine + [wide], axis=0))
        rk_out[...] = rk[...]
        g1.arrivals(1, g1.third)
        g1.arrivals(2, g1.second)
        g2.arrivals(1, g2.take)
        g1.arrivals(2, g1.third)
        g1.arrivals(3, g1.second)
        g2.second(z)
        g2.arrivals(2, g2.take)
        g1.arrivals(3, g1.third)
        g2.third(z)
        g1.finish(z)
        for step in range(1, line):
            g1.arrivals(step, g1.finish)
        local[2].wait()
        g2.arrivals(1, g2.second)
        g2.arrivals(3, g2.take)
    else:
        loads = [
            pltpu.make_async_copy(qkv_from, qkv, load_sem.at[0]),
            pltpu.make_async_copy(out_from, w_o, load_sem.at[1]),
        ]
        for one in loads:
            one.start()
    for one in weights:
        one.start()
    gain = 2 * experts_n + 2 * layer
    x = stream[...].astype(f32)
    normed_a[...] = normalized(x, table[pl.ds(gain, 1), :]).astype(bf16)
    if not first:
        loads[0].wait()
    width = queries.shape[1]
    projected[...] = mul(normed_a[...], qkv[...].reshape(width, -1))
    keys_n = KEY_VALUE_HEADS * HEAD_SIZE
    cos, sin = cosine[...], sine[...]
    for h in range(KEY_VALUE_HEADS):
        key = turn(projected[:, head_of(QUERY_HEADS + h)], cos, sin)
        kv[1, :, head_of(h)] = key.astype(bf16)
    kv[1, :, pl.ds(keys_n, keys_n)] = projected[:, pl.ds(width + keys_n, keys_n)].astype(bf16)

    def pass_on(target):
        return pltpu.make_async_remote_copy(
            src_ref=kv.at[1],
            dst_ref=kv.at[0],
            send_sem=chain_sem.at[0],
            recv_sem=chain_sem.at[1],
            device_id={DP: target[0], EX: target[1]},
            device_id_type=MESH,
        )

    @pl.when(has_ahead)
    def pass_ahead():
        pass_on(ahead).start()

    if first:
        g2.arrivals(1, g2.third)
        g2.arrivals(2, g2.second)
        g3.line_first()
        g3.first(z, g3.ins)
    else:
        cross.spread(2, cross_from, cross_keep)
    for h in range(QUERY_HEADS):
        queries[:, head_of(h)] = turn(projected[:, head_of(h)], cos, sin).astype(bf16)
    allowed = allowed_keys(rk, layers_n * experts_n, z, e, behind, has_behind, seg_column[...])

    @pl.when(has_behind)
    def from_behind_here():
        pass_on(behind).wait_recv()

    @pl.when(jnp.logical_not(has_behind))
    def nobody_behind():
        kv[0] = jnp.zeros_like(kv[0])

    for h in range(QUERY_HEADS):
        group = h // (QUERY_HEADS // KEY_VALUE_HEADS)
        keys = kv[:, :, head_of(group)].reshape(2 * rows, HEAD_SIZE)
        values = kv[:, :, head_of(KEY_VALUE_HEADS + group)].reshape(2 * rows, HEAD_SIZE)
        probs = head_probs(queries[:, head_of(h)], keys, allowed).astype(bf16)
        attended[:, head_of(h)] = mul(probs, values).astype(bf16)
        if first and h == 3:
            g2.arrivals(2, g2.third)
            g2.arrivals(3, g2.second)
        if first and h == 7:
            g2.arrivals(3, g2.third)
            g3.arrivals(1, g3.take)
            g4.line_first()
        if not first and h == 8:
            cross.second(cross.plane_of(1))
    kv_out[...] = kv[...]
    if first:
        g2.finish(z)
        for step in range(1, line):
            g2.arrivals(step, g2.finish)
        local[3].wait()
    else:
        loads[1].wait()
    mixed[...] = x + mul(attended[...], w_o[...].reshape(width, -1))
    normed_b[...] = normalized(mixed[...], table[pl.ds(gain + 1, 1), :]).astype(bf16)

    one, two, three, four = plane_gather(normed_b, tokens, send, recv, near)
    one()
    if first:
        g3.second(z)
        g3.arrivals(2, g3.take)
    two()
    three()
    if not first:
        cross.second(cross.plane_of(2))
        cross.spread(3, cross_from, cross_keep)
        cross.third(cross.plane_of(1))
    if first:
        g3.third(z)
        g3.arrivals(1, g3.second)
        g3.arrivals(3, g3.take)
    four()
    quads = [
        pltpu.make_async_copy(tokens.at[near[name]], quad.at[i], quad_sem.at[i])
        for i, name in enumerate(QUAD)
    ]
    for copied in quads:
        copied.start()
    everyone = tokens[...].reshape(-1, width)
    router = table[pl.ds(layer * experts_n, experts_n), :].astype(bf16)
    gates[...] = masked_gates(mul(router, everyone, LAST), hit[layer, z] > 0)
    pick = seat_rows(seats[layer, z], number)
    for k in range(local_n):
        here = pl.ds(k * number, number)
        mine = gates[pl.ds(e * local_n + k, 1), :]
        gate_seat[here] = jnp.sum(
            pick[k * number : (k + 1) * number].astype(f32) * mine, axis=1, keepdims=True
        )
    rows_in[...] = mul(pick, everyone).astype(bf16)
    for copied in weights:
        copied.wait()
    if first:
        g3.arrivals(1, g3.third)
        g3.arrivals(2, g3.second)
        g4.arrivals(1, g4.carry)
    def expert(k, carry):
        here = pl.ds(pl.multiple_of(k * number, 32), number)
        x = rows_in[here]
        gate = mul(x, gate_w[k])
        up = mul(x, up_w[k])
        gate_pre[here] = gate
        up_pre[here] = up
        hidden = (gate * (1.0 / (1.0 + jnp.exp(-gate))) * up).astype(bf16)
        weighted[here] = (mul(hidden, down_w[k]) * gate_seat[here]).astype(bf16)
        return carry

    lax.fori_loop(0, local_n, expert, 0)
    leaving = [
        pltpu.make_async_copy(src, dst, leave_sem.at[i])
        for i, (src, dst) in enumerate(((rows_in, rows_out), (gate_pre, gate_out), (up_pre, up_out)))
    ]
    for copied in leaving:
        copied.start()
    if first:
        g3.arrivals(2, g3.third)
        g3.arrivals(3, g3.second)
        g4.arrivals(2, g4.carry)
        out_copies = [
            pltpu.make_async_copy(qkv, qkv_out, load_sem.at[0]),
            pltpu.make_async_copy(w_o, out_out, load_sem.at[1]),
        ]
        for copied in out_copies:
            copied.start()
    else:
        cross.third(cross.plane_of(2))
        cross.second(cross.plane_of(3))

    def make(name):
        d = near[name]
        lanes = pl.ds(pl.multiple_of(d * rows, rows), rows)
        mine = turned[lanes, pl.ds(layer * local_n, local_n)]
        scratch[0][d] = mul(seat_columns(mine, number), weighted[...]).astype(bf16)

    plane_sum(make, new_stream, mixed, scratch, near)
    layer_out[...] = new_stream[...].astype(bf16)

    for copied in quads + leaving:
        copied.wait()

    @pl.when(has_ahead)
    def passed_on():
        pass_on(ahead).wait_send()

    if first:
        g3.arrivals(3, g3.third)
        g4.arrivals(3, g4.carry)
        g3.finish(z)
        for step in range(1, line):
            g3.arrivals(step, g3.finish)
        for copied in local[4:] + out_copies:
            copied.wait()
        for g in (g0, g1, g2, g3, g4):
            g.line_done()
    else:
        cross.third(cross.plane_of(3))
        cross.spread_done(cross_from, cross_keep)


def layer_forward(layer, number, shapes, stream, tables, given, weights):
    layers_n, n_dp, n_expert, local_n, capacity = shapes
    first = layer == 0
    rows, width = stream.shape
    hidden = weights[0].shape[3]
    experts_n = local_n * n_expert
    seats_n = local_n * capacity
    keys_n = KEY_VALUE_HEADS * HEAD_SIZE
    group = n_expert * rows
    cut_rows = width // (n_dp * n_expert)
    shape = jax.ShapeDtypeStruct
    outs = [
        shape((rows, width), f32),
        shape((rows, width), bf16),
        shape((rows, width), bf16),
        shape((rows, width), bf16),
        shape((2, rows, 2 * keys_n), bf16),
        shape((rows, width), bf16),
        shape((rows, width), f32),
        shape((rows, width), bf16),
        shape((seats_n, width), bf16),
        shape((seats_n, hidden), f32),
        shape((seats_n, hidden), f32),
        shape((seats_n, 1), f32),
        shape((len(QUAD), rows, width), bf16),
    ]
    specs = [VMEM] * 8 + [HBM] * 3 + [VMEM, HBM]
    scratch = []
    full_qkv = (n_dp, n_expert, cut_rows, width + 2 * keys_n)
    full_out = (n_dp, n_expert, cut_rows, width)
    if first:
        rank_rows = given[1].shape[0]
        outs += [
            shape((128, width), f32),
            shape((n_dp, n_expert, rank_rows, rows), jnp.int32),
            shape((layers_n, n_dp, experts_n, group), f32),
            shape((layers_n, n_dp, local_n, group), f32),
            shape((group, 128), f32),
        ]
        outs += [shape(full_qkv, bf16), shape(full_out, bf16)] * 2
        outs.append(shape((n_dp, rows, width), bf16))
        specs += [VMEM] * 5 + [HBM] * 5
        scratch += [
            pltpu.VMEM((n_dp, n_expert, cut_rows, 128), bf16),
            pltpu.VMEM((n_dp, n_expert, rank_rows, rows), jnp.int32),
            pltpu.VMEM((n_dp, layers_n * experts_n, group), f32),
        ]
    else:
        outs.append(shape((n_dp, n_expert, rows, width), bf16))
        specs.append(HBM)
    scratch += [
        pltpu.VMEM(full_qkv, bf16),
        pltpu.VMEM(full_out, bf16),
        pltpu.VMEM((2, rows, 2 * keys_n), bf16),
        pltpu.VMEM((rows, width + 2 * keys_n), f32),
        pltpu.VMEM((n_expert, rows, width), bf16),
        pltpu.VMEM((experts_n, group), f32),
        pltpu.VMEM((seats_n, width), bf16),
        pltpu.VMEM((local_n, width, hidden), bf16),
        pltpu.VMEM((local_n, width, hidden), bf16),
        pltpu.VMEM((local_n, hidden, width), bf16),
        pltpu.SemaphoreType.DMA((3,)),
        pltpu.SemaphoreType.DMA((2,)),
        pltpu.SemaphoreType.DMA((2,)),
        pltpu.SemaphoreType.DMA((len(QUAD),)),
        pltpu.SemaphoreType.DMA((8,)),
        pltpu.SemaphoreType.DMA((8,)),
        pltpu.VMEM((seats_n, width), bf16),
        pltpu.VMEM((seats_n, hidden), f32),
        pltpu.VMEM((seats_n, hidden), f32),
        pltpu.SemaphoreType.DMA((3,)),
    ]
    if first:
        for count in (2, 1, 1, 2, 1):
            scratch += [pltpu.SemaphoreType.DMA((count, n_dp, KINDS)) for i in range(2)]
        scratch.append(pltpu.SemaphoreType.DMA((6,)))
    else:
        scratch += [pltpu.SemaphoreType.DMA((1, n_dp, KINDS)) for i in range(2)]
        scratch.append(pltpu.SemaphoreType.DMA((n_dp,)))
    given_specs = [HBM] * 5 if first else [VMEM] * 5 + [HBM] * 3
    return pl.pallas_call(
        partial(forward_kernel, layer, layers_n, capacity),
        out_shape=outs,
        in_specs=[VMEM] * 4 + given_specs + [HBM] * 3,
        out_specs=specs,
        scratch_shapes=scratch + sum_scratch(rows, width),
        compiler_params=settings(number),
        name="layer_forward",
    )(stream, *tables, *given, *weights)


def norm_back(value, gain, grad):
    scale = lax.rsqrt(jnp.mean(value * value, axis=-1, keepdims=True) + epsilon)
    unit = value * scale
    inner = grad * gain
    back = scale * (inner - unit * jnp.mean(inner * unit, axis=-1, keepdims=True))
    return back, jnp.sum(grad * unit, axis=0, keepdims=True)


def backward_kernel(layer, layers_n, number, *refs):
    refs = list(refs)

    def some(count):
        taken = refs[:count]
        del refs[:count]
        return taken

    grad_stream, stream, cosine, sine, seg_column = some(5)
    mixed, normed_b, queries, kv, gate_seat = some(5)
    table, rk, hit, seats, turned = some(5)
    row_sources = some(2)
    qkv_from, out_from, w_gate, w_up, w_down = some(5)
    gate_from, up_from = some(2)
    grad_out, grad_low, *leaving_to = some(6)
    dprojected, grad_attn, small = some(3)
    row_lands = some(2)
    (
        summed,
        qkv,
        w_o,
        datt,
        dkv,
        dkv_send,
        dkv_got,
        all_probs,
        tokens,
        back_rows,
        gate_w,
        up_w,
        down_w,
        weight_sem,
        load_sem,
        chain_sem,
        send,
        recv,
        row_send,
        row_recv,
        row_keep,
        gate_pre,
        up_pre,
        rows_grad,
        hidden_low,
        dgate_low,
        dup_low,
        leave_sem,
    ) = some(28)
    scratch = refs
    z, near = place()
    e = near["own"]
    line = lax.axis_size(DP)
    local_n = seats.shape[2]
    rows, width = stream.shape
    experts_n = hit.shape[2]
    behind, ahead, has_behind, has_ahead = chain(z, e)
    weights = [
        pltpu.make_async_copy(src.at[layer], dst, weight_sem.at[i])
        for i, (src, dst) in enumerate(((w_gate, gate_w), (w_up, up_w), (w_down, down_w)))
    ]
    loads = [
        pltpu.make_async_copy(qkv_from, qkv, load_sem.at[0]),
        pltpu.make_async_copy(out_from, w_o, load_sem.at[1]),
    ]
    weights += [
        pltpu.make_async_copy(gate_from, gate_pre, leave_sem.at[4]),
        pltpu.make_async_copy(up_from, up_pre, leave_sem.at[5]),
    ]
    grad_low[...] = grad_stream[...].astype(bf16)
    greet(z, near, ("x", "y", "c"), None, (behind, ahead, has_behind, has_ahead))

    spreads = [
        Gather([src], [dst], row_send.at[i], row_recv.at[i], 0, near, None)
        for i, (src, dst) in enumerate(zip(row_sources, row_lands))
    ]
    kept = [
        pltpu.make_async_copy(src, dst.at[0, e], row_keep.at[i])
        for i, (src, dst) in enumerate(zip(row_sources, row_lands))
    ]

    first, second, third, finish = plane_gather(grad_low, tokens, send, recv, near)
    first()
    for one in weights + loads:
        one.start()
    allowed = allowed_keys(rk, layers_n * experts_n, z, e, behind, has_behind, seg_column[...])
    per_group = QUERY_HEADS // KEY_VALUE_HEADS

    def keys_of(group):
        return kv[:, :, head_of(group)].reshape(2 * rows, HEAD_SIZE)

    def prepare(heads):
        for h in heads:
            all_probs[h] = head_probs(queries[:, head_of(h)], keys_of(h // per_group), allowed)

    prepare(range(0, 5))
    second()
    prepare(range(5, 9))
    third()
    spreads[0].first(0, spreads[0].ins)
    spreads[1].first(0, spreads[1].ins)
    for one in kept:
        one.start()
    prepare(range(9, QUERY_HEADS))
    finish()
    everyone = tokens[...].reshape(-1, width)
    picked = mul(seat_rows(seats[layer, z], number), everyone)
    back_rows[:, pl.ds(0, width)] = picked.astype(bf16)
    rows_grad[...] = (picked * gate_seat[...]).astype(bf16)
    for one in weights:
        one.wait()

    def expert(k, carry):
        here = pl.ds(pl.multiple_of(k * number, 32), number)
        gate, up = gate_pre[here], up_pre[here]
        raw = mul(back_rows[here, pl.ds(0, width)], down_w[k], LAST)
        sigmoid = 1.0 / (1.0 + jnp.exp(-gate))
        silu = gate * sigmoid
        hidden = (silu * up).astype(bf16)
        hidden_low[here] = hidden
        dgate_seat = jnp.sum(hidden.astype(f32) * raw, axis=1, keepdims=True)
        raw = raw * gate_seat[here]
        dgate = (raw * up * sigmoid * (1.0 + gate * (1.0 - sigmoid))).astype(bf16)
        dup = (raw * silu).astype(bf16)
        dgate_low[here] = dgate
        dup_low[here] = dup
        back_rows[here, pl.ds(0, width)] = (
            mul(dgate, gate_w[k], LAST) + mul(dup, up_w[k], LAST)
        ).astype(bf16)
        high = dgate_seat.astype(bf16).astype(f32)
        lane = lax.broadcasted_iota(jnp.int32, (number, 128), 1)
        mine = e * local_n + k
        back_rows[here, pl.ds(width, 128)] = jnp.where(
            lane == mine, high, jnp.where(lane == experts_n + mine, dgate_seat - high, 0.0)
        ).astype(bf16)
        return carry

    lax.fori_loop(0, local_n, expert, 0)
    leaving = [
        pltpu.make_async_copy(src, dst, leave_sem.at[i])
        for i, (src, dst) in enumerate(zip((rows_grad, hidden_low, dgate_low, dup_low), leaving_to))
    ]
    for one in leaving:
        one.start()

    def make(name):
        d = near[name]
        lanes = pl.ds(pl.multiple_of(d * rows, rows), rows)
        mine = turned[lanes, pl.ds(layer * local_n, local_n)]
        scratch[0][d] = mul(seat_columns(mine, number), back_rows[...]).astype(bf16)

    spreads[0].second(0)
    plane_sum(make, summed, None, scratch, near)
    spreads[0].third(0)
    spreads[1].second(0)

    over = ((0,), (0,))
    gain = 2 * experts_n + 2 * layer
    router = table[pl.ds(layer * experts_n, experts_n), :].astype(bf16)
    own_lanes = pl.ds(pl.multiple_of(e * rows, rows), rows)
    gates = masked_gates(mul(router, normed_b[...], LAST), hit[layer, z, :, own_lanes] > 0)
    turned_sum = jnp.transpose(summed[:, pl.ds(width, 128)])
    dgates = turned_sum[:experts_n] + turned_sum[experts_n : 2 * experts_n]
    inner = jnp.sum(gates * dgates, axis=0, keepdims=True)
    dlogits = (gates * (dgates - inner)).astype(bf16)
    small[...] = jnp.zeros_like(small)
    small[pl.ds(0, experts_n)] = mul(dlogits, normed_b[...])
    dnormed = summed[:, pl.ds(0, width)] + mul(dlogits, router, over)
    back, dgain = norm_back(mixed[...], table[pl.ds(gain + 1, 1), :], dnormed)
    small[pl.ds(experts_n + 1, 1)] = dgain
    dmixed = grad_stream[...].astype(f32) + back
    grad_out[...] = dmixed
    grad_attn[...] = dmixed.astype(bf16)

    loads[1].wait()
    datt[...] = mul(grad_attn[...], w_o[...].reshape(width, -1), LAST).astype(bf16)
    cos, sin = cosine[...], sine[...]
    scale = 1.0 / math.sqrt(HEAD_SIZE)
    for group in range(KEY_VALUE_HEADS):
        keys = keys_of(group)
        values = keys_of(KEY_VALUE_HEADS + group)
        dkeys = jnp.zeros((2 * rows, HEAD_SIZE), f32)
        dvalues = jnp.zeros((2 * rows, HEAD_SIZE), f32)
        for h in range(group * per_group, (group + 1) * per_group):
            query = queries[:, head_of(h)]
            probs = all_probs[h]
            given = datt[:, head_of(h)]
            dprobs = mul(given, values, LAST)
            delta = jnp.sum(probs * dprobs, axis=-1, keepdims=True)
            dscores = (probs * (dprobs - delta)).astype(bf16)
            dquery = mul(dscores, keys) * scale
            dprojected[:, head_of(h)] = turn(dquery, cos, -sin).astype(bf16)
            dkeys = dkeys + mul(dscores, query, over)
            dvalues = dvalues + mul(probs.astype(bf16), given, over)
        if group == 0:
            spreads[1].third(0)
        dkv[:, head_of(group)] = dkeys * scale
        dkv[:, head_of(KEY_VALUE_HEADS + group)] = dvalues
    dkv_send[...] = dkv[pl.ds(0, rows)].astype(bf16)

    def pass_on(target):
        return pltpu.make_async_remote_copy(
            src_ref=dkv_send,
            dst_ref=dkv_got,
            send_sem=chain_sem.at[0],
            recv_sem=chain_sem.at[1],
            device_id={DP: target[0], EX: target[1]},
            device_id_type=MESH,
        )

    @pl.when(has_behind)
    def pass_back():
        pass_on(behind).start()

    loads[0].wait()
    query_part = pl.ds(0, width)
    key_part = pl.ds(width, dkv.shape[1])
    weights_q = qkv[:, :, :, query_part].reshape(-1, width)
    dnormed = mul(dprojected[:, query_part], weights_q, LAST)

    @pl.when(has_ahead)
    def from_ahead_here():
        pass_on(ahead).wait_recv()
        dkv[pl.ds(rows, rows)] += dkv_got[...].astype(f32)

    for h in range(KEY_VALUE_HEADS):
        dkey = turn(dkv[pl.ds(rows, rows), head_of(h)], cos, -sin)
        dprojected[:, head_of(QUERY_HEADS + h)] = dkey.astype(bf16)
        dvalue = dkv[pl.ds(rows, rows), head_of(KEY_VALUE_HEADS + h)]
        dprojected[:, head_of(QUERY_HEADS + KEY_VALUE_HEADS + h)] = dvalue.astype(bf16)
    weights_kv = qkv[:, :, :, key_part].reshape(-1, dkv.shape[1])
    dnormed = dnormed + mul(dprojected[:, key_part], weights_kv, LAST)
    back, dgain = norm_back(stream[...].astype(f32), table[pl.ds(gain, 1), :], dnormed)
    small[pl.ds(experts_n, 1)] = dgain
    grad_out[...] += back

    @pl.when(has_behind)
    def passed_back():
        pass_on(behind).wait_send()

    for one in leaving:
        one.wait()

    for i in range(2):
        spreads[i].finish(0)
        kept[i].wait()


def layer_backward(layer, number, shapes, grads, stream, tables, saved, plan, weights):
    layers_n, n_dp, n_expert, local_n, capacity = shapes
    rows, width = stream.shape
    hidden = weights[-1].shape[1]
    experts_n = local_n * n_expert
    seats_n = local_n * capacity
    keys_n = KEY_VALUE_HEADS * HEAD_SIZE
    cut_rows = width // (n_dp * n_expert)
    shape = jax.ShapeDtypeStruct
    outs = [
        shape((rows, width), f32),
        shape((rows, width), bf16),
        shape((seats_n, width), bf16),
        shape((seats_n, hidden), bf16),
        shape((seats_n, hidden), bf16),
        shape((seats_n, hidden), bf16),
        shape((rows, width + 2 * keys_n), bf16),
        shape((rows, width), bf16),
        shape((SMALL, width), f32),
        shape((1, n_expert, rows, width), bf16),
        shape((1, n_expert, rows, width), bf16),
    ]
    scratch = [
        pltpu.VMEM((rows, width + 128), f32),
        pltpu.VMEM((n_dp, n_expert, cut_rows, width + 2 * keys_n), bf16),
        pltpu.VMEM((n_dp, n_expert, cut_rows, width), bf16),
        pltpu.VMEM((rows, width), bf16),
        pltpu.VMEM((2 * rows, 2 * keys_n), f32),
        pltpu.VMEM((rows, 2 * keys_n), bf16),
        pltpu.VMEM((rows, 2 * keys_n), bf16),
        pltpu.VMEM((QUERY_HEADS, rows, 2 * rows), f32),
        pltpu.VMEM((n_expert, rows, width), bf16),
        pltpu.VMEM((seats_n, width + 128), bf16),
        pltpu.VMEM((local_n, width, hidden), bf16),
        pltpu.VMEM((local_n, width, hidden), bf16),
        pltpu.VMEM((local_n, hidden, width), bf16),
        pltpu.SemaphoreType.DMA((3,)),
        pltpu.SemaphoreType.DMA((2,)),
        pltpu.SemaphoreType.DMA((2,)),
        pltpu.SemaphoreType.DMA((8,)),
        pltpu.SemaphoreType.DMA((8,)),
        pltpu.SemaphoreType.DMA((2, 1, 1, KINDS)),
        pltpu.SemaphoreType.DMA((2, 1, 1, KINDS)),
        pltpu.SemaphoreType.DMA((2,)),
        pltpu.VMEM((seats_n, hidden), f32),
        pltpu.VMEM((seats_n, hidden), f32),
        pltpu.VMEM((seats_n, width), bf16),
        pltpu.VMEM((seats_n, hidden), bf16),
        pltpu.VMEM((seats_n, hidden), bf16),
        pltpu.VMEM((seats_n, hidden), bf16),
        pltpu.SemaphoreType.DMA((6,)),
    ]
    return pl.pallas_call(
        partial(backward_kernel, layer, layers_n, capacity),
        out_shape=outs,
        in_specs=[VMEM] * 15 + [HBM] * 9,
        out_specs=[VMEM] * 2 + [HBM] * 4 + [VMEM] * 3 + [HBM] * 2,
        scratch_shapes=scratch + sum_scratch(rows, width + 128),
        compiler_params=settings(number),
        name="layer_backward",
    )(grads, stream, *tables, *saved, *plan, *weights)


class Sums:
    def __init__(self, ins, outs, held, send, recv, keep, z, near, line):
        self.ins, self.outs, self.held = ins, outs, held
        self.send, self.recv, self.keep = send, recv, keep
        self.z, self.near, self.line = z, near, line
        self.all = range(len(ins))

    def split(self, a):
        half = self.outs[a].shape[1] // 2
        return pl.ds(0, half), pl.ds(half, half)

    def move(self, a, j, name):
        part = self.ins[a]
        fromx, fromy, late, later, total, got = self.held[a]
        A, B = self.split(a)
        near = self.near
        kind, src, dst, to = {
            "xd": lambda: (0, part.at[j, near["d"], :, A], fromx.at[j, 0], "x"),
            "xx": lambda: (1, part.at[j, near["x"], :, A], fromx.at[j, 1], "x"),
            "yd": lambda: (2, part.at[j, near["d"], :, B], fromy.at[j, 0], "y"),
            "yy": lambda: (3, part.at[j, near["y"], :, B], fromy.at[j, 1], "y"),
            "ly": lambda: (4, late.at[j, 0], later.at[j, 0], "y"),
            "lx": lambda: (5, late.at[j, 1], later.at[j, 1], "x"),
            "up": lambda: (6, total.at[j], got.at[j], self.z + 1),
            "down": lambda: (7, total.at[j], got.at[j], self.z - 1),
        }[name]()
        if name == "down":
            slot = jnp.where(j == self.z - 1, self.line, j)
            dst = got.at[slot]
        return pltpu.make_async_remote_copy(
            src_ref=src,
            dst_ref=dst,
            send_sem=self.send.at[a, j, kind],
            recv_sem=self.recv.at[a, j, kind],
            device_id={DP: to} if kind >= 6 else {EX: near[to]},
            device_id_type=MESH,
        )

    def own_down(self, a):
        got = self.held[a][5]
        return pltpu.make_async_remote_copy(
            src_ref=got.at[self.line],
            dst_ref=got.at[self.line],
            send_sem=self.send.at[a, self.z, 7],
            recv_sem=self.recv.at[a, self.z, 7],
            device_id={DP: self.z},
            device_id_type=MESH,
        )

    def prepare(self, a, j):
        late, total = self.held[a][2], self.held[a][4]
        A, B = self.split(a)
        near, part = self.near, self.ins[a]
        return [
            pltpu.make_async_copy(src, dst, self.keep.at[a, j, i])
            for i, (src, dst) in enumerate(
                (
                    (part.at[j, near["y"], :, A], late.at[j, 0]),
                    (part.at[j, near["x"], :, B], late.at[j, 1]),
                    (part.at[j, near["own"]], total.at[j]),
                )
            )
        ]

    def at(self, step, act):
        if step == 0:
            act(self.z, 0)
            return

        @pl.when(self.z + step <= self.line - 1)
        def above():
            act(self.z + step, 1)

        @pl.when(self.z - step >= 0)
        def below():
            act(self.z - step, -1)

    def first(self, j, way):
        for a in self.all:
            for name in ("xd", "yd", "xx", "yy"):
                self.move(a, j, name).start()
            for one in self.prepare(a, j):
                one.start()

    def second(self, j, way):
        for a in self.all:
            fromx, fromy, late = self.held[a][:3]
            ready = self.prepare(a, j)
            ready[0].wait()
            self.move(a, j, "xd").wait_recv()
            late[j, 0] = (late[j, 0].astype(f32) + fromx[j, 0].astype(f32)).astype(bf16)
            self.move(a, j, "ly").start()
            ready[1].wait()
            self.move(a, j, "yd").wait_recv()
            late[j, 1] = (late[j, 1].astype(f32) + fromy[j, 0].astype(f32)).astype(bf16)
            self.move(a, j, "lx").start()

    def third(self, j, way):
        for a in self.all:
            fromx, fromy, late, later, total, got = self.held[a]
            for name in ("xx", "yy", "ly", "lx"):
                self.move(a, j, name).wait_recv()
            self.prepare(a, j)[2].wait()
            for side, (columns, here) in enumerate(zip(self.split(a), (fromx, fromy))):
                value = (
                    total[j, :, columns].astype(f32)
                    + here[j, 1].astype(f32)
                    + later[j, side].astype(f32)
                )
                if way == 0:
                    self.outs[a][:, columns] = value
                else:
                    total[j, :, columns] = value.astype(bf16)
            if way == 1:

                @pl.when(self.z > 0)
                def more_up():
                    self.move(a, j, "up").wait_recv()
                    total[j] = (total[j].astype(f32) + got[j].astype(f32)).astype(bf16)

                self.move(a, j, "up").start()
            elif way == -1:

                @pl.when(self.z < self.line - 1)
                def more_down():
                    self.move(a, j, "down").wait_recv()
                    total[j] = (total[j].astype(f32) + got[j].astype(f32)).astype(bf16)

                self.move(a, j, "down").start()
            else:

                @pl.when(self.z > 0)
                def end_up():
                    self.move(a, j, "up").wait_recv()
                    self.outs[a][...] += got[j].astype(f32)

                @pl.when(self.z < self.line - 1)
                def end_down():
                    self.own_down(a).wait_recv()
                    self.outs[a][...] += got[self.line].astype(f32)

    def finish(self, j, way):
        for a in self.all:
            for name in ("xd", "yd", "xx", "yy", "lx", "ly"):
                self.move(a, j, name).wait_send()
            if way == 1:
                self.move(a, j, "up").wait_send()
            elif way == -1:
                self.move(a, j, "down").wait_send()


def sums_scratch(shapes, line):
    scratch = []
    for rows, columns in shapes:
        half = columns // 2
        scratch += [pltpu.VMEM((line, 2, rows, half), bf16) for i in range(4)]
        scratch += [
            pltpu.VMEM((line, rows, columns), bf16),
            pltpu.VMEM((line + 1, rows, columns), bf16),
        ]
    return scratch + [
        pltpu.SemaphoreType.DMA((len(shapes), line, 8)),
        pltpu.SemaphoreType.DMA((len(shapes), line, 8)),
        pltpu.SemaphoreType.DMA((len(shapes), line, 3)),
    ]


def from_behind(value, axis, steps):
    count = lax.axis_size(axis)
    leading, last = (max(0, -steps), min(count, count - steps))
    return lax.ppermute(value, axis, [(source, source + steps) for source in range(leading, last)])


def from_sibling(value):
    count = lax.axis_size(EX)
    return lax.ppermute(value, EX, [(s, s + 1 - 2 * (s % 2)) for s in range(count)])


def rms_norm(stream, gain_row):
    return (
        stream * lax.rsqrt(jnp.mean(stream * stream, axis=-1, keepdims=True) + epsilon) * gain_row
    )


def rotary_tables(token_positions):
    half_dim = HEAD_SIZE // 2
    steps_up = jnp.arange(half_dim).astype(f32)
    frequency = jnp.exp(steps_up * (-2.0 * math.log(rope_base) / HEAD_SIZE))
    angles = token_positions.astype(f32)[:, None] * frequency[None, :]
    return jnp.cos(angles)[:, None, :], jnp.sin(angles)[:, None, :]


def apply_rotary(heads_in, cosine, sine_part):
    half_dim = heads_in.shape[-1] // 2
    first_half = heads_in[..., :half_dim]
    second_half = heads_in[..., half_dim:]
    return jnp.concatenate(
        [
            first_half * cosine - second_half * sine_part,
            second_half * cosine + first_half * sine_part,
        ],
        axis=-1,
    )


def gated_unit(gate_pre, up_pre):
    return jax.nn.silu(gate_pre) * up_pre


def masked_scores(query_rows, gathered_keys, allowed):
    token_rows = query_rows.shape[0]
    grouped_queries = query_rows.reshape(
        token_rows, KEY_VALUE_HEADS, QUERY_HEADS // KEY_VALUE_HEADS, HEAD_SIZE
    )
    score_scale = 1.0 / math.sqrt(HEAD_SIZE)
    scores = (
        jnp.einsum(
            "tkgd,skd->kgts", grouped_queries, gathered_keys, preferred_element_type=f32
        )
        * score_scale
    )
    return (jnp.where(allowed, scores, masked_score), grouped_queries)


def rank_table(routes, pair_order, experts_n):
    layers_n, token_rows, topk_n = routes.shape
    chosen = jnp.swapaxes(routes, 1, 2)
    order = jnp.swapaxes(pair_order.reshape(layers_n, token_rows, topk_n), 1, 2)
    ids = jnp.arange(experts_n, dtype=jnp.int32)[None, :, None]
    none = token_rows * topk_n
    place_of = jnp.full((layers_n, experts_n, token_rows), none, jnp.int32)
    for k in range(topk_n):
        place_of = jnp.where(chosen[:, k][:, None, :] == ids, order[:, k][:, None, :], place_of)
    smaller = (place_of[:, :, :, None] < place_of[:, :, None, :]).astype(jnp.int32)
    return jnp.where(place_of < none, jnp.sum(smaller, axis=2) + 1, 0)


def dense_gates(logits, mask):
    top = jnp.max(jnp.where(mask, logits, masked_score), axis=0, keepdims=True)
    powers = jnp.where(mask, jnp.exp(jnp.where(mask, logits - top, 0.0)), 0.0)
    return powers / jnp.sum(powers, axis=0, keepdims=True)


def local_chips(
    tokens,
    w_qkv,
    w_out,
    w_router,
    norm_gains,
    w_gate,
    w_up,
    w_down,
    out_grad,
    segment_ids,
    routes,
    pair_order,
):
    token_rows = tokens.shape[0]
    layers_n = w_qkv.shape[0]
    topk_n = routes.shape[2]
    n_expert = lax.axis_size(EX)
    n_dp = lax.axis_size(DP)
    local_n = w_gate.shape[1]
    experts_n = local_n * n_expert
    capacity = 9 * n_expert * token_rows * topk_n // (8 * experts_n)
    shapes = (layers_n, n_dp, n_expert, local_n, capacity)
    positions = lax.axis_index(EX) * token_rows + jnp.arange(token_rows, dtype=jnp.int32)
    cosine, sine = rotary_tables(positions)
    tables = (
        jnp.concatenate([cosine, cosine], axis=-1)[:, 0],
        jnp.concatenate([-sine, sine], axis=-1)[:, 0],
        segment_ids[:, None],
    )
    ranks = rank_table(routes, pair_order, experts_n).reshape(layers_n * experts_n, token_rows)
    ranks = jnp.concatenate([ranks, segment_ids[None], jnp.zeros((7, token_rows), jnp.int32)])
    small = jnp.concatenate(
        [w_router[l] for l in range(layers_n)]
        + [jnp.swapaxes(norm_gains.reshape(2 * layers_n, -1), 0, 1)],
        axis=1,
    )
    small = jnp.pad(small, ((0, 0), (0, 128 - small.shape[1])))
    experts = (w_gate, w_up, w_down)

    def along_line(rows):
        return lax.all_gather(rows, DP, axis=0)

    saved, outputs, normed_all, streams = [], [], [], [tokens]
    for l in range(layers_n):
        given = (small, ranks, w_qkv, w_out, out_grad)
        if l > 0:
            given = (*plan, line_grads, *full[l])
        results = layer_forward(l, 1 + l, shapes, streams[l], tables, given, experts)
        if l == 0:
            plan = results[13:18]
            full = [results[18:20], results[20:22]]
            line_grads = results[22]
        else:
            grads_all = [results[13]]
        streams.append(results[0])
        outputs.append(results[1])
        saved.append(results[2:12])
        normed_all.append(along_line(results[12]))

    grads = out_grad
    owns, smalls = [None] * layers_n, [None] * layers_n
    row_sources, column_sources = [None] * layers_n, [None] * layers_n
    for l in reversed(range(layers_n)):
        normed_a, queries, kv, attended, mixed, normed_b, rows_in = saved[l][:7]
        gate_pre, up_pre, gate_seat = saved[l][7:]
        kept = (mixed, normed_b, queries, kv, gate_seat)
        sources = (normed_a, attended, *full[l], *experts, gate_pre, up_pre)
        results = layer_backward(l, 4 + l, shapes, grads, streams[l], tables, kept, plan, sources)
        grads, own_shard = results[:2]
        owns[l] = (rows_in, *results[2:6])
        column_sources[l] = results[6:8]
        smalls[l] = results[8]
        row_sources[l] = results[9:11]
    grad_experts, (small_sum, grad_qkv, grad_out) = tail(
        capacity,
        8,
        normed_all,
        grads_all,
        own_shard,
        (plan[0], plan[2], plan[3]),
        experts,
        owns,
        row_sources,
        column_sources,
        smalls,
    )
    small_sum = small_sum[:, :128] + small_sum[:, 128:]
    small_sum = small_sum[:, : layers_n * SMALL].reshape(-1, layers_n, SMALL)
    small_sum = jnp.swapaxes(small_sum, 0, 1)
    grad_router = small_sum[:, :, :experts_n]
    grad_gains = jnp.swapaxes(small_sum[:, :, experts_n : experts_n + 2], 1, 2)
    return (
        jnp.stack(outputs),
        grads,
        grad_qkv,
        grad_out,
        grad_router,
        grad_gains,
        *grad_experts,
    )


def local(
    tokens,
    w_qkv,
    w_out,
    w_router,
    norm_gains,
    w_gate,
    w_up,
    w_down,
    out_grad,
    segment_ids,
    routes,
    pair_order,
):
    token_rows = tokens.shape[0]
    layers_n = w_qkv.shape[0]
    topk_n = routes.shape[2]
    n_expert = lax.axis_size(EX)
    n_dp = lax.axis_size(DP)
    expert_here = lax.axis_index(EX)
    dp_here = lax.axis_index(DP)
    device_here = dp_here * n_expert + expert_here
    local_n = w_gate.shape[1]
    experts_n = local_n * n_expert
    capacity = 9 * n_expert * token_rows * topk_n // (8 * experts_n)
    group_rows = n_expert * token_rows
    query_width = QUERY_HEADS * HEAD_SIZE
    key_width = KEY_VALUE_HEADS * HEAD_SIZE
    score_scale = 1.0 / math.sqrt(HEAD_SIZE)
    token_positions = expert_here * token_rows + jnp.arange(token_rows, dtype=jnp.int32)
    cosine, sine_part = rotary_tables(token_positions)
    seg_prev = from_behind(segment_ids, everywhere, 1)
    has_prev = device_here > 0
    row_index = jnp.arange(token_rows)
    own_mask = (segment_ids[None, :] == segment_ids[:, None]) & (
        row_index[None, :] <= row_index[:, None]
    )
    prev_mask = (seg_prev[None, :] == segment_ids[:, None]) & has_prev
    allowed = jnp.concatenate([prev_mask, own_mask], axis=1)

    ranks = rank_table(routes, pair_order, experts_n)
    small = jnp.concatenate(
        [w_router[l] for l in range(layers_n)]
        + [jnp.swapaxes(norm_gains.reshape(2 * layers_n, -1), 0, 1)],
        axis=1,
    )
    small = jnp.pad(small, ((0, 0), (0, 128 - small.shape[1])))
    small_full, ranks_full, qkv_0, out_0 = [
        lax.all_gather(one, everywhere, axis=0)
        for one in (small, ranks.reshape(layers_n * experts_n, token_rows), w_qkv[0], w_out[0])
    ]
    qkv_fulls = [qkv_0.reshape(D, -1)]
    out_fulls = [out_0.reshape(query_width, D)]
    for layer_idx in range(1, layers_n):
        qkv_fulls.append(lax.all_gather(w_qkv[layer_idx], everywhere, axis=0, tiled=True))
        out_fulls.append(lax.all_gather(w_out[layer_idx], everywhere, axis=0, tiled=True))
    small_full = small_full.reshape(D, 128)
    gains = jnp.swapaxes(
        small_full[:, layers_n * experts_n : layers_n * (experts_n + 2)], 0, 1
    ).astype(f32)
    routers = [small_full[:, l * experts_n : (l + 1) * experts_n] for l in range(layers_n)]
    routers_turned = [jnp.swapaxes(router, 0, 1) for router in routers]
    ranks_full = ranks_full.reshape(n_dp, n_expert, layers_n, experts_n, token_rows)
    ranks_full = lax.dynamic_slice_in_dim(ranks_full, dp_here, 1, 0)
    groups = ranks_full.shape[0]
    hit_all = jnp.transpose(ranks_full > 0, (2, 0, 3, 1, 4)).reshape(
        layers_n, groups, experts_n, group_rows
    )
    mine = lax.dynamic_slice_in_dim(ranks_full, expert_here * local_n, local_n, 3)
    counts = jnp.sum((mine > 0).astype(jnp.int32), axis=-1)
    before = jnp.cumsum(counts, axis=1) - counts
    seats = jnp.where(mine > 0, before[..., None] + mine, 0)
    seats = jnp.transpose(seats, (2, 0, 3, 1, 4)).reshape(layers_n, groups, local_n, group_rows)
    seat_ids = jnp.arange(1, capacity + 1, dtype=jnp.int32)

    def own_of(array):
        return lax.dynamic_index_in_dim(array, 0, 0, keepdims=False)

    def seat_map(l):
        return (seats[l][:, :, None, :] == seat_ids[:, None]).astype(bf16)

    def gates_of(normed_rows, l, hit):
        logits = jnp.einsum("de,td->et", routers[l], normed_rows, preferred_element_type=f32)
        return dense_gates(logits, hit)

    own_hit = [(ranks[l] > 0) for l in range(layers_n)]

    stream = tokens.astype(f32)
    saved_layers = []
    outputs = []
    for l in range(layers_n):
        qkv_full, out_full = qkv_fulls[l], out_fulls[l]
        normed_a = rms_norm(stream, gains[2 * l]).astype(bf16)
        projected_output = jnp.dot(normed_a, qkv_full, preferred_element_type=f32)
        query_rows = apply_rotary(
            projected_output[:, :query_width].reshape(token_rows, QUERY_HEADS, HEAD_SIZE),
            cosine,
            sine_part,
        ).astype(bf16)
        key_own = apply_rotary(
            projected_output[:, query_width : query_width + key_width].reshape(
                token_rows, KEY_VALUE_HEADS, HEAD_SIZE
            ),
            cosine,
            sine_part,
        ).astype(bf16)
        value_own = (
            projected_output[:, query_width + key_width :]
            .reshape(token_rows, KEY_VALUE_HEADS, HEAD_SIZE)
            .astype(bf16)
        )
        key_prev, value_prev = from_behind((key_own, value_own), everywhere, 1)
        gathered_keys = jnp.concatenate([key_prev, key_own], axis=0)
        gathered_values = jnp.concatenate([value_prev, value_own], axis=0)
        scores, grouped_queries = masked_scores(query_rows, gathered_keys, allowed)
        top_score = jnp.max(scores, axis=-1, keepdims=True)
        exp_scores = jnp.exp(scores - top_score)
        row_total = jnp.sum(exp_scores, axis=-1, keepdims=True)
        prob_low = (exp_scores / row_total).astype(bf16)
        log_total = top_score + jnp.log(row_total)
        attended = (
            jnp.einsum("kgts,skd->tkgd", prob_low, gathered_values, preferred_element_type=f32)
            .reshape(token_rows, query_width)
            .astype(bf16)
        )
        mixed_sum = stream + jnp.dot(attended, out_full, preferred_element_type=f32)
        normed_b = rms_norm(mixed_sum, gains[2 * l + 1]).astype(bf16)

        if True:
            kept = {}
            group_normed = lax.all_gather(normed_b, EX, axis=0, tiled=True)
            kept["normed_all"] = group_normed[None]
            seat_own = own_of(seat_map(l))
            gates_own = gates_of(group_normed, l, own_of(hit_all[l]))
            gates_own = lax.dynamic_slice_in_dim(gates_own, expert_here * local_n, local_n, 0)
            gate_seat = jnp.sum(seat_own.astype(f32) * gates_own[:, None, :], axis=-1)
            expert_in = jnp.einsum(
                "est,td->esd", seat_own, group_normed, preferred_element_type=f32
            ).astype(bf16)
            gate_pre = jnp.einsum("esd,edf->esf", expert_in, w_gate[l], preferred_element_type=f32)
            up_pre = jnp.einsum("esd,edf->esf", expert_in, w_up[l], preferred_element_type=f32)
            hidden = gated_unit(gate_pre, up_pre).astype(bf16)
            expert_out = jnp.einsum("esf,efd->esd", hidden, w_down[l], preferred_element_type=f32)
            weighted = (expert_out * gate_seat[..., None]).astype(bf16)
            branch_part = jnp.einsum("est,esd->td", seat_own, weighted, preferred_element_type=f32)
            new_stream = mixed_sum + lax.psum_scatter(
                branch_part, EX, scatter_dimension=0, tiled=True
            )
        saved_layers.append(
            {
                "stream_in": stream,
                "normed_a": normed_a,
                "queries": query_rows,
                "key_all": gathered_keys,
                "value_all": gathered_values,
                "log_total": log_total,
                "attended": attended,
                "mixed_sum": mixed_sum,
                "normed_b": normed_b,
            }
            | kept
        )
        outputs.append(new_stream)
        stream = new_stream

    grad_stream = out_grad.astype(f32)
    weight_parts = [None] * layers_n
    expert_parts = [None] * layers_n
    owns = [None] * layers_n
    for l in reversed(range(layers_n)):
        record = saved_layers[l]
        qkv_full, out_full = qkv_fulls[l], out_fulls[l]
        grad_low = grad_stream.astype(bf16)
        if True:
            normed_all = record["normed_all"]
            grad_all = lax.all_gather(grad_low, EX, axis=0, tiled=True)[None]
            seat_all = seat_map(l)
            gates_all = jax.vmap(lambda rows, hit: gates_of(rows, l, hit))(normed_all, hit_all[l])
            gates_mine = lax.dynamic_slice_in_dim(gates_all, expert_here * local_n, local_n, 1)
            gate_seat = jnp.sum(seat_all.astype(f32) * gates_mine[:, :, None, :], axis=-1)
            rows_in = jnp.einsum(
                "gest,gtd->egsd", seat_all, normed_all, preferred_element_type=f32
            ).astype(bf16)
            rows_grad = jnp.einsum(
                "gest,gtd->egsd", seat_all, grad_all, preferred_element_type=f32
            ).astype(bf16)
            gate_seat = jnp.swapaxes(gate_seat, 0, 1)[..., None]
            gate_pre = jnp.einsum("egsd,edf->egsf", rows_in, w_gate[l], preferred_element_type=f32)
            up_pre = jnp.einsum("egsd,edf->egsf", rows_in, w_up[l], preferred_element_type=f32)
            dhidden_raw = jnp.einsum(
                "egsd,efd->egsf", rows_grad, w_down[l], preferred_element_type=f32
            )
            hidden, gate_pull = jax.vjp(gated_unit, gate_pre, up_pre)
            hidden_low = hidden.astype(bf16)
            dgate_pre, dup_pre = gate_pull(dhidden_raw * gate_seat)
            dgate_low = dgate_pre.astype(bf16)
            dup_low = dup_pre.astype(bf16)
            dgate_seat = jnp.sum(hidden_low.astype(f32) * dhidden_raw, axis=-1)
            rows_grad = (rows_grad.astype(f32) * gate_seat).astype(bf16)

        def by_expert(array):
            return array.reshape(local_n, -1, array.shape[-1])

        def outer(one, other):
            return jnp.einsum(
                "esa,esb->eab", by_expert(one), by_expert(other), preferred_element_type=f32
            )

        if True:
            grad_gate_l = outer(rows_in, dgate_low)
            grad_up_l = outer(rows_in, dup_low)
            grad_down_l = outer(hidden_low, rows_grad)
            grad_gate_l = lax.psum_scatter(
                grad_gate_l.astype(bf16), DP, scatter_dimension=1, tiled=True
            ).astype(f32)
            grad_up_l = lax.psum_scatter(
                grad_up_l.astype(bf16), DP, scatter_dimension=1, tiled=True
            ).astype(f32)
            grad_down_l = lax.psum_scatter(
                grad_down_l.astype(bf16), DP, scatter_dimension=2, tiled=True
            ).astype(f32)
            expert_parts[l] = (grad_gate_l, grad_up_l, grad_down_l)

        if True:
            dexpert_in = (
                jnp.einsum("egsf,edf->egsd", dgate_low, w_gate[l], preferred_element_type=f32)
                + jnp.einsum("egsf,edf->egsd", dup_low, w_up[l], preferred_element_type=f32)
            ).astype(bf16)
            back_part = jnp.einsum(
                "gest,egsd->td", seat_all, dexpert_in, preferred_element_type=f32
            )
            dgates_part = jnp.sum(
                seat_all[0].astype(f32) * dgate_seat[:, 0, :, None], axis=1
            )
            mine = expert_here * local_n + jnp.arange(local_n, dtype=jnp.int32)
            lane = jnp.arange(experts_n, dtype=jnp.int32)
            dgates_part = jnp.sum(
                jnp.where(mine[:, None, None] == lane, dgates_part[..., None], 0.0), axis=0
            )
            dnormed_b, dgates = [
                lax.psum_scatter(part, EX, scatter_dimension=0, tiled=True)
                for part in (back_part, dgates_part)
            ]
        gates_token = gates_of(record["normed_b"], l, own_hit[l]).T
        dlogits = (
            gates_token * (dgates - jnp.sum(gates_token * dgates, axis=1, keepdims=True))
        ).astype(bf16)
        dnormed_b = dnormed_b + jnp.einsum(
            "te,de->td", dlogits, routers[l], preferred_element_type=f32
        )
        unused_norm, norm_pull = jax.vjp(rms_norm, record["mixed_sum"], gains[2 * l + 1])
        dmixed_part, dgain_b = norm_pull(dnormed_b)
        dmixed = grad_stream + dmixed_part
        grad_attn = dmixed.astype(bf16)
        attended_gradient = jnp.einsum(
            "td,qd->tq", grad_attn, out_full, preferred_element_type=f32
        ).astype(bf16)
        gathered_keys = record["key_all"]
        gathered_values = record["value_all"]
        scores, grouped_queries = masked_scores(record["queries"], gathered_keys, allowed)
        prob_float = jnp.exp(scores - record["log_total"])
        prob_low = prob_float.astype(bf16)
        grouped_gradient = attended_gradient.reshape(
            token_rows, KEY_VALUE_HEADS, QUERY_HEADS // KEY_VALUE_HEADS, HEAD_SIZE
        )
        dvalue_all = jnp.einsum(
            "kgts,tkgd->skd", prob_low, grouped_gradient, preferred_element_type=f32
        )
        dprobs = jnp.einsum(
            "tkgd,skd->kgts", grouped_gradient, gathered_values, preferred_element_type=f32
        )
        delta_row = jnp.sum(prob_float * dprobs, axis=-1, keepdims=True)
        dscores = (prob_float * (dprobs - delta_row)).astype(bf16)
        dqueries = (
            jnp.einsum(
                "kgts,skd->tkgd", dscores, gathered_keys, preferred_element_type=f32
            ).reshape(token_rows, QUERY_HEADS, HEAD_SIZE)
            * score_scale
        )
        dkey_all = (
            jnp.einsum("kgts,tkgd->skd", dscores, grouped_queries, preferred_element_type=f32)
            * score_scale
        )
        dkey_next, dvalue_next = from_behind(
            (dkey_all[:token_rows].astype(bf16), dvalue_all[:token_rows].astype(bf16)),
            everywhere,
            -1,
        )
        dkey_own = dkey_all[token_rows:] + dkey_next.astype(f32)
        dvalue_own = dvalue_all[token_rows:] + dvalue_next.astype(f32)
        dq_raw = apply_rotary(dqueries, cosine, -sine_part)
        dk_raw = apply_rotary(dkey_own, cosine, -sine_part)
        dprojected = jnp.concatenate(
            [
                dq_raw.reshape(token_rows, query_width),
                dk_raw.reshape(token_rows, key_width),
                dvalue_own.reshape(token_rows, key_width),
            ],
            axis=1,
        ).astype(bf16)
        dnormed_a = jnp.einsum("tq,dq->td", dprojected, qkv_full, preferred_element_type=f32)
        unused_first, first_pull = jax.vjp(rms_norm, record["stream_in"], gains[2 * l])
        dstream_part, dgain_a = first_pull(dnormed_a)
        grad_stream = dmixed + dstream_part

        small_grad = jnp.concatenate(
            [
                jnp.einsum("td,te->de", record["normed_b"], dlogits, preferred_element_type=f32),
                dgain_a[:, None],
                dgain_b[:, None],
            ],
            axis=1,
        )
        normed_a, attended = record["normed_a"], record["attended"]
        grad_qkv_l = jnp.einsum("td,tq->dq", normed_a, dprojected, preferred_element_type=f32)
        grad_out_l = jnp.einsum("tq,td->qd", attended, grad_attn, preferred_element_type=f32)
        weight_parts[l] = (grad_qkv_l, grad_out_l, small_grad)

    small_grads = jnp.concatenate([weight_parts[l][2] for l in range(layers_n)], axis=1)
    if True:

        def scatter(array):
            return lax.psum_scatter(array, everywhere, scatter_dimension=0, tiled=True)

        small_sum = scatter(small_grads)
        grad_qkv = jnp.stack([scatter(weight_parts[l][0]) for l in range(layers_n)])
        grad_out = jnp.stack([scatter(weight_parts[l][1]) for l in range(layers_n)])
    wide = experts_n + 2
    grad_router = jnp.stack(
        [small_sum[:, l * wide : l * wide + experts_n] for l in range(layers_n)]
    )
    grad_gains = jnp.stack(
        [
            jnp.swapaxes(small_sum[:, l * wide + experts_n : (l + 1) * wide], 0, 1)
            for l in range(layers_n)
        ]
    )
    if True:
        grad_gate, grad_up, grad_down = [
            jnp.stack([expert_parts[l][member] for l in range(layers_n)]) for member in range(3)
        ]
    layer_outs = jnp.stack(outputs).astype(bf16)
    return (
        layer_outs,
        grad_stream,
        grad_qkv,
        grad_out,
        grad_router,
        grad_gains,
        grad_gate,
        grad_up,
        grad_down,
    )


def solution(mesh):
    sizes = (mesh.shape[DP], mesh.shape[EX])
    return jax.shard_map(
        local_chips if sizes == (4, 8) else local,
        mesh=mesh,
        in_specs=(
            P((DP, EX), None),
            P(None, (DP, EX), None),
            P(None, (DP, EX), None),
            P(None, (DP, EX), None),
            P(None, None, (DP, EX)),
            P(None, EX, None, None),
            P(None, EX, None, None),
            P(None, EX, None, None),
            P((DP, EX), None),
            P((DP, EX)),
            P(None, (DP, EX), None),
            P(None, (DP, EX), None),
        ),
        out_specs=(
            P(None, (DP, EX), None),
            P((DP, EX), None),
            P(None, (DP, EX), None),
            P(None, (DP, EX), None),
            P(None, (DP, EX), None),
            P(None, None, (DP, EX)),
            P(None, EX, DP, None),
            P(None, EX, DP, None),
            P(None, EX, None, DP),
        ),
        check_vma=False,
    )
```

```python
from functools import partial
import math

import jax
import jax.numpy as jnp
from jax import lax
from jax.experimental import pallas as pl
from jax.experimental.pallas import tpu as pltpu
from jax.sharding import PartitionSpec as P

D = 1536
QUERY_HEADS = 12
KEY_VALUE_HEADS = 2
HEAD_SIZE = 128
MESH = pl.DeviceIdType.MESH
DP, EX = "dp", "expert"
ANY = pl.ANY
bf16 = jnp.bfloat16
f32 = jnp.float32

epsilon = 1e-06
rope_base = 1000000.0
masked_score = -1e30
everywhere = (DP, EX)


def place():
    z = lax.axis_index(DP)
    e = lax.axis_index(EX)
    y, x, c = e // 4, (e // 2) % 2, e % 2
    near = {
        "own": e,
        "x": y * 4 + (1 - x) * 2 + c,
        "y": (1 - y) * 4 + x * 2 + c,
        "d": (1 - y) * 4 + (1 - x) * 2 + c,
        "c": y * 4 + x * 2 + (1 - c),
        "cx": y * 4 + (1 - x) * 2 + (1 - c),
        "cy": (1 - y) * 4 + x * 2 + (1 - c),
        "cd": (1 - y) * 4 + (1 - x) * 2 + (1 - c),
    }
    return z, near


def greet(z, near, plane, line, order=None):
    barrier = pltpu.get_barrier_semaphore()

    def tell(**target):
        pl.semaphore_signal(barrier, inc=1, device_id=target, device_id_type=MESH)

    for name in plane:
        tell(**{EX: near[name]})
    count = len(plane)
    links = []
    if line is not None:
        links += [(z < line - 1, {DP: z + 1}), (z > 0, {DP: z - 1})]
    if order is not None:
        behind, ahead, has_behind, has_ahead = order
        links += [
            (has_behind, {DP: behind[0], EX: behind[1]}),
            (has_ahead, {DP: ahead[0], EX: ahead[1]}),
        ]
    for there, target in links:

        @pl.when(there)
        def one():
            tell(**target)

        count = count + jnp.where(there, 1, 0)
    pl.semaphore_wait(barrier, count)


def halves(rows, columns):
    if rows % 32 == 0:
        return ((0, rows // 2), (0, columns)), ((rows // 2, rows // 2), (0, columns))
    if columns % 256 == 0:
        return ((0, rows), (0, columns // 2)), ((0, rows), (columns // 2, columns // 2))
    return ((0, 16), (0, columns)), ((16, rows - 16), (0, columns))


def cut(ref, part):
    (row, rows), (column, columns) = part
    return ref.at[pl.ds(row, rows), pl.ds(column, columns)]


KINDS = 10
SMALL = 24
BLOCK = 512
QUAD = ("own", "x", "y", "d")
BESIDE = ("c", "cx", "cy", "cd")


class Gather:
    def __init__(self, ins, outs, send, recv, z, near, line, flat=False):
        self.ins, self.outs, self.send, self.recv = ins, outs, send, recv
        self.z, self.near, self.line, self.flat = z, near, line, flat
        self.parts = [halves(*ref.shape) for ref in ins]
        self.all = range(len(ins))

    def hop(self, a, j, kind, whose, to, part=None, src=None):
        dst = self.outs[a].at[j] if self.flat else self.outs[a].at[j, self.near[whose]]
        src = dst if src is None else src
        if part is not None:
            src, dst = cut(src, part), cut(dst, part)
        return pltpu.make_async_remote_copy(
            src_ref=src,
            dst_ref=dst,
            send_sem=self.send.at[a, j, kind],
            recv_sem=self.recv.at[a, j, kind],
            device_id={DP: to} if kind >= 8 else {EX: self.near[to]},
            device_id_type=MESH,
        )

    def landed(self, a, j, kind, whose, part=None):
        if kind < 8:
            self.hop(a, j, kind, whose, "c", part).wait_recv()
        else:
            self.hop(a, j, kind, whose, self.z).wait_recv()

    def line_first(self):
        z = self.z

        @pl.when(z < self.line - 1)
        def up_first():
            for a in self.all:
                self.hop(a, z, 8, "own", z + 1, src=self.ins[a]).start()

        @pl.when(z > 0)
        def down_first():
            for a in self.all:
                self.hop(a, z, 9, "own", z - 1, src=self.ins[a]).start()

    def first(self, j, src=None):
        for a in self.all:
            one = None if src is None else src[a]
            self.hop(a, j, 0, "own", "x", src=one).start()
            self.hop(a, j, 1, "own", "y", src=one).start()
            self.hop(a, j, 2, "own", "c", src=one).start()

    def second(self, j, kind=0):
        for a in self.all:
            self.landed(a, j, 0, "x")
            self.hop(a, j, 4, "x", "y", self.parts[a][1]).start()
            self.hop(a, j, 5, "x", "c").start()
            self.landed(a, j, 1, "y")
            self.hop(a, j, 3, "y", "x", self.parts[a][0]).start()
            self.hop(a, j, 6, "y", "c").start()

    def third(self, j, kind=0):
        for a in self.all:
            self.landed(a, j, 3, "d", self.parts[a][0])
            self.landed(a, j, 4, "d", self.parts[a][1])
            self.hop(a, j, 7, "d", "c").start()

    def finish(self, j, kind=0):
        for a in self.all:
            for kind, whose in ((2, "c"), (5, "cx"), (6, "cy"), (7, "cd")):
                self.landed(a, j, kind, whose)
            for kind in (0, 1, 2):
                self.hop(a, j, kind, "own", "c").wait_send()
            self.hop(a, j, 3, "y", "x", self.parts[a][0]).wait_send()
            self.hop(a, j, 4, "x", "y", self.parts[a][1]).wait_send()
            for kind in (5, 6, 7):
                self.hop(a, j, kind, "x", "c").wait_send()

    def arrivals(self, step, act):
        z = self.z

        @pl.when(z - step >= 0)
        def below():
            act(z - step, 8)

        @pl.when(z + step <= self.line - 1)
        def above():
            act(z + step, 9)

    def take(self, j, kind):
        for a in self.all:
            self.landed(a, j, kind, "own")
        z = self.z
        if kind == 8:

            @pl.when(z < self.line - 1)
            def on_up():
                for a in self.all:
                    self.hop(a, j, 8, "own", z + 1).start()

        else:

            @pl.when(z > 0)
            def on_down():
                for a in self.all:
                    self.hop(a, j, 9, "own", z - 1).start()

        self.first(j)

    def carry(self, j, kind):
        z = self.z
        for a in self.all:
            self.landed(a, j, kind, "own")
        more, target = (z < self.line - 1, z + 1) if kind == 8 else (z > 0, z - 1)

        @pl.when(more)
        def on():
            for a in self.all:
                self.hop(a, j, kind, "own", target).start()

    def plane_of(self, k):
        return lax.rem(self.z + k, self.line)

    def spread(self, k, rows, sem):
        j = self.plane_of(k)
        self.first(j, [rows.at[j]])
        self.kept(k, rows, sem).start()

    def kept(self, k, rows, sem):
        j = self.plane_of(k)
        return pltpu.make_async_copy(rows.at[j], self.outs[0].at[j, self.near["own"]], sem.at[k])

    def spread_done(self, rows, sem):
        for k in range(1, self.line):
            self.finish(self.plane_of(k))
            self.kept(k, rows, sem).wait()

    def line_done(self):
        z = self.z
        for step in range(self.line):

            @pl.when((z - step >= 0) & (z < self.line - 1))
            def up_done():
                for a in self.all:
                    self.hop(a, z - step, 8, "own", z + 1).wait_send()

            @pl.when((z + step <= self.line - 1) & (z > 0))
            def down_done():
                for a in self.all:
                    self.hop(a, z + step, 9, "own", z - 1).wait_send()


def plane_gather(src, dst, send, recv, near):
    parts = halves(*src.shape)

    def hop(kind, whose, to, part=None):
        one = dst.at[near[whose]] if part is None else cut(dst.at[near[whose]], part)
        return pltpu.make_async_remote_copy(
            src_ref=src if whose == "own" else one,
            dst_ref=one,
            send_sem=send.at[kind],
            recv_sem=recv.at[kind],
            device_id={EX: near[to]},
            device_id_type=MESH,
        )

    def first():
        hop(0, "own", "x").start()
        hop(1, "own", "y").start()
        hop(2, "own", "c").start()
        dst[near["own"]] = src[...]

    def second():
        hop(0, "x", "c").wait_recv()
        hop(4, "x", "y", parts[1]).start()
        hop(5, "x", "c").start()
        hop(1, "y", "c").wait_recv()
        hop(3, "y", "x", parts[0]).start()
        hop(6, "y", "c").start()

    def third():
        hop(3, "d", "c", parts[0]).wait_recv()
        hop(4, "d", "c", parts[1]).wait_recv()
        hop(7, "d", "c").start()

    def finish():
        for kind, whose in ((2, "c"), (5, "cx"), (6, "cy"), (7, "cd")):
            hop(kind, whose, "c").wait_recv()
        for kind in (0, 1, 2):
            hop(kind, "own", "c").wait_send()
        hop(3, "y", "x", parts[0]).wait_send()
        hop(4, "x", "y", parts[1]).wait_send()
        for kind in (5, 6, 7):
            hop(kind, "x", "c").wait_send()

    return first, second, third, finish


def sum_scratch(rows, columns):
    return [
        pltpu.VMEM((8, rows, columns), bf16),
        pltpu.VMEM((3, rows, columns), bf16),
        pltpu.VMEM((4, rows, columns), bf16),
        pltpu.VMEM((2, rows // 2, columns), bf16),
        pltpu.VMEM((2, rows // 2, columns), bf16),
        pltpu.VMEM((2, rows // 2, columns), bf16),
        pltpu.SemaphoreType.DMA((10,)),
        pltpu.SemaphoreType.DMA((10,)),
    ]


def plane_sum(make, out_ref, base, scratch, near):
    part_ref, paired, fromc, fromx, fromy, last, send, recv = scratch
    rows = out_ref.shape[0]
    half = rows // 2
    A, B = pl.ds(0, half), pl.ds(half, half)

    def copy(number, src, dst, to):
        return pltpu.make_async_remote_copy(
            src_ref=src,
            dst_ref=dst,
            send_sem=send.at[number],
            recv_sem=recv.at[number],
            device_id={EX: near[to]},
            device_id_type=MESH,
        )

    order = ("d", "x", "y", "own")
    across = ("cd", "cx", "cy", "c")
    core = [copy(s, part_ref.at[near[name]], fromc.at[s], "c") for s, name in enumerate(across)]
    to_x = [copy(4, paired.at[0, A], fromx.at[0], "x"), copy(5, paired.at[1, A], fromx.at[1], "x")]
    to_y = [copy(6, paired.at[0, B], fromy.at[0], "y"), copy(7, paired.at[2, B], fromy.at[1], "y")]
    late_y = copy(8, paired.at[2, A], last.at[0], "y")
    late_x = copy(9, paired.at[1, B], last.at[1], "x")

    def pair(s):
        core[s].wait_recv()
        paired[s] = (part_ref[near[order[s]]].astype(f32) + fromc[s].astype(f32)).astype(bf16)

    for s in range(3):
        make(across[s])
        core[s].start()
        make(order[s])
    pair(0)
    to_x[0].start()
    to_y[0].start()
    make(across[3])
    core[3].start()
    pair(1)
    to_x[1].start()
    pair(2)
    to_y[1].start()
    make(order[3])
    core[3].wait_recv()
    total = part_ref[near["own"]].astype(f32) + fromc[3].astype(f32)
    out_ref[...] = total if base is None else base[...] + total
    to_x[0].wait_recv()
    paired[2, A] = (paired[2, A].astype(f32) + fromx[0].astype(f32)).astype(bf16)
    late_y.start()
    to_y[0].wait_recv()
    paired[1, B] = (paired[1, B].astype(f32) + fromy[0].astype(f32)).astype(bf16)
    late_x.start()
    to_x[1].wait_recv()
    out_ref[A] += fromx[1].astype(f32)
    to_y[1].wait_recv()
    out_ref[B] += fromy[1].astype(f32)
    late_y.wait_recv()
    out_ref[A] += last[0].astype(f32)
    late_x.wait_recv()
    out_ref[B] += last[1].astype(f32)
    for one in core + to_x + to_y + [late_x, late_y]:
        one.wait_send()


def mul(a, b, over=((1,), (0,))):
    return lax.dot_general(a, b, (over, ((), ())), preferred_element_type=f32)


LAST = ((1,), (1,))


def seat_rows(seats, number):
    local_n, tokens_n = seats.shape
    rows = lax.broadcasted_iota(jnp.int32, (local_n * number, tokens_n), 0).astype(f32)
    hot = rows < 0
    for e in range(local_n):
        one = seats[e : e + 1, :]
        hot = hot | ((rows == one + (e * number - 1)) & (one > 0) & (one <= number))
    return jnp.where(hot, 1.0, 0.0).astype(bf16)


def seat_columns(seats, number):
    tokens_n, local_n = seats.shape
    columns = lax.broadcasted_iota(jnp.int32, (tokens_n, local_n * number), 1).astype(f32)
    hot = columns < 0
    for e in range(local_n):
        one = seats[:, e : e + 1]
        hot = hot | ((columns == one + (e * number - 1)) & (one > 0) & (one <= number))
    return jnp.where(hot, 1.0, 0.0).astype(bf16)


def masked_gates(logits, hit):
    top = jnp.max(jnp.where(hit, logits, masked_score), axis=0, keepdims=True)
    powers = jnp.where(hit, jnp.exp(jnp.where(hit, logits - top, 0.0)), 0.0)
    return powers / jnp.sum(powers, axis=0, keepdims=True)


def tail_kernel(layers_n, number, *refs):
    refs = list(refs)

    def some(count):
        taken = refs[:count]
        del refs[:count]
        return taken

    tokens_all, grads_all = some(layers_n), some(layers_n - 1)
    (own_shard,) = some(1)
    table, hit, seats = some(3)
    w_gate, w_up, w_down = some(3)
    owns = [some(5) for l in range(layers_n)]
    row_sources = [some(2) for l in range(layers_n)]
    column_sources = [some(2) for l in range(layers_n)]
    smalls = some(layers_n)
    grad_gate, grad_up, grad_down, landing = some(4)
    beside = some(layers_n)
    small_sum, grad_qkv, grad_out = some(3)
    (
        tokens,
        grads,
        gates,
        rows_in,
        rows_grad,
        cols_in,
        cols_grad,
        hidden_low,
        dgate_low,
        dup_low,
        gate_w,
        up_w,
        down_w,
        stage_wide,
        stage_tall,
        weight_sem,
        token_sem,
        own_sem,
        out_sem,
        gather_send,
        gather_recv,
        beside_send,
        beside_recv,
        small_own,
        small_got,
        small_part,
        small_sem,
        columns,
        row_block,
        block_sum,
        block_got,
        final,
        final_got,
        column_send,
        column_recv,
        column_keep,
        row_sem,
        block_send,
        block_recv,
        final_send,
        final_recv,
    ) = some(41)
    held = [some(6)]
    z, near = place()
    n_dp, local_n = seats.shape[1], seats.shape[2]
    width = cols_in.shape[1]
    ours = pl.ds(pl.multiple_of(z * width, 128), width)
    gather = Gather([own_shard], [landing], gather_send, gather_recv, z, near, n_dp)
    total = Sums([small_part], [small_sum], held, *refs, z, near, n_dp)
    own_e = near["own"]
    plane_n = columns.shape[1]
    over = ((0,), (0,))
    per_expert = n_dp - 1
    per_layer = local_n * per_expert
    steps = layers_n * per_layer

    def layer_of(i):
        return layers_n - 1 - i // per_layer

    def across(l, j):
        return pltpu.make_async_remote_copy(
            src_ref=tokens_all[l].at[j],
            dst_ref=beside[l].at[j],
            send_sem=beside_send.at[l, j],
            recv_sem=beside_recv.at[l, j],
            device_id={EX: near["c"]},
            device_id_type=MESH,
        )

    def start(one):
        one.start()

    def wait(one):
        one.wait()

    def fetch(i, slot, act):
        j = lax.rem(z + 1 + lax.rem(i, per_expert), n_dp)
        for l in range(layers_n):

            @pl.when(layer_of(i) == l)
            def of_layer():
                if act is start:

                    @pl.when(lax.rem(i, per_layer) < per_expert)
                    def arrived():
                        across(l, j).wait_recv()

                for source, names, base in ((tokens_all[l], QUAD, 0), (beside[l], BESIDE, 4)):
                    for q, name in enumerate(names):
                        dst = tokens.at[slot, near[name]]
                        sem = token_sem.at[slot, base + q]
                        act(pltpu.make_async_copy(source.at[j, q], dst, sem))
                grads_from = (landing if l == 0 else grads_all[l - 1]).at[j]
                act(pltpu.make_async_copy(grads_from, grads.at[slot], token_sem.at[slot, 8]))

    def weights(l, e):
        return [
            pltpu.make_async_copy(src.at[l, e], dst, weight_sem.at[i])
            for i, (src, dst) in enumerate(((w_gate, gate_w), (w_up, up_w), (w_down, down_w)))
        ]

    def own(l, e):
        here = pl.ds(pl.multiple_of(e * number, 32), number)
        inner = pl.ds(0, number)
        pairs = (
            (owns[l][0].at[here, ours], cols_in.at[inner]),
            (owns[l][1].at[here, ours], cols_grad.at[inner]),
            (owns[l][2].at[here], hidden_low.at[inner]),
            (owns[l][3].at[here], dgate_low.at[inner]),
            (owns[l][4].at[here], dup_low.at[inner]),
        )
        return [
            pltpu.make_async_copy(src, dst, own_sem.at[i]) for i, (src, dst) in enumerate(pairs)
        ]

    def of(i, make, act):
        e = lax.rem(i // per_expert, local_n)
        for l in range(layers_n):

            @pl.when(layer_of(i) == l)
            def of_layer():
                for one in make(l, e):
                    act(one)

    def results(l, e):
        return [
            pltpu.make_async_copy(stage_wide.at[0], grad_gate.at[l, e], out_sem.at[0]),
            pltpu.make_async_copy(stage_wide.at[1], grad_up.at[l, e], out_sem.at[1]),
            pltpu.make_async_copy(stage_tall, grad_down.at[l, e], out_sem.at[2]),
        ]

    def column_pieces(l, owner):
        first, second = column_sources[l]
        extra = second.shape[1] // 128 - plane_n
        return [
            (first.at[:, pl.ds(pl.multiple_of(owner * 256, 256), 256)], 0, 256),
            (second.at[:, pl.ds(pl.multiple_of(owner * 128, 128), 128)], 256, 128),
            (
                second.at[
                    :, pl.ds(pl.multiple_of((plane_n + owner // 2 % extra) * 128, 128), 128)
                ],
                384,
                128,
            ),
        ]

    def column_copy(l, owner, source, piece):
        src, at, size = column_pieces(l, owner)[piece]
        return pltpu.make_async_remote_copy(
            src_ref=src,
            dst_ref=columns.at[l, source, :, pl.ds(at, size)],
            send_sem=column_send.at[l, owner, piece],
            recv_sem=column_recv.at[l, source, piece],
            device_id={EX: owner},
            device_id_type=MESH,
        )

    def column_own(l, piece):
        src, at, size = column_pieces(l, own_e)[piece]
        dst = columns.at[l, own_e, :, pl.ds(at, size)]
        return pltpu.make_async_copy(src, dst, column_keep.at[l, piece])

    def column_each(l, act_send, act_recv, act_own):
        for d in range(1, plane_n):
            owner = lax.rem(own_e + d, plane_n)
            source = lax.rem(own_e + plane_n - d, plane_n)
            for piece in range(3):
                if piece < 2:
                    if act_send is not None:
                        act_send(column_copy(l, owner, own_e, piece))
                    if act_recv is not None:
                        act_recv(column_copy(l, owner, source, piece))
                    continue
                if act_send is not None:

                    @pl.when(lax.rem(owner, 2) == 0)
                    def extra_out():
                        act_send(column_copy(l, owner, own_e, piece))

                if act_recv is not None:

                    @pl.when(lax.rem(own_e, 2) == 0)
                    def extra_in():
                        act_recv(column_copy(l, owner, source, piece))

        if act_own is not None:
            act_own(column_own(l, 0))
            act_own(column_own(l, 1))

            @pl.when(lax.rem(own_e, 2) == 0)
            def extra_own():
                act_own(column_own(l, 2))

    def row_loads(l):
        return [
            pltpu.make_async_copy(src.at[0], row_block.at[i], row_sem.at[i])
            for i, src in enumerate(row_sources[l])
        ]

    def blocks(l):
        column_each(l, None, lambda one: one.wait_recv(), wait)
        for one in row_loads(l):
            one.wait()
        height = block_sum.shape[2]
        for i in range(2):
            here = pl.ds(i * 256, 256)
            given = columns[l, :, :, here].reshape(-1, 256)
            for j in range(n_dp):
                rows = row_block[i, :, :, pl.ds(j * height, height)].reshape(-1, height)
                block_sum[l, j, :, here] = mul(rows, given, over).astype(bf16)
        if l > 0:
            for one in row_loads(l - 1):
                one.start()

    def block_move(l, j, way):
        slot = jnp.where(j == z + way, n_dp, j) if way < 0 else j
        return pltpu.make_async_remote_copy(
            src_ref=block_sum.at[l, j],
            dst_ref=block_got.at[l, slot],
            send_sem=block_send.at[l, j],
            recv_sem=block_recv.at[l, slot],
            device_id={DP: z + way},
            device_id_type=MESH,
        )

    def block_landed(l, slot):
        pltpu.make_async_remote_copy(
            src_ref=block_got.at[l, slot],
            dst_ref=block_got.at[l, slot],
            send_sem=block_send.at[l, 0],
            recv_sem=block_recv.at[l, slot],
            device_id={DP: z},
            device_id_type=MESH,
        ).wait_recv()

    def block_step(l):
        def act(j, way):
            if way == 0:
                return
            more = (z > 0) if way > 0 else (z < n_dp - 1)

            @pl.when(more)
            def add():
                block_landed(l, j)
                block_sum[l, j] = (
                    block_sum[l, j].astype(f32) + block_got[l, j].astype(f32)
                ).astype(bf16)

            block_move(l, j, way).start()

        return act

    def final_copy(l, owner, source):
        return pltpu.make_async_remote_copy(
            src_ref=final.at[l, owner],
            dst_ref=final_got.at[l, source],
            send_sem=final_send.at[l, owner],
            recv_sem=final_recv.at[l, source],
            device_id={EX: owner},
            device_id_type=MESH,
        )

    def block_end(l):
        final[l] = block_sum[l, z].reshape(final.shape[1:])

        @pl.when(z > 0)
        def below():
            block_landed(l, z)
            got = block_got[l, z].reshape(final.shape[1:])
            final[l] = (final[l].astype(f32) + got.astype(f32)).astype(bf16)

        @pl.when(z < n_dp - 1)
        def above():
            block_landed(l, n_dp)
            got = block_got[l, n_dp].reshape(final.shape[1:])
            final[l] = (final[l].astype(f32) + got.astype(f32)).astype(bf16)

        for d in range(1, plane_n):
            final_copy(l, lax.rem(own_e + d, plane_n), own_e).start()
        final_got[l, own_e] = final[l, own_e]

    def block_out(l):
        for d in range(1, plane_n):
            final_copy(l, own_e, lax.rem(own_e + d, plane_n)).wait_recv()
        for source in range(plane_n):
            got = final_got[l, source].astype(f32)
            grad_qkv[l, :, pl.ds(source * 256, 256)] = got[:, :256]
            grad_out[l, :, pl.ds(source * 128, 128)] = got[:, 256:384]
            if source % 2 == 0:
                grad_out[l, :, pl.ds((plane_n + source // 2) * 128, 128)] = got[:, 384:]

    def small_exchange():
        return pltpu.make_async_remote_copy(
            src_ref=small_own,
            dst_ref=small_got,
            send_sem=small_sem.at[0],
            recv_sem=small_sem.at[1],
            device_id={EX: near["c"]},
            device_id_type=MESH,
        )

    def small_parts():
        small_exchange().wait_recv()
        both = small_own[...] + small_got[...]
        rest = jnp.zeros((128 - both.shape[0], both.shape[1]), f32)
        turned = jnp.transpose(jnp.concatenate([both, rest], axis=0))
        high = turned.astype(bf16)
        low = (turned - high.astype(f32)).astype(bf16)
        shape = small_part.shape[:3] + (128,)
        small_part[:, :, :, pl.ds(0, 128)] = high.reshape(shape)
        small_part[:, :, :, pl.ds(128, 128)] = low.reshape(shape)
        for distance in (3, 2, 1, 0):
            total.at(distance, total.first)

    for l in range(layers_n):
        small_own[pl.ds(l * SMALL, SMALL)] = smalls[l][...]

    @pl.when(lax.rem(own_e, 2) == 1)
    def no_extra():
        columns[:, :, :, pl.ds(384, 128)] = jnp.zeros(columns.shape[:3] + (128,), bf16)

    greet(z, near, ("x", "y", "d", "c", "cx", "cy", "cd"), n_dp)
    gather.line_first()
    small_exchange().start()
    for l in reversed(range(layers_n)):
        for k in range(1, n_dp):
            across(l, lax.rem(z + k, n_dp)).start()
    for l in reversed(range(layers_n)):
        column_each(l, start, None, start)
    for one in row_loads(layers_n - 1):
        one.start()
    of(0, weights, start)
    fetch(0, 0, start)

    def block_at(l, distance):
        return lambda: total.at(distance, block_step(l))

    services = {
        0: [lambda: gather.arrivals(1, gather.take), small_parts],
        1: [lambda: gather.arrivals(2, gather.take), lambda: blocks(1)],
        2: [
            lambda: gather.arrivals(1, gather.second),
            lambda: gather.arrivals(3, gather.take),
            block_at(1, 3),
        ],
        3: [
            lambda: gather.arrivals(1, gather.third),
            lambda: gather.arrivals(2, gather.second),
            block_at(1, 2),
            lambda: blocks(0),
        ],
        4: [
            lambda: gather.arrivals(2, gather.third),
            lambda: gather.arrivals(3, gather.second),
            block_at(0, 3),
            block_at(1, 1),
        ],
        5: [
            lambda: gather.arrivals(3, gather.third),
            lambda: gather.arrivals(1, gather.finish),
            lambda: gather.arrivals(2, gather.finish),
            lambda: gather.arrivals(3, gather.finish),
            block_at(0, 2),
        ],
        6: [
            lambda: total.at(3, total.second),
            lambda: total.at(2, total.second),
            lambda: total.at(1, total.second),
            lambda: total.at(0, total.second),
            block_at(0, 1),
        ],
        7: [lambda: block_end(1)],
        8: [lambda: total.at(3, total.third), lambda: total.at(2, total.third)],
        9: [lambda: total.at(1, total.third)],
        10: [lambda: block_end(0)],
        11: [lambda: total.at(0, total.third), lambda: block_out(1)],
    }

    def step(i, carry):
        slot = lax.rem(i, 2)
        l = layer_of(i)
        k = lax.rem(i, per_expert)
        e = lax.rem(i // per_expert, local_n)
        j = lax.rem(z + 1 + k, n_dp)

        @pl.when(k == 0)
        def begin():
            of(i, own, start)

        @pl.when((i + 1 < steps) & (i != per_layer - 1))
        def ahead():
            fetch(i + 1, 1 - slot, start)

        fetch(i, slot, wait)
        everyone = tokens[slot].reshape(-1, tokens.shape[3])
        experts_n = hit.shape[2]

        @pl.when(e == 0)
        def gates_here():
            here = pl.ds(pl.multiple_of(l * experts_n, experts_n), experts_n)
            router = table[here, :].astype(bf16)
            gates[k] = masked_gates(mul(router, everyone, LAST), hit[l, j] > 0)

        pick = seat_rows(seats[l, j, pl.ds(e, 1)], number)
        rows_in[...] = mul(pick, everyone).astype(bf16)
        rows_grad[...] = mul(pick, grads[slot].reshape(-1, tokens.shape[3])).astype(bf16)
        place_of = pl.ds(pl.multiple_of((k + 1) * number, 32), number)
        mine = gates[k, pl.ds(own_e * local_n + e, 1), :]
        gate_seat = jnp.sum(pick.astype(f32) * mine, axis=1, keepdims=True)

        @pl.when(k == 0)
        def weights_here():
            of(i, weights, wait)

        gate = mul(rows_in[...], gate_w[...])
        up = mul(rows_in[...], up_w[...])
        raw = mul(rows_grad[...], down_w[...], LAST) * gate_seat
        sigmoid = 1.0 / (1.0 + jnp.exp(-gate))
        silu = gate * sigmoid
        hidden_low[place_of] = (silu * up).astype(bf16)
        dgate_low[place_of] = (raw * up * sigmoid * (1.0 + gate * (1.0 - sigmoid))).astype(bf16)
        dup_low[place_of] = (raw * silu).astype(bf16)
        cols_in[place_of] = rows_in[:, ours]
        cols_grad[place_of] = (rows_grad[:, ours].astype(f32) * gate_seat).astype(bf16)

        @pl.when(k == per_expert - 1)
        def close():
            @pl.when(i + 1 < steps)
            def next_weights():
                of(i + 1, weights, start)

            of(i, own, wait)

            @pl.when(i >= per_expert)
            def staged():
                of(i - per_expert, results, wait)

            stage_wide[0] = mul(cols_in[...], dgate_low[...], over)
            stage_wide[1] = mul(cols_in[...], dup_low[...], over)
            stage_tall[...] = mul(hidden_low[...], cols_grad[...], over)
            of(i, results, start)

        for at, acts in services.items():

            @pl.when(i == at)
            def serve():
                for act in acts:
                    act()

        @pl.when(i == per_layer - 1)
        def late_ahead():
            fetch(i + 1, 1 - slot, start)

        return carry

    lax.fori_loop(0, steps, step, 0)
    block_out(0)
    for distance in (3, 2, 1, 0):
        total.at(distance, total.finish)
    small_exchange().wait_send()
    for l in range(layers_n):
        column_each(l, lambda one: one.wait_send(), None, None)
        for d in range(1, plane_n):
            final_copy(l, lax.rem(own_e + d, plane_n), own_e).wait_send()
        for distance in (3, 2, 1):
            total.at(distance, lambda j, way: block_move(l, j, way).wait_send())
    gather.line_done()
    for l in range(layers_n):
        for k in range(1, n_dp):
            across(l, lax.rem(z + k, n_dp)).wait_send()
    of(steps - 1, results, wait)


def tail(
    capacity,
    number,
    tokens_all,
    grads_all,
    own_shard,
    plan,
    weights,
    owns,
    row_sources,
    column_sources,
    smalls,
):
    table, hit, seats = plan
    layers_n, n_dp, local_n, group_rows = seats.shape
    n_expert = lax.axis_size(EX)
    rows, width = own_shard.shape
    hidden = weights[0].shape[3]
    part = width // n_dp
    cut_rows = part // n_expert
    wide = column_sources[0][0].shape[1]
    shape = jax.ShapeDtypeStruct
    several = [one for group in (owns, row_sources, column_sources) for l in group for one in l]
    results = pl.pallas_call(
        partial(tail_kernel, layers_n, capacity),
        out_shape=[
            shape((layers_n, local_n, part, hidden), f32),
            shape((layers_n, local_n, part, hidden), f32),
            shape((layers_n, local_n, hidden, part), f32),
            shape((n_dp, n_expert, rows, width), bf16),
        ]
        + [shape(tokens_all[0].shape, bf16)] * layers_n
        + [
            shape((cut_rows, 256), f32),
            shape((layers_n, cut_rows, wide), f32),
            shape((layers_n, cut_rows, width), f32),
        ],
        in_specs=[HBM] * (2 * layers_n) + [VMEM] * 3 + [HBM] * (3 + len(several)) + [VMEM] * layers_n,
        out_specs=[HBM] * (4 + layers_n) + [VMEM] * 3,
        scratch_shapes=[
            pltpu.VMEM((2, n_expert, rows, width), bf16),
            pltpu.VMEM((2, n_expert, rows, width), bf16),
            pltpu.VMEM((n_dp - 1,) + hit.shape[2:], f32),
            pltpu.VMEM((capacity, width), bf16),
            pltpu.VMEM((capacity, width), bf16),
            pltpu.VMEM((n_dp * capacity, part), bf16),
            pltpu.VMEM((n_dp * capacity, part), bf16),
            pltpu.VMEM((n_dp * capacity, hidden), bf16),
            pltpu.VMEM((n_dp * capacity, hidden), bf16),
            pltpu.VMEM((n_dp * capacity, hidden), bf16),
            pltpu.VMEM((width, hidden), bf16),
            pltpu.VMEM((width, hidden), bf16),
            pltpu.VMEM((hidden, width), bf16),
            pltpu.VMEM((2, part, hidden), f32),
            pltpu.VMEM((hidden, part), f32),
            pltpu.SemaphoreType.DMA((3,)),
            pltpu.SemaphoreType.DMA((2, 9)),
            pltpu.SemaphoreType.DMA((5,)),
            pltpu.SemaphoreType.DMA((3,)),
            pltpu.SemaphoreType.DMA((1, n_dp, KINDS)),
            pltpu.SemaphoreType.DMA((1, n_dp, KINDS)),
            pltpu.SemaphoreType.DMA((layers_n, n_dp)),
            pltpu.SemaphoreType.DMA((layers_n, n_dp)),
            pltpu.VMEM((layers_n * SMALL, width), f32),
            pltpu.VMEM((layers_n * SMALL, width), f32),
            pltpu.VMEM((n_dp, n_expert, cut_rows, 256), bf16),
            pltpu.SemaphoreType.DMA((2,)),
            pltpu.VMEM((layers_n, n_expert, rows, BLOCK), bf16),
            pltpu.VMEM((2, n_expert, rows, width), bf16),
            pltpu.VMEM((layers_n, n_dp, part, BLOCK), bf16),
            pltpu.VMEM((layers_n, n_dp + 1, part, BLOCK), bf16),
            pltpu.VMEM((layers_n, n_expert, cut_rows, BLOCK), bf16),
            pltpu.VMEM((layers_n, n_expert, cut_rows, BLOCK), bf16),
            pltpu.SemaphoreType.DMA((layers_n, n_expert, 3)),
            pltpu.SemaphoreType.DMA((layers_n, n_expert, 3)),
            pltpu.SemaphoreType.DMA((layers_n, 3)),
            pltpu.SemaphoreType.DMA((2,)),
            pltpu.SemaphoreType.DMA((layers_n, n_dp)),
            pltpu.SemaphoreType.DMA((layers_n, n_dp + 1)),
            pltpu.SemaphoreType.DMA((layers_n, n_expert)),
            pltpu.SemaphoreType.DMA((layers_n, n_expert)),
        ]
        + sums_scratch([(cut_rows, 256)], n_dp),
        compiler_params=settings(number),
        name="tail",
    )(
        *tokens_all,
        *grads_all,
        own_shard,
        *plan,
        *weights,
        *several,
        *smalls,
    )
    return results[:3], results[4 + layers_n :]


VMEM = pl.BlockSpec(memory_space=pltpu.VMEM)
HBM = pl.BlockSpec(memory_space=ANY)


def settings(number):
    return pltpu.CompilerParams(
        collective_id=number, has_side_effects=True, vmem_limit_bytes=63 << 20
    )


def chain(z, e):
    n_expert = 8
    behind = (z, lax.rem(e + n_expert - 1, n_expert))
    ahead = (z, lax.rem(e + 1, n_expert))
    return behind, ahead, e > 0, e < n_expert - 1


def normalized(value, gain):
    scale = lax.rsqrt(jnp.mean(value * value, axis=-1, keepdims=True) + epsilon)
    return value * scale * gain


def turn(head, cosine, signed_sine):
    return head * cosine + pltpu.roll(head, HEAD_SIZE // 2, 1) * signed_sine


def head_of(h):
    return pl.ds(h * HEAD_SIZE, HEAD_SIZE)


def allowed_keys(rk, row, z, e, behind, has_behind, seg_column):
    own = rk[z, e, pl.ds(row, 1), :]
    first = rk[z, behind[1], pl.ds(row, 1), :]
    rows = seg_column.shape[0]
    query = lax.broadcasted_iota(jnp.int32, (rows, rows), 0)
    key = lax.broadcasted_iota(jnp.int32, (rows, rows), 1)
    reach = jnp.where(has_behind, 0, -1)
    return jnp.concatenate(
        [(first == seg_column) & (key >= rows * -reach), (own == seg_column) & (key <= query)],
        axis=1,
    )


def head_probs(query, keys, allowed):
    scores = mul(query, keys, LAST) * (1.0 / math.sqrt(HEAD_SIZE))
    scores = jnp.where(allowed, scores, masked_score)
    powers = jnp.exp(scores - jnp.max(scores, axis=-1, keepdims=True))
    return powers / jnp.sum(powers, axis=-1, keepdims=True)


def forward_kernel(layer, layers_n, number, *refs):
    first = layer == 0
    refs = list(refs)

    def some(count):
        taken = refs[:count]
        del refs[:count]
        return taken

    stream, cosine, sine, seg_column = some(4)
    if first:
        small, ranks, w_qkv, w_out, out_grad = some(5)
    else:
        table, rk, hit, seats, turned, cross_from, qkv_from, out_from = some(8)
    w_gate, w_up, w_down = some(3)
    new_stream, layer_out, normed_a, queries, kv_out, attended, mixed, normed_b = some(8)
    rows_out, gate_out, up_out, gate_seat, quad = some(5)
    if first:
        table, rk_out, hit, seats, turned, qkv_out, out_out, qkv_next, out_next = some(9)
        (line_grads,) = some(1)
        small_land, rk, seat_all = some(3)
    else:
        (cross_to,) = some(1)
    (
        qkv,
        w_o,
        kv,
        projected,
        tokens,
        gates,
        weighted,
        gate_w,
        up_w,
        down_w,
        weight_sem,
        load_sem,
        chain_sem,
        quad_sem,
        send,
        recv,
        rows_in,
        gate_pre,
        up_pre,
        leave_sem,
    ) = some(20)
    if first:
        send_0, recv_0, send_1, recv_1, send_2, recv_2, send_3, recv_3 = some(8)
        send_4, recv_4, keep = some(3)
    else:
        cross_send, cross_recv, cross_keep = some(3)
    scratch = refs
    z, near = place()
    e = near["own"]
    line = lax.axis_size(DP)
    local_n = seats.shape[2]
    rows = stream.shape[0]
    experts_n = hit.shape[2]
    behind, ahead, has_behind, has_ahead = chain(z, e)

    weights = [
        pltpu.make_async_copy(src.at[layer], dst, weight_sem.at[i])
        for i, (src, dst) in enumerate(((w_gate, gate_w), (w_up, up_w), (w_down, down_w)))
    ]
    order = (behind, ahead, has_behind, has_ahead)
    greet(z, near, ("x", "y", "c"), line if first else None, order)
    if not first:
        cross = Gather([cross_from.at[0]], [cross_to], cross_send, cross_recv, z, near, line)
        cross.spread(1, cross_from, cross_keep)
    if first:
        g0 = Gather([small, ranks], [small_land, rk], send_0, recv_0, z, near, line)
        g1 = Gather([w_qkv.at[0]], [qkv], send_1, recv_1, z, near, line)
        g2 = Gather([w_out.at[0]], [w_o], send_2, recv_2, z, near, line)
        g3 = Gather(
            [w_qkv.at[1], w_out.at[1]], [qkv_next, out_next], send_3, recv_3, z, near, line
        )
        g4 = Gather([out_grad], [line_grads], send_4, recv_4, z, near, line, flat=True)
        local = [
            pltpu.make_async_copy(one, g.outs[i].at[z, e], keep.at[k])
            for k, (g, i, one) in enumerate(
                (g, i, one) for g in (g0, g1, g2, g3) for i, one in enumerate(g.ins)
            )
        ]
        g0.line_first()
        g0.first(z, g0.ins)
        g1.line_first()
        g1.first(z, g1.ins)
        for one in local:
            one.start()
        g0.arrivals(1, g0.take)
        g0.second(z)
        g0.arrivals(2, g0.take)
        g0.third(z)
        g0.arrivals(1, g0.second)
        g0.arrivals(3, g0.take)
        g1.arrivals(1, g1.take)
        g2.line_first()
        g2.first(z, g2.ins)
        g3.line_first()
        g0.arrivals(1, g0.third)
        g0.arrivals(2, g0.second)
        g1.second(z)
        g0.arrivals(2, g0.third)
        g0.arrivals(3, g0.second)
        g1.arrivals(2, g1.take)
        g0.arrivals(3, g0.third)
        g0.finish(z)
        for step in range(1, line):
            g0.arrivals(step, g0.finish)
        local[0].wait()
        local[1].wait()
        table[...] = jnp.transpose(small_land[...].reshape(-1, 128).astype(f32))
        g1.third(z)
        g1.arrivals(1, g1.second)
        for g in range(line):
            before = jnp.zeros((layers_n * experts_n, 1), f32)
            for d in range(8):
                lanes = pl.ds(d * rows, rows)
                rank = rk[g, d, pl.ds(0, layers_n * experts_n), :].astype(f32)
                seat_all[g, :, lanes] = jnp.where(rank > 0, rank + before, 0.0)
                for l in range(layers_n):
                    hit[l, g, :, lanes] = rank[l * experts_n : (l + 1) * experts_n]
                here = jnp.where(rank > 0, 1.0, 0.0)
                before = before + jnp.sum(here, axis=1, keepdims=True)
            for l in range(layers_n):
                for k in range(local_n):
                    row = pl.ds(l * experts_n + e * local_n + k, 1)
                    seats[l, g, pl.ds(k, 1), :] = seat_all[g, row, :]
        g1.arrivals(3, g1.take)
        wide = jnp.zeros((rows - layers_n * local_n, rows), f32)
        for d in range(8):
            lanes = pl.ds(d * rows, rows)
            mine = [seats[l, z, :, lanes] for l in range(layers_n)]
            turned[lanes, :] = jnp.transpose(jnp.concatenate(mine + [wide], axis=0))
        rk_out[...] = rk[...]
        g1.arrivals(1, g1.third)
        g1.arrivals(2, g1.second)
        g2.arrivals(1, g2.take)
        g1.arrivals(2, g1.third)
        g1.arrivals(3, g1.second)
        g2.second(z)
        g2.arrivals(2, g2.take)
        g1.arrivals(3, g1.third)
        g2.third(z)
        g1.finish(z)
        for step in range(1, line):
            g1.arrivals(step, g1.finish)
        local[2].wait()
        g2.arrivals(1, g2.second)
        g2.arrivals(3, g2.take)
    else:
        loads = [
            pltpu.make_async_copy(qkv_from, qkv, load_sem.at[0]),
            pltpu.make_async_copy(out_from, w_o, load_sem.at[1]),
        ]
        for one in loads:
            one.start()
    for one in weights:
        one.start()
    gain = 2 * experts_n + 2 * layer
    x = stream[...].astype(f32)
    normed_a[...] = normalized(x, table[pl.ds(gain, 1), :]).astype(bf16)
    if not first:
        loads[0].wait()
    width = queries.shape[1]
    projected[...] = mul(normed_a[...], qkv[...].reshape(width, -1))
    keys_n = KEY_VALUE_HEADS * HEAD_SIZE
    cos, sin = cosine[...], sine[...]
    for h in range(KEY_VALUE_HEADS):
        key = turn(projected[:, head_of(QUERY_HEADS + h)], cos, sin)
        kv[1, :, head_of(h)] = key.astype(bf16)
    kv[1, :, pl.ds(keys_n, keys_n)] = projected[:, pl.ds(width + keys_n, keys_n)].astype(bf16)

    def pass_on(target):
        return pltpu.make_async_remote_copy(
            src_ref=kv.at[1],
            dst_ref=kv.at[0],
            send_sem=chain_sem.at[0],
            recv_sem=chain_sem.at[1],
            device_id={DP: target[0], EX: target[1]},
            device_id_type=MESH,
        )

    @pl.when(has_ahead)
    def pass_ahead():
        pass_on(ahead).start()

    if first:
        g2.arrivals(1, g2.third)
        g2.arrivals(2, g2.second)
        g3.first(z, g3.ins)
    else:
        cross.spread(2, cross_from, cross_keep)
    for h in range(QUERY_HEADS):
        queries[:, head_of(h)] = turn(projected[:, head_of(h)], cos, sin).astype(bf16)
    allowed = allowed_keys(rk, layers_n * experts_n, z, e, behind, has_behind, seg_column[...])

    @pl.when(has_behind)
    def from_behind_here():
        pass_on(behind).wait_recv()

    @pl.when(jnp.logical_not(has_behind))
    def nobody_behind():
        kv[0] = jnp.zeros_like(kv[0])

    for h in range(QUERY_HEADS):
        group = h // (QUERY_HEADS // KEY_VALUE_HEADS)
        keys = kv[:, :, head_of(group)].reshape(2 * rows, HEAD_SIZE)
        values = kv[:, :, head_of(KEY_VALUE_HEADS + group)].reshape(2 * rows, HEAD_SIZE)
        probs = head_probs(queries[:, head_of(h)], keys, allowed).astype(bf16)
        attended[:, head_of(h)] = mul(probs, values).astype(bf16)
        if first and h == 3:
            g2.arrivals(2, g2.third)
            g2.arrivals(3, g2.second)
        if first and h == 7:
            g2.arrivals(3, g2.third)
            g3.arrivals(1, g3.take)
            g4.line_first()
        if not first and h == 8:
            cross.second(cross.plane_of(1))
    kv_out[...] = kv[...]
    if first:
        g2.finish(z)
        for step in range(1, line):
            g2.arrivals(step, g2.finish)
        local[3].wait()
    else:
        loads[1].wait()
    mixed[...] = x + mul(attended[...], w_o[...].reshape(width, -1))
    normed_b[...] = normalized(mixed[...], table[pl.ds(gain + 1, 1), :]).astype(bf16)

    one, two, three, four = plane_gather(normed_b, tokens, send, recv, near)
    one()
    if first:
        g3.second(z)
        g3.arrivals(2, g3.take)
    two()
    three()
    if not first:
        cross.second(cross.plane_of(2))
        cross.spread(3, cross_from, cross_keep)
        cross.third(cross.plane_of(1))
    if first:
        g3.third(z)
        g3.arrivals(1, g3.second)
        g3.arrivals(3, g3.take)
    four()
    quads = [
        pltpu.make_async_copy(tokens.at[near[name]], quad.at[i], quad_sem.at[i])
        for i, name in enumerate(QUAD)
    ]
    for copied in quads:
        copied.start()
    everyone = tokens[...].reshape(-1, width)
    router = table[pl.ds(layer * experts_n, experts_n), :].astype(bf16)
    gates[...] = masked_gates(mul(router, everyone, LAST), hit[layer, z] > 0)
    pick = seat_rows(seats[layer, z], number)
    for k in range(local_n):
        here = pl.ds(k * number, number)
        mine = gates[pl.ds(e * local_n + k, 1), :]
        gate_seat[here] = jnp.sum(
            pick[k * number : (k + 1) * number].astype(f32) * mine, axis=1, keepdims=True
        )
    rows_in[...] = mul(pick, everyone).astype(bf16)
    for copied in weights:
        copied.wait()
    if first:
        g3.arrivals(1, g3.third)
        g3.arrivals(2, g3.second)
        g4.arrivals(1, g4.carry)
    def expert(k, carry):
        here = pl.ds(pl.multiple_of(k * number, 32), number)
        x = rows_in[here]
        gate = mul(x, gate_w[k])
        up = mul(x, up_w[k])
        gate_pre[here] = gate
        up_pre[here] = up
        hidden = (gate * (1.0 / (1.0 + jnp.exp(-gate))) * up).astype(bf16)
        weighted[here] = (mul(hidden, down_w[k]) * gate_seat[here]).astype(bf16)
        return carry

    lax.fori_loop(0, local_n, expert, 0)
    leaving = [
        pltpu.make_async_copy(src, dst, leave_sem.at[i])
        for i, (src, dst) in enumerate(((rows_in, rows_out), (gate_pre, gate_out), (up_pre, up_out)))
    ]
    for copied in leaving:
        copied.start()
    if first:
        g3.arrivals(2, g3.third)
        g3.arrivals(3, g3.second)
        g4.arrivals(2, g4.carry)
        out_copies = [
            pltpu.make_async_copy(qkv, qkv_out, load_sem.at[0]),
            pltpu.make_async_copy(w_o, out_out, load_sem.at[1]),
        ]
        for copied in out_copies:
            copied.start()
    else:
        cross.third(cross.plane_of(2))
        cross.second(cross.plane_of(3))

    def make(name):
        d = near[name]
        lanes = pl.ds(pl.multiple_of(d * rows, rows), rows)
        mine = turned[lanes, pl.ds(layer * local_n, local_n)]
        scratch[0][d] = mul(seat_columns(mine, number), weighted[...]).astype(bf16)

    plane_sum(make, new_stream, mixed, scratch, near)
    layer_out[...] = new_stream[...].astype(bf16)

    for copied in quads + leaving:
        copied.wait()

    @pl.when(has_ahead)
    def passed_on():
        pass_on(ahead).wait_send()

    if first:
        g3.arrivals(3, g3.third)
        g4.arrivals(3, g4.carry)
        g3.finish(z)
        for step in range(1, line):
            g3.arrivals(step, g3.finish)
        for copied in local[4:] + out_copies:
            copied.wait()
        for g in (g0, g1, g2, g3, g4):
            g.line_done()
    else:
        cross.third(cross.plane_of(3))
        cross.spread_done(cross_from, cross_keep)


def layer_forward(layer, number, shapes, stream, tables, given, weights):
    layers_n, n_dp, n_expert, local_n, capacity = shapes
    first = layer == 0
    rows, width = stream.shape
    hidden = weights[0].shape[3]
    experts_n = local_n * n_expert
    seats_n = local_n * capacity
    keys_n = KEY_VALUE_HEADS * HEAD_SIZE
    group = n_expert * rows
    cut_rows = width // (n_dp * n_expert)
    shape = jax.ShapeDtypeStruct
    outs = [
        shape((rows, width), f32),
        shape((rows, width), bf16),
        shape((rows, width), bf16),
        shape((rows, width), bf16),
        shape((2, rows, 2 * keys_n), bf16),
        shape((rows, width), bf16),
        shape((rows, width), f32),
        shape((rows, width), bf16),
        shape((seats_n, width), bf16),
        shape((seats_n, hidden), f32),
        shape((seats_n, hidden), f32),
        shape((seats_n, 1), f32),
        shape((len(QUAD), rows, width), bf16),
    ]
    specs = [VMEM] * 8 + [HBM] * 3 + [VMEM, HBM]
    scratch = []
    full_qkv = (n_dp, n_expert, cut_rows, width + 2 * keys_n)
    full_out = (n_dp, n_expert, cut_rows, width)
    if first:
        rank_rows = given[1].shape[0]
        outs += [
            shape((128, width), f32),
            shape((n_dp, n_expert, rank_rows, rows), jnp.int32),
            shape((layers_n, n_dp, experts_n, group), f32),
            shape((layers_n, n_dp, local_n, group), f32),
            shape((group, 128), f32),
        ]
        outs += [shape(full_qkv, bf16), shape(full_out, bf16)] * 2
        outs.append(shape((n_dp, rows, width), bf16))
        specs += [VMEM] * 5 + [HBM] * 5
        scratch += [
            pltpu.VMEM((n_dp, n_expert, cut_rows, 128), bf16),
            pltpu.VMEM((n_dp, n_expert, rank_rows, rows), jnp.int32),
            pltpu.VMEM((n_dp, layers_n * experts_n, group), f32),
        ]
    else:
        outs.append(shape((n_dp, n_expert, rows, width), bf16))
        specs.append(HBM)
    scratch += [
        pltpu.VMEM(full_qkv, bf16),
        pltpu.VMEM(full_out, bf16),
        pltpu.VMEM((2, rows, 2 * keys_n), bf16),
        pltpu.VMEM((rows, width + 2 * keys_n), f32),
        pltpu.VMEM((n_expert, rows, width), bf16),
        pltpu.VMEM((experts_n, group), f32),
        pltpu.VMEM((seats_n, width), bf16),
        pltpu.VMEM((local_n, width, hidden), bf16),
        pltpu.VMEM((local_n, width, hidden), bf16),
        pltpu.VMEM((local_n, hidden, width), bf16),
        pltpu.SemaphoreType.DMA((3,)),
        pltpu.SemaphoreType.DMA((2,)),
        pltpu.SemaphoreType.DMA((2,)),
        pltpu.SemaphoreType.DMA((len(QUAD),)),
        pltpu.SemaphoreType.DMA((8,)),
        pltpu.SemaphoreType.DMA((8,)),
        pltpu.VMEM((seats_n, width), bf16),
        pltpu.VMEM((seats_n, hidden), f32),
        pltpu.VMEM((seats_n, hidden), f32),
        pltpu.SemaphoreType.DMA((3,)),
    ]
    if first:
        for count in (2, 1, 1, 2, 1):
            scratch += [pltpu.SemaphoreType.DMA((count, n_dp, KINDS)) for i in range(2)]
        scratch.append(pltpu.SemaphoreType.DMA((6,)))
    else:
        scratch += [pltpu.SemaphoreType.DMA((1, n_dp, KINDS)) for i in range(2)]
        scratch.append(pltpu.SemaphoreType.DMA((n_dp,)))
    given_specs = [HBM] * 5 if first else [VMEM] * 5 + [HBM] * 3
    return pl.pallas_call(
        partial(forward_kernel, layer, layers_n, capacity),
        out_shape=outs,
        in_specs=[VMEM] * 4 + given_specs + [HBM] * 3,
        out_specs=specs,
        scratch_shapes=scratch + sum_scratch(rows, width),
        compiler_params=settings(number),
        name="layer_forward",
    )(stream, *tables, *given, *weights)


def norm_back(value, gain, grad):
    scale = lax.rsqrt(jnp.mean(value * value, axis=-1, keepdims=True) + epsilon)
    unit = value * scale
    inner = grad * gain
    back = scale * (inner - unit * jnp.mean(inner * unit, axis=-1, keepdims=True))
    return back, jnp.sum(grad * unit, axis=0, keepdims=True)


def backward_kernel(layer, layers_n, number, *refs):
    refs = list(refs)

    def some(count):
        taken = refs[:count]
        del refs[:count]
        return taken

    grad_stream, stream, cosine, sine, seg_column = some(5)
    mixed, normed_b, queries, kv, gate_seat = some(5)
    table, rk, hit, seats, turned = some(5)
    row_sources = some(2)
    qkv_from, out_from, w_gate, w_up, w_down = some(5)
    gate_from, up_from = some(2)
    grad_out, grad_low, *leaving_to = some(6)
    dprojected, grad_attn, small = some(3)
    row_lands = some(2)
    (
        summed,
        qkv,
        w_o,
        datt,
        dkv,
        dkv_send,
        dkv_got,
        all_probs,
        tokens,
        back_rows,
        gate_w,
        up_w,
        down_w,
        weight_sem,
        load_sem,
        chain_sem,
        send,
        recv,
        row_send,
        row_recv,
        row_keep,
        gate_pre,
        up_pre,
        rows_grad,
        hidden_low,
        dgate_low,
        dup_low,
        leave_sem,
    ) = some(28)
    scratch = refs
    z, near = place()
    e = near["own"]
    line = lax.axis_size(DP)
    local_n = seats.shape[2]
    rows, width = stream.shape
    experts_n = hit.shape[2]
    behind, ahead, has_behind, has_ahead = chain(z, e)
    weights = [
        pltpu.make_async_copy(src.at[layer], dst, weight_sem.at[i])
        for i, (src, dst) in enumerate(((w_gate, gate_w), (w_up, up_w), (w_down, down_w)))
    ]
    loads = [
        pltpu.make_async_copy(qkv_from, qkv, load_sem.at[0]),
        pltpu.make_async_copy(out_from, w_o, load_sem.at[1]),
    ]
    weights += [
        pltpu.make_async_copy(gate_from, gate_pre, leave_sem.at[4]),
        pltpu.make_async_copy(up_from, up_pre, leave_sem.at[5]),
    ]
    grad_low[...] = grad_stream[...].astype(bf16)
    greet(z, near, ("x", "y", "c"), None, (behind, ahead, has_behind, has_ahead))

    spreads = [
        Gather([src], [dst], row_send.at[i], row_recv.at[i], 0, near, None)
        for i, (src, dst) in enumerate(zip(row_sources, row_lands))
    ]
    kept = [
        pltpu.make_async_copy(src, dst.at[0, e], row_keep.at[i])
        for i, (src, dst) in enumerate(zip(row_sources, row_lands))
    ]

    first, second, third, finish = plane_gather(grad_low, tokens, send, recv, near)
    first()
    for one in weights + loads:
        one.start()
    allowed = allowed_keys(rk, layers_n * experts_n, z, e, behind, has_behind, seg_column[...])
    per_group = QUERY_HEADS // KEY_VALUE_HEADS

    def keys_of(group):
        return kv[:, :, head_of(group)].reshape(2 * rows, HEAD_SIZE)

    def prepare(heads):
        for h in heads:
            all_probs[h] = head_probs(queries[:, head_of(h)], keys_of(h // per_group), allowed)

    prepare(range(0, 5))
    second()
    prepare(range(5, 9))
    third()
    spreads[0].first(0, spreads[0].ins)
    spreads[1].first(0, spreads[1].ins)
    for one in kept:
        one.start()
    prepare(range(9, QUERY_HEADS))
    finish()
    everyone = tokens[...].reshape(-1, width)
    picked = mul(seat_rows(seats[layer, z], number), everyone)
    back_rows[:, pl.ds(0, width)] = picked.astype(bf16)
    rows_grad[...] = (picked * gate_seat[...]).astype(bf16)
    for one in weights:
        one.wait()

    def expert(k, carry):
        here = pl.ds(pl.multiple_of(k * number, 32), number)
        gate, up = gate_pre[here], up_pre[here]
        raw = mul(back_rows[here, pl.ds(0, width)], down_w[k], LAST)
        sigmoid = 1.0 / (1.0 + jnp.exp(-gate))
        silu = gate * sigmoid
        hidden = (silu * up).astype(bf16)
        hidden_low[here] = hidden
        dgate_seat = jnp.sum(hidden.astype(f32) * raw, axis=1, keepdims=True)
        raw = raw * gate_seat[here]
        dgate = (raw * up * sigmoid * (1.0 + gate * (1.0 - sigmoid))).astype(bf16)
        dup = (raw * silu).astype(bf16)
        dgate_low[here] = dgate
        dup_low[here] = dup
        back_rows[here, pl.ds(0, width)] = (
            mul(dgate, gate_w[k], LAST) + mul(dup, up_w[k], LAST)
        ).astype(bf16)
        high = dgate_seat.astype(bf16).astype(f32)
        lane = lax.broadcasted_iota(jnp.int32, (number, 128), 1)
        mine = e * local_n + k
        back_rows[here, pl.ds(width, 128)] = jnp.where(
            lane == mine, high, jnp.where(lane == experts_n + mine, dgate_seat - high, 0.0)
        ).astype(bf16)
        return carry

    lax.fori_loop(0, local_n, expert, 0)
    leaving = [
        pltpu.make_async_copy(src, dst, leave_sem.at[i])
        for i, (src, dst) in enumerate(zip((rows_grad, hidden_low, dgate_low, dup_low), leaving_to))
    ]
    for one in leaving:
        one.start()

    def make(name):
        d = near[name]
        lanes = pl.ds(pl.multiple_of(d * rows, rows), rows)
        mine = turned[lanes, pl.ds(layer * local_n, local_n)]
        scratch[0][d] = mul(seat_columns(mine, number), back_rows[...]).astype(bf16)

    spreads[0].second(0)
    plane_sum(make, summed, None, scratch, near)
    spreads[0].third(0)
    spreads[1].second(0)

    over = ((0,), (0,))
    gain = 2 * experts_n + 2 * layer
    router = table[pl.ds(layer * experts_n, experts_n), :].astype(bf16)
    own_lanes = pl.ds(pl.multiple_of(e * rows, rows), rows)
    gates = masked_gates(mul(router, normed_b[...], LAST), hit[layer, z, :, own_lanes] > 0)
    turned_sum = jnp.transpose(summed[:, pl.ds(width, 128)])
    dgates = turned_sum[:experts_n] + turned_sum[experts_n : 2 * experts_n]
    inner = jnp.sum(gates * dgates, axis=0, keepdims=True)
    dlogits = (gates * (dgates - inner)).astype(bf16)
    small[...] = jnp.zeros_like(small)
    small[pl.ds(0, experts_n)] = mul(dlogits, normed_b[...])
    dnormed = summed[:, pl.ds(0, width)] + mul(dlogits, router, over)
    back, dgain = norm_back(mixed[...], table[pl.ds(gain + 1, 1), :], dnormed)
    small[pl.ds(experts_n + 1, 1)] = dgain
    dmixed = grad_stream[...].astype(f32) + back
    grad_out[...] = dmixed
    grad_attn[...] = dmixed.astype(bf16)

    loads[1].wait()
    datt[...] = mul(grad_attn[...], w_o[...].reshape(width, -1), LAST).astype(bf16)
    cos, sin = cosine[...], sine[...]
    scale = 1.0 / math.sqrt(HEAD_SIZE)
    for group in range(KEY_VALUE_HEADS):
        keys = keys_of(group)
        values = keys_of(KEY_VALUE_HEADS + group)
        dkeys = jnp.zeros((2 * rows, HEAD_SIZE), f32)
        dvalues = jnp.zeros((2 * rows, HEAD_SIZE), f32)
        for h in range(group * per_group, (group + 1) * per_group):
            query = queries[:, head_of(h)]
            probs = all_probs[h]
            given = datt[:, head_of(h)]
            dprobs = mul(given, values, LAST)
            delta = jnp.sum(probs * dprobs, axis=-1, keepdims=True)
            dscores = (probs * (dprobs - delta)).astype(bf16)
            dquery = mul(dscores, keys) * scale
            dprojected[:, head_of(h)] = turn(dquery, cos, -sin).astype(bf16)
            dkeys = dkeys + mul(dscores, query, over)
            dvalues = dvalues + mul(probs.astype(bf16), given, over)
        if group == 0:
            spreads[1].third(0)
        dkv[:, head_of(group)] = dkeys * scale
        dkv[:, head_of(KEY_VALUE_HEADS + group)] = dvalues
    dkv_send[...] = dkv[pl.ds(0, rows)].astype(bf16)

    def pass_on(target):
        return pltpu.make_async_remote_copy(
            src_ref=dkv_send,
            dst_ref=dkv_got,
            send_sem=chain_sem.at[0],
            recv_sem=chain_sem.at[1],
            device_id={DP: target[0], EX: target[1]},
            device_id_type=MESH,
        )

    @pl.when(has_behind)
    def pass_back():
        pass_on(behind).start()

    loads[0].wait()
    query_part = pl.ds(0, width)
    key_part = pl.ds(width, dkv.shape[1])
    weights_q = qkv[:, :, :, query_part].reshape(-1, width)
    dnormed = mul(dprojected[:, query_part], weights_q, LAST)

    @pl.when(has_ahead)
    def from_ahead_here():
        pass_on(ahead).wait_recv()
        dkv[pl.ds(rows, rows)] += dkv_got[...].astype(f32)

    for h in range(KEY_VALUE_HEADS):
        dkey = turn(dkv[pl.ds(rows, rows), head_of(h)], cos, -sin)
        dprojected[:, head_of(QUERY_HEADS + h)] = dkey.astype(bf16)
        dvalue = dkv[pl.ds(rows, rows), head_of(KEY_VALUE_HEADS + h)]
        dprojected[:, head_of(QUERY_HEADS + KEY_VALUE_HEADS + h)] = dvalue.astype(bf16)
    weights_kv = qkv[:, :, :, key_part].reshape(-1, dkv.shape[1])
    dnormed = dnormed + mul(dprojected[:, key_part], weights_kv, LAST)
    back, dgain = norm_back(stream[...].astype(f32), table[pl.ds(gain, 1), :], dnormed)
    small[pl.ds(experts_n, 1)] = dgain
    grad_out[...] += back

    @pl.when(has_behind)
    def passed_back():
        pass_on(behind).wait_send()

    for one in leaving:
        one.wait()

    for i in range(2):
        spreads[i].finish(0)
        kept[i].wait()


def layer_backward(layer, number, shapes, grads, stream, tables, saved, plan, weights):
    layers_n, n_dp, n_expert, local_n, capacity = shapes
    rows, width = stream.shape
    hidden = weights[-1].shape[1]
    experts_n = local_n * n_expert
    seats_n = local_n * capacity
    keys_n = KEY_VALUE_HEADS * HEAD_SIZE
    cut_rows = width // (n_dp * n_expert)
    shape = jax.ShapeDtypeStruct
    outs = [
        shape((rows, width), f32),
        shape((rows, width), bf16),
        shape((seats_n, width), bf16),
        shape((seats_n, hidden), bf16),
        shape((seats_n, hidden), bf16),
        shape((seats_n, hidden), bf16),
        shape((rows, width + 2 * keys_n), bf16),
        shape((rows, width), bf16),
        shape((SMALL, width), f32),
        shape((1, n_expert, rows, width), bf16),
        shape((1, n_expert, rows, width), bf16),
    ]
    scratch = [
        pltpu.VMEM((rows, width + 128), f32),
        pltpu.VMEM((n_dp, n_expert, cut_rows, width + 2 * keys_n), bf16),
        pltpu.VMEM((n_dp, n_expert, cut_rows, width), bf16),
        pltpu.VMEM((rows, width), bf16),
        pltpu.VMEM((2 * rows, 2 * keys_n), f32),
        pltpu.VMEM((rows, 2 * keys_n), bf16),
        pltpu.VMEM((rows, 2 * keys_n), bf16),
        pltpu.VMEM((QUERY_HEADS, rows, 2 * rows), f32),
        pltpu.VMEM((n_expert, rows, width), bf16),
        pltpu.VMEM((seats_n, width + 128), bf16),
        pltpu.VMEM((local_n, width, hidden), bf16),
        pltpu.VMEM((local_n, width, hidden), bf16),
        pltpu.VMEM((local_n, hidden, width), bf16),
        pltpu.SemaphoreType.DMA((3,)),
        pltpu.SemaphoreType.DMA((2,)),
        pltpu.SemaphoreType.DMA((2,)),
        pltpu.SemaphoreType.DMA((8,)),
        pltpu.SemaphoreType.DMA((8,)),
        pltpu.SemaphoreType.DMA((2, 1, 1, KINDS)),
        pltpu.SemaphoreType.DMA((2, 1, 1, KINDS)),
        pltpu.SemaphoreType.DMA((2,)),
        pltpu.VMEM((seats_n, hidden), f32),
        pltpu.VMEM((seats_n, hidden), f32),
        pltpu.VMEM((seats_n, width), bf16),
        pltpu.VMEM((seats_n, hidden), bf16),
        pltpu.VMEM((seats_n, hidden), bf16),
        pltpu.VMEM((seats_n, hidden), bf16),
        pltpu.SemaphoreType.DMA((6,)),
    ]
    return pl.pallas_call(
        partial(backward_kernel, layer, layers_n, capacity),
        out_shape=outs,
        in_specs=[VMEM] * 15 + [HBM] * 9,
        out_specs=[VMEM] * 2 + [HBM] * 4 + [VMEM] * 3 + [HBM] * 2,
        scratch_shapes=scratch + sum_scratch(rows, width + 128),
        compiler_params=settings(number),
        name="layer_backward",
    )(grads, stream, *tables, *saved, *plan, *weights)


class Sums:
    def __init__(self, ins, outs, held, send, recv, keep, z, near, line):
        self.ins, self.outs, self.held = ins, outs, held
        self.send, self.recv, self.keep = send, recv, keep
        self.z, self.near, self.line = z, near, line
        self.all = range(len(ins))

    def split(self, a):
        half = self.outs[a].shape[1] // 2
        return pl.ds(0, half), pl.ds(half, half)

    def move(self, a, j, name):
        part = self.ins[a]
        fromx, fromy, late, later, total, got = self.held[a]
        A, B = self.split(a)
        near = self.near
        kind, src, dst, to = {
            "xd": lambda: (0, part.at[j, near["d"], :, A], fromx.at[j, 0], "x"),
            "xx": lambda: (1, part.at[j, near["x"], :, A], fromx.at[j, 1], "x"),
            "yd": lambda: (2, part.at[j, near["d"], :, B], fromy.at[j, 0], "y"),
            "yy": lambda: (3, part.at[j, near["y"], :, B], fromy.at[j, 1], "y"),
            "ly": lambda: (4, late.at[j, 0], later.at[j, 0], "y"),
            "lx": lambda: (5, late.at[j, 1], later.at[j, 1], "x"),
            "up": lambda: (6, total.at[j], got.at[j], self.z + 1),
            "down": lambda: (7, total.at[j], got.at[j], self.z - 1),
        }[name]()
        if name == "down":
            slot = jnp.where(j == self.z - 1, self.line, j)
            dst = got.at[slot]
        return pltpu.make_async_remote_copy(
            src_ref=src,
            dst_ref=dst,
            send_sem=self.send.at[a, j, kind],
            recv_sem=self.recv.at[a, j, kind],
            device_id={DP: to} if kind >= 6 else {EX: near[to]},
            device_id_type=MESH,
        )

    def own_down(self, a):
        got = self.held[a][5]
        return pltpu.make_async_remote_copy(
            src_ref=got.at[self.line],
            dst_ref=got.at[self.line],
            send_sem=self.send.at[a, self.z, 7],
            recv_sem=self.recv.at[a, self.z, 7],
            device_id={DP: self.z},
            device_id_type=MESH,
        )

    def prepare(self, a, j):
        late, total = self.held[a][2], self.held[a][4]
        A, B = self.split(a)
        near, part = self.near, self.ins[a]
        return [
            pltpu.make_async_copy(src, dst, self.keep.at[a, j, i])
            for i, (src, dst) in enumerate(
                (
                    (part.at[j, near["y"], :, A], late.at[j, 0]),
                    (part.at[j, near["x"], :, B], late.at[j, 1]),
                    (part.at[j, near["own"]], total.at[j]),
                )
            )
        ]

    def at(self, step, act):
        if step == 0:
            act(self.z, 0)
            return

        @pl.when(self.z + step <= self.line - 1)
        def above():
            act(self.z + step, 1)

        @pl.when(self.z - step >= 0)
        def below():
            act(self.z - step, -1)

    def first(self, j, way):
        for a in self.all:
            for name in ("xd", "yd", "xx", "yy"):
                self.move(a, j, name).start()
            for one in self.prepare(a, j):
                one.start()

    def second(self, j, way):
        for a in self.all:
            fromx, fromy, late = self.held[a][:3]
            ready = self.prepare(a, j)
            ready[0].wait()
            self.move(a, j, "xd").wait_recv()
            late[j, 0] = (late[j, 0].astype(f32) + fromx[j, 0].astype(f32)).astype(bf16)
            self.move(a, j, "ly").start()
            ready[1].wait()
            self.move(a, j, "yd").wait_recv()
            late[j, 1] = (late[j, 1].astype(f32) + fromy[j, 0].astype(f32)).astype(bf16)
            self.move(a, j, "lx").start()

    def third(self, j, way):
        for a in self.all:
            fromx, fromy, late, later, total, got = self.held[a]
            for name in ("xx", "yy", "ly", "lx"):
                self.move(a, j, name).wait_recv()
            self.prepare(a, j)[2].wait()
            for side, (columns, here) in enumerate(zip(self.split(a), (fromx, fromy))):
                value = (
                    total[j, :, columns].astype(f32)
                    + here[j, 1].astype(f32)
                    + later[j, side].astype(f32)
                )
                if way == 0:
                    self.outs[a][:, columns] = value
                else:
                    total[j, :, columns] = value.astype(bf16)
            if way == 1:

                @pl.when(self.z > 0)
                def more_up():
                    self.move(a, j, "up").wait_recv()
                    total[j] = (total[j].astype(f32) + got[j].astype(f32)).astype(bf16)

                self.move(a, j, "up").start()
            elif way == -1:

                @pl.when(self.z < self.line - 1)
                def more_down():
                    self.move(a, j, "down").wait_recv()
                    total[j] = (total[j].astype(f32) + got[j].astype(f32)).astype(bf16)

                self.move(a, j, "down").start()
            else:

                @pl.when(self.z > 0)
                def end_up():
                    self.move(a, j, "up").wait_recv()
                    self.outs[a][...] += got[j].astype(f32)

                @pl.when(self.z < self.line - 1)
                def end_down():
                    self.own_down(a).wait_recv()
                    self.outs[a][...] += got[self.line].astype(f32)

    def finish(self, j, way):
        for a in self.all:
            for name in ("xd", "yd", "xx", "yy", "lx", "ly"):
                self.move(a, j, name).wait_send()
            if way == 1:
                self.move(a, j, "up").wait_send()
            elif way == -1:
                self.move(a, j, "down").wait_send()


def sums_scratch(shapes, line):
    scratch = []
    for rows, columns in shapes:
        half = columns // 2
        scratch += [pltpu.VMEM((line, 2, rows, half), bf16) for i in range(4)]
        scratch += [
            pltpu.VMEM((line, rows, columns), bf16),
            pltpu.VMEM((line + 1, rows, columns), bf16),
        ]
    return scratch + [
        pltpu.SemaphoreType.DMA((len(shapes), line, 8)),
        pltpu.SemaphoreType.DMA((len(shapes), line, 8)),
        pltpu.SemaphoreType.DMA((len(shapes), line, 3)),
    ]


def from_behind(value, axis, steps):
    count = lax.axis_size(axis)
    leading, last = (max(0, -steps), min(count, count - steps))
    return lax.ppermute(value, axis, [(source, source + steps) for source in range(leading, last)])


def from_sibling(value):
    count = lax.axis_size(EX)
    return lax.ppermute(value, EX, [(s, s + 1 - 2 * (s % 2)) for s in range(count)])


def rms_norm(stream, gain_row):
    return (
        stream * lax.rsqrt(jnp.mean(stream * stream, axis=-1, keepdims=True) + epsilon) * gain_row
    )


def rotary_tables(token_positions):
    half_dim = HEAD_SIZE // 2
    steps_up = jnp.arange(half_dim).astype(f32)
    frequency = jnp.exp(steps_up * (-2.0 * math.log(rope_base) / HEAD_SIZE))
    angles = token_positions.astype(f32)[:, None] * frequency[None, :]
    return jnp.cos(angles)[:, None, :], jnp.sin(angles)[:, None, :]


def apply_rotary(heads_in, cosine, sine_part):
    half_dim = heads_in.shape[-1] // 2
    first_half = heads_in[..., :half_dim]
    second_half = heads_in[..., half_dim:]
    return jnp.concatenate(
        [
            first_half * cosine - second_half * sine_part,
            second_half * cosine + first_half * sine_part,
        ],
        axis=-1,
    )


def gated_unit(gate_pre, up_pre):
    return jax.nn.silu(gate_pre) * up_pre


def masked_scores(query_rows, gathered_keys, allowed):
    token_rows = query_rows.shape[0]
    grouped_queries = query_rows.reshape(
        token_rows, KEY_VALUE_HEADS, QUERY_HEADS // KEY_VALUE_HEADS, HEAD_SIZE
    )
    score_scale = 1.0 / math.sqrt(HEAD_SIZE)
    scores = (
        jnp.einsum(
            "tkgd,skd->kgts", grouped_queries, gathered_keys, preferred_element_type=f32
        )
        * score_scale
    )
    return (jnp.where(allowed, scores, masked_score), grouped_queries)


def rank_table(routes, pair_order, experts_n):
    layers_n, token_rows, topk_n = routes.shape
    chosen = jnp.swapaxes(routes, 1, 2)
    order = jnp.swapaxes(pair_order.reshape(layers_n, token_rows, topk_n), 1, 2)
    ids = jnp.arange(experts_n, dtype=jnp.int32)[None, :, None]
    none = token_rows * topk_n
    place_of = jnp.full((layers_n, experts_n, token_rows), none, jnp.int32)
    for k in range(topk_n):
        place_of = jnp.where(chosen[:, k][:, None, :] == ids, order[:, k][:, None, :], place_of)
    smaller = (place_of[:, :, :, None] < place_of[:, :, None, :]).astype(jnp.int32)
    return jnp.where(place_of < none, jnp.sum(smaller, axis=2) + 1, 0)


def dense_gates(logits, mask):
    top = jnp.max(jnp.where(mask, logits, masked_score), axis=0, keepdims=True)
    powers = jnp.where(mask, jnp.exp(jnp.where(mask, logits - top, 0.0)), 0.0)
    return powers / jnp.sum(powers, axis=0, keepdims=True)


def local_chips(
    tokens,
    w_qkv,
    w_out,
    w_router,
    norm_gains,
    w_gate,
    w_up,
    w_down,
    out_grad,
    segment_ids,
    routes,
    pair_order,
):
    token_rows = tokens.shape[0]
    layers_n = w_qkv.shape[0]
    topk_n = routes.shape[2]
    n_expert = lax.axis_size(EX)
    n_dp = lax.axis_size(DP)
    local_n = w_gate.shape[1]
    experts_n = local_n * n_expert
    capacity = 9 * n_expert * token_rows * topk_n // (8 * experts_n)
    shapes = (layers_n, n_dp, n_expert, local_n, capacity)
    positions = lax.axis_index(EX) * token_rows + jnp.arange(token_rows, dtype=jnp.int32)
    cosine, sine = rotary_tables(positions)
    tables = (
        jnp.concatenate([cosine, cosine], axis=-1)[:, 0],
        jnp.concatenate([-sine, sine], axis=-1)[:, 0],
        segment_ids[:, None],
    )
    ranks = rank_table(routes, pair_order, experts_n).reshape(layers_n * experts_n, token_rows)
    ranks = jnp.concatenate([ranks, segment_ids[None], jnp.zeros((7, token_rows), jnp.int32)])
    small = jnp.concatenate(
        [w_router[l] for l in range(layers_n)]
        + [jnp.swapaxes(norm_gains.reshape(2 * layers_n, -1), 0, 1)],
        axis=1,
    )
    small = jnp.pad(small, ((0, 0), (0, 128 - small.shape[1])))
    experts = (w_gate, w_up, w_down)

    def along_line(rows):
        return lax.all_gather(rows, DP, axis=0)

    saved, outputs, normed_all, streams = [], [], [], [tokens]
    for l in range(layers_n):
        given = (small, ranks, w_qkv, w_out, out_grad)
        if l > 0:
            given = (*plan, line_grads, *full[l])
        results = layer_forward(l, 1 + l, shapes, streams[l], tables, given, experts)
        if l == 0:
            plan = results[13:18]
            full = [results[18:20], results[20:22]]
            line_grads = results[22]
        else:
            grads_all = [results[13]]
        streams.append(results[0])
        outputs.append(results[1])
        saved.append(results[2:12])
        normed_all.append(along_line(results[12]))

    grads = out_grad
    owns, smalls = [None] * layers_n, [None] * layers_n
    row_sources, column_sources = [None] * layers_n, [None] * layers_n
    for l in reversed(range(layers_n)):
        normed_a, queries, kv, attended, mixed, normed_b, rows_in = saved[l][:7]
        gate_pre, up_pre, gate_seat = saved[l][7:]
        kept = (mixed, normed_b, queries, kv, gate_seat)
        sources = (normed_a, attended, *full[l], *experts, gate_pre, up_pre)
        results = layer_backward(l, 4 + l, shapes, grads, streams[l], tables, kept, plan, sources)
        grads, own_shard = results[:2]
        owns[l] = (rows_in, *results[2:6])
        column_sources[l] = results[6:8]
        smalls[l] = results[8]
        row_sources[l] = results[9:11]
    grad_experts, (small_sum, grad_qkv, grad_out) = tail(
        capacity,
        8,
        normed_all,
        grads_all,
        own_shard,
        (plan[0], plan[2], plan[3]),
        experts,
        owns,
        row_sources,
        column_sources,
        smalls,
    )
    small_sum = small_sum[:, :128] + small_sum[:, 128:]
    small_sum = small_sum[:, : layers_n * SMALL].reshape(-1, layers_n, SMALL)
    small_sum = jnp.swapaxes(small_sum, 0, 1)
    grad_router = small_sum[:, :, :experts_n]
    grad_gains = jnp.swapaxes(small_sum[:, :, experts_n : experts_n + 2], 1, 2)
    return (
        jnp.stack(outputs),
        grads,
        grad_qkv,
        grad_out,
        grad_router,
        grad_gains,
        *grad_experts,
    )


def local(
    tokens,
    w_qkv,
    w_out,
    w_router,
    norm_gains,
    w_gate,
    w_up,
    w_down,
    out_grad,
    segment_ids,
    routes,
    pair_order,
):
    token_rows = tokens.shape[0]
    layers_n = w_qkv.shape[0]
    topk_n = routes.shape[2]
    n_expert = lax.axis_size(EX)
    n_dp = lax.axis_size(DP)
    expert_here = lax.axis_index(EX)
    dp_here = lax.axis_index(DP)
    device_here = dp_here * n_expert + expert_here
    local_n = w_gate.shape[1]
    experts_n = local_n * n_expert
    capacity = 9 * n_expert * token_rows * topk_n // (8 * experts_n)
    group_rows = n_expert * token_rows
    query_width = QUERY_HEADS * HEAD_SIZE
    key_width = KEY_VALUE_HEADS * HEAD_SIZE
    score_scale = 1.0 / math.sqrt(HEAD_SIZE)
    token_positions = expert_here * token_rows + jnp.arange(token_rows, dtype=jnp.int32)
    cosine, sine_part = rotary_tables(token_positions)
    seg_prev = from_behind(segment_ids, everywhere, 1)
    has_prev = device_here > 0
    row_index = jnp.arange(token_rows)
    own_mask = (segment_ids[None, :] == segment_ids[:, None]) & (
        row_index[None, :] <= row_index[:, None]
    )
    prev_mask = (seg_prev[None, :] == segment_ids[:, None]) & has_prev
    allowed = jnp.concatenate([prev_mask, own_mask], axis=1)

    ranks = rank_table(routes, pair_order, experts_n)
    small = jnp.concatenate(
        [w_router[l] for l in range(layers_n)]
        + [jnp.swapaxes(norm_gains.reshape(2 * layers_n, -1), 0, 1)],
        axis=1,
    )
    small = jnp.pad(small, ((0, 0), (0, 128 - small.shape[1])))
    small_full, ranks_full, qkv_0, out_0 = [
        lax.all_gather(one, everywhere, axis=0)
        for one in (small, ranks.reshape(layers_n * experts_n, token_rows), w_qkv[0], w_out[0])
    ]
    qkv_fulls = [qkv_0.reshape(D, -1)]
    out_fulls = [out_0.reshape(query_width, D)]
    for layer_idx in range(1, layers_n):
        qkv_fulls.append(lax.all_gather(w_qkv[layer_idx], everywhere, axis=0, tiled=True))
        out_fulls.append(lax.all_gather(w_out[layer_idx], everywhere, axis=0, tiled=True))
    small_full = small_full.reshape(D, 128)
    gains = jnp.swapaxes(
        small_full[:, layers_n * experts_n : layers_n * (experts_n + 2)], 0, 1
    ).astype(f32)
    routers = [small_full[:, l * experts_n : (l + 1) * experts_n] for l in range(layers_n)]
    routers_turned = [jnp.swapaxes(router, 0, 1) for router in routers]
    ranks_full = ranks_full.reshape(n_dp, n_expert, layers_n, experts_n, token_rows)
    ranks_full = lax.dynamic_slice_in_dim(ranks_full, dp_here, 1, 0)
    groups = ranks_full.shape[0]
    hit_all = jnp.transpose(ranks_full > 0, (2, 0, 3, 1, 4)).reshape(
        layers_n, groups, experts_n, group_rows
    )
    mine = lax.dynamic_slice_in_dim(ranks_full, expert_here * local_n, local_n, 3)
    counts = jnp.sum((mine > 0).astype(jnp.int32), axis=-1)
    before = jnp.cumsum(counts, axis=1) - counts
    seats = jnp.where(mine > 0, before[..., None] + mine, 0)
    seats = jnp.transpose(seats, (2, 0, 3, 1, 4)).reshape(layers_n, groups, local_n, group_rows)
    seat_ids = jnp.arange(1, capacity + 1, dtype=jnp.int32)

    def own_of(array):
        return lax.dynamic_index_in_dim(array, 0, 0, keepdims=False)

    def seat_map(l):
        return (seats[l][:, :, None, :] == seat_ids[:, None]).astype(bf16)

    def gates_of(normed_rows, l, hit):
        logits = jnp.einsum("de,td->et", routers[l], normed_rows, preferred_element_type=f32)
        return dense_gates(logits, hit)

    own_hit = [(ranks[l] > 0) for l in range(layers_n)]

    stream = tokens.astype(f32)
    saved_layers = []
    outputs = []
    for l in range(layers_n):
        qkv_full, out_full = qkv_fulls[l], out_fulls[l]
        normed_a = rms_norm(stream, gains[2 * l]).astype(bf16)
        projected_output = jnp.dot(normed_a, qkv_full, preferred_element_type=f32)
        query_rows = apply_rotary(
            projected_output[:, :query_width].reshape(token_rows, QUERY_HEADS, HEAD_SIZE),
            cosine,
            sine_part,
        ).astype(bf16)
        key_own = apply_rotary(
            projected_output[:, query_width : query_width + key_width].reshape(
                token_rows, KEY_VALUE_HEADS, HEAD_SIZE
            ),
            cosine,
            sine_part,
        ).astype(bf16)
        value_own = (
            projected_output[:, query_width + key_width :]
            .reshape(token_rows, KEY_VALUE_HEADS, HEAD_SIZE)
            .astype(bf16)
        )
        key_prev, value_prev = from_behind((key_own, value_own), everywhere, 1)
        gathered_keys = jnp.concatenate([key_prev, key_own], axis=0)
        gathered_values = jnp.concatenate([value_prev, value_own], axis=0)
        scores, grouped_queries = masked_scores(query_rows, gathered_keys, allowed)
        top_score = jnp.max(scores, axis=-1, keepdims=True)
        exp_scores = jnp.exp(scores - top_score)
        row_total = jnp.sum(exp_scores, axis=-1, keepdims=True)
        prob_low = (exp_scores / row_total).astype(bf16)
        log_total = top_score + jnp.log(row_total)
        attended = (
            jnp.einsum("kgts,skd->tkgd", prob_low, gathered_values, preferred_element_type=f32)
            .reshape(token_rows, query_width)
            .astype(bf16)
        )
        mixed_sum = stream + jnp.dot(attended, out_full, preferred_element_type=f32)
        normed_b = rms_norm(mixed_sum, gains[2 * l + 1]).astype(bf16)

        if True:
            kept = {}
            group_normed = lax.all_gather(normed_b, EX, axis=0, tiled=True)
            kept["normed_all"] = group_normed[None]
            seat_own = own_of(seat_map(l))
            gates_own = gates_of(group_normed, l, own_of(hit_all[l]))
            gates_own = lax.dynamic_slice_in_dim(gates_own, expert_here * local_n, local_n, 0)
            gate_seat = jnp.sum(seat_own.astype(f32) * gates_own[:, None, :], axis=-1)
            expert_in = jnp.einsum(
                "est,td->esd", seat_own, group_normed, preferred_element_type=f32
            ).astype(bf16)
            gate_pre = jnp.einsum("esd,edf->esf", expert_in, w_gate[l], preferred_element_type=f32)
            up_pre = jnp.einsum("esd,edf->esf", expert_in, w_up[l], preferred_element_type=f32)
            hidden = gated_unit(gate_pre, up_pre).astype(bf16)
            expert_out = jnp.einsum("esf,efd->esd", hidden, w_down[l], preferred_element_type=f32)
            weighted = (expert_out * gate_seat[..., None]).astype(bf16)
            branch_part = jnp.einsum("est,esd->td", seat_own, weighted, preferred_element_type=f32)
            new_stream = mixed_sum + lax.psum_scatter(
                branch_part, EX, scatter_dimension=0, tiled=True
            )
        saved_layers.append(
            {
                "stream_in": stream,
                "normed_a": normed_a,
                "queries": query_rows,
                "key_all": gathered_keys,
                "value_all": gathered_values,
                "log_total": log_total,
                "attended": attended,
                "mixed_sum": mixed_sum,
                "normed_b": normed_b,
            }
            | kept
        )
        outputs.append(new_stream)
        stream = new_stream

    grad_stream = out_grad.astype(f32)
    weight_parts = [None] * layers_n
    expert_parts = [None] * layers_n
    owns = [None] * layers_n
    for l in reversed(range(layers_n)):
        record = saved_layers[l]
        qkv_full, out_full = qkv_fulls[l], out_fulls[l]
        grad_low = grad_stream.astype(bf16)
        if True:
            normed_all = record["normed_all"]
            grad_all = lax.all_gather(grad_low, EX, axis=0, tiled=True)[None]
            seat_all = seat_map(l)
            gates_all = jax.vmap(lambda rows, hit: gates_of(rows, l, hit))(normed_all, hit_all[l])
            gates_mine = lax.dynamic_slice_in_dim(gates_all, expert_here * local_n, local_n, 1)
            gate_seat = jnp.sum(seat_all.astype(f32) * gates_mine[:, :, None, :], axis=-1)
            rows_in = jnp.einsum(
                "gest,gtd->egsd", seat_all, normed_all, preferred_element_type=f32
            ).astype(bf16)
            rows_grad = jnp.einsum(
                "gest,gtd->egsd", seat_all, grad_all, preferred_element_type=f32
            ).astype(bf16)
            gate_seat = jnp.swapaxes(gate_seat, 0, 1)[..., None]
            gate_pre = jnp.einsum("egsd,edf->egsf", rows_in, w_gate[l], preferred_element_type=f32)
            up_pre = jnp.einsum("egsd,edf->egsf", rows_in, w_up[l], preferred_element_type=f32)
            dhidden_raw = jnp.einsum(
                "egsd,efd->egsf", rows_grad, w_down[l], preferred_element_type=f32
            )
            hidden, gate_pull = jax.vjp(gated_unit, gate_pre, up_pre)
            hidden_low = hidden.astype(bf16)
            dgate_pre, dup_pre = gate_pull(dhidden_raw * gate_seat)
            dgate_low = dgate_pre.astype(bf16)
            dup_low = dup_pre.astype(bf16)
            dgate_seat = jnp.sum(hidden_low.astype(f32) * dhidden_raw, axis=-1)
            rows_grad = (rows_grad.astype(f32) * gate_seat).astype(bf16)

        def by_expert(array):
            return array.reshape(local_n, -1, array.shape[-1])

        def outer(one, other):
            return jnp.einsum(
                "esa,esb->eab", by_expert(one), by_expert(other), preferred_element_type=f32
            )

        if True:
            grad_gate_l = outer(rows_in, dgate_low)
            grad_up_l = outer(rows_in, dup_low)
            grad_down_l = outer(hidden_low, rows_grad)
            grad_gate_l = lax.psum_scatter(
                grad_gate_l.astype(bf16), DP, scatter_dimension=1, tiled=True
            ).astype(f32)
            grad_up_l = lax.psum_scatter(
                grad_up_l.astype(bf16), DP, scatter_dimension=1, tiled=True
            ).astype(f32)
            grad_down_l = lax.psum_scatter(
                grad_down_l.astype(bf16), DP, scatter_dimension=2, tiled=True
            ).astype(f32)
            expert_parts[l] = (grad_gate_l, grad_up_l, grad_down_l)

        if True:
            dexpert_in = (
                jnp.einsum("egsf,edf->egsd", dgate_low, w_gate[l], preferred_element_type=f32)
                + jnp.einsum("egsf,edf->egsd", dup_low, w_up[l], preferred_element_type=f32)
            ).astype(bf16)
            back_part = jnp.einsum(
                "gest,egsd->td", seat_all, dexpert_in, preferred_element_type=f32
            )
            dgates_part = jnp.sum(
                seat_all[0].astype(f32) * dgate_seat[:, 0, :, None], axis=1
            )
            mine = expert_here * local_n + jnp.arange(local_n, dtype=jnp.int32)
            lane = jnp.arange(experts_n, dtype=jnp.int32)
            dgates_part = jnp.sum(
                jnp.where(mine[:, None, None] == lane, dgates_part[..., None], 0.0), axis=0
            )
            dnormed_b, dgates = [
                lax.psum_scatter(part, EX, scatter_dimension=0, tiled=True)
                for part in (back_part, dgates_part)
            ]
        gates_token = gates_of(record["normed_b"], l, own_hit[l]).T
        dlogits = (
            gates_token * (dgates - jnp.sum(gates_token * dgates, axis=1, keepdims=True))
        ).astype(bf16)
        dnormed_b = dnormed_b + jnp.einsum(
            "te,de->td", dlogits, routers[l], preferred_element_type=f32
        )
        unused_norm, norm_pull = jax.vjp(rms_norm, record["mixed_sum"], gains[2 * l + 1])
        dmixed_part, dgain_b = norm_pull(dnormed_b)
        dmixed = grad_stream + dmixed_part
        grad_attn = dmixed.astype(bf16)
        attended_gradient = jnp.einsum(
            "td,qd->tq", grad_attn, out_full, preferred_element_type=f32
        ).astype(bf16)
        gathered_keys = record["key_all"]
        gathered_values = record["value_all"]
        scores, grouped_queries = masked_scores(record["queries"], gathered_keys, allowed)
        prob_float = jnp.exp(scores - record["log_total"])
        prob_low = prob_float.astype(bf16)
        grouped_gradient = attended_gradient.reshape(
            token_rows, KEY_VALUE_HEADS, QUERY_HEADS // KEY_VALUE_HEADS, HEAD_SIZE
        )
        dvalue_all = jnp.einsum(
            "kgts,tkgd->skd", prob_low, grouped_gradient, preferred_element_type=f32
        )
        dprobs = jnp.einsum(
            "tkgd,skd->kgts", grouped_gradient, gathered_values, preferred_element_type=f32
        )
        delta_row = jnp.sum(prob_float * dprobs, axis=-1, keepdims=True)
        dscores = (prob_float * (dprobs - delta_row)).astype(bf16)
        dqueries = (
            jnp.einsum(
                "kgts,skd->tkgd", dscores, gathered_keys, preferred_element_type=f32
            ).reshape(token_rows, QUERY_HEADS, HEAD_SIZE)
            * score_scale
        )
        dkey_all = (
            jnp.einsum("kgts,tkgd->skd", dscores, grouped_queries, preferred_element_type=f32)
            * score_scale
        )
        dkey_next, dvalue_next = from_behind(
            (dkey_all[:token_rows].astype(bf16), dvalue_all[:token_rows].astype(bf16)),
            everywhere,
            -1,
        )
        dkey_own = dkey_all[token_rows:] + dkey_next.astype(f32)
        dvalue_own = dvalue_all[token_rows:] + dvalue_next.astype(f32)
        dq_raw = apply_rotary(dqueries, cosine, -sine_part)
        dk_raw = apply_rotary(dkey_own, cosine, -sine_part)
        dprojected = jnp.concatenate(
            [
                dq_raw.reshape(token_rows, query_width),
                dk_raw.reshape(token_rows, key_width),
                dvalue_own.reshape(token_rows, key_width),
            ],
            axis=1,
        ).astype(bf16)
        dnormed_a = jnp.einsum("tq,dq->td", dprojected, qkv_full, preferred_element_type=f32)
        unused_first, first_pull = jax.vjp(rms_norm, record["stream_in"], gains[2 * l])
        dstream_part, dgain_a = first_pull(dnormed_a)
        grad_stream = dmixed + dstream_part

        small_grad = jnp.concatenate(
            [
                jnp.einsum("td,te->de", record["normed_b"], dlogits, preferred_element_type=f32),
                dgain_a[:, None],
                dgain_b[:, None],
            ],
            axis=1,
        )
        normed_a, attended = record["normed_a"], record["attended"]
        grad_qkv_l = jnp.einsum("td,tq->dq", normed_a, dprojected, preferred_element_type=f32)
        grad_out_l = jnp.einsum("tq,td->qd", attended, grad_attn, preferred_element_type=f32)
        weight_parts[l] = (grad_qkv_l, grad_out_l, small_grad)

    small_grads = jnp.concatenate([weight_parts[l][2] for l in range(layers_n)], axis=1)
    if True:

        def scatter(array):
            return lax.psum_scatter(array, everywhere, scatter_dimension=0, tiled=True)

        small_sum = scatter(small_grads)
        grad_qkv = jnp.stack([scatter(weight_parts[l][0]) for l in range(layers_n)])
        grad_out = jnp.stack([scatter(weight_parts[l][1]) for l in range(layers_n)])
    wide = experts_n + 2
    grad_router = jnp.stack(
        [small_sum[:, l * wide : l * wide + experts_n] for l in range(layers_n)]
    )
    grad_gains = jnp.stack(
        [
            jnp.swapaxes(small_sum[:, l * wide + experts_n : (l + 1) * wide], 0, 1)
            for l in range(layers_n)
        ]
    )
    if True:
        grad_gate, grad_up, grad_down = [
            jnp.stack([expert_parts[l][member] for l in range(layers_n)]) for member in range(3)
        ]
    layer_outs = jnp.stack(outputs).astype(bf16)
    return (
        layer_outs,
        grad_stream,
        grad_qkv,
        grad_out,
        grad_router,
        grad_gains,
        grad_gate,
        grad_up,
        grad_down,
    )


def solution(mesh):
    sizes = (mesh.shape[DP], mesh.shape[EX])
    return jax.shard_map(
        local_chips if sizes == (4, 8) else local,
        mesh=mesh,
        in_specs=(
            P((DP, EX), None),
            P(None, (DP, EX), None),
            P(None, (DP, EX), None),
            P(None, (DP, EX), None),
            P(None, None, (DP, EX)),
            P(None, EX, None, None),
            P(None, EX, None, None),
            P(None, EX, None, None),
            P((DP, EX), None),
            P((DP, EX)),
            P(None, (DP, EX), None),
            P(None, (DP, EX), None),
        ),
        out_specs=(
            P(None, (DP, EX), None),
            P((DP, EX), None),
            P(None, (DP, EX), None),
            P(None, (DP, EX), None),
            P(None, (DP, EX), None),
            P(None, None, (DP, EX)),
            P(None, EX, DP, None),
            P(None, EX, DP, None),
            P(None, EX, None, DP),
        ),
        check_vma=False,
    )
```

```python
from functools import partial
import math

import jax
import jax.numpy as jnp
from jax import lax
from jax.experimental import pallas as pl
from jax.experimental.pallas import tpu as pltpu
from jax.sharding import PartitionSpec as P

D = 1536
QUERY_HEADS = 12
KEY_VALUE_HEADS = 2
HEAD_SIZE = 128
MESH = pl.DeviceIdType.MESH
DP, EX = "dp", "expert"
ANY = pl.ANY
bf16 = jnp.bfloat16
f32 = jnp.float32

epsilon = 1e-06
rope_base = 1000000.0
masked_score = -1e30
everywhere = (DP, EX)


def place():
    z = lax.axis_index(DP)
    e = lax.axis_index(EX)
    y, x, c = e // 4, (e // 2) % 2, e % 2
    near = {
        "own": e,
        "x": y * 4 + (1 - x) * 2 + c,
        "y": (1 - y) * 4 + x * 2 + c,
        "d": (1 - y) * 4 + (1 - x) * 2 + c,
        "c": y * 4 + x * 2 + (1 - c),
        "cx": y * 4 + (1 - x) * 2 + (1 - c),
        "cy": (1 - y) * 4 + x * 2 + (1 - c),
        "cd": (1 - y) * 4 + (1 - x) * 2 + (1 - c),
    }
    return z, near


def greet(z, near, plane, line, order=None):
    barrier = pltpu.get_barrier_semaphore()

    def tell(**target):
        pl.semaphore_signal(barrier, inc=1, device_id=target, device_id_type=MESH)

    for name in plane:
        tell(**{EX: near[name]})
    count = len(plane)
    links = []
    if line is not None:
        links += [(z < line - 1, {DP: z + 1}), (z > 0, {DP: z - 1})]
    if order is not None:
        behind, ahead, has_behind, has_ahead = order
        links += [
            (has_behind, {DP: behind[0], EX: behind[1]}),
            (has_ahead, {DP: ahead[0], EX: ahead[1]}),
        ]
    for there, target in links:

        @pl.when(there)
        def one():
            tell(**target)

        count = count + jnp.where(there, 1, 0)
    pl.semaphore_wait(barrier, count)


def halves(rows, columns):
    if rows % 32 == 0:
        return ((0, rows // 2), (0, columns)), ((rows // 2, rows // 2), (0, columns))
    if columns % 256 == 0:
        return ((0, rows), (0, columns // 2)), ((0, rows), (columns // 2, columns // 2))
    return ((0, 16), (0, columns)), ((16, rows - 16), (0, columns))


def cut(ref, part):
    (row, rows), (column, columns) = part
    return ref.at[pl.ds(row, rows), pl.ds(column, columns)]


KINDS = 10
SMALL = 24
BLOCK = 512
QUAD = ("own", "x", "y", "d")
BESIDE = ("c", "cx", "cy", "cd")


class Gather:
    def __init__(self, ins, outs, send, recv, z, near, line, flat=False):
        self.ins, self.outs, self.send, self.recv = ins, outs, send, recv
        self.z, self.near, self.line, self.flat = z, near, line, flat
        self.parts = [halves(*ref.shape) for ref in ins]
        self.all = range(len(ins))

    def hop(self, a, j, kind, whose, to, part=None, src=None):
        dst = self.outs[a].at[j] if self.flat else self.outs[a].at[j, self.near[whose]]
        src = dst if src is None else src
        if part is not None:
            src, dst = cut(src, part), cut(dst, part)
        return pltpu.make_async_remote_copy(
            src_ref=src,
            dst_ref=dst,
            send_sem=self.send.at[a, j, kind],
            recv_sem=self.recv.at[a, j, kind],
            device_id={DP: to} if kind >= 8 else {EX: self.near[to]},
            device_id_type=MESH,
        )

    def landed(self, a, j, kind, whose, part=None):
        if kind < 8:
            self.hop(a, j, kind, whose, "c", part).wait_recv()
        else:
            self.hop(a, j, kind, whose, self.z).wait_recv()

    def line_first(self):
        z = self.z

        @pl.when(z < self.line - 1)
        def up_first():
            for a in self.all:
                self.hop(a, z, 8, "own", z + 1, src=self.ins[a]).start()

        @pl.when(z > 0)
        def down_first():
            for a in self.all:
                self.hop(a, z, 9, "own", z - 1, src=self.ins[a]).start()

    def first(self, j, src=None):
        for a in self.all:
            one = None if src is None else src[a]
            self.hop(a, j, 0, "own", "x", src=one).start()
            self.hop(a, j, 1, "own", "y", src=one).start()
            self.hop(a, j, 2, "own", "c", src=one).start()

    def second(self, j, kind=0):
        for a in self.all:
            self.landed(a, j, 0, "x")
            self.hop(a, j, 4, "x", "y", self.parts[a][1]).start()
            self.hop(a, j, 5, "x", "c").start()
            self.landed(a, j, 1, "y")
            self.hop(a, j, 3, "y", "x", self.parts[a][0]).start()
            self.hop(a, j, 6, "y", "c").start()

    def third(self, j, kind=0):
        for a in self.all:
            self.landed(a, j, 3, "d", self.parts[a][0])
            self.landed(a, j, 4, "d", self.parts[a][1])
            self.hop(a, j, 7, "d", "c").start()

    def finish(self, j, kind=0):
        for a in self.all:
            for kind, whose in ((2, "c"), (5, "cx"), (6, "cy"), (7, "cd")):
                self.landed(a, j, kind, whose)
            for kind in (0, 1, 2):
                self.hop(a, j, kind, "own", "c").wait_send()
            self.hop(a, j, 3, "y", "x", self.parts[a][0]).wait_send()
            self.hop(a, j, 4, "x", "y", self.parts[a][1]).wait_send()
            for kind in (5, 6, 7):
                self.hop(a, j, kind, "x", "c").wait_send()

    def arrivals(self, step, act):
        z = self.z

        @pl.when(z - step >= 0)
        def below():
            act(z - step, 8)

        @pl.when(z + step <= self.line - 1)
        def above():
            act(z + step, 9)

    def take(self, j, kind):
        for a in self.all:
            self.landed(a, j, kind, "own")
        z = self.z
        if kind == 8:

            @pl.when(z < self.line - 1)
            def on_up():
                for a in self.all:
                    self.hop(a, j, 8, "own", z + 1).start()

        else:

            @pl.when(z > 0)
            def on_down():
                for a in self.all:
                    self.hop(a, j, 9, "own", z - 1).start()

        self.first(j)

    def carry(self, j, kind):
        z = self.z
        for a in self.all:
            self.landed(a, j, kind, "own")
        more, target = (z < self.line - 1, z + 1) if kind == 8 else (z > 0, z - 1)

        @pl.when(more)
        def on():
            for a in self.all:
                self.hop(a, j, kind, "own", target).start()

    def plane_of(self, k):
        return lax.rem(self.z + k, self.line)

    def spread(self, k, rows, sem):
        j = self.plane_of(k)
        self.first(j, [rows.at[j]])
        self.kept(k, rows, sem).start()

    def kept(self, k, rows, sem):
        j = self.plane_of(k)
        return pltpu.make_async_copy(rows.at[j], self.outs[0].at[j, self.near["own"]], sem.at[k])

    def spread_done(self, rows, sem):
        for k in range(1, self.line):
            self.finish(self.plane_of(k))
            self.kept(k, rows, sem).wait()

    def line_done(self):
        z = self.z
        for step in range(self.line):

            @pl.when((z - step >= 0) & (z < self.line - 1))
            def up_done():
                for a in self.all:
                    self.hop(a, z - step, 8, "own", z + 1).wait_send()

            @pl.when((z + step <= self.line - 1) & (z > 0))
            def down_done():
                for a in self.all:
                    self.hop(a, z + step, 9, "own", z - 1).wait_send()


def plane_gather(src, dst, send, recv, near):
    parts = halves(*src.shape)

    def hop(kind, whose, to, part=None):
        one = dst.at[near[whose]] if part is None else cut(dst.at[near[whose]], part)
        return pltpu.make_async_remote_copy(
            src_ref=src if whose == "own" else one,
            dst_ref=one,
            send_sem=send.at[kind],
            recv_sem=recv.at[kind],
            device_id={EX: near[to]},
            device_id_type=MESH,
        )

    def first():
        hop(0, "own", "x").start()
        hop(1, "own", "y").start()
        hop(2, "own", "c").start()
        dst[near["own"]] = src[...]

    def second():
        hop(0, "x", "c").wait_recv()
        hop(4, "x", "y", parts[1]).start()
        hop(5, "x", "c").start()
        hop(1, "y", "c").wait_recv()
        hop(3, "y", "x", parts[0]).start()
        hop(6, "y", "c").start()

    def third():
        hop(3, "d", "c", parts[0]).wait_recv()
        hop(4, "d", "c", parts[1]).wait_recv()
        hop(7, "d", "c").start()

    def finish():
        for kind, whose in ((2, "c"), (5, "cx"), (6, "cy"), (7, "cd")):
            hop(kind, whose, "c").wait_recv()
        for kind in (0, 1, 2):
            hop(kind, "own", "c").wait_send()
        hop(3, "y", "x", parts[0]).wait_send()
        hop(4, "x", "y", parts[1]).wait_send()
        for kind in (5, 6, 7):
            hop(kind, "x", "c").wait_send()

    return first, second, third, finish


def sum_scratch(rows, columns):
    return [
        pltpu.VMEM((8, rows, columns), bf16),
        pltpu.VMEM((3, rows, columns), bf16),
        pltpu.VMEM((4, rows, columns), bf16),
        pltpu.VMEM((2, rows // 2, columns), bf16),
        pltpu.VMEM((2, rows // 2, columns), bf16),
        pltpu.VMEM((2, rows // 2, columns), bf16),
        pltpu.SemaphoreType.DMA((10,)),
        pltpu.SemaphoreType.DMA((10,)),
    ]


def plane_sum(make, out_ref, base, scratch, near):
    part_ref, paired, fromc, fromx, fromy, last, send, recv = scratch
    rows = out_ref.shape[0]
    half = rows // 2
    A, B = pl.ds(0, half), pl.ds(half, half)

    def copy(number, src, dst, to):
        return pltpu.make_async_remote_copy(
            src_ref=src,
            dst_ref=dst,
            send_sem=send.at[number],
            recv_sem=recv.at[number],
            device_id={EX: near[to]},
            device_id_type=MESH,
        )

    order = ("d", "x", "y", "own")
    across = ("cd", "cx", "cy", "c")
    core = [copy(s, part_ref.at[near[name]], fromc.at[s], "c") for s, name in enumerate(across)]
    to_x = [copy(4, paired.at[0, A], fromx.at[0], "x"), copy(5, paired.at[1, A], fromx.at[1], "x")]
    to_y = [copy(6, paired.at[0, B], fromy.at[0], "y"), copy(7, paired.at[2, B], fromy.at[1], "y")]
    late_y = copy(8, paired.at[2, A], last.at[0], "y")
    late_x = copy(9, paired.at[1, B], last.at[1], "x")

    def pair(s):
        core[s].wait_recv()
        paired[s] = (part_ref[near[order[s]]].astype(f32) + fromc[s].astype(f32)).astype(bf16)

    for s in range(3):
        make(across[s])
        core[s].start()
        make(order[s])
    pair(0)
    to_x[0].start()
    to_y[0].start()
    make(across[3])
    core[3].start()
    pair(1)
    to_x[1].start()
    pair(2)
    to_y[1].start()
    make(order[3])
    core[3].wait_recv()
    total = part_ref[near["own"]].astype(f32) + fromc[3].astype(f32)
    out_ref[...] = total if base is None else base[...] + total
    to_x[0].wait_recv()
    paired[2, A] = (paired[2, A].astype(f32) + fromx[0].astype(f32)).astype(bf16)
    late_y.start()
    to_y[0].wait_recv()
    paired[1, B] = (paired[1, B].astype(f32) + fromy[0].astype(f32)).astype(bf16)
    late_x.start()
    to_x[1].wait_recv()
    out_ref[A] += fromx[1].astype(f32)
    to_y[1].wait_recv()
    out_ref[B] += fromy[1].astype(f32)
    late_y.wait_recv()
    out_ref[A] += last[0].astype(f32)
    late_x.wait_recv()
    out_ref[B] += last[1].astype(f32)
    for one in core + to_x + to_y + [late_x, late_y]:
        one.wait_send()


def mul(a, b, over=((1,), (0,))):
    return lax.dot_general(a, b, (over, ((), ())), preferred_element_type=f32)


LAST = ((1,), (1,))


def seat_rows(seats, number):
    local_n, tokens_n = seats.shape
    rows = lax.broadcasted_iota(jnp.int32, (local_n * number, tokens_n), 0).astype(f32)
    hot = rows < 0
    for e in range(local_n):
        one = seats[e : e + 1, :]
        hot = hot | ((rows == one + (e * number - 1)) & (one > 0) & (one <= number))
    return jnp.where(hot, 1.0, 0.0).astype(bf16)


def seat_columns(seats, number):
    tokens_n, local_n = seats.shape
    columns = lax.broadcasted_iota(jnp.int32, (tokens_n, local_n * number), 1).astype(f32)
    hot = columns < 0
    for e in range(local_n):
        one = seats[:, e : e + 1]
        hot = hot | ((columns == one + (e * number - 1)) & (one > 0) & (one <= number))
    return jnp.where(hot, 1.0, 0.0).astype(bf16)


def masked_gates(logits, hit):
    top = jnp.max(jnp.where(hit, logits, masked_score), axis=0, keepdims=True)
    powers = jnp.where(hit, jnp.exp(jnp.where(hit, logits - top, 0.0)), 0.0)
    return powers / jnp.sum(powers, axis=0, keepdims=True)


def tail_kernel(layers_n, number, *refs):
    refs = list(refs)

    def some(count):
        taken = refs[:count]
        del refs[:count]
        return taken

    tokens_all, grads_all = some(layers_n), some(layers_n - 1)
    (own_shard,) = some(1)
    table, hit, seats = some(3)
    w_gate, w_up, w_down = some(3)
    owns = [some(5) for l in range(layers_n)]
    row_sources = [some(2) for l in range(layers_n)]
    column_sources = [some(2) for l in range(layers_n)]
    smalls = some(layers_n)
    grad_gate, grad_up, grad_down, landing = some(4)
    beside = some(layers_n)
    small_sum, grad_qkv, grad_out = some(3)
    (
        tokens,
        grads,
        gates,
        rows_in,
        rows_grad,
        cols_in,
        cols_grad,
        hidden_low,
        dgate_low,
        dup_low,
        gate_w,
        up_w,
        down_w,
        stage_wide,
        stage_tall,
        weight_sem,
        token_sem,
        own_sem,
        out_sem,
        gather_send,
        gather_recv,
        beside_send,
        beside_recv,
        small_own,
        small_got,
        small_part,
        small_sem,
        columns,
        row_block,
        block_sum,
        block_got,
        final,
        final_got,
        column_send,
        column_recv,
        column_keep,
        row_sem,
        block_send,
        block_recv,
        final_send,
        final_recv,
    ) = some(41)
    held = [some(6)]
    z, near = place()
    n_dp, local_n = seats.shape[1], seats.shape[2]
    width = cols_in.shape[1]
    ours = pl.ds(pl.multiple_of(z * width, 128), width)
    gather = Gather([own_shard], [landing], gather_send, gather_recv, z, near, n_dp)
    total = Sums([small_part], [small_sum], held, *refs, z, near, n_dp)
    own_e = near["own"]
    plane_n = columns.shape[1]
    over = ((0,), (0,))
    per_expert = n_dp - 1
    per_layer = local_n * per_expert
    steps = layers_n * per_layer

    def layer_of(i):
        return layers_n - 1 - i // per_layer

    def across(l, j):
        return pltpu.make_async_remote_copy(
            src_ref=tokens_all[l].at[j],
            dst_ref=beside[l].at[j],
            send_sem=beside_send.at[l, j],
            recv_sem=beside_recv.at[l, j],
            device_id={EX: near["c"]},
            device_id_type=MESH,
        )

    def start(one):
        one.start()

    def wait(one):
        one.wait()

    def fetch(i, slot, act):
        j = lax.rem(z + 1 + lax.rem(i, per_expert), n_dp)
        for l in range(layers_n):

            @pl.when(layer_of(i) == l)
            def of_layer():
                if act is start:

                    @pl.when(lax.rem(i, per_layer) < per_expert)
                    def arrived():
                        across(l, j).wait_recv()

                for source, names, base in ((tokens_all[l], QUAD, 0), (beside[l], BESIDE, 4)):
                    for q, name in enumerate(names):
                        dst = tokens.at[slot, near[name]]
                        sem = token_sem.at[slot, base + q]
                        act(pltpu.make_async_copy(source.at[j, q], dst, sem))
                grads_from = (landing if l == 0 else grads_all[l - 1]).at[j]
                act(pltpu.make_async_copy(grads_from, grads.at[slot], token_sem.at[slot, 8]))

    def weights(l, e):
        return [
            pltpu.make_async_copy(src.at[l, e], dst, weight_sem.at[i])
            for i, (src, dst) in enumerate(((w_gate, gate_w), (w_up, up_w), (w_down, down_w)))
        ]

    def own(l, e):
        here = pl.ds(pl.multiple_of(e * number, 32), number)
        inner = pl.ds(0, number)
        pairs = (
            (owns[l][0].at[here, ours], cols_in.at[inner]),
            (owns[l][1].at[here, ours], cols_grad.at[inner]),
            (owns[l][2].at[here], hidden_low.at[inner]),
            (owns[l][3].at[here], dgate_low.at[inner]),
            (owns[l][4].at[here], dup_low.at[inner]),
        )
        return [
            pltpu.make_async_copy(src, dst, own_sem.at[i]) for i, (src, dst) in enumerate(pairs)
        ]

    def of(i, make, act):
        e = lax.rem(i // per_expert, local_n)
        for l in range(layers_n):

            @pl.when(layer_of(i) == l)
            def of_layer():
                for one in make(l, e):
                    act(one)

    def results(l, e):
        return [
            pltpu.make_async_copy(stage_wide.at[0], grad_gate.at[l, e], out_sem.at[0]),
            pltpu.make_async_copy(stage_wide.at[1], grad_up.at[l, e], out_sem.at[1]),
            pltpu.make_async_copy(stage_tall, grad_down.at[l, e], out_sem.at[2]),
        ]

    def column_pieces(l, owner):
        first, second = column_sources[l]
        extra = second.shape[1] // 128 - plane_n
        return [
            (first.at[:, pl.ds(pl.multiple_of(owner * 256, 256), 256)], 0, 256),
            (second.at[:, pl.ds(pl.multiple_of(owner * 128, 128), 128)], 256, 128),
            (
                second.at[
                    :, pl.ds(pl.multiple_of((plane_n + owner // 2 % extra) * 128, 128), 128)
                ],
                384,
                128,
            ),
        ]

    def column_copy(l, owner, source, piece):
        src, at, size = column_pieces(l, owner)[piece]
        return pltpu.make_async_remote_copy(
            src_ref=src,
            dst_ref=columns.at[l, source, :, pl.ds(at, size)],
            send_sem=column_send.at[l, owner, piece],
            recv_sem=column_recv.at[l, source, piece],
            device_id={EX: owner},
            device_id_type=MESH,
        )

    def column_own(l, piece):
        src, at, size = column_pieces(l, own_e)[piece]
        dst = columns.at[l, own_e, :, pl.ds(at, size)]
        return pltpu.make_async_copy(src, dst, column_keep.at[l, piece])

    def column_each(l, act_send, act_recv, act_own):
        for d in range(1, plane_n):
            owner = lax.rem(own_e + d, plane_n)
            source = lax.rem(own_e + plane_n - d, plane_n)
            for piece in range(3):
                if piece < 2:
                    if act_send is not None:
                        act_send(column_copy(l, owner, own_e, piece))
                    if act_recv is not None:
                        act_recv(column_copy(l, owner, source, piece))
                    continue
                if act_send is not None:

                    @pl.when(lax.rem(owner, 2) == 0)
                    def extra_out():
                        act_send(column_copy(l, owner, own_e, piece))

                if act_recv is not None:

                    @pl.when(lax.rem(own_e, 2) == 0)
                    def extra_in():
                        act_recv(column_copy(l, owner, source, piece))

        if act_own is not None:
            act_own(column_own(l, 0))
            act_own(column_own(l, 1))

            @pl.when(lax.rem(own_e, 2) == 0)
            def extra_own():
                act_own(column_own(l, 2))

    def row_loads(l):
        return [
            pltpu.make_async_copy(src.at[0], row_block.at[i], row_sem.at[i])
            for i, src in enumerate(row_sources[l])
        ]

    def blocks(l):
        column_each(l, None, lambda one: one.wait_recv(), wait)
        for one in row_loads(l):
            one.wait()
        height = block_sum.shape[2]
        for i in range(2):
            here = pl.ds(i * 256, 256)
            given = columns[l, :, :, here].reshape(-1, 256)
            for j in range(n_dp):
                rows = row_block[i, :, :, pl.ds(j * height, height)].reshape(-1, height)
                block_sum[l, j, :, here] = mul(rows, given, over).astype(bf16)
        if l > 0:
            for one in row_loads(l - 1):
                one.start()

    def block_move(l, j, way):
        slot = jnp.where(j == z + way, n_dp, j) if way < 0 else j
        return pltpu.make_async_remote_copy(
            src_ref=block_sum.at[l, j],
            dst_ref=block_got.at[l, slot],
            send_sem=block_send.at[l, j],
            recv_sem=block_recv.at[l, slot],
            device_id={DP: z + way},
            device_id_type=MESH,
        )

    def block_landed(l, slot):
        pltpu.make_async_remote_copy(
            src_ref=block_got.at[l, slot],
            dst_ref=block_got.at[l, slot],
            send_sem=block_send.at[l, 0],
            recv_sem=block_recv.at[l, slot],
            device_id={DP: z},
            device_id_type=MESH,
        ).wait_recv()

    def block_step(l):
        def act(j, way):
            if way == 0:
                return
            more = (z > 0) if way > 0 else (z < n_dp - 1)

            @pl.when(more)
            def add():
                block_landed(l, j)
                block_sum[l, j] = (
                    block_sum[l, j].astype(f32) + block_got[l, j].astype(f32)
                ).astype(bf16)

            block_move(l, j, way).start()

        return act

    def final_copy(l, owner, source):
        return pltpu.make_async_remote_copy(
            src_ref=final.at[l, owner],
            dst_ref=final_got.at[l, source],
            send_sem=final_send.at[l, owner],
            recv_sem=final_recv.at[l, source],
            device_id={EX: owner},
            device_id_type=MESH,
        )

    def block_end(l):
        final[l] = block_sum[l, z].reshape(final.shape[1:])

        @pl.when(z > 0)
        def below():
            block_landed(l, z)
            got = block_got[l, z].reshape(final.shape[1:])
            final[l] = (final[l].astype(f32) + got.astype(f32)).astype(bf16)

        @pl.when(z < n_dp - 1)
        def above():
            block_landed(l, n_dp)
            got = block_got[l, n_dp].reshape(final.shape[1:])
            final[l] = (final[l].astype(f32) + got.astype(f32)).astype(bf16)

        for d in range(1, plane_n):
            final_copy(l, lax.rem(own_e + d, plane_n), own_e).start()
        final_got[l, own_e] = final[l, own_e]

    def block_out(l):
        for d in range(1, plane_n):
            final_copy(l, own_e, lax.rem(own_e + d, plane_n)).wait_recv()
        for source in range(plane_n):
            got = final_got[l, source].astype(f32)
            grad_qkv[l, :, pl.ds(source * 256, 256)] = got[:, :256]
            grad_out[l, :, pl.ds(source * 128, 128)] = got[:, 256:384]
            if source % 2 == 0:
                grad_out[l, :, pl.ds((plane_n + source // 2) * 128, 128)] = got[:, 384:]

    def small_exchange():
        return pltpu.make_async_remote_copy(
            src_ref=small_own,
            dst_ref=small_got,
            send_sem=small_sem.at[0],
            recv_sem=small_sem.at[1],
            device_id={EX: near["c"]},
            device_id_type=MESH,
        )

    def small_parts():
        small_exchange().wait_recv()
        both = small_own[...] + small_got[...]
        rest = jnp.zeros((128 - both.shape[0], both.shape[1]), f32)
        turned = jnp.transpose(jnp.concatenate([both, rest], axis=0))
        high = turned.astype(bf16)
        low = (turned - high.astype(f32)).astype(bf16)
        shape = small_part.shape[:3] + (128,)
        small_part[:, :, :, pl.ds(0, 128)] = high.reshape(shape)
        small_part[:, :, :, pl.ds(128, 128)] = low.reshape(shape)
        for distance in (3, 2, 1, 0):
            total.at(distance, total.first)

    for l in range(layers_n):
        small_own[pl.ds(l * SMALL, SMALL)] = smalls[l][...]

    @pl.when(lax.rem(own_e, 2) == 1)
    def no_extra():
        columns[:, :, :, pl.ds(384, 128)] = jnp.zeros(columns.shape[:3] + (128,), bf16)

    greet(z, near, ("x", "y", "d", "c", "cx", "cy", "cd"), n_dp)
    gather.line_first()
    small_exchange().start()
    for l in reversed(range(layers_n)):
        for k in range(1, n_dp):
            across(l, lax.rem(z + k, n_dp)).start()
    for l in reversed(range(layers_n)):
        column_each(l, start, None, start)
    for one in row_loads(layers_n - 1):
        one.start()
    of(0, weights, start)
    fetch(0, 0, start)

    def block_at(l, distance):
        return lambda: total.at(distance, block_step(l))

    services = {
        0: [lambda: gather.arrivals(1, gather.take), small_parts],
        1: [lambda: gather.arrivals(2, gather.take), lambda: blocks(1)],
        2: [
            lambda: gather.arrivals(1, gather.second),
            lambda: gather.arrivals(3, gather.take),
            block_at(1, 3),
        ],
        3: [
            lambda: gather.arrivals(1, gather.third),
            lambda: gather.arrivals(2, gather.second),
            block_at(1, 2),
            lambda: blocks(0),
        ],
        4: [
            lambda: gather.arrivals(2, gather.third),
            lambda: gather.arrivals(3, gather.second),
            block_at(0, 3),
            block_at(1, 1),
        ],
        5: [
            lambda: gather.arrivals(3, gather.third),
            lambda: gather.arrivals(1, gather.finish),
            lambda: gather.arrivals(2, gather.finish),
            lambda: gather.arrivals(3, gather.finish),
            block_at(0, 2),
        ],
        6: [
            lambda: total.at(3, total.second),
            lambda: total.at(2, total.second),
            lambda: total.at(1, total.second),
            lambda: total.at(0, total.second),
            block_at(0, 1),
        ],
        7: [lambda: block_end(1)],
        8: [lambda: total.at(3, total.third), lambda: total.at(2, total.third)],
        9: [lambda: total.at(1, total.third)],
        10: [lambda: block_end(0)],
        11: [lambda: total.at(0, total.third), lambda: block_out(1)],
    }

    def step(i, carry):
        slot = lax.rem(i, 2)
        l = layer_of(i)
        k = lax.rem(i, per_expert)
        e = lax.rem(i // per_expert, local_n)
        j = lax.rem(z + 1 + k, n_dp)

        @pl.when(k == 0)
        def begin():
            of(i, own, start)

        @pl.when((i + 1 < steps) & (i != per_layer - 1))
        def ahead():
            fetch(i + 1, 1 - slot, start)

        fetch(i, slot, wait)
        everyone = tokens[slot].reshape(-1, tokens.shape[3])
        experts_n = hit.shape[2]

        @pl.when(e == 0)
        def gates_here():
            here = pl.ds(pl.multiple_of(l * experts_n, experts_n), experts_n)
            router = table[here, :].astype(bf16)
            gates[k] = masked_gates(mul(router, everyone, LAST), hit[l, j] > 0)

        pick = seat_rows(seats[l, j, pl.ds(e, 1)], number)
        rows_in[...] = mul(pick, everyone).astype(bf16)
        rows_grad[...] = mul(pick, grads[slot].reshape(-1, tokens.shape[3])).astype(bf16)
        place_of = pl.ds(pl.multiple_of((k + 1) * number, 32), number)
        mine = gates[k, pl.ds(own_e * local_n + e, 1), :]
        gate_seat = jnp.sum(pick.astype(f32) * mine, axis=1, keepdims=True)

        @pl.when(k == 0)
        def weights_here():
            of(i, weights, wait)

        gate = mul(rows_in[...], gate_w[...])
        up = mul(rows_in[...], up_w[...])
        raw = mul(rows_grad[...], down_w[...], LAST) * gate_seat
        sigmoid = 1.0 / (1.0 + jnp.exp(-gate))
        silu = gate * sigmoid
        hidden_low[place_of] = (silu * up).astype(bf16)
        dgate_low[place_of] = (raw * up * sigmoid * (1.0 + gate * (1.0 - sigmoid))).astype(bf16)
        dup_low[place_of] = (raw * silu).astype(bf16)
        cols_in[place_of] = rows_in[:, ours]
        cols_grad[place_of] = (rows_grad[:, ours].astype(f32) * gate_seat).astype(bf16)

        @pl.when(k == per_expert - 1)
        def close():
            @pl.when(i + 1 < steps)
            def next_weights():
                of(i + 1, weights, start)

            of(i, own, wait)

            @pl.when(i >= per_expert)
            def staged():
                of(i - per_expert, results, wait)

            stage_wide[0] = mul(cols_in[...], dgate_low[...], over)
            stage_wide[1] = mul(cols_in[...], dup_low[...], over)
            stage_tall[...] = mul(hidden_low[...], cols_grad[...], over)
            of(i, results, start)

        for at, acts in services.items():

            @pl.when(i == at)
            def serve():
                for act in acts:
                    act()

        @pl.when(i == per_layer - 1)
        def late_ahead():
            fetch(i + 1, 1 - slot, start)

        return carry

    lax.fori_loop(0, steps, step, 0)
    block_out(0)
    for distance in (3, 2, 1, 0):
        total.at(distance, total.finish)
    small_exchange().wait_send()
    for l in range(layers_n):
        column_each(l, lambda one: one.wait_send(), None, None)
        for d in range(1, plane_n):
            final_copy(l, lax.rem(own_e + d, plane_n), own_e).wait_send()
        for distance in (3, 2, 1):
            total.at(distance, lambda j, way: block_move(l, j, way).wait_send())
    gather.line_done()
    for l in range(layers_n):
        for k in range(1, n_dp):
            across(l, lax.rem(z + k, n_dp)).wait_send()
    of(steps - 1, results, wait)


def tail(
    capacity,
    number,
    tokens_all,
    grads_all,
    own_shard,
    plan,
    weights,
    owns,
    row_sources,
    column_sources,
    smalls,
):
    table, hit, seats = plan
    layers_n, n_dp, local_n, group_rows = seats.shape
    n_expert = lax.axis_size(EX)
    rows, width = own_shard.shape
    hidden = weights[0].shape[3]
    part = width // n_dp
    cut_rows = part // n_expert
    wide = column_sources[0][0].shape[1]
    shape = jax.ShapeDtypeStruct
    several = [one for group in (owns, row_sources, column_sources) for l in group for one in l]
    results = pl.pallas_call(
        partial(tail_kernel, layers_n, capacity),
        out_shape=[
            shape((layers_n, local_n, part, hidden), f32),
            shape((layers_n, local_n, part, hidden), f32),
            shape((layers_n, local_n, hidden, part), f32),
            shape((n_dp, n_expert, rows, width), bf16),
        ]
        + [shape(tokens_all[0].shape, bf16)] * layers_n
        + [
            shape((cut_rows, 256), f32),
            shape((layers_n, cut_rows, wide), f32),
            shape((layers_n, cut_rows, width), f32),
        ],
        in_specs=[HBM] * (2 * layers_n) + [VMEM] * 3 + [HBM] * (3 + len(several)) + [VMEM] * layers_n,
        out_specs=[HBM] * (4 + layers_n) + [VMEM] * 3,
        scratch_shapes=[
            pltpu.VMEM((2, n_expert, rows, width), bf16),
            pltpu.VMEM((2, n_expert, rows, width), bf16),
            pltpu.VMEM((n_dp - 1,) + hit.shape[2:], f32),
            pltpu.VMEM((capacity, width), bf16),
            pltpu.VMEM((capacity, width), bf16),
            pltpu.VMEM((n_dp * capacity, part), bf16),
            pltpu.VMEM((n_dp * capacity, part), bf16),
            pltpu.VMEM((n_dp * capacity, hidden), bf16),
            pltpu.VMEM((n_dp * capacity, hidden), bf16),
            pltpu.VMEM((n_dp * capacity, hidden), bf16),
            pltpu.VMEM((width, hidden), bf16),
            pltpu.VMEM((width, hidden), bf16),
            pltpu.VMEM((hidden, width), bf16),
            pltpu.VMEM((2, part, hidden), f32),
            pltpu.VMEM((hidden, part), f32),
            pltpu.SemaphoreType.DMA((3,)),
            pltpu.SemaphoreType.DMA((2, 9)),
            pltpu.SemaphoreType.DMA((5,)),
            pltpu.SemaphoreType.DMA((3,)),
            pltpu.SemaphoreType.DMA((1, n_dp, KINDS)),
            pltpu.SemaphoreType.DMA((1, n_dp, KINDS)),
            pltpu.SemaphoreType.DMA((layers_n, n_dp)),
            pltpu.SemaphoreType.DMA((layers_n, n_dp)),
            pltpu.VMEM((layers_n * SMALL, width), f32),
            pltpu.VMEM((layers_n * SMALL, width), f32),
            pltpu.VMEM((n_dp, n_expert, cut_rows, 256), bf16),
            pltpu.SemaphoreType.DMA((2,)),
            pltpu.VMEM((layers_n, n_expert, rows, BLOCK), bf16),
            pltpu.VMEM((2, n_expert, rows, width), bf16),
            pltpu.VMEM((layers_n, n_dp, part, BLOCK), bf16),
            pltpu.VMEM((layers_n, n_dp + 1, part, BLOCK), bf16),
            pltpu.VMEM((layers_n, n_expert, cut_rows, BLOCK), bf16),
            pltpu.VMEM((layers_n, n_expert, cut_rows, BLOCK), bf16),
            pltpu.SemaphoreType.DMA((layers_n, n_expert, 3)),
            pltpu.SemaphoreType.DMA((layers_n, n_expert, 3)),
            pltpu.SemaphoreType.DMA((layers_n, 3)),
            pltpu.SemaphoreType.DMA((2,)),
            pltpu.SemaphoreType.DMA((layers_n, n_dp)),
            pltpu.SemaphoreType.DMA((layers_n, n_dp + 1)),
            pltpu.SemaphoreType.DMA((layers_n, n_expert)),
            pltpu.SemaphoreType.DMA((layers_n, n_expert)),
        ]
        + sums_scratch([(cut_rows, 256)], n_dp),
        compiler_params=settings(number),
        name="tail",
    )(
        *tokens_all,
        *grads_all,
        own_shard,
        *plan,
        *weights,
        *several,
        *smalls,
    )
    return results[:3], results[4 + layers_n :]


VMEM = pl.BlockSpec(memory_space=pltpu.VMEM)
HBM = pl.BlockSpec(memory_space=ANY)


def settings(number):
    return pltpu.CompilerParams(
        collective_id=number, has_side_effects=True, vmem_limit_bytes=63 << 20
    )


def chain(z, e):
    n_expert = 8
    behind = (z, lax.rem(e + n_expert - 1, n_expert))
    ahead = (z, lax.rem(e + 1, n_expert))
    return behind, ahead, e > 0, e < n_expert - 1


def normalized(value, gain):
    scale = lax.rsqrt(jnp.mean(value * value, axis=-1, keepdims=True) + epsilon)
    return value * scale * gain


def turn(head, cosine, signed_sine):
    return head * cosine + pltpu.roll(head, HEAD_SIZE // 2, 1) * signed_sine


def head_of(h):
    return pl.ds(h * HEAD_SIZE, HEAD_SIZE)


def allowed_keys(rk, row, z, e, behind, has_behind, seg_column):
    own = rk[z, e, pl.ds(row, 1), :]
    first = rk[z, behind[1], pl.ds(row, 1), :]
    rows = seg_column.shape[0]
    query = lax.broadcasted_iota(jnp.int32, (rows, rows), 0)
    key = lax.broadcasted_iota(jnp.int32, (rows, rows), 1)
    reach = jnp.where(has_behind, 0, -1)
    return jnp.concatenate(
        [(first == seg_column) & (key >= rows * -reach), (own == seg_column) & (key <= query)],
        axis=1,
    )


def head_probs(query, keys, allowed):
    scores = mul(query, keys, LAST) * (1.0 / math.sqrt(HEAD_SIZE))
    scores = jnp.where(allowed, scores, masked_score)
    powers = jnp.exp(scores - jnp.max(scores, axis=-1, keepdims=True))
    return powers / jnp.sum(powers, axis=-1, keepdims=True)


def forward_kernel(layer, layers_n, number, *refs):
    first = layer == 0
    refs = list(refs)

    def some(count):
        taken = refs[:count]
        del refs[:count]
        return taken

    stream, cosine, sine, seg_column = some(4)
    if first:
        small, ranks, w_qkv, w_out, out_grad = some(5)
    else:
        table, rk, hit, seats, turned, cross_from, qkv_from, out_from = some(8)
    w_gate, w_up, w_down = some(3)
    new_stream, layer_out, normed_a, queries, kv_out, attended, mixed, normed_b = some(8)
    rows_out, gate_out, up_out, gate_seat, quad = some(5)
    if first:
        table, rk_out, hit, seats, turned, qkv_out, out_out, qkv_next, out_next = some(9)
        (line_grads,) = some(1)
        small_land, rk, seat_all = some(3)
    else:
        (cross_to,) = some(1)
    (
        qkv,
        w_o,
        kv,
        projected,
        tokens,
        gates,
        weighted,
        gate_w,
        up_w,
        down_w,
        weight_sem,
        load_sem,
        chain_sem,
        quad_sem,
        send,
        recv,
        rows_in,
        gate_pre,
        up_pre,
        leave_sem,
    ) = some(20)
    if first:
        send_0, recv_0, send_1, recv_1, send_2, recv_2, send_3, recv_3 = some(8)
        send_4, recv_4, keep = some(3)
    else:
        cross_send, cross_recv, cross_keep = some(3)
    scratch = refs
    z, near = place()
    e = near["own"]
    line = lax.axis_size(DP)
    local_n = seats.shape[2]
    rows = stream.shape[0]
    experts_n = hit.shape[2]
    behind, ahead, has_behind, has_ahead = chain(z, e)

    weights = [
        pltpu.make_async_copy(src.at[layer], dst, weight_sem.at[i])
        for i, (src, dst) in enumerate(((w_gate, gate_w), (w_up, up_w), (w_down, down_w)))
    ]
    order = (behind, ahead, has_behind, has_ahead)
    greet(z, near, ("x", "y", "c"), line if first else None, order)
    if not first:
        cross = Gather([cross_from.at[0]], [cross_to], cross_send, cross_recv, z, near, line)
        cross.spread(1, cross_from, cross_keep)
    if first:
        g0 = Gather([small, ranks], [small_land, rk], send_0, recv_0, z, near, line)
        g1 = Gather([w_qkv.at[0]], [qkv], send_1, recv_1, z, near, line)
        g2 = Gather([w_out.at[0]], [w_o], send_2, recv_2, z, near, line)
        g3 = Gather(
            [w_qkv.at[1], w_out.at[1]], [qkv_next, out_next], send_3, recv_3, z, near, line
        )
        g4 = Gather([out_grad], [line_grads], send_4, recv_4, z, near, line, flat=True)
        local = [
            pltpu.make_async_copy(one, g.outs[i].at[z, e], keep.at[k])
            for k, (g, i, one) in enumerate(
                (g, i, one) for g in (g0, g1, g2, g3) for i, one in enumerate(g.ins)
            )
        ]
        g0.line_first()
        g0.first(z, g0.ins)
        g1.line_first()
        g1.first(z, g1.ins)
        for one in local:
            one.start()
        g0.arrivals(1, g0.take)
        g0.second(z)
        g0.arrivals(2, g0.take)
        g0.third(z)
        g0.arrivals(1, g0.second)
        g0.arrivals(3, g0.take)
        g1.arrivals(1, g1.take)
        g2.line_first()
        g2.first(z, g2.ins)
        g0.arrivals(1, g0.third)
        g0.arrivals(2, g0.second)
        g1.second(z)
        g0.arrivals(2, g0.third)
        g0.arrivals(3, g0.second)
        g1.arrivals(2, g1.take)
        g0.arrivals(3, g0.third)
        g0.finish(z)
        for step in range(1, line):
            g0.arrivals(step, g0.finish)
        local[0].wait()
        local[1].wait()
        table[...] = jnp.transpose(small_land[...].reshape(-1, 128).astype(f32))
        g1.third(z)
        g1.arrivals(1, g1.second)
        for g in range(line):
            before = jnp.zeros((layers_n * experts_n, 1), f32)
            for d in range(8):
                lanes = pl.ds(d * rows, rows)
                rank = rk[g, d, pl.ds(0, layers_n * experts_n), :].astype(f32)
                seat_all[g, :, lanes] = jnp.where(rank > 0, rank + before, 0.0)
                for l in range(layers_n):
                    hit[l, g, :, lanes] = rank[l * experts_n : (l + 1) * experts_n]
                here = jnp.where(rank > 0, 1.0, 0.0)
                before = before + jnp.sum(here, axis=1, keepdims=True)
            for l in range(layers_n):
                for k in range(local_n):
                    row = pl.ds(l * experts_n + e * local_n + k, 1)
                    seats[l, g, pl.ds(k, 1), :] = seat_all[g, row, :]
        g1.arrivals(3, g1.take)
        wide = jnp.zeros((rows - layers_n * local_n, rows), f32)
        for d in range(8):
            lanes = pl.ds(d * rows, rows)
            mine = [seats[l, z, :, lanes] for l in range(layers_n)]
            turned[lanes, :] = jnp.transpose(jnp.concatenate(mine + [wide], axis=0))
        rk_out[...] = rk[...]
        g1.arrivals(1, g1.third)
        g1.arrivals(2, g1.second)
        g2.arrivals(1, g2.take)
        g1.arrivals(2, g1.third)
        g1.arrivals(3, g1.second)
        g2.second(z)
        g2.arrivals(2, g2.take)
        g1.arrivals(3, g1.third)
        g2.third(z)
        g1.finish(z)
        for step in range(1, line):
            g1.arrivals(step, g1.finish)
        local[2].wait()
        g2.arrivals(1, g2.second)
        g2.arrivals(3, g2.take)
    else:
        loads = [
            pltpu.make_async_copy(qkv_from, qkv, load_sem.at[0]),
            pltpu.make_async_copy(out_from, w_o, load_sem.at[1]),
        ]
        for one in loads:
            one.start()
    for one in weights:
        one.start()
    gain = 2 * experts_n + 2 * layer
    x = stream[...].astype(f32)
    normed_a[...] = normalized(x, table[pl.ds(gain, 1), :]).astype(bf16)
    if not first:
        loads[0].wait()
    width = queries.shape[1]
    projected[...] = mul(normed_a[...], qkv[...].reshape(width, -1))
    keys_n = KEY_VALUE_HEADS * HEAD_SIZE
    cos, sin = cosine[...], sine[...]
    for h in range(KEY_VALUE_HEADS):
        key = turn(projected[:, head_of(QUERY_HEADS + h)], cos, sin)
        kv[1, :, head_of(h)] = key.astype(bf16)
    kv[1, :, pl.ds(keys_n, keys_n)] = projected[:, pl.ds(width + keys_n, keys_n)].astype(bf16)

    def pass_on(target):
        return pltpu.make_async_remote_copy(
            src_ref=kv.at[1],
            dst_ref=kv.at[0],
            send_sem=chain_sem.at[0],
            recv_sem=chain_sem.at[1],
            device_id={DP: target[0], EX: target[1]},
            device_id_type=MESH,
        )

    @pl.when(has_ahead)
    def pass_ahead():
        pass_on(ahead).start()

    if first:
        g2.arrivals(1, g2.third)
        g2.arrivals(2, g2.second)
        g3.line_first()
        g3.first(z, g3.ins)
    else:
        cross.spread(2, cross_from, cross_keep)
    for h in range(QUERY_HEADS):
        queries[:, head_of(h)] = turn(projected[:, head_of(h)], cos, sin).astype(bf16)
    allowed = allowed_keys(rk, layers_n * experts_n, z, e, behind, has_behind, seg_column[...])

    @pl.when(has_behind)
    def from_behind_here():
        pass_on(behind).wait_recv()

    @pl.when(jnp.logical_not(has_behind))
    def nobody_behind():
        kv[0] = jnp.zeros_like(kv[0])

    for h in range(QUERY_HEADS):
        group = h // (QUERY_HEADS // KEY_VALUE_HEADS)
        keys = kv[:, :, head_of(group)].reshape(2 * rows, HEAD_SIZE)
        values = kv[:, :, head_of(KEY_VALUE_HEADS + group)].reshape(2 * rows, HEAD_SIZE)
        probs = head_probs(queries[:, head_of(h)], keys, allowed).astype(bf16)
        attended[:, head_of(h)] = mul(probs, values).astype(bf16)
        if first and h == 3:
            g2.arrivals(2, g2.third)
            g2.arrivals(3, g2.second)
        if first and h == 7:
            g2.arrivals(3, g2.third)
            g3.arrivals(1, g3.take)
            g4.line_first()
        if not first and h == 8:
            cross.second(cross.plane_of(1))
    kv_out[...] = kv[...]
    if first:
        g2.finish(z)
        for step in range(1, line):
            g2.arrivals(step, g2.finish)
        local[3].wait()
    else:
        loads[1].wait()
    mixed[...] = x + mul(attended[...], w_o[...].reshape(width, -1))
    normed_b[...] = normalized(mixed[...], table[pl.ds(gain + 1, 1), :]).astype(bf16)

    one, two, three, four = plane_gather(normed_b, tokens, send, recv, near)
    one()
    two()
    three()
    if not first:
        cross.second(cross.plane_of(2))
        cross.spread(3, cross_from, cross_keep)
        cross.third(cross.plane_of(1))
    if first:
        g3.second(z)
        g3.arrivals(1, g3.second)
        g3.arrivals(2, g3.take)
    four()
    quads = [
        pltpu.make_async_copy(tokens.at[near[name]], quad.at[i], quad_sem.at[i])
        for i, name in enumerate(QUAD)
    ]
    for copied in quads:
        copied.start()
    everyone = tokens[...].reshape(-1, width)
    router = table[pl.ds(layer * experts_n, experts_n), :].astype(bf16)
    gates[...] = masked_gates(mul(router, everyone, LAST), hit[layer, z] > 0)
    pick = seat_rows(seats[layer, z], number)
    for k in range(local_n):
        here = pl.ds(k * number, number)
        mine = gates[pl.ds(e * local_n + k, 1), :]
        gate_seat[here] = jnp.sum(
            pick[k * number : (k + 1) * number].astype(f32) * mine, axis=1, keepdims=True
        )
    rows_in[...] = mul(pick, everyone).astype(bf16)
    for copied in weights:
        copied.wait()
    if first:
        g3.third(z)
        g3.arrivals(3, g3.take)
        g3.arrivals(1, g3.third)
        g3.arrivals(2, g3.second)
        g4.arrivals(1, g4.carry)
    def expert(k, carry):
        here = pl.ds(pl.multiple_of(k * number, 32), number)
        x = rows_in[here]
        gate = mul(x, gate_w[k])
        up = mul(x, up_w[k])
        gate_pre[here] = gate
        up_pre[here] = up
        hidden = (gate * (1.0 / (1.0 + jnp.exp(-gate))) * up).astype(bf16)
        weighted[here] = (mul(hidden, down_w[k]) * gate_seat[here]).astype(bf16)
        return carry

    lax.fori_loop(0, local_n, expert, 0)
    leaving = [
        pltpu.make_async_copy(src, dst, leave_sem.at[i])
        for i, (src, dst) in enumerate(((rows_in, rows_out), (gate_pre, gate_out), (up_pre, up_out)))
    ]
    for copied in leaving:
        copied.start()
    if first:
        g3.arrivals(2, g3.third)
        g3.arrivals(3, g3.second)
        g4.arrivals(2, g4.carry)
        out_copies = [
            pltpu.make_async_copy(qkv, qkv_out, load_sem.at[0]),
            pltpu.make_async_copy(w_o, out_out, load_sem.at[1]),
        ]
        for copied in out_copies:
            copied.start()
    else:
        cross.third(cross.plane_of(2))
        cross.second(cross.plane_of(3))

    def make(name):
        d = near[name]
        lanes = pl.ds(pl.multiple_of(d * rows, rows), rows)
        mine = turned[lanes, pl.ds(layer * local_n, local_n)]
        scratch[0][d] = mul(seat_columns(mine, number), weighted[...]).astype(bf16)

    plane_sum(make, new_stream, mixed, scratch, near)
    layer_out[...] = new_stream[...].astype(bf16)

    for copied in quads + leaving:
        copied.wait()

    @pl.when(has_ahead)
    def passed_on():
        pass_on(ahead).wait_send()

    if first:
        g3.arrivals(3, g3.third)
        g4.arrivals(3, g4.carry)
        g3.finish(z)
        for step in range(1, line):
            g3.arrivals(step, g3.finish)
        for copied in local[4:] + out_copies:
            copied.wait()
        for g in (g0, g1, g2, g3, g4):
            g.line_done()
    else:
        cross.third(cross.plane_of(3))
        cross.spread_done(cross_from, cross_keep)


def layer_forward(layer, number, shapes, stream, tables, given, weights):
    layers_n, n_dp, n_expert, local_n, capacity = shapes
    first = layer == 0
    rows, width = stream.shape
    hidden = weights[0].shape[3]
    experts_n = local_n * n_expert
    seats_n = local_n * capacity
    keys_n = KEY_VALUE_HEADS * HEAD_SIZE
    group = n_expert * rows
    cut_rows = width // (n_dp * n_expert)
    shape = jax.ShapeDtypeStruct
    outs = [
        shape((rows, width), f32),
        shape((rows, width), bf16),
        shape((rows, width), bf16),
        shape((rows, width), bf16),
        shape((2, rows, 2 * keys_n), bf16),
        shape((rows, width), bf16),
        shape((rows, width), f32),
        shape((rows, width), bf16),
        shape((seats_n, width), bf16),
        shape((seats_n, hidden), f32),
        shape((seats_n, hidden), f32),
        shape((seats_n, 1), f32),
        shape((len(QUAD), rows, width), bf16),
    ]
    specs = [VMEM] * 8 + [HBM] * 3 + [VMEM, HBM]
    scratch = []
    full_qkv = (n_dp, n_expert, cut_rows, width + 2 * keys_n)
    full_out = (n_dp, n_expert, cut_rows, width)
    if first:
        rank_rows = given[1].shape[0]
        outs += [
            shape((128, width), f32),
            shape((n_dp, n_expert, rank_rows, rows), jnp.int32),
            shape((layers_n, n_dp, experts_n, group), f32),
            shape((layers_n, n_dp, local_n, group), f32),
            shape((group, 128), f32),
        ]
        outs += [shape(full_qkv, bf16), shape(full_out, bf16)] * 2
        outs.append(shape((n_dp, rows, width), bf16))
        specs += [VMEM] * 5 + [HBM] * 5
        scratch += [
            pltpu.VMEM((n_dp, n_expert, cut_rows, 128), bf16),
            pltpu.VMEM((n_dp, n_expert, rank_rows, rows), jnp.int32),
            pltpu.VMEM((n_dp, layers_n * experts_n, group), f32),
        ]
    else:
        outs.append(shape((n_dp, n_expert, rows, width), bf16))
        specs.append(HBM)
    scratch += [
        pltpu.VMEM(full_qkv, bf16),
        pltpu.VMEM(full_out, bf16),
        pltpu.VMEM((2, rows, 2 * keys_n), bf16),
        pltpu.VMEM((rows, width + 2 * keys_n), f32),
        pltpu.VMEM((n_expert, rows, width), bf16),
        pltpu.VMEM((experts_n, group), f32),
        pltpu.VMEM((seats_n, width), bf16),
        pltpu.VMEM((local_n, width, hidden), bf16),
        pltpu.VMEM((local_n, width, hidden), bf16),
        pltpu.VMEM((local_n, hidden, width), bf16),
        pltpu.SemaphoreType.DMA((3,)),
        pltpu.SemaphoreType.DMA((2,)),
        pltpu.SemaphoreType.DMA((2,)),
        pltpu.SemaphoreType.DMA((len(QUAD),)),
        pltpu.SemaphoreType.DMA((8,)),
        pltpu.SemaphoreType.DMA((8,)),
        pltpu.VMEM((seats_n, width), bf16),
        pltpu.VMEM((seats_n, hidden), f32),
        pltpu.VMEM((seats_n, hidden), f32),
        pltpu.SemaphoreType.DMA((3,)),
    ]
    if first:
        for count in (2, 1, 1, 2, 1):
            scratch += [pltpu.SemaphoreType.DMA((count, n_dp, KINDS)) for i in range(2)]
        scratch.append(pltpu.SemaphoreType.DMA((6,)))
    else:
        scratch += [pltpu.SemaphoreType.DMA((1, n_dp, KINDS)) for i in range(2)]
        scratch.append(pltpu.SemaphoreType.DMA((n_dp,)))
    given_specs = [HBM] * 5 if first else [VMEM] * 5 + [HBM] * 3
    return pl.pallas_call(
        partial(forward_kernel, layer, layers_n, capacity),
        out_shape=outs,
        in_specs=[VMEM] * 4 + given_specs + [HBM] * 3,
        out_specs=specs,
        scratch_shapes=scratch + sum_scratch(rows, width),
        compiler_params=settings(number),
        name="layer_forward",
    )(stream, *tables, *given, *weights)


def norm_back(value, gain, grad):
    scale = lax.rsqrt(jnp.mean(value * value, axis=-1, keepdims=True) + epsilon)
    unit = value * scale
    inner = grad * gain
    back = scale * (inner - unit * jnp.mean(inner * unit, axis=-1, keepdims=True))
    return back, jnp.sum(grad * unit, axis=0, keepdims=True)


def backward_kernel(layer, layers_n, number, *refs):
    refs = list(refs)

    def some(count):
        taken = refs[:count]
        del refs[:count]
        return taken

    grad_stream, stream, cosine, sine, seg_column = some(5)
    mixed, normed_b, queries, kv, gate_seat = some(5)
    table, rk, hit, seats, turned = some(5)
    row_sources = some(2)
    qkv_from, out_from, w_gate, w_up, w_down = some(5)
    gate_from, up_from = some(2)
    grad_out, grad_low, *leaving_to = some(6)
    dprojected, grad_attn, small = some(3)
    row_lands = some(2)
    (
        summed,
        qkv,
        w_o,
        datt,
        dkv,
        dkv_send,
        dkv_got,
        all_probs,
        tokens,
        back_rows,
        gate_w,
        up_w,
        down_w,
        weight_sem,
        load_sem,
        chain_sem,
        send,
        recv,
        row_send,
        row_recv,
        row_keep,
        gate_pre,
        up_pre,
        rows_grad,
        hidden_low,
        dgate_low,
        dup_low,
        leave_sem,
    ) = some(28)
    scratch = refs
    z, near = place()
    e = near["own"]
    line = lax.axis_size(DP)
    local_n = seats.shape[2]
    rows, width = stream.shape
    experts_n = hit.shape[2]
    behind, ahead, has_behind, has_ahead = chain(z, e)
    weights = [
        pltpu.make_async_copy(src.at[layer], dst, weight_sem.at[i])
        for i, (src, dst) in enumerate(((w_gate, gate_w), (w_up, up_w), (w_down, down_w)))
    ]
    loads = [
        pltpu.make_async_copy(qkv_from, qkv, load_sem.at[0]),
        pltpu.make_async_copy(out_from, w_o, load_sem.at[1]),
    ]
    weights += [
        pltpu.make_async_copy(gate_from, gate_pre, leave_sem.at[4]),
        pltpu.make_async_copy(up_from, up_pre, leave_sem.at[5]),
    ]
    grad_low[...] = grad_stream[...].astype(bf16)
    greet(z, near, ("x", "y", "c"), None, (behind, ahead, has_behind, has_ahead))

    spreads = [
        Gather([src], [dst], row_send.at[i], row_recv.at[i], 0, near, None)
        for i, (src, dst) in enumerate(zip(row_sources, row_lands))
    ]
    kept = [
        pltpu.make_async_copy(src, dst.at[0, e], row_keep.at[i])
        for i, (src, dst) in enumerate(zip(row_sources, row_lands))
    ]

    first, second, third, finish = plane_gather(grad_low, tokens, send, recv, near)
    first()
    for one in weights + loads:
        one.start()
    allowed = allowed_keys(rk, layers_n * experts_n, z, e, behind, has_behind, seg_column[...])
    per_group = QUERY_HEADS // KEY_VALUE_HEADS

    def keys_of(group):
        return kv[:, :, head_of(group)].reshape(2 * rows, HEAD_SIZE)

    def prepare(heads):
        for h in heads:
            all_probs[h] = head_probs(queries[:, head_of(h)], keys_of(h // per_group), allowed)

    prepare(range(0, 5))
    second()
    prepare(range(5, 9))
    third()
    spreads[0].first(0, spreads[0].ins)
    spreads[1].first(0, spreads[1].ins)
    for one in kept:
        one.start()
    prepare(range(9, QUERY_HEADS))
    finish()
    everyone = tokens[...].reshape(-1, width)
    picked = mul(seat_rows(seats[layer, z], number), everyone)
    back_rows[:, pl.ds(0, width)] = picked.astype(bf16)
    rows_grad[...] = (picked * gate_seat[...]).astype(bf16)
    for one in weights:
        one.wait()

    def expert(k, carry):
        here = pl.ds(pl.multiple_of(k * number, 32), number)
        gate, up = gate_pre[here], up_pre[here]
        raw = mul(back_rows[here, pl.ds(0, width)], down_w[k], LAST)
        sigmoid = 1.0 / (1.0 + jnp.exp(-gate))
        silu = gate * sigmoid
        hidden = (silu * up).astype(bf16)
        hidden_low[here] = hidden
        dgate_seat = jnp.sum(hidden.astype(f32) * raw, axis=1, keepdims=True)
        raw = raw * gate_seat[here]
        dgate = (raw * up * sigmoid * (1.0 + gate * (1.0 - sigmoid))).astype(bf16)
        dup = (raw * silu).astype(bf16)
        dgate_low[here] = dgate
        dup_low[here] = dup
        back_rows[here, pl.ds(0, width)] = (
            mul(dgate, gate_w[k], LAST) + mul(dup, up_w[k], LAST)
        ).astype(bf16)
        high = dgate_seat.astype(bf16).astype(f32)
        lane = lax.broadcasted_iota(jnp.int32, (number, 128), 1)
        mine = e * local_n + k
        back_rows[here, pl.ds(width, 128)] = jnp.where(
            lane == mine, high, jnp.where(lane == experts_n + mine, dgate_seat - high, 0.0)
        ).astype(bf16)
        return carry

    lax.fori_loop(0, local_n, expert, 0)
    leaving = [
        pltpu.make_async_copy(src, dst, leave_sem.at[i])
        for i, (src, dst) in enumerate(zip((rows_grad, hidden_low, dgate_low, dup_low), leaving_to))
    ]
    for one in leaving:
        one.start()

    def make(name):
        d = near[name]
        lanes = pl.ds(pl.multiple_of(d * rows, rows), rows)
        mine = turned[lanes, pl.ds(layer * local_n, local_n)]
        scratch[0][d] = mul(seat_columns(mine, number), back_rows[...]).astype(bf16)

    spreads[0].second(0)
    plane_sum(make, summed, None, scratch, near)
    spreads[0].third(0)
    spreads[1].second(0)

    over = ((0,), (0,))
    gain = 2 * experts_n + 2 * layer
    router = table[pl.ds(layer * experts_n, experts_n), :].astype(bf16)
    own_lanes = pl.ds(pl.multiple_of(e * rows, rows), rows)
    gates = masked_gates(mul(router, normed_b[...], LAST), hit[layer, z, :, own_lanes] > 0)
    turned_sum = jnp.transpose(summed[:, pl.ds(width, 128)])
    dgates = turned_sum[:experts_n] + turned_sum[experts_n : 2 * experts_n]
    inner = jnp.sum(gates * dgates, axis=0, keepdims=True)
    dlogits = (gates * (dgates - inner)).astype(bf16)
    small[...] = jnp.zeros_like(small)
    small[pl.ds(0, experts_n)] = mul(dlogits, normed_b[...])
    dnormed = summed[:, pl.ds(0, width)] + mul(dlogits, router, over)
    back, dgain = norm_back(mixed[...], table[pl.ds(gain + 1, 1), :], dnormed)
    small[pl.ds(experts_n + 1, 1)] = dgain
    dmixed = grad_stream[...].astype(f32) + back
    grad_out[...] = dmixed
    grad_attn[...] = dmixed.astype(bf16)

    loads[1].wait()
    datt[...] = mul(grad_attn[...], w_o[...].reshape(width, -1), LAST).astype(bf16)
    cos, sin = cosine[...], sine[...]
    scale = 1.0 / math.sqrt(HEAD_SIZE)
    for group in range(KEY_VALUE_HEADS):
        keys = keys_of(group)
        values = keys_of(KEY_VALUE_HEADS + group)
        dkeys = jnp.zeros((2 * rows, HEAD_SIZE), f32)
        dvalues = jnp.zeros((2 * rows, HEAD_SIZE), f32)
        for h in range(group * per_group, (group + 1) * per_group):
            query = queries[:, head_of(h)]
            probs = all_probs[h]
            given = datt[:, head_of(h)]
            dprobs = mul(given, values, LAST)
            delta = jnp.sum(probs * dprobs, axis=-1, keepdims=True)
            dscores = (probs * (dprobs - delta)).astype(bf16)
            dquery = mul(dscores, keys) * scale
            dprojected[:, head_of(h)] = turn(dquery, cos, -sin).astype(bf16)
            dkeys = dkeys + mul(dscores, query, over)
            dvalues = dvalues + mul(probs.astype(bf16), given, over)
        if group == 0:
            spreads[1].third(0)
        dkv[:, head_of(group)] = dkeys * scale
        dkv[:, head_of(KEY_VALUE_HEADS + group)] = dvalues
    dkv_send[...] = dkv[pl.ds(0, rows)].astype(bf16)

    def pass_on(target):
        return pltpu.make_async_remote_copy(
            src_ref=dkv_send,
            dst_ref=dkv_got,
            send_sem=chain_sem.at[0],
            recv_sem=chain_sem.at[1],
            device_id={DP: target[0], EX: target[1]},
            device_id_type=MESH,
        )

    @pl.when(has_behind)
    def pass_back():
        pass_on(behind).start()

    loads[0].wait()
    query_part = pl.ds(0, width)
    key_part = pl.ds(width, dkv.shape[1])
    weights_q = qkv[:, :, :, query_part].reshape(-1, width)
    dnormed = mul(dprojected[:, query_part], weights_q, LAST)

    @pl.when(has_ahead)
    def from_ahead_here():
        pass_on(ahead).wait_recv()
        dkv[pl.ds(rows, rows)] += dkv_got[...].astype(f32)

    for h in range(KEY_VALUE_HEADS):
        dkey = turn(dkv[pl.ds(rows, rows), head_of(h)], cos, -sin)
        dprojected[:, head_of(QUERY_HEADS + h)] = dkey.astype(bf16)
        dvalue = dkv[pl.ds(rows, rows), head_of(KEY_VALUE_HEADS + h)]
        dprojected[:, head_of(QUERY_HEADS + KEY_VALUE_HEADS + h)] = dvalue.astype(bf16)
    weights_kv = qkv[:, :, :, key_part].reshape(-1, dkv.shape[1])
    dnormed = dnormed + mul(dprojected[:, key_part], weights_kv, LAST)
    back, dgain = norm_back(stream[...].astype(f32), table[pl.ds(gain, 1), :], dnormed)
    small[pl.ds(experts_n, 1)] = dgain
    grad_out[...] += back

    @pl.when(has_behind)
    def passed_back():
        pass_on(behind).wait_send()

    for one in leaving:
        one.wait()

    for i in range(2):
        spreads[i].finish(0)
        kept[i].wait()


def layer_backward(layer, number, shapes, grads, stream, tables, saved, plan, weights):
    layers_n, n_dp, n_expert, local_n, capacity = shapes
    rows, width = stream.shape
    hidden = weights[-1].shape[1]
    experts_n = local_n * n_expert
    seats_n = local_n * capacity
    keys_n = KEY_VALUE_HEADS * HEAD_SIZE
    cut_rows = width // (n_dp * n_expert)
    shape = jax.ShapeDtypeStruct
    outs = [
        shape((rows, width), f32),
        shape((rows, width), bf16),
        shape((seats_n, width), bf16),
        shape((seats_n, hidden), bf16),
        shape((seats_n, hidden), bf16),
        shape((seats_n, hidden), bf16),
        shape((rows, width + 2 * keys_n), bf16),
        shape((rows, width), bf16),
        shape((SMALL, width), f32),
        shape((1, n_expert, rows, width), bf16),
        shape((1, n_expert, rows, width), bf16),
    ]
    scratch = [
        pltpu.VMEM((rows, width + 128), f32),
        pltpu.VMEM((n_dp, n_expert, cut_rows, width + 2 * keys_n), bf16),
        pltpu.VMEM((n_dp, n_expert, cut_rows, width), bf16),
        pltpu.VMEM((rows, width), bf16),
        pltpu.VMEM((2 * rows, 2 * keys_n), f32),
        pltpu.VMEM((rows, 2 * keys_n), bf16),
        pltpu.VMEM((rows, 2 * keys_n), bf16),
        pltpu.VMEM((QUERY_HEADS, rows, 2 * rows), f32),
        pltpu.VMEM((n_expert, rows, width), bf16),
        pltpu.VMEM((seats_n, width + 128), bf16),
        pltpu.VMEM((local_n, width, hidden), bf16),
        pltpu.VMEM((local_n, width, hidden), bf16),
        pltpu.VMEM((local_n, hidden, width), bf16),
        pltpu.SemaphoreType.DMA((3,)),
        pltpu.SemaphoreType.DMA((2,)),
        pltpu.SemaphoreType.DMA((2,)),
        pltpu.SemaphoreType.DMA((8,)),
        pltpu.SemaphoreType.DMA((8,)),
        pltpu.SemaphoreType.DMA((2, 1, 1, KINDS)),
        pltpu.SemaphoreType.DMA((2, 1, 1, KINDS)),
        pltpu.SemaphoreType.DMA((2,)),
        pltpu.VMEM((seats_n, hidden), f32),
        pltpu.VMEM((seats_n, hidden), f32),
        pltpu.VMEM((seats_n, width), bf16),
        pltpu.VMEM((seats_n, hidden), bf16),
        pltpu.VMEM((seats_n, hidden), bf16),
        pltpu.VMEM((seats_n, hidden), bf16),
        pltpu.SemaphoreType.DMA((6,)),
    ]
    return pl.pallas_call(
        partial(backward_kernel, layer, layers_n, capacity),
        out_shape=outs,
        in_specs=[VMEM] * 15 + [HBM] * 9,
        out_specs=[VMEM] * 2 + [HBM] * 4 + [VMEM] * 3 + [HBM] * 2,
        scratch_shapes=scratch + sum_scratch(rows, width + 128),
        compiler_params=settings(number),
        name="layer_backward",
    )(grads, stream, *tables, *saved, *plan, *weights)


class Sums:
    def __init__(self, ins, outs, held, send, recv, keep, z, near, line):
        self.ins, self.outs, self.held = ins, outs, held
        self.send, self.recv, self.keep = send, recv, keep
        self.z, self.near, self.line = z, near, line
        self.all = range(len(ins))

    def split(self, a):
        half = self.outs[a].shape[1] // 2
        return pl.ds(0, half), pl.ds(half, half)

    def move(self, a, j, name):
        part = self.ins[a]
        fromx, fromy, late, later, total, got = self.held[a]
        A, B = self.split(a)
        near = self.near
        kind, src, dst, to = {
            "xd": lambda: (0, part.at[j, near["d"], :, A], fromx.at[j, 0], "x"),
            "xx": lambda: (1, part.at[j, near["x"], :, A], fromx.at[j, 1], "x"),
            "yd": lambda: (2, part.at[j, near["d"], :, B], fromy.at[j, 0], "y"),
            "yy": lambda: (3, part.at[j, near["y"], :, B], fromy.at[j, 1], "y"),
            "ly": lambda: (4, late.at[j, 0], later.at[j, 0], "y"),
            "lx": lambda: (5, late.at[j, 1], later.at[j, 1], "x"),
            "up": lambda: (6, total.at[j], got.at[j], self.z + 1),
            "down": lambda: (7, total.at[j], got.at[j], self.z - 1),
        }[name]()
        if name == "down":
            slot = jnp.where(j == self.z - 1, self.line, j)
            dst = got.at[slot]
        return pltpu.make_async_remote_copy(
            src_ref=src,
            dst_ref=dst,
            send_sem=self.send.at[a, j, kind],
            recv_sem=self.recv.at[a, j, kind],
            device_id={DP: to} if kind >= 6 else {EX: near[to]},
            device_id_type=MESH,
        )

    def own_down(self, a):
        got = self.held[a][5]
        return pltpu.make_async_remote_copy(
            src_ref=got.at[self.line],
            dst_ref=got.at[self.line],
            send_sem=self.send.at[a, self.z, 7],
            recv_sem=self.recv.at[a, self.z, 7],
            device_id={DP: self.z},
            device_id_type=MESH,
        )

    def prepare(self, a, j):
        late, total = self.held[a][2], self.held[a][4]
        A, B = self.split(a)
        near, part = self.near, self.ins[a]
        return [
            pltpu.make_async_copy(src, dst, self.keep.at[a, j, i])
            for i, (src, dst) in enumerate(
                (
                    (part.at[j, near["y"], :, A], late.at[j, 0]),
                    (part.at[j, near["x"], :, B], late.at[j, 1]),
                    (part.at[j, near["own"]], total.at[j]),
                )
            )
        ]

    def at(self, step, act):
        if step == 0:
            act(self.z, 0)
            return

        @pl.when(self.z + step <= self.line - 1)
        def above():
            act(self.z + step, 1)

        @pl.when(self.z - step >= 0)
        def below():
            act(self.z - step, -1)

    def first(self, j, way):
        for a in self.all:
            for name in ("xd", "yd", "xx", "yy"):
                self.move(a, j, name).start()
            for one in self.prepare(a, j):
                one.start()

    def second(self, j, way):
        for a in self.all:
            fromx, fromy, late = self.held[a][:3]
            ready = self.prepare(a, j)
            ready[0].wait()
            self.move(a, j, "xd").wait_recv()
            late[j, 0] = (late[j, 0].astype(f32) + fromx[j, 0].astype(f32)).astype(bf16)
            self.move(a, j, "ly").start()
            ready[1].wait()
            self.move(a, j, "yd").wait_recv()
            late[j, 1] = (late[j, 1].astype(f32) + fromy[j, 0].astype(f32)).astype(bf16)
            self.move(a, j, "lx").start()

    def third(self, j, way):
        for a in self.all:
            fromx, fromy, late, later, total, got = self.held[a]
            for name in ("xx", "yy", "ly", "lx"):
                self.move(a, j, name).wait_recv()
            self.prepare(a, j)[2].wait()
            for side, (columns, here) in enumerate(zip(self.split(a), (fromx, fromy))):
                value = (
                    total[j, :, columns].astype(f32)
                    + here[j, 1].astype(f32)
                    + later[j, side].astype(f32)
                )
                if way == 0:
                    self.outs[a][:, columns] = value
                else:
                    total[j, :, columns] = value.astype(bf16)
            if way == 1:

                @pl.when(self.z > 0)
                def more_up():
                    self.move(a, j, "up").wait_recv()
                    total[j] = (total[j].astype(f32) + got[j].astype(f32)).astype(bf16)

                self.move(a, j, "up").start()
            elif way == -1:

                @pl.when(self.z < self.line - 1)
                def more_down():
                    self.move(a, j, "down").wait_recv()
                    total[j] = (total[j].astype(f32) + got[j].astype(f32)).astype(bf16)

                self.move(a, j, "down").start()
            else:

                @pl.when(self.z > 0)
                def end_up():
                    self.move(a, j, "up").wait_recv()
                    self.outs[a][...] += got[j].astype(f32)

                @pl.when(self.z < self.line - 1)
                def end_down():
                    self.own_down(a).wait_recv()
                    self.outs[a][...] += got[self.line].astype(f32)

    def finish(self, j, way):
        for a in self.all:
            for name in ("xd", "yd", "xx", "yy", "lx", "ly"):
                self.move(a, j, name).wait_send()
            if way == 1:
                self.move(a, j, "up").wait_send()
            elif way == -1:
                self.move(a, j, "down").wait_send()


def sums_scratch(shapes, line):
    scratch = []
    for rows, columns in shapes:
        half = columns // 2
        scratch += [pltpu.VMEM((line, 2, rows, half), bf16) for i in range(4)]
        scratch += [
            pltpu.VMEM((line, rows, columns), bf16),
            pltpu.VMEM((line + 1, rows, columns), bf16),
        ]
    return scratch + [
        pltpu.SemaphoreType.DMA((len(shapes), line, 8)),
        pltpu.SemaphoreType.DMA((len(shapes), line, 8)),
        pltpu.SemaphoreType.DMA((len(shapes), line, 3)),
    ]


def from_behind(value, axis, steps):
    count = lax.axis_size(axis)
    leading, last = (max(0, -steps), min(count, count - steps))
    return lax.ppermute(value, axis, [(source, source + steps) for source in range(leading, last)])


def from_sibling(value):
    count = lax.axis_size(EX)
    return lax.ppermute(value, EX, [(s, s + 1 - 2 * (s % 2)) for s in range(count)])


def rms_norm(stream, gain_row):
    return (
        stream * lax.rsqrt(jnp.mean(stream * stream, axis=-1, keepdims=True) + epsilon) * gain_row
    )


def rotary_tables(token_positions):
    half_dim = HEAD_SIZE // 2
    steps_up = jnp.arange(half_dim).astype(f32)
    frequency = jnp.exp(steps_up * (-2.0 * math.log(rope_base) / HEAD_SIZE))
    angles = token_positions.astype(f32)[:, None] * frequency[None, :]
    return jnp.cos(angles)[:, None, :], jnp.sin(angles)[:, None, :]


def apply_rotary(heads_in, cosine, sine_part):
    half_dim = heads_in.shape[-1] // 2
    first_half = heads_in[..., :half_dim]
    second_half = heads_in[..., half_dim:]
    return jnp.concatenate(
        [
            first_half * cosine - second_half * sine_part,
            second_half * cosine + first_half * sine_part,
        ],
        axis=-1,
    )


def gated_unit(gate_pre, up_pre):
    return jax.nn.silu(gate_pre) * up_pre


def masked_scores(query_rows, gathered_keys, allowed):
    token_rows = query_rows.shape[0]
    grouped_queries = query_rows.reshape(
        token_rows, KEY_VALUE_HEADS, QUERY_HEADS // KEY_VALUE_HEADS, HEAD_SIZE
    )
    score_scale = 1.0 / math.sqrt(HEAD_SIZE)
    scores = (
        jnp.einsum(
            "tkgd,skd->kgts", grouped_queries, gathered_keys, preferred_element_type=f32
        )
        * score_scale
    )
    return (jnp.where(allowed, scores, masked_score), grouped_queries)


def rank_table(routes, pair_order, experts_n):
    layers_n, token_rows, topk_n = routes.shape
    chosen = jnp.swapaxes(routes, 1, 2)
    order = jnp.swapaxes(pair_order.reshape(layers_n, token_rows, topk_n), 1, 2)
    ids = jnp.arange(experts_n, dtype=jnp.int32)[None, :, None]
    none = token_rows * topk_n
    place_of = jnp.full((layers_n, experts_n, token_rows), none, jnp.int32)
    for k in range(topk_n):
        place_of = jnp.where(chosen[:, k][:, None, :] == ids, order[:, k][:, None, :], place_of)
    smaller = (place_of[:, :, :, None] < place_of[:, :, None, :]).astype(jnp.int32)
    return jnp.where(place_of < none, jnp.sum(smaller, axis=2) + 1, 0)


def dense_gates(logits, mask):
    top = jnp.max(jnp.where(mask, logits, masked_score), axis=0, keepdims=True)
    powers = jnp.where(mask, jnp.exp(jnp.where(mask, logits - top, 0.0)), 0.0)
    return powers / jnp.sum(powers, axis=0, keepdims=True)


def local_chips(
    tokens,
    w_qkv,
    w_out,
    w_router,
    norm_gains,
    w_gate,
    w_up,
    w_down,
    out_grad,
    segment_ids,
    routes,
    pair_order,
):
    token_rows = tokens.shape[0]
    layers_n = w_qkv.shape[0]
    topk_n = routes.shape[2]
    n_expert = lax.axis_size(EX)
    n_dp = lax.axis_size(DP)
    local_n = w_gate.shape[1]
    experts_n = local_n * n_expert
    capacity = 9 * n_expert * token_rows * topk_n // (8 * experts_n)
    shapes = (layers_n, n_dp, n_expert, local_n, capacity)
    positions = lax.axis_index(EX) * token_rows + jnp.arange(token_rows, dtype=jnp.int32)
    cosine, sine = rotary_tables(positions)
    tables = (
        jnp.concatenate([cosine, cosine], axis=-1)[:, 0],
        jnp.concatenate([-sine, sine], axis=-1)[:, 0],
        segment_ids[:, None],
    )
    ranks = rank_table(routes, pair_order, experts_n).reshape(layers_n * experts_n, token_rows)
    ranks = jnp.concatenate([ranks, segment_ids[None], jnp.zeros((7, token_rows), jnp.int32)])
    small = jnp.concatenate(
        [w_router[l] for l in range(layers_n)]
        + [jnp.swapaxes(norm_gains.reshape(2 * layers_n, -1), 0, 1)],
        axis=1,
    )
    small = jnp.pad(small, ((0, 0), (0, 128 - small.shape[1])))
    experts = (w_gate, w_up, w_down)

    def along_line(rows):
        return lax.all_gather(rows, DP, axis=0)

    saved, outputs, normed_all, streams = [], [], [], [tokens]
    for l in range(layers_n):
        given = (small, ranks, w_qkv, w_out, out_grad)
        if l > 0:
            given = (*plan, line_grads, *full[l])
        results = layer_forward(l, 1 + l, shapes, streams[l], tables, given, experts)
        if l == 0:
            plan = results[13:18]
            full = [results[18:20], results[20:22]]
            line_grads = results[22]
        else:
            grads_all = [results[13]]
        streams.append(results[0])
        outputs.append(results[1])
        saved.append(results[2:12])
        normed_all.append(along_line(results[12]))

    grads = out_grad
    owns, smalls = [None] * layers_n, [None] * layers_n
    row_sources, column_sources = [None] * layers_n, [None] * layers_n
    for l in reversed(range(layers_n)):
        normed_a, queries, kv, attended, mixed, normed_b, rows_in = saved[l][:7]
        gate_pre, up_pre, gate_seat = saved[l][7:]
        kept = (mixed, normed_b, queries, kv, gate_seat)
        sources = (normed_a, attended, *full[l], *experts, gate_pre, up_pre)
        results = layer_backward(l, 4 + l, shapes, grads, streams[l], tables, kept, plan, sources)
        grads, own_shard = results[:2]
        owns[l] = (rows_in, *results[2:6])
        column_sources[l] = results[6:8]
        smalls[l] = results[8]
        row_sources[l] = results[9:11]
    grad_experts, (small_sum, grad_qkv, grad_out) = tail(
        capacity,
        8,
        normed_all,
        grads_all,
        own_shard,
        (plan[0], plan[2], plan[3]),
        experts,
        owns,
        row_sources,
        column_sources,
        smalls,
    )
    small_sum = small_sum[:, :128] + small_sum[:, 128:]
    small_sum = small_sum[:, : layers_n * SMALL].reshape(-1, layers_n, SMALL)
    small_sum = jnp.swapaxes(small_sum, 0, 1)
    grad_router = small_sum[:, :, :experts_n]
    grad_gains = jnp.swapaxes(small_sum[:, :, experts_n : experts_n + 2], 1, 2)
    return (
        jnp.stack(outputs),
        grads,
        grad_qkv,
        grad_out,
        grad_router,
        grad_gains,
        *grad_experts,
    )


def local(
    tokens,
    w_qkv,
    w_out,
    w_router,
    norm_gains,
    w_gate,
    w_up,
    w_down,
    out_grad,
    segment_ids,
    routes,
    pair_order,
):
    token_rows = tokens.shape[0]
    layers_n = w_qkv.shape[0]
    topk_n = routes.shape[2]
    n_expert = lax.axis_size(EX)
    n_dp = lax.axis_size(DP)
    expert_here = lax.axis_index(EX)
    dp_here = lax.axis_index(DP)
    device_here = dp_here * n_expert + expert_here
    local_n = w_gate.shape[1]
    experts_n = local_n * n_expert
    capacity = 9 * n_expert * token_rows * topk_n // (8 * experts_n)
    group_rows = n_expert * token_rows
    query_width = QUERY_HEADS * HEAD_SIZE
    key_width = KEY_VALUE_HEADS * HEAD_SIZE
    score_scale = 1.0 / math.sqrt(HEAD_SIZE)
    token_positions = expert_here * token_rows + jnp.arange(token_rows, dtype=jnp.int32)
    cosine, sine_part = rotary_tables(token_positions)
    seg_prev = from_behind(segment_ids, everywhere, 1)
    has_prev = device_here > 0
    row_index = jnp.arange(token_rows)
    own_mask = (segment_ids[None, :] == segment_ids[:, None]) & (
        row_index[None, :] <= row_index[:, None]
    )
    prev_mask = (seg_prev[None, :] == segment_ids[:, None]) & has_prev
    allowed = jnp.concatenate([prev_mask, own_mask], axis=1)

    ranks = rank_table(routes, pair_order, experts_n)
    small = jnp.concatenate(
        [w_router[l] for l in range(layers_n)]
        + [jnp.swapaxes(norm_gains.reshape(2 * layers_n, -1), 0, 1)],
        axis=1,
    )
    small = jnp.pad(small, ((0, 0), (0, 128 - small.shape[1])))
    small_full, ranks_full, qkv_0, out_0 = [
        lax.all_gather(one, everywhere, axis=0)
        for one in (small, ranks.reshape(layers_n * experts_n, token_rows), w_qkv[0], w_out[0])
    ]
    qkv_fulls = [qkv_0.reshape(D, -1)]
    out_fulls = [out_0.reshape(query_width, D)]
    for layer_idx in range(1, layers_n):
        qkv_fulls.append(lax.all_gather(w_qkv[layer_idx], everywhere, axis=0, tiled=True))
        out_fulls.append(lax.all_gather(w_out[layer_idx], everywhere, axis=0, tiled=True))
    small_full = small_full.reshape(D, 128)
    gains = jnp.swapaxes(
        small_full[:, layers_n * experts_n : layers_n * (experts_n + 2)], 0, 1
    ).astype(f32)
    routers = [small_full[:, l * experts_n : (l + 1) * experts_n] for l in range(layers_n)]
    routers_turned = [jnp.swapaxes(router, 0, 1) for router in routers]
    ranks_full = ranks_full.reshape(n_dp, n_expert, layers_n, experts_n, token_rows)
    ranks_full = lax.dynamic_slice_in_dim(ranks_full, dp_here, 1, 0)
    groups = ranks_full.shape[0]
    hit_all = jnp.transpose(ranks_full > 0, (2, 0, 3, 1, 4)).reshape(
        layers_n, groups, experts_n, group_rows
    )
    mine = lax.dynamic_slice_in_dim(ranks_full, expert_here * local_n, local_n, 3)
    counts = jnp.sum((mine > 0).astype(jnp.int32), axis=-1)
    before = jnp.cumsum(counts, axis=1) - counts
    seats = jnp.where(mine > 0, before[..., None] + mine, 0)
    seats = jnp.transpose(seats, (2, 0, 3, 1, 4)).reshape(layers_n, groups, local_n, group_rows)
    seat_ids = jnp.arange(1, capacity + 1, dtype=jnp.int32)

    def own_of(array):
        return lax.dynamic_index_in_dim(array, 0, 0, keepdims=False)

    def seat_map(l):
        return (seats[l][:, :, None, :] == seat_ids[:, None]).astype(bf16)

    def gates_of(normed_rows, l, hit):
        logits = jnp.einsum("de,td->et", routers[l], normed_rows, preferred_element_type=f32)
        return dense_gates(logits, hit)

    own_hit = [(ranks[l] > 0) for l in range(layers_n)]

    stream = tokens.astype(f32)
    saved_layers = []
    outputs = []
    for l in range(layers_n):
        qkv_full, out_full = qkv_fulls[l], out_fulls[l]
        normed_a = rms_norm(stream, gains[2 * l]).astype(bf16)
        projected_output = jnp.dot(normed_a, qkv_full, preferred_element_type=f32)
        query_rows = apply_rotary(
            projected_output[:, :query_width].reshape(token_rows, QUERY_HEADS, HEAD_SIZE),
            cosine,
            sine_part,
        ).astype(bf16)
        key_own = apply_rotary(
            projected_output[:, query_width : query_width + key_width].reshape(
                token_rows, KEY_VALUE_HEADS, HEAD_SIZE
            ),
            cosine,
            sine_part,
        ).astype(bf16)
        value_own = (
            projected_output[:, query_width + key_width :]
            .reshape(token_rows, KEY_VALUE_HEADS, HEAD_SIZE)
            .astype(bf16)
        )
        key_prev, value_prev = from_behind((key_own, value_own), everywhere, 1)
        gathered_keys = jnp.concatenate([key_prev, key_own], axis=0)
        gathered_values = jnp.concatenate([value_prev, value_own], axis=0)
        scores, grouped_queries = masked_scores(query_rows, gathered_keys, allowed)
        top_score = jnp.max(scores, axis=-1, keepdims=True)
        exp_scores = jnp.exp(scores - top_score)
        row_total = jnp.sum(exp_scores, axis=-1, keepdims=True)
        prob_low = (exp_scores / row_total).astype(bf16)
        log_total = top_score + jnp.log(row_total)
        attended = (
            jnp.einsum("kgts,skd->tkgd", prob_low, gathered_values, preferred_element_type=f32)
            .reshape(token_rows, query_width)
            .astype(bf16)
        )
        mixed_sum = stream + jnp.dot(attended, out_full, preferred_element_type=f32)
        normed_b = rms_norm(mixed_sum, gains[2 * l + 1]).astype(bf16)

        if True:
            kept = {}
            group_normed = lax.all_gather(normed_b, EX, axis=0, tiled=True)
            kept["normed_all"] = group_normed[None]
            seat_own = own_of(seat_map(l))
            gates_own = gates_of(group_normed, l, own_of(hit_all[l]))
            gates_own = lax.dynamic_slice_in_dim(gates_own, expert_here * local_n, local_n, 0)
            gate_seat = jnp.sum(seat_own.astype(f32) * gates_own[:, None, :], axis=-1)
            expert_in = jnp.einsum(
                "est,td->esd", seat_own, group_normed, preferred_element_type=f32
            ).astype(bf16)
            gate_pre = jnp.einsum("esd,edf->esf", expert_in, w_gate[l], preferred_element_type=f32)
            up_pre = jnp.einsum("esd,edf->esf", expert_in, w_up[l], preferred_element_type=f32)
            hidden = gated_unit(gate_pre, up_pre).astype(bf16)
            expert_out = jnp.einsum("esf,efd->esd", hidden, w_down[l], preferred_element_type=f32)
            weighted = (expert_out * gate_seat[..., None]).astype(bf16)
            branch_part = jnp.einsum("est,esd->td", seat_own, weighted, preferred_element_type=f32)
            new_stream = mixed_sum + lax.psum_scatter(
                branch_part, EX, scatter_dimension=0, tiled=True
            )
        saved_layers.append(
            {
                "stream_in": stream,
                "normed_a": normed_a,
                "queries": query_rows,
                "key_all": gathered_keys,
                "value_all": gathered_values,
                "log_total": log_total,
                "attended": attended,
                "mixed_sum": mixed_sum,
                "normed_b": normed_b,
            }
            | kept
        )
        outputs.append(new_stream)
        stream = new_stream

    grad_stream = out_grad.astype(f32)
    weight_parts = [None] * layers_n
    expert_parts = [None] * layers_n
    owns = [None] * layers_n
    for l in reversed(range(layers_n)):
        record = saved_layers[l]
        qkv_full, out_full = qkv_fulls[l], out_fulls[l]
        grad_low = grad_stream.astype(bf16)
        if True:
            normed_all = record["normed_all"]
            grad_all = lax.all_gather(grad_low, EX, axis=0, tiled=True)[None]
            seat_all = seat_map(l)
            gates_all = jax.vmap(lambda rows, hit: gates_of(rows, l, hit))(normed_all, hit_all[l])
            gates_mine = lax.dynamic_slice_in_dim(gates_all, expert_here * local_n, local_n, 1)
            gate_seat = jnp.sum(seat_all.astype(f32) * gates_mine[:, :, None, :], axis=-1)
            rows_in = jnp.einsum(
                "gest,gtd->egsd", seat_all, normed_all, preferred_element_type=f32
            ).astype(bf16)
            rows_grad = jnp.einsum(
                "gest,gtd->egsd", seat_all, grad_all, preferred_element_type=f32
            ).astype(bf16)
            gate_seat = jnp.swapaxes(gate_seat, 0, 1)[..., None]
            gate_pre = jnp.einsum("egsd,edf->egsf", rows_in, w_gate[l], preferred_element_type=f32)
            up_pre = jnp.einsum("egsd,edf->egsf", rows_in, w_up[l], preferred_element_type=f32)
            dhidden_raw = jnp.einsum(
                "egsd,efd->egsf", rows_grad, w_down[l], preferred_element_type=f32
            )
            hidden, gate_pull = jax.vjp(gated_unit, gate_pre, up_pre)
            hidden_low = hidden.astype(bf16)
            dgate_pre, dup_pre = gate_pull(dhidden_raw * gate_seat)
            dgate_low = dgate_pre.astype(bf16)
            dup_low = dup_pre.astype(bf16)
            dgate_seat = jnp.sum(hidden_low.astype(f32) * dhidden_raw, axis=-1)
            rows_grad = (rows_grad.astype(f32) * gate_seat).astype(bf16)

        def by_expert(array):
            return array.reshape(local_n, -1, array.shape[-1])

        def outer(one, other):
            return jnp.einsum(
                "esa,esb->eab", by_expert(one), by_expert(other), preferred_element_type=f32
            )

        if True:
            grad_gate_l = outer(rows_in, dgate_low)
            grad_up_l = outer(rows_in, dup_low)
            grad_down_l = outer(hidden_low, rows_grad)
            grad_gate_l = lax.psum_scatter(
                grad_gate_l.astype(bf16), DP, scatter_dimension=1, tiled=True
            ).astype(f32)
            grad_up_l = lax.psum_scatter(
                grad_up_l.astype(bf16), DP, scatter_dimension=1, tiled=True
            ).astype(f32)
            grad_down_l = lax.psum_scatter(
                grad_down_l.astype(bf16), DP, scatter_dimension=2, tiled=True
            ).astype(f32)
            expert_parts[l] = (grad_gate_l, grad_up_l, grad_down_l)

        if True:
            dexpert_in = (
                jnp.einsum("egsf,edf->egsd", dgate_low, w_gate[l], preferred_element_type=f32)
                + jnp.einsum("egsf,edf->egsd", dup_low, w_up[l], preferred_element_type=f32)
            ).astype(bf16)
            back_part = jnp.einsum(
                "gest,egsd->td", seat_all, dexpert_in, preferred_element_type=f32
            )
            dgates_part = jnp.sum(
                seat_all[0].astype(f32) * dgate_seat[:, 0, :, None], axis=1
            )
            mine = expert_here * local_n + jnp.arange(local_n, dtype=jnp.int32)
            lane = jnp.arange(experts_n, dtype=jnp.int32)
            dgates_part = jnp.sum(
                jnp.where(mine[:, None, None] == lane, dgates_part[..., None], 0.0), axis=0
            )
            dnormed_b, dgates = [
                lax.psum_scatter(part, EX, scatter_dimension=0, tiled=True)
                for part in (back_part, dgates_part)
            ]
        gates_token = gates_of(record["normed_b"], l, own_hit[l]).T
        dlogits = (
            gates_token * (dgates - jnp.sum(gates_token * dgates, axis=1, keepdims=True))
        ).astype(bf16)
        dnormed_b = dnormed_b + jnp.einsum(
            "te,de->td", dlogits, routers[l], preferred_element_type=f32
        )
        unused_norm, norm_pull = jax.vjp(rms_norm, record["mixed_sum"], gains[2 * l + 1])
        dmixed_part, dgain_b = norm_pull(dnormed_b)
        dmixed = grad_stream + dmixed_part
        grad_attn = dmixed.astype(bf16)
        attended_gradient = jnp.einsum(
            "td,qd->tq", grad_attn, out_full, preferred_element_type=f32
        ).astype(bf16)
        gathered_keys = record["key_all"]
        gathered_values = record["value_all"]
        scores, grouped_queries = masked_scores(record["queries"], gathered_keys, allowed)
        prob_float = jnp.exp(scores - record["log_total"])
        prob_low = prob_float.astype(bf16)
        grouped_gradient = attended_gradient.reshape(
            token_rows, KEY_VALUE_HEADS, QUERY_HEADS // KEY_VALUE_HEADS, HEAD_SIZE
        )
        dvalue_all = jnp.einsum(
            "kgts,tkgd->skd", prob_low, grouped_gradient, preferred_element_type=f32
        )
        dprobs = jnp.einsum(
            "tkgd,skd->kgts", grouped_gradient, gathered_values, preferred_element_type=f32
        )
        delta_row = jnp.sum(prob_float * dprobs, axis=-1, keepdims=True)
        dscores = (prob_float * (dprobs - delta_row)).astype(bf16)
        dqueries = (
            jnp.einsum(
                "kgts,skd->tkgd", dscores, gathered_keys, preferred_element_type=f32
            ).reshape(token_rows, QUERY_HEADS, HEAD_SIZE)
            * score_scale
        )
        dkey_all = (
            jnp.einsum("kgts,tkgd->skd", dscores, grouped_queries, preferred_element_type=f32)
            * score_scale
        )
        dkey_next, dvalue_next = from_behind(
            (dkey_all[:token_rows].astype(bf16), dvalue_all[:token_rows].astype(bf16)),
            everywhere,
            -1,
        )
        dkey_own = dkey_all[token_rows:] + dkey_next.astype(f32)
        dvalue_own = dvalue_all[token_rows:] + dvalue_next.astype(f32)
        dq_raw = apply_rotary(dqueries, cosine, -sine_part)
        dk_raw = apply_rotary(dkey_own, cosine, -sine_part)
        dprojected = jnp.concatenate(
            [
                dq_raw.reshape(token_rows, query_width),
                dk_raw.reshape(token_rows, key_width),
                dvalue_own.reshape(token_rows, key_width),
            ],
            axis=1,
        ).astype(bf16)
        dnormed_a = jnp.einsum("tq,dq->td", dprojected, qkv_full, preferred_element_type=f32)
        unused_first, first_pull = jax.vjp(rms_norm, record["stream_in"], gains[2 * l])
        dstream_part, dgain_a = first_pull(dnormed_a)
        grad_stream = dmixed + dstream_part

        small_grad = jnp.concatenate(
            [
                jnp.einsum("td,te->de", record["normed_b"], dlogits, preferred_element_type=f32),
                dgain_a[:, None],
                dgain_b[:, None],
            ],
            axis=1,
        )
        normed_a, attended = record["normed_a"], record["attended"]
        grad_qkv_l = jnp.einsum("td,tq->dq", normed_a, dprojected, preferred_element_type=f32)
        grad_out_l = jnp.einsum("tq,td->qd", attended, grad_attn, preferred_element_type=f32)
        weight_parts[l] = (grad_qkv_l, grad_out_l, small_grad)

    small_grads = jnp.concatenate([weight_parts[l][2] for l in range(layers_n)], axis=1)
    if True:

        def scatter(array):
            return lax.psum_scatter(array, everywhere, scatter_dimension=0, tiled=True)

        small_sum = scatter(small_grads)
        grad_qkv = jnp.stack([scatter(weight_parts[l][0]) for l in range(layers_n)])
        grad_out = jnp.stack([scatter(weight_parts[l][1]) for l in range(layers_n)])
    wide = experts_n + 2
    grad_router = jnp.stack(
        [small_sum[:, l * wide : l * wide + experts_n] for l in range(layers_n)]
    )
    grad_gains = jnp.stack(
        [
            jnp.swapaxes(small_sum[:, l * wide + experts_n : (l + 1) * wide], 0, 1)
            for l in range(layers_n)
        ]
    )
    if True:
        grad_gate, grad_up, grad_down = [
            jnp.stack([expert_parts[l][member] for l in range(layers_n)]) for member in range(3)
        ]
    layer_outs = jnp.stack(outputs).astype(bf16)
    return (
        layer_outs,
        grad_stream,
        grad_qkv,
        grad_out,
        grad_router,
        grad_gains,
        grad_gate,
        grad_up,
        grad_down,
    )


def solution(mesh):
    sizes = (mesh.shape[DP], mesh.shape[EX])
    return jax.shard_map(
        local_chips if sizes == (4, 8) else local,
        mesh=mesh,
        in_specs=(
            P((DP, EX), None),
            P(None, (DP, EX), None),
            P(None, (DP, EX), None),
            P(None, (DP, EX), None),
            P(None, None, (DP, EX)),
            P(None, EX, None, None),
            P(None, EX, None, None),
            P(None, EX, None, None),
            P((DP, EX), None),
            P((DP, EX)),
            P(None, (DP, EX), None),
            P(None, (DP, EX), None),
        ),
        out_specs=(
            P(None, (DP, EX), None),
            P((DP, EX), None),
            P(None, (DP, EX), None),
            P(None, (DP, EX), None),
            P(None, (DP, EX), None),
            P(None, None, (DP, EX)),
            P(None, EX, DP, None),
            P(None, EX, DP, None),
            P(None, EX, None, DP),
        ),
        check_vma=False,
    )
```
